32 devices in a mesh: dp: 8 (over y, x, core), expert: 4 (over z).
Axes of the slice: x: 2, y: 2, z: 4, core: 2. Of those that a mesh axis runs over, the one named last changes fastest.
Arguments:
- tokens: bfloat16 [16384, 768], P(('dp', 'expert')), may hold values from -6 to 6
- memory: bfloat16 [65536, 768], P(('dp', 'expert')), may hold values from -6 to 6
- target_mask: int32 [128, 128], P(('dp', 'expert')), may hold values from 0 to 1, as said below
- buckets: int32 [128, 128], replicated, may hold values from 0 to 31
- expert_ids: int32 [16384], P(('dp', 'expert')), may hold values from 0 to 3
- slots: int32 [16384], P(('dp', 'expert')), may hold values from 0 to 319, as said below
- gain_self: bfloat16 [768], replicated, may hold values from 0.5 to 1.5
- w_query: bfloat16 [768, 768], replicated, may hold values from -0.0546875 to 0.0546875
- w_key: bfloat16 [768, 768], replicated, may hold values from -0.21875 to 0.21875
- w_value: bfloat16 [768, 768], replicated, may hold values from -0.21875 to 0.21875
- w_output: bfloat16 [768, 768], replicated, may hold values from -0.625 to 0.625
- rel_table: bfloat16 [32, 12], replicated, may hold values from -4 to 4
- gain_cross: bfloat16 [768], replicated, may hold values from 0.5 to 1.5
- c_query: bfloat16 [768, 768], replicated, may hold values from -0.0546875 to 0.0546875
- c_key: bfloat16 [768, 768], replicated, may hold values from -0.21875 to 0.21875
- c_value: bfloat16 [768, 768], replicated, may hold values from -0.21875 to 0.21875
- c_output: bfloat16 [768, 768], replicated, may hold values from -0.875 to 0.875
- gain_moe: bfloat16 [768], replicated, may hold values from 0.5 to 1.5
- router: bfloat16 [768, 4], replicated, may hold values from -0.14941406 to 0.14941406
- expert_in: bfloat16 [4, 768, 3072], P('expert'), may hold values from -0.21875 to 0.21875
- expert_out: bfloat16 [4, 3072, 768], P('expert'), may hold values from -0.4375 to 0.4375
- cotangent: bfloat16 [16384, 768], P(('dp', 'expert')), may hold values from -6 to 6
Outputs:
- output: bfloat16 [16384, 768], P(('dp', 'expert'))
- grad_tokens: float32 [16384, 768], P(('dp', 'expert'))
- grad_memory: bfloat16 [65536, 768], P(('dp', 'expert'))
- grad_gain_self: float32 [768], replicated
- grad_w_query: float32 [768, 768], replicated
- grad_w_key: float32 [768, 768], replicated
- grad_w_value: float32 [768, 768], replicated
- grad_w_output: float32 [768, 768], replicated
- grad_rel_table: float32 [32, 12], replicated
- grad_gain_cross: float32 [768], replicated
- grad_c_query: float32 [768, 768], replicated
- grad_c_key: float32 [768, 768], replicated
- grad_c_value: float32 [768, 768], replicated
- grad_c_output: float32 [768, 768], replicated
- grad_gain_moe: float32 [768], replicated
- grad_router: float32 [768, 4], replicated
- grad_expert_in: float32 [4, 768, 3072], P('expert', None, 'dp')
- grad_expert_out: float32 [4, 3072, 768], P('expert', 'dp')
The draws below stay inside these ranges and needn't reach their ends.
Inputs may be any that keep to these rules, and one draw needn't show every extreme that they name: `target_mask`: each target's ones form a leading run of its slots; every device's 4 targets include one with all 128 slots true. Within one device's 512 tokens, the tokens that name one expert hold the slots 0, 1, 2, ... once each; a token is kept when its slot is below 160.
All inputs are finite; a program needn't handle non-finite values.
Results may differ from the reference program's by a relative error of at most 0.022.
The reference program's roundings to bfloat16 on the way count: a program that leaves them out, or rounds other values in their place, can miss the bound.
Values may be sent and summed in bfloat16 or wider, within the bound.
A program may use at most 256 MiB of HBM per device.

```python
import jax
import jax.numpy as jnp
from jax import lax

D = 768
HEADS = 12
HEAD_DIM = 64
FF = 3072
BUCKETS = 32
TLEN = 128
MLEN = 512
SEQ_DEV = 4
EXP_DEV = 1
EXPERTS = 4
TOK_DEV = 512
TARGETS = 128
TOKENS = 16384
CAP = 160


def routing(key):
    blocks = TOKENS // TOK_DEV
    group = EXPERTS // EXP_DEV
    key_heavy, key_other, key_pick, key_order = jax.random.split(key, 4)
    heavy = jax.random.randint(key_heavy, (blocks // group,), 0, EXPERTS)
    heavy = jnp.repeat(heavy, group)[:, None]
    others = jax.random.randint(key_other, (blocks, TOK_DEV), 1, EXPERTS)
    picks = jax.vmap(lambda k: jax.random.permutation(k, TOK_DEV))(jax.random.split(key_pick, blocks))
    chosen = picks < 2 * CAP
    expert_ids = jnp.where(chosen, heavy, (heavy + others) % EXPERTS).astype(jnp.int32)
    priority = jax.vmap(lambda k: jax.random.permutation(k, TOK_DEV))(jax.random.split(key_order, blocks))
    sort_key = expert_ids * TOK_DEV + priority.astype(jnp.int32)
    order = jnp.argsort(sort_key, axis=1)
    placed = jnp.argsort(order, axis=1).astype(jnp.int32)
    counts = jnp.sum((expert_ids[:, :, None] == jnp.arange(EXPERTS, dtype=jnp.int32)[None, None, :]).astype(jnp.int32), axis=1)
    starts = jnp.cumsum(counts, axis=1) - counts
    first = jnp.take_along_axis(starts, expert_ids, axis=1)
    slots = (placed - first).astype(jnp.int32)
    return (expert_ids.reshape(-1), slots.reshape(-1))


def draw_expert_ids(key, part):
    shared = routing(key)
    return shared[0]


def draw_slots(key, part):
    shared = routing(key)
    return shared[1]


def draw_target_mask(key, part):
    key = jax.random.fold_in(key, 5)
    key_len, key_full = jax.random.split(key)
    lengths = jax.random.randint(key_len, (TARGETS,), 1, TLEN + 1)
    devices = TARGETS // SEQ_DEV
    full = jax.random.randint(key_full, (devices,), 0, SEQ_DEV) + jnp.arange(devices, dtype=jnp.int32) * SEQ_DEV
    lengths = lengths.at[full].set(TLEN)
    return (jnp.arange(TLEN, dtype=jnp.int32)[None, :] < lengths[:, None]).astype(jnp.int32)


def set_ends(drawn, stream_key, low, top_value):
    shape = drawn.shape
    spot = [jax.random.randint(jax.random.fold_in(stream_key, axis), (), 0, shape[axis]) for axis in range(len(shape))]
    drawn = drawn.at[tuple(spot)].set(low)
    longest = shape.index(max(shape))
    spot[longest] = (spot[longest] + 1) % shape[longest]
    return drawn.at[tuple(spot)].set(top_value)


def shard_levels(stream_key, extent, cuts, low, top_value):
    def one(axis_at, shards_of):
        draws = jax.random.uniform(jax.random.fold_in(jax.random.fold_in(stream_key, 6), axis_at), (shards_of,), jnp.float32, low / len(cuts), top_value / len(cuts))
        return jnp.repeat(jnp.exp(draws), extent[axis_at] // shards_of).reshape((-1,) + (1,) * (len(extent) - axis_at - 1))

    factor_of = one(*cuts[0])
    for cut in cuts[1:]:
        factor_of = factor_of * one(*cut)
    return factor_of


def noise(stream_key, extent, scale, reach, cuts=(), kind=jnp.bfloat16):
    level = shard_levels(stream_key, extent, cuts, -0.22, 0.18) if cuts else 1.0
    values = jax.random.normal(stream_key, extent, jnp.float32) * scale * level
    return jnp.minimum(jnp.maximum(values, -reach), reach).astype(kind)


def setup_inputs(seed: int = 0) -> dict:
    keys = jax.random.split(jax.random.key(seed), 23)
    return {
        "tokens": noise(keys[0], (TOKENS, D), 1.0, 6.0, ((0, 32),)),
        "memory": noise(keys[1], (TARGETS * MLEN, D), 1.0, 6.0, ((0, 32),)),
        "target_mask": draw_target_mask(jax.random.fold_in(keys[22], 71), 0),
        "buckets": set_ends(jax.random.randint(keys[3], (TLEN, TLEN), 0, BUCKETS), jax.random.fold_in(keys[3], 1), 0, BUCKETS - 1).astype(jnp.int32),
        "expert_ids": draw_expert_ids(jax.random.fold_in(keys[22], 71), 0),
        "slots": draw_slots(jax.random.fold_in(keys[22], 71), 0),
        "gain_self": jnp.clip(1.0 + 0.1 * jax.random.normal(keys[6], (D,), jnp.float32), 0.5, 1.5).astype(jnp.bfloat16),
        "w_query": noise(keys[7], (D, D), (16 * D) ** -0.5, 0.0546875),
        "w_key": noise(keys[8], (D, D), D ** -0.5, 0.21875),
        "w_value": noise(keys[9], (D, D), D ** -0.5, 0.21875),
        "w_output": noise(keys[10], (D, D), (D // 8) ** -0.5, 0.625),
        "rel_table": noise(keys[11], (BUCKETS, HEADS), 1.0, 4.0),
        "gain_cross": jnp.clip(1.0 + 0.1 * jax.random.normal(keys[12], (D,), jnp.float32), 0.5, 1.5).astype(jnp.bfloat16),
        "c_query": noise(keys[13], (D, D), (16 * D) ** -0.5, 0.0546875),
        "c_key": noise(keys[14], (D, D), D ** -0.5, 0.21875),
        "c_value": noise(keys[15], (D, D), D ** -0.5, 0.21875),
        "c_output": noise(keys[16], (D, D), (D // 16) ** -0.5, 0.875),
        "gain_moe": jnp.clip(1.0 + 0.1 * jax.random.normal(keys[17], (D,), jnp.float32), 0.5, 1.5).astype(jnp.bfloat16),
        "router": noise(keys[18], (D, EXPERTS), 0.025, 0.14941406),
        "expert_in": noise(keys[19], (EXPERTS, D, FF), D ** -0.5, 0.21875, ((0, 4),)),
        "expert_out": noise(keys[20], (EXPERTS, FF, D), (FF // (EXPERTS * EXPERTS)) ** -0.5, 0.4375, ((0, 4),)),
        "cotangent": noise(keys[21], (TOKENS, D), 1.0, 6.0, ((0, 32),)),
    }


@jax.custom_vjp
def low(v):
    return lax.optimization_barrier(v.astype(jnp.bfloat16)).astype(jnp.float32)

@jax.custom_vjp
def low_back(v):
    return v

def low_keep(v):
    return (low(v), None)

def low_pass(kept, grad):
    return (grad,)

def back_keep(v):
    return (v, None)

def back_low(kept, grad):
    return (low(grad),)
low.defvjp(low_keep, low_pass)
low_back.defvjp(back_keep, back_low)
EPS = 1e-06
NEG = -1000000000.0

def product(left, right):
    return jnp.dot(left, right, precision=lax.Precision.HIGHEST)

def normed(values, gain):
    return values * lax.rsqrt(lax.optimization_barrier(jnp.mean(values * values, axis=-1, keepdims=True)) + EPS) * gain

def split_heads(values, count):
    return values.reshape(count, -1, HEADS, HEAD_DIM)

def attend(queries, keys_in, values, bias, allowed):
    scores = low_back(jnp.einsum('sqhd,skhd->shqk', queries, keys_in, precision=lax.Precision.HIGHEST) + bias)
    scores = jnp.where(allowed, scores, NEG)
    top = lax.optimization_barrier(jnp.max(scores, axis=-1, keepdims=True))
    expo = jnp.exp(scores - top)
    weights = expo / lax.optimization_barrier(jnp.sum(expo, axis=-1, keepdims=True))
    context = jnp.einsum('shqk,skhd->sqhd', low(weights), values, precision=lax.Precision.HIGHEST)
    return low_back(low(context))

def reference(tokens, memory, target_mask, buckets, expert_ids, slots, gain_self, w_query, w_key, w_value, w_output, rel_table, gain_cross, c_query, c_key, c_value, c_output, gain_moe, router, expert_in, expert_out, cotangent):
    blocks = TOKENS // TOK_DEV
    keep = (slots < CAP).astype(jnp.float32)
    rows = jnp.arange(TOKENS, dtype=jnp.int32) // TOK_DEV * CAP + jnp.minimum(slots, CAP - 1)
    picked = (expert_ids[:, None] == jnp.arange(EXPERTS, dtype=jnp.int32)[None, :]).astype(jnp.float32)
    spots = jnp.arange(TLEN, dtype=jnp.int32)
    causal = spots[None, :] <= spots[:, None]
    allowed = causal[None, None] & (target_mask[:, None, None, :] == 1)
    allowed = allowed.reshape(blocks, SEQ_DEV, 1, TLEN, TLEN)

    def layer(x, mem, g_one, wq, wk, wv, wo, table, g_two, cq, ck, cv, co, g_three, wr, w_first, w_second):
        bias = jnp.transpose(table[buckets], (2, 0, 1))[None]

        def self_block(pieces):
            rows_in, mask_here = pieces
            hidden = low(normed(rows_in, g_one))
            queries = low_back(low(product(hidden, wq)))
            keys_in = low_back(low(product(hidden, wk)))
            values = low_back(low(product(hidden, wv)))
            context = attend(split_heads(queries, SEQ_DEV), split_heads(keys_in, SEQ_DEV), split_heads(values, SEQ_DEV), bias, mask_here)
            return rows_in + low_back(product(context.reshape(TOK_DEV, D), wo))
        x_one = lax.map(jax.checkpoint(self_block), (x.reshape(blocks, TOK_DEV, D), allowed)).reshape(TOKENS, D)

        def cross_block(pieces):
            rows_in, mem_rows = pieces
            hidden = low(normed(rows_in, g_two))
            queries = low_back(low(product(hidden, cq)))
            keys_in = low_back(low(product(mem_rows, ck)))
            values = low_back(low(product(mem_rows, cv)))
            context = attend(split_heads(queries, SEQ_DEV), split_heads(keys_in, SEQ_DEV), split_heads(values, SEQ_DEV), 0.0, True)
            return rows_in + low_back(product(context.reshape(TOK_DEV, D), co))
        x_two = lax.map(jax.checkpoint(cross_block), (x_one.reshape(blocks, TOK_DEV, D), mem.reshape(blocks, SEQ_DEV * MLEN, D))).reshape(TOKENS, D)
        hidden = low(normed(x_two, g_three))
        logits = product(hidden, wr)
        logits = logits - lax.optimization_barrier(jnp.max(logits, axis=-1, keepdims=True))
        expo = jnp.exp(logits)
        probs = expo / lax.optimization_barrier(jnp.sum(expo, axis=-1, keepdims=True))
        gate = lax.optimization_barrier(jnp.sum(probs * picked, axis=-1)) * keep
        sent = low_back(hidden) * keep[:, None]
        inbound = jnp.zeros((EXPERTS, blocks * CAP, D), jnp.float32).at[expert_ids, rows].add(sent)
        pre = low_back(jnp.einsum('erd,edf->erf', inbound, w_first, precision=lax.Precision.HIGHEST))
        act = low(jax.nn.gelu(pre))
        result = low_back(low(jnp.einsum('erf,efd->erd', act, w_second, precision=lax.Precision.HIGHEST)))
        back = result[expert_ids, rows]
        return x_two + gate[:, None] * back
    primals = (tokens.astype(jnp.float32), memory.astype(jnp.float32), gain_self.astype(jnp.float32), w_query.astype(jnp.float32), w_key.astype(jnp.float32), w_value.astype(jnp.float32), w_output.astype(jnp.float32), rel_table.astype(jnp.float32), gain_cross.astype(jnp.float32), c_query.astype(jnp.float32), c_key.astype(jnp.float32), c_value.astype(jnp.float32), c_output.astype(jnp.float32), gain_moe.astype(jnp.float32), router.astype(jnp.float32), expert_in.astype(jnp.float32), expert_out.astype(jnp.float32))
    final, pullback = jax.vjp(layer, *primals)
    grads = pullback(cotangent.astype(jnp.float32))
    return (final.astype(jnp.bfloat16), grads[0], grads[1].astype(jnp.bfloat16), grads[2], grads[3], grads[4], grads[5], grads[6], grads[7], grads[8], grads[9], grads[10], grads[11], grads[12], grads[13], grads[14], grads[15], grads[16])
```

```python
import functools

import jax
import jax.numpy as jnp
from jax import lax
from jax.experimental import pallas as pl
from jax.experimental.pallas import tpu as pltpu
from jax.sharding import PartitionSpec as P

EPS = 1e-06
NEG = -1000000000.0
F32 = jnp.float32
BF16 = jnp.bfloat16
LANES = 128
VMEM_LIMIT = 60 * 1024 * 1024
ANY = pl.BlockSpec(memory_space=pl.ANY)
VMEM = pl.BlockSpec(memory_space=pltpu.VMEM)
SMEM = pl.BlockSpec(memory_space=pltpu.SMEM)


def dot(left, right):
    return lax.dot_general(left, right, (((1,), (0,)), ((), ())), preferred_element_type=F32)


def dot_nt(left, right):
    return lax.dot_general(left, right, (((1,), (1,)), ((), ())), preferred_element_type=F32)


def dot_tn(left, right):
    return lax.dot_general(left, right, (((0,), (0,)), ((), ())), preferred_element_type=F32)


def row_loop(count, step, body):
    def one(i, carry):
        body(pl.ds(pl.multiple_of(i * step, step), step))
        return carry

    lax.fori_loop(0, count // step, one, 0)


def half_masks():
    lane = lax.broadcasted_iota(jnp.int32, (1, LANES), 1)
    low = jnp.where(lane < LANES // 2, 1.0, 0.0).astype(BF16)
    high = jnp.where(lane < LANES // 2, 0.0, 1.0).astype(BF16)
    return lane < LANES // 2, low, high


def stacked(pair, low, high):
    return jnp.concatenate([pair * low, pair * high], axis=0)


def norm_rows(values, gain):
    return values * lax.rsqrt(jnp.mean(values * values, axis=-1, keepdims=True) + EPS) * gain


def norm_back(values, gain, grad):
    scale = lax.rsqrt(jnp.mean(values * values, axis=-1, keepdims=True) + EPS)
    scaled = grad * gain
    inner = jnp.mean(scaled * values, axis=-1, keepdims=True)
    back = scale * scaled - values * (scale * scale * scale * inner)
    gain_rows = grad * values * scale
    return back, jnp.sum(gain_rows.reshape(-1, 8, gain_rows.shape[-1]), axis=0)


def allowed_of(mask_row, length):
    row = lax.broadcasted_iota(jnp.int32, (length, length), 0)
    col = lax.broadcasted_iota(jnp.int32, (length, length), 1)
    return (col <= row) & (mask_row == 1)


class Loads:
    def __init__(self, sems):
        self.sems = sems
        self.count = 0
        self.open = {}

    def start(self, name, source, target):
        copy = pltpu.make_async_copy(source, target, self.sems.at[self.count])
        self.count += 1
        copy.start()
        self.open[name] = copy

    def wait(self, *names):
        for name in names:
            self.open.pop(name).wait()

    def drain(self):
        self.wait(*list(self.open))


def forward_kernel(
    targets, length, memory_length, heads, table, tokens, memory, mask, buckets, gains, place, wq, wk, wv, wo, cq, ck, cv, co,
    h1_out, q1_out, k1_out, v1_out, c1_out, h2_out, q2_out, c2_out, x1_out, x2_out, p1_out, p2_out, k2_out, v2_out, sent_out,
    tokens_v, memory_v, weights_v, h1, q1, k1, v1, c1, h2, q2, c2, x1, x2, p1, p2, k2, v2, sent, bias, scores, in_sems, out_sems,
):
    rows, width = tokens_v.shape
    pairs = heads // 2
    loads, stores = Loads(in_sems), Loads(out_sems)
    loads.start("tokens", tokens, tokens_v)
    for index, (name, ref) in enumerate(zip(("wq", "wk", "wv"), (wq, wk, wv))):
        loads.start(name, ref, weights_v.at[index])
    loads.start("ck", ck, weights_v.at[5])
    loads.start("memory", memory, memory_v)
    loads.start("cv", cv, weights_v.at[6])
    loads.start("wo", wo, weights_v.at[3])
    loads.start("cq", cq, weights_v.at[4])
    loads.start("co", co, weights_v.at[7])
    gain = [gains[i : i + 1, :] for i in range(3)]
    low_lane, low, high = half_masks()

    bucket_count = table.shape[0]

    def bias_rows(r):
        here = buckets[r, :]
        hits = [here == b for b in range(bucket_count)]
        for head in range(heads):
            total = jnp.zeros(here.shape, F32)
            for b in range(bucket_count):
                total = jnp.where(hits[b], table[b, head], total)
            start = (head % 2) * length
            bias[head // 2, pl.ds(pl.multiple_of(r.start + start, 8), r.size), :] = total

    row_loop(length, 16, bias_rows)

    loads.wait("tokens")

    def first_norm(r):
        h1[r, :] = norm_rows(tokens_v[r, :].astype(F32), gain[0]).astype(BF16)

    row_loop(rows, 32, first_norm)
    stores.start("h1", h1, h1_out)
    for index, (name, ref) in enumerate(zip(("wq", "wk", "wv"), (q1, k1, v1))):
        loads.wait(name)

        def project(r, index=index, ref=ref):
            ref[r, :] = dot(h1[r, :], weights_v[index]).astype(BF16)

        row_loop(rows, 256, project)
    stores.start("q1", q1, q1_out)
    stores.start("k1", k1, k1_out)
    stores.start("v1", v1, v1_out)

    def self_target(t, carry):
        r = pl.ds(pl.multiple_of(t * length, length), length)
        allowed = allowed_of(mask[pl.ds(t, 1), :], length)
        for pair in range(pairs):
            lanes = slice(pair * LANES, (pair + 1) * LANES)
            both = dot_nt(stacked(q1[r, lanes], low, high), k1[r, lanes])
            for half in range(2):
                part = slice(half * length, (half + 1) * length)
                score = jnp.where(allowed, both[part] + bias[pair, part, :], NEG)
                expo = jnp.exp(score - jnp.max(score, axis=-1, keepdims=True))
                total = jnp.sum(expo, axis=-1, keepdims=True)
                p1[t, pair, part, :] = (expo / total).astype(BF16)
            context = dot(p1[t, pair], v1[r, lanes])
            c1[r, lanes] = jnp.where(low_lane, context[:length], context[length:]).astype(BF16)
        return carry

    lax.fori_loop(0, targets, self_target, 0)
    stores.start("p1", p1, p1_out)
    stores.start("c1", c1, c1_out)
    loads.wait("wo")

    def self_out(r):
        x1[r, :] = tokens_v[r, :].astype(F32) + dot(c1[r, :], weights_v[3])

    row_loop(rows, 256, self_out)
    stores.start("x1", x1, x1_out)

    def second_norm(r):
        h2[r, :] = norm_rows(x1[r, :], gain[1]).astype(BF16)

    row_loop(rows, 32, second_norm)
    stores.start("h2", h2, h2_out)
    loads.wait("cq")

    def cross_query(r):
        q2[r, :] = dot(h2[r, :], weights_v[4]).astype(BF16)

    row_loop(rows, 256, cross_query)
    stores.start("q2", q2, q2_out)
    loads.wait("memory", "ck", "cv")

    def cross_keys(r):
        k2[r, :] = dot(memory_v[r, :], weights_v[5]).astype(BF16)
        v2[r, :] = dot(memory_v[r, :], weights_v[6]).astype(BF16)

    row_loop(targets * memory_length, 256, cross_keys)
    stores.start("k2", k2, k2_out)
    stores.start("v2", v2, v2_out)

    def cross_target(t, carry):
        r = pl.ds(pl.multiple_of(t * length, length), length)
        m = pl.ds(pl.multiple_of(t * memory_length, memory_length), memory_length)
        for pair in range(pairs):
            lanes = slice(pair * LANES, (pair + 1) * LANES)
            slot = pair % 2
            scores[slot] = dot_nt(stacked(q2[r, lanes], low, high), k2[m, lanes])
            for chunk in range(2 * length // 32):
                part = slice(chunk * 32, (chunk + 1) * 32)
                score = scores[slot, part, :]
                expo = jnp.exp(score - jnp.max(score, axis=-1, keepdims=True))
                total = jnp.sum(expo, axis=-1, keepdims=True)
                p2[t, pair, part, :] = (expo / total).astype(BF16)
            context = dot(p2[t, pair], v2[m, lanes])
            c2[r, lanes] = jnp.where(low_lane, context[:length], context[length:]).astype(BF16)
        return carry

    lax.fori_loop(0, targets, cross_target, 0)
    stores.start("p2", p2, p2_out)
    stores.start("c2", c2, c2_out)
    loads.wait("co")

    def cross_out(r):
        x2[r, :] = x1[r, :] + dot(c2[r, :], weights_v[7])

    row_loop(rows, 256, cross_out)
    stores.start("x2", x2, x2_out)

    def third_norm(r):
        tokens_v[r, :] = norm_rows(x2[r, :], gain[2]).astype(BF16)

    row_loop(rows, 32, third_norm)
    dispatch(place, tokens_v, sent)
    stores.start("sent", sent, sent_out)
    stores.drain()


def dispatch(place, source, target):
    step = 128

    def one(r):
        spot = lax.broadcasted_iota(jnp.int32, (step, source.shape[0]), 0) + r.start
        hit = jnp.where(spot == place[...], 1.0, 0.0).astype(BF16)
        target[r, :] = dot(hit, source[...]).astype(target.dtype)

    row_loop(target.shape[0], step, one)


def collect(place_column, step, r, source):
    spot = lax.broadcasted_iota(jnp.int32, (step, source.shape[0]), 1)
    hit = jnp.where(spot == place_column[r, :], 1.0, 0.0).astype(BF16)
    return dot(hit, source[...])


def dispatch_kernel(place, source, target):
    dispatch(place, source, target)


def output_kernel(place_column, x2, rows, out):
    def one(r):
        out[r, :] = (x2[r, :] + collect(place_column, 128, r, rows)).astype(BF16)

    row_loop(out.shape[0], 128, one)


def expert_kernel(
    experts, inbound, grows, router, first, second,
    ret_out, dh_out, grad_first, grad_second, grad_router,
    first_v, second_v, inbound_t, dret, dret_t, probs, pre, dact, act, dpre, ret, dinb, gf, gs, in_sems, out_sems,
):
    rows, width = inbound.shape
    hidden = first.shape[1]
    step = width
    loads = Loads(in_sems)
    for f in range(hidden // step):
        cols = slice(f * step, (f + 1) * step)
        loads.start(("first", f), first.at[:, cols], first_v.at[:, cols])
        loads.start(("second", f), second.at[cols, :], second_v.at[cols, :])
    me = lax.axis_index("expert")
    lane = lax.broadcasted_iota(jnp.int32, (1, LANES), 1)
    mine = lane == me

    def route(r):
        logits = jnp.where(lane < experts, dot(inbound[r, :], router[...]), -1e30)
        expo = jnp.exp(logits - jnp.max(logits, axis=-1, keepdims=True))
        prob = expo / jnp.sum(expo, axis=-1, keepdims=True)
        probs[r, :] = prob
        gate = jnp.sum(jnp.where(mine, prob, 0.0), axis=-1, keepdims=True)
        dret[r, :] = (gate * grows[r, :].astype(F32)).astype(BF16)

    row_loop(rows, 128, route)
    for c in range(width // LANES):
        cols = slice(c * LANES, (c + 1) * LANES)
        inbound_t[cols, :] = inbound[:, cols].T
        dret_t[cols, :] = dret[:, cols].T

    stores = Loads(out_sems)
    root = (2.0 / jnp.pi) ** 0.5
    for f in range(hidden // step):
        cols = slice(f * step, (f + 1) * step)
        loads.wait(("first", f), ("second", f))
        slot = f % 2

        def up(r, cols=cols):
            pre[r, :] = dot(inbound[r, :], first_v[:, cols])
            dact[r, :] = dot_nt(dret[r, :], second_v[cols, :])

        row_loop(rows, 128, up)

        def middle(r):
            u = pre[r, :]
            square = u * u
            t = jnp.tanh(root * (u + 0.044715 * (square * u)))
            half = 0.5 * (1.0 + t)
            act[r, :] = (u * half).astype(BF16)
            slope = half + (0.5 * root) * u * (1.0 - t * t) * (1.0 + (3 * 0.044715) * square)
            dpre[r, :] = (dact[r, :] * slope).astype(BF16)

        row_loop(rows, 16, middle)

        def down(r, cols=cols, f=f):
            one, two = dot(act[r, :], second_v[cols, :]), dot_nt(dpre[r, :], first_v[:, cols])
            if f:
                one, two = one + ret[r, :], two + dinb[r, :]
            ret[r, :] = one
            dinb[r, :] = two

        row_loop(rows, 128, down)
        if f >= 2:
            stores.wait(("first", f - 2), ("second", f - 2))

        def weights(r, slot=slot):
            gf[slot, r, :] = dot(inbound_t[r, :], dpre[...]).astype(BF16)
            gs[slot, r, :] = dot(dret_t[r, :], act[...]).astype(BF16)

        row_loop(width, 256, weights)
        stores.start(("first", f), gf.at[slot], grad_first.at[:, cols])
        stores.start(("second", f), gs.at[slot], grad_second.at[:, cols])

    grad_router[...] = jnp.zeros_like(grad_router)

    def finish(r):
        result = ret[r, :].astype(BF16).astype(F32)
        prob = probs[r, :]
        gate = jnp.sum(jnp.where(mine, prob, 0.0), axis=-1, keepdims=True)
        dgate = jnp.sum(result * grows[r, :].astype(F32), axis=-1, keepdims=True)
        dlogits = (prob * (jnp.where(mine, 1.0, 0.0) - gate) * dgate).astype(BF16)
        ret_out[r, :] = (gate * result).astype(BF16)
        dh_out[r, :] = (dinb[r, :].astype(BF16).astype(F32) + dot_nt(dlogits, router[...])).astype(BF16)
        grad_router[...] += dot_tn(dlogits, inbound[r, :])

    row_loop(rows, 128, finish)
    stores.drain()


def backward_kernel(
    targets, length, memory_length, heads,
    dh_rows, place_column, mask, buckets, gains, cotangent, tokens, h1, q1, k1, v1, c1, h2, q2, c2, x1, x2, p1, p2, k2, v2, memory,
    wq, wk, wv, wo, cq, ck, cv, co,
    grads_out, grad_tokens_out, grad_memory_out, gain_grads, table_out,
    rows_v, tokens_v, cot_v, h1_v, q1_v, k1_v, v1_v, c1_v, h2_v, q2_v, c2_v, x1_v, x2_v, p1_v, weights_v,
    p2_v, k2_v, v2_v, mem_v, gmem_v, dx, du, do, dctx, dq, dk, dv, dk2, dv2, gk, gv, grads, dscores, ds, dsum, gain_acc,
    in_sems, out_sems, ring_sems, gmem_sems,
):
    rows, width = tokens_v.shape
    pairs = heads // 2
    loads, stores = Loads(in_sems), Loads(out_sems)
    loads.start("rows", dh_rows, rows_v)
    loads.start("cot", cotangent, cot_v)
    loads.start("x2", x2, x2_v)
    loads.start("c2", c2, c2_v)
    loads.start("co", co, weights_v.at[7])

    def ring(t, slot, action):
        m = pl.ds(pl.multiple_of(t * memory_length, memory_length), memory_length)
        for index, (source, target) in enumerate(((p2.at[t], p2_v), (k2.at[m, :], k2_v), (v2.at[m, :], v2_v), (memory.at[m, :], mem_v))):
            copy = pltpu.make_async_copy(source, target.at[slot], ring_sems.at[index, slot])
            if action == "start":
                copy.start()
            else:
                copy.wait()

    ring(0, 0, "start")
    for name, source, target in (
        ("q2", q2, q2_v), ("ck", ck, weights_v.at[5]), ("cv", cv, weights_v.at[6]), ("cq", cq, weights_v.at[4]), ("h2", h2, h2_v),
        ("x1", x1, x1_v), ("c1", c1, c1_v), ("wo", wo, weights_v.at[3]), ("p1", p1, p1_v), ("q1", q1, q1_v), ("k1", k1, k1_v),
        ("v1", v1, v1_v), ("h1", h1, h1_v), ("wq", wq, weights_v.at[0]), ("wk", wk, weights_v.at[1]), ("wv", wv, weights_v.at[2]),
        ("tokens", tokens, tokens_v),
    ):
        loads.start(name, source, target)
    gain = [gains[i : i + 1, :] for i in range(3)]
    low_lane, low, high = half_masks()
    gain_acc[...] = jnp.zeros_like(gain_acc)

    def inner_grad(index, left, right):
        for c in range(width // 256):
            cols = slice(c * 256, (c + 1) * 256)
            grads[index, cols, :] = dot_tn(left[:, cols], right[...]).astype(BF16)
        stores.start(("grad", index), grads.at[index], grads_out.at[index])

    def back_through(values, index, base, target):
        def one(r):
            back, gain_rows = norm_back(values[r, :].astype(F32), gain[index], du[r, :])
            total = base[r, :].astype(F32) + back
            target[r, :] = total
            do[r, :] = total.astype(BF16)
            gain_acc[index] += gain_rows

        row_loop(rows, 32, one)

    loads.wait("rows", "cot", "x2")

    def gather(r):
        du[r, :] = collect(place_column, 128, r, rows_v)

    row_loop(rows, 128, gather)
    back_through(x2_v, 2, cot_v, dx)
    loads.wait("c2", "co")
    inner_grad(7, c2_v, do)

    def out_back(r, index):
        dctx[r, :] = dot_nt(do[r, :], weights_v[index]).astype(BF16)

    row_loop(rows, 256, functools.partial(out_back, index=7))
    loads.wait("q2", "ck", "cv")

    def cross_target(t, carry):
        slot = lax.rem(t, 2)

        @pl.when(t + 1 < targets)
        def _():
            ring(t + 1, 1 - slot, "start")

        ring(t, slot, "wait")
        r = pl.ds(pl.multiple_of(t * length, length), length)
        for pair in range(pairs):
            lanes = slice(pair * LANES, (pair + 1) * LANES)
            side = pair % 2
            grad_rows = stacked(dctx[r, lanes], low, high)
            dscores[side] = dot_nt(grad_rows, v2_v[slot, :, lanes])
            for chunk in range(2 * length // 32):
                part = slice(chunk * 32, (chunk + 1) * 32)
                prob = p2_v[slot, pair, part, :].astype(F32)
                dprob = dscores[side, part, :]
                inner = jnp.sum(prob * dprob, axis=-1, keepdims=True)
                ds[side, part, :] = (prob * (dprob - inner)).astype(BF16)
            dv2[:, lanes] = dot_tn(p2_v[slot, pair], grad_rows).astype(BF16)
            dk2[:, lanes] = dot_tn(ds[side], stacked(q2_v[r, lanes], low, high)).astype(BF16)
            back = dot(ds[side], k2_v[slot, :, lanes])
            dq[r, lanes] = jnp.where(low_lane, back[:length], back[length:]).astype(BF16)
        for c in range(width // 256):
            cols = slice(c * 256, (c + 1) * 256)
            one = dot_tn(mem_v[slot, :, cols], dk2[...])
            two = dot_tn(mem_v[slot, :, cols], dv2[...])
            first = t == 0
            gk[cols, :] = jnp.where(first, one, gk[cols, :] + one)
            gv[cols, :] = jnp.where(first, two, gv[cols, :] + two)

        m = pl.ds(pl.multiple_of(t * memory_length, memory_length), memory_length)
        out = pltpu.make_async_copy(gmem_v.at[slot], grad_memory_out.at[m, :], gmem_sems.at[slot])

        @pl.when(t >= 2)
        def _():
            out.wait()

        def memory_rows(q):
            gmem_v[slot, q, :] = (dot_nt(dk2[q, :], weights_v[5]) + dot_nt(dv2[q, :], weights_v[6])).astype(BF16)

        row_loop(memory_length, 256, memory_rows)
        out.start()
        return carry

    lax.fori_loop(0, targets, cross_target, 0)
    for slot in range(min(2, targets)):
        pltpu.make_async_copy(gmem_v.at[slot], grad_memory_out.at[pl.ds(0, memory_length), :], gmem_sems.at[slot]).wait()
    grads[5] = gk[...].astype(BF16)
    stores.start(("grad", 5), grads.at[5], grads_out.at[5])
    grads[6] = gv[...].astype(BF16)
    stores.start(("grad", 6), grads.at[6], grads_out.at[6])
    loads.wait("h2", "cq", "x1")
    inner_grad(4, h2_v, dq)

    def query_back(r):
        du[r, :] = dot_nt(dq[r, :], weights_v[4])

    row_loop(rows, 256, query_back)
    back_through(x1_v, 1, dx, dx)
    loads.wait("c1", "wo")
    inner_grad(3, c1_v, do)
    row_loop(rows, 256, functools.partial(out_back, index=3))
    loads.wait("p1", "q1", "k1", "v1")

    def self_target(t, carry):
        r = pl.ds(pl.multiple_of(t * length, length), length)
        allowed = allowed_of(mask[pl.ds(t, 1), :], length)
        for pair in range(pairs):
            lanes = slice(pair * LANES, (pair + 1) * LANES)
            side = pair % 2
            grad_rows = stacked(dctx[r, lanes], low, high)
            both = dot_nt(grad_rows, v1_v[r, lanes])
            for half in range(2):
                part = slice(half * length, (half + 1) * length)
                prob = p1_v[t, pair, part, :].astype(F32)
                dprob = both[part]
                inner = jnp.sum(prob * dprob, axis=-1, keepdims=True)
                score = jnp.where(allowed, prob * (dprob - inner), 0.0).astype(BF16)
                ds[side, part, :length] = score
                dsum[pair, part, :] = jnp.where(t == 0, 0.0, dsum[pair, part, :]) + score.astype(F32)
            dv[r, lanes] = dot_tn(p1_v[t, pair], grad_rows).astype(BF16)
            dk[r, lanes] = dot_tn(ds[side, :, :length], stacked(q1_v[r, lanes], low, high)).astype(BF16)
            back = dot(ds[side, :, :length], k1_v[r, lanes])
            dq[r, lanes] = jnp.where(low_lane, back[:length], back[length:]).astype(BF16)
        return carry

    lax.fori_loop(0, targets, self_target, 0)
    loads.wait("h1", "wq", "wk", "wv", "tokens")
    inner_grad(0, h1_v, dq)
    inner_grad(1, h1_v, dk)
    inner_grad(2, h1_v, dv)

    def self_back(r):
        du[r, :] = dot_nt(dq[r, :], weights_v[0]) + dot_nt(dk[r, :], weights_v[1]) + dot_nt(dv[r, :], weights_v[2])

    row_loop(rows, 256, self_back)
    back_through(tokens_v, 0, dx, dx)
    stores.start("tokens", dx, grad_tokens_out)
    for i in range(3):
        gain_grads[i : i + 1, :] = jnp.sum(gain_acc[i], axis=0, keepdims=True)

    def table_rows(b, carry):
        hit = buckets[...] == b
        for head in range(heads):
            start = (head % 2) * length
            part = jnp.where(hit, dsum[head // 2, start : start + length, :], 0.0)
            table_out[pl.ds(b, 1), head, :] = jnp.sum(part, axis=0, keepdims=True)
        return carry

    lax.fori_loop(0, table_out.shape[0], table_rows, 0)
    stores.drain()


def params(**more):
    return pltpu.CompilerParams(vmem_limit_bytes=VMEM_LIMIT, **more)


def on_device(
    tokens, memory, target_mask, buckets, expert_ids, slots, gain_self, w_query, w_key, w_value, w_output, rel_table, gain_cross,
    c_query, c_key, c_value, c_output, gain_moe, router, expert_in, expert_out, cotangent,
):
    rows, width = tokens.shape
    targets, length = target_mask.shape
    bucket_count, heads = rel_table.shape
    memory_length = memory.shape[0] // targets
    pairs = heads // 2
    experts = lax.axis_size("expert")
    hidden = expert_in.shape[2]
    capacity = (5 * rows + 4 * experts - 1) // (4 * experts)
    slot_rows = experts * capacity
    place = jnp.where(slots < capacity, expert_ids * capacity + slots, -1)
    place_row, place_column = place.reshape(1, rows), place.reshape(rows, 1)
    gains = jnp.stack([gain_self, gain_cross, gain_moe]).astype(F32)
    weights = (w_query, w_key, w_value, w_output, c_query, c_key, c_value, c_output)

    def exchange(buffer):
        buffer = buffer.reshape(experts, capacity, width)
        return lax.all_to_all(buffer, "expert", split_axis=0, concat_axis=0, tiled=True).reshape(slot_rows, width)

    row_shape = jax.ShapeDtypeStruct((slot_rows, width), BF16)
    gsent = pl.pallas_call(
        dispatch_kernel, out_shape=row_shape, in_specs=[VMEM, VMEM], out_specs=VMEM, compiler_params=params(), name="dispatch"
    )(place_row, cotangent)
    grows = exchange(gsent)

    act_shape = ((rows, width), BF16)
    wide_shape = ((rows, width), F32)
    key_shape = ((targets * memory_length, width), BF16)
    kept = (
        [act_shape] * 8
        + [wide_shape] * 2
        + [((targets, pairs, 2 * length, length), BF16), ((targets, pairs, 2 * length, memory_length), BF16), key_shape, key_shape]
        + [((slot_rows, width), BF16)]
    )
    h1, q1, k1, v1, c1, h2, q2, c2, x1, x2, p1, p2, k2, v2, sent = pl.pallas_call(
        functools.partial(forward_kernel, targets, length, memory_length, heads),
        out_shape=[jax.ShapeDtypeStruct(*k) for k in kept],
        in_specs=[SMEM, ANY, ANY, VMEM, VMEM, VMEM, VMEM] + [ANY] * 8,
        out_specs=[ANY] * len(kept),
        scratch_shapes=[pltpu.VMEM((rows, width), BF16), pltpu.VMEM(*key_shape), pltpu.VMEM((8, width, width), BF16)]
        + [pltpu.VMEM(*k) for k in kept]
        + [
            pltpu.VMEM((pairs, 2 * length, length), F32),
            pltpu.VMEM((2, 2 * length, memory_length), F32),
            pltpu.SemaphoreType.DMA((10,)),
            pltpu.SemaphoreType.DMA((len(kept),)),
        ],
        compiler_params=params(),
        name="forward",
    )(rel_table.astype(F32), tokens, memory, target_mask, buckets, gains, place_row, *weights)

    inbound = exchange(sent)
    router_wide = jnp.pad(router, ((0, 0), (0, LANES - experts)))
    weight_grad = jax.ShapeDtypeStruct((width, hidden), BF16)
    ret, dh, grad_first, grad_second, grad_router = pl.pallas_call(
        functools.partial(expert_kernel, experts),
        out_shape=[row_shape, row_shape, weight_grad, weight_grad, jax.ShapeDtypeStruct((LANES, width), F32)],
        in_specs=[VMEM, VMEM, VMEM, ANY, ANY],
        out_specs=[VMEM, VMEM, ANY, ANY, VMEM],
        scratch_shapes=[
            pltpu.VMEM((width, hidden), BF16),
            pltpu.VMEM((hidden, width), BF16),
            pltpu.VMEM((width, slot_rows), BF16),
            pltpu.VMEM((slot_rows, width), BF16),
            pltpu.VMEM((width, slot_rows), BF16),
            pltpu.VMEM((slot_rows, LANES), F32),
            pltpu.VMEM((slot_rows, width), F32),
            pltpu.VMEM((slot_rows, width), F32),
            pltpu.VMEM((slot_rows, width), BF16),
            pltpu.VMEM((slot_rows, width), BF16),
            pltpu.VMEM((slot_rows, width), F32),
            pltpu.VMEM((slot_rows, width), F32),
            pltpu.VMEM((2, width, width), BF16),
            pltpu.VMEM((2, width, width), BF16),
            pltpu.SemaphoreType.DMA((2 * (hidden // width),)),
            pltpu.SemaphoreType.DMA((2 * (hidden // width),)),
        ],
        compiler_params=params(),
        name="experts",
    )(inbound, grows, router_wide, expert_in[0], expert_out[0])

    dh_rows = exchange(dh)
    ret_rows = exchange(ret)
    grad_first = lax.psum_scatter(grad_first, "dp", scatter_dimension=1, tiled=True)
    grad_second = lax.psum_scatter(grad_second, "dp", scatter_dimension=1, tiled=True)

    square = (width, width)
    act, wide = pltpu.VMEM(*act_shape), pltpu.VMEM(*wide_shape)
    grads, grad_tokens, grad_memory, gain_grads, table_grads = pl.pallas_call(
        functools.partial(backward_kernel, targets, length, memory_length, heads),
        out_shape=[
            jax.ShapeDtypeStruct((8,) + square, BF16),
            jax.ShapeDtypeStruct((rows, width), F32),
            jax.ShapeDtypeStruct(memory.shape, BF16),
            jax.ShapeDtypeStruct((3, width), F32),
            jax.ShapeDtypeStruct((bucket_count, heads, length), F32),
        ],
        in_specs=[ANY, VMEM, VMEM, VMEM, VMEM] + [ANY] * 25,
        out_specs=[ANY, ANY, ANY, VMEM, VMEM],
        scratch_shapes=[pltpu.VMEM((slot_rows, width), BF16)]
        + [act] * 10
        + [wide] * 2
        + [
            pltpu.VMEM((targets, pairs, 2 * length, length), BF16),
            pltpu.VMEM((8,) + square, BF16),
            pltpu.VMEM((2, pairs, 2 * length, memory_length), BF16),
            pltpu.VMEM((2, memory_length, width), BF16),
            pltpu.VMEM((2, memory_length, width), BF16),
            pltpu.VMEM((2, memory_length, width), BF16),
            pltpu.VMEM((2, memory_length, width), BF16),
            wide,
            wide,
        ]
        + [act] * 5
        + [
            pltpu.VMEM((memory_length, width), BF16),
            pltpu.VMEM((memory_length, width), BF16),
            pltpu.VMEM(square, F32),
            pltpu.VMEM(square, F32),
            pltpu.VMEM((8,) + square, BF16),
            pltpu.VMEM((2, 2 * length, memory_length), F32),
            pltpu.VMEM((2, 2 * length, memory_length), BF16),
            pltpu.VMEM((pairs, 2 * length, length), F32),
            pltpu.VMEM((3, 8, width), F32),
            pltpu.SemaphoreType.DMA((22,)),
            pltpu.SemaphoreType.DMA((9,)),
            pltpu.SemaphoreType.DMA((4, 2)),
            pltpu.SemaphoreType.DMA((2,)),
        ],
        compiler_params=params(),
        name="backward",
    )(
        dh_rows, place_column, target_mask, buckets, gains, cotangent, tokens, h1, q1, k1, v1, c1, h2, q2, c2, x1, x2, p1, p2, k2, v2,
        memory, *weights,
    )

    output = pl.pallas_call(
        output_kernel,
        out_shape=jax.ShapeDtypeStruct((rows, width), BF16),
        in_specs=[VMEM, VMEM, VMEM],
        out_specs=VMEM,
        compiler_params=params(),
        name="output",
    )(place_column, x2, ret_rows)

    summed = lax.psum(grads, ("dp", "expert")).astype(F32)
    small = lax.psum((gain_grads, jnp.sum(table_grads, axis=-1), grad_router[:experts].T), ("dp", "expert"))
    return (
        output, grad_tokens, grad_memory, small[0][0], summed[0], summed[1], summed[2], summed[3], small[1], small[0][1], summed[4],
        summed[5], summed[6], summed[7], small[0][2], small[2], grad_first.astype(F32)[None], grad_second.astype(F32).T[None],
    )


def solution(mesh):
    both, spread = P(("dp", "expert")), P(("dp", "expert"), None)
    placed = (
        (spread, spread, spread, P(), both, both) + (P(),) * 13 + (P("expert", None, None), P("expert", None, None), spread)
    )
    return jax.shard_map(
        on_device,
        mesh=mesh,
        in_specs=placed,
        out_specs=(spread, spread, spread) + (P(),) * 13 + (P("expert", None, "dp"), P("expert", "dp", None)),
        check_vma=False,
    )
```

```python
import functools

import jax
import jax.numpy as jnp
from jax import lax
from jax.experimental import pallas as pl
from jax.experimental.pallas import tpu as pltpu
from jax.sharding import PartitionSpec as P

EPS = 1e-06
NEG = -1000000000.0
F32 = jnp.float32
BF16 = jnp.bfloat16
LANES = 128
VMEM_LIMIT = 60 * 1024 * 1024
ANY = pl.BlockSpec(memory_space=pl.ANY)
VMEM = pl.BlockSpec(memory_space=pltpu.VMEM)
SMEM = pl.BlockSpec(memory_space=pltpu.SMEM)


def dot(left, right):
    return lax.dot_general(left, right, (((1,), (0,)), ((), ())), preferred_element_type=F32)


def dot_nt(left, right):
    return lax.dot_general(left, right, (((1,), (1,)), ((), ())), preferred_element_type=F32)


def dot_tn(left, right):
    return lax.dot_general(left, right, (((0,), (0,)), ((), ())), preferred_element_type=F32)


def row_loop(count, step, body):
    def one(i, carry):
        body(pl.ds(pl.multiple_of(i * step, step), step))
        return carry

    lax.fori_loop(0, count // step, one, 0)


def half_masks():
    lane = lax.broadcasted_iota(jnp.int32, (1, LANES), 1)
    low = jnp.where(lane < LANES // 2, 1.0, 0.0).astype(BF16)
    high = jnp.where(lane < LANES // 2, 0.0, 1.0).astype(BF16)
    return lane < LANES // 2, low, high


def stacked(pair, low, high):
    return jnp.concatenate([pair * low, pair * high], axis=0)


def norm_rows(values, gain):
    return values * lax.rsqrt(jnp.mean(values * values, axis=-1, keepdims=True) + EPS) * gain


def norm_back(values, gain, grad):
    scale = lax.rsqrt(jnp.mean(values * values, axis=-1, keepdims=True) + EPS)
    scaled = grad * gain
    inner = jnp.mean(scaled * values, axis=-1, keepdims=True)
    back = scale * scaled - values * (scale * scale * scale * inner)
    gain_rows = grad * values * scale
    return back, jnp.sum(gain_rows.reshape(-1, 8, gain_rows.shape[-1]), axis=0)


def allowed_of(mask_row, length):
    row = lax.broadcasted_iota(jnp.int32, (length, length), 0)
    col = lax.broadcasted_iota(jnp.int32, (length, length), 1)
    return (col <= row) & (mask_row == 1)


class Loads:
    def __init__(self, sems):
        self.sems = sems
        self.count = 0
        self.open = {}

    def start(self, name, source, target):
        copy = pltpu.make_async_copy(source, target, self.sems.at[self.count])
        self.count += 1
        copy.start()
        self.open[name] = copy

    def wait(self, *names):
        for name in names:
            self.open.pop(name).wait()

    def drain(self):
        self.wait(*list(self.open))


def forward_kernel(
    targets, length, memory_length, heads, table, tokens, memory, mask, buckets, gains, place, wq, wk, wv, wo, cq, ck, cv, co,
    h1_out, q1_out, k1_out, v1_out, c1_out, h2_out, q2_out, c2_out, x1_out, x2_out, p1_out, p2_out, k2_out, v2_out, sent_out,
    tokens_v, memory_v, weights_v, h1, q1, k1, v1, c1, h2, q2, c2, x1, x2, p1, p2, k2, v2, sent, bias, scores, in_sems, out_sems,
):
    rows, width = tokens_v.shape
    pairs = heads // 2
    loads, stores = Loads(in_sems), Loads(out_sems)
    loads.start("tokens", tokens, tokens_v)
    for index, (name, ref) in enumerate(zip(("wq", "wk", "wv"), (wq, wk, wv))):
        loads.start(name, ref, weights_v.at[index])
    loads.start("ck", ck, weights_v.at[5])
    loads.start("memory", memory, memory_v)
    loads.start("cv", cv, weights_v.at[6])
    loads.start("wo", wo, weights_v.at[3])
    loads.start("cq", cq, weights_v.at[4])
    loads.start("co", co, weights_v.at[7])
    gain = [gains[i : i + 1, :] for i in range(3)]
    low_lane, low, high = half_masks()

    bucket_count = table.shape[0]

    def bias_rows(r):
        here = buckets[r, :]
        hits = [here == b for b in range(bucket_count)]
        for head in range(heads):
            total = jnp.zeros(here.shape, F32)
            for b in range(bucket_count):
                total = jnp.where(hits[b], table[b, head], total)
            start = (head % 2) * length
            bias[head // 2, pl.ds(pl.multiple_of(r.start + start, 8), r.size), :] = total

    row_loop(length, 16, bias_rows)

    loads.wait("tokens")

    def first_norm(r):
        h1[r, :] = norm_rows(tokens_v[r, :].astype(F32), gain[0]).astype(BF16)

    row_loop(rows, 32, first_norm)
    stores.start("h1", h1, h1_out)
    for index, (name, ref) in enumerate(zip(("wq", "wk", "wv"), (q1, k1, v1))):
        loads.wait(name)

        def project(r, index=index, ref=ref):
            ref[r, :] = dot(h1[r, :], weights_v[index]).astype(BF16)

        row_loop(rows, 256, project)
    stores.start("q1", q1, q1_out)
    stores.start("k1", k1, k1_out)
    stores.start("v1", v1, v1_out)

    def self_target(t, carry):
        r = pl.ds(pl.multiple_of(t * length, length), length)
        allowed = allowed_of(mask[pl.ds(t, 1), :], length)
        for pair in range(pairs):
            lanes = slice(pair * LANES, (pair + 1) * LANES)
            both = dot_nt(stacked(q1[r, lanes], low, high), k1[r, lanes])
            for half in range(2):
                part = slice(half * length, (half + 1) * length)
                score = jnp.where(allowed, both[part] + bias[pair, part, :], NEG)
                expo = jnp.exp(score - jnp.max(score, axis=-1, keepdims=True))
                total = jnp.sum(expo, axis=-1, keepdims=True)
                p1[t, pair, part, :] = (expo / total).astype(BF16)
            context = dot(p1[t, pair], v1[r, lanes])
            c1[r, lanes] = jnp.where(low_lane, context[:length], context[length:]).astype(BF16)
        return carry

    lax.fori_loop(0, targets, self_target, 0)
    stores.start("p1", p1, p1_out)
    stores.start("c1", c1, c1_out)
    loads.wait("wo")

    def self_out(r):
        x1[r, :] = tokens_v[r, :].astype(F32) + dot(c1[r, :], weights_v[3])

    row_loop(rows, 256, self_out)
    stores.start("x1", x1, x1_out)

    def second_norm(r):
        h2[r, :] = norm_rows(x1[r, :], gain[1]).astype(BF16)

    row_loop(rows, 32, second_norm)
    stores.start("h2", h2, h2_out)
    loads.wait("cq")

    def cross_query(r):
        q2[r, :] = dot(h2[r, :], weights_v[4]).astype(BF16)

    row_loop(rows, 256, cross_query)
    stores.start("q2", q2, q2_out)
    loads.wait("memory", "ck", "cv")

    def cross_keys(r):
        k2[r, :] = dot(memory_v[r, :], weights_v[5]).astype(BF16)
        v2[r, :] = dot(memory_v[r, :], weights_v[6]).astype(BF16)

    row_loop(targets * memory_length, 256, cross_keys)
    stores.start("k2", k2, k2_out)
    stores.start("v2", v2, v2_out)

    def cross_target(t, carry):
        r = pl.ds(pl.multiple_of(t * length, length), length)
        m = pl.ds(pl.multiple_of(t * memory_length, memory_length), memory_length)
        for pair in range(pairs):
            lanes = slice(pair * LANES, (pair + 1) * LANES)
            slot = pair % 2
            scores[slot] = dot_nt(stacked(q2[r, lanes], low, high), k2[m, lanes])
            for chunk in range(2 * length // 32):
                part = slice(chunk * 32, (chunk + 1) * 32)
                score = scores[slot, part, :]
                expo = jnp.exp(score - jnp.max(score, axis=-1, keepdims=True))
                total = jnp.sum(expo, axis=-1, keepdims=True)
                p2[t, pair, part, :] = (expo / total).astype(BF16)
            context = dot(p2[t, pair], v2[m, lanes])
            c2[r, lanes] = jnp.where(low_lane, context[:length], context[length:]).astype(BF16)
        return carry

    lax.fori_loop(0, targets, cross_target, 0)
    stores.start("p2", p2, p2_out)
    stores.start("c2", c2, c2_out)
    loads.wait("co")

    def cross_out(r):
        x2[r, :] = x1[r, :] + dot(c2[r, :], weights_v[7])

    row_loop(rows, 256, cross_out)
    stores.start("x2", x2, x2_out)

    def third_norm(r):
        tokens_v[r, :] = norm_rows(x2[r, :], gain[2]).astype(BF16)

    row_loop(rows, 32, third_norm)
    dispatch(place, tokens_v, sent)
    stores.start("sent", sent, sent_out)
    stores.drain()


def dispatch(place, source, target):
    step = 128

    def one(r):
        spot = lax.broadcasted_iota(jnp.int32, (step, source.shape[0]), 0) + r.start
        hit = jnp.where(spot == place[...], 1.0, 0.0).astype(BF16)
        target[r, :] = dot(hit, source[...]).astype(target.dtype)

    row_loop(target.shape[0], step, one)


def collect(place_column, step, r, source):
    spot = lax.broadcasted_iota(jnp.int32, (step, source.shape[0]), 1)
    hit = jnp.where(spot == place_column[r, :], 1.0, 0.0).astype(BF16)
    return dot(hit, source[...])


def dispatch_kernel(place, source, target):
    dispatch(place, source, target)


def output_kernel(place_column, x2, rows, out):
    def one(r):
        out[r, :] = (x2[r, :] + collect(place_column, 128, r, rows)).astype(BF16)

    row_loop(out.shape[0], 128, one)


def expert_kernel(
    experts, inbound, grows, router, first, second,
    ret_out, dh_out, grad_first, grad_second, grad_router,
    first_v, second_v, inbound_t, dret, dret_t, probs, pre, dact, act, dpre, ret, dinb, gf, gs, in_sems, out_sems,
):
    rows, width = inbound.shape
    hidden = first.shape[1]
    step = width
    loads = Loads(in_sems)
    for f in range(hidden // step):
        cols = slice(f * step, (f + 1) * step)
        loads.start(("first", f), first.at[:, cols], first_v.at[:, cols])
        loads.start(("second", f), second.at[cols, :], second_v.at[cols, :])
    me = lax.axis_index("expert")
    lane = lax.broadcasted_iota(jnp.int32, (1, LANES), 1)
    mine = lane == me

    def route(r):
        logits = jnp.where(lane < experts, dot(inbound[r, :], router[...]), -1e30)
        expo = jnp.exp(logits - jnp.max(logits, axis=-1, keepdims=True))
        prob = expo / jnp.sum(expo, axis=-1, keepdims=True)
        probs[r, :] = prob
        gate = jnp.sum(jnp.where(mine, prob, 0.0), axis=-1, keepdims=True)
        dret[r, :] = (gate * grows[r, :].astype(F32)).astype(BF16)

    row_loop(rows, 128, route)
    for c in range(width // LANES):
        cols = slice(c * LANES, (c + 1) * LANES)
        inbound_t[cols, :] = inbound[:, cols].T
        dret_t[cols, :] = dret[:, cols].T

    stores = Loads(out_sems)
    root = (2.0 / jnp.pi) ** 0.5
    for f in range(hidden // step):
        cols = slice(f * step, (f + 1) * step)
        loads.wait(("first", f), ("second", f))
        slot = f % 2

        def up(r, cols=cols):
            pre[r, :] = dot(inbound[r, :], first_v[:, cols])
            dact[r, :] = dot_nt(dret[r, :], second_v[cols, :])

        row_loop(rows, 128, up)

        def middle(r):
            u = pre[r, :]
            square = u * u
            t = jnp.tanh(root * (u + 0.044715 * (square * u)))
            half = 0.5 * (1.0 + t)
            act[r, :] = (u * half).astype(BF16)
            slope = half + (0.5 * root) * u * (1.0 - t * t) * (1.0 + (3 * 0.044715) * square)
            dpre[r, :] = (dact[r, :] * slope).astype(BF16)

        row_loop(rows, 16, middle)

        def down(r, cols=cols, f=f):
            one, two = dot(act[r, :], second_v[cols, :]), dot_nt(dpre[r, :], first_v[:, cols])
            if f:
                one, two = one + ret[r, :], two + dinb[r, :]
            ret[r, :] = one
            dinb[r, :] = two

        row_loop(rows, 128, down)
        if f >= 2:
            stores.wait(("first", f - 2), ("second", f - 2))

        def weights(r, slot=slot):
            gf[slot, r, :] = dot(inbound_t[r, :], dpre[...]).astype(BF16)
            gs[slot, r, :] = dot(dret_t[r, :], act[...]).astype(BF16)

        row_loop(width, 256, weights)
        stores.start(("first", f), gf.at[slot], grad_first.at[:, cols])
        stores.start(("second", f), gs.at[slot], grad_second.at[:, cols])

    grad_router[...] = jnp.zeros_like(grad_router)

    def finish(r):
        result = ret[r, :].astype(BF16).astype(F32)
        prob = probs[r, :]
        gate = jnp.sum(jnp.where(mine, prob, 0.0), axis=-1, keepdims=True)
        dgate = jnp.sum(result * grows[r, :].astype(F32), axis=-1, keepdims=True)
        dlogits = (prob * (jnp.where(mine, 1.0, 0.0) - gate) * dgate).astype(BF16)
        ret_out[r, :] = (gate * result).astype(BF16)
        dh_out[r, :] = (dinb[r, :].astype(BF16).astype(F32) + dot_nt(dlogits, router[...])).astype(BF16)
        grad_router[...] += dot_tn(dlogits, inbound[r, :])

    row_loop(rows, 128, finish)
    stores.drain()


class Ring:
    def __init__(self, send_sems, recv_sems):
        self.send_sems, self.recv_sems = send_sems, recv_sems
        self.count = 0
        dp, self.expert = lax.axis_index("dp"), lax.axis_index("expert")
        self.experts = lax.axis_size("expert")
        self.dp = dp
        self.spot = {"core": lax.rem(dp, 2), "x": lax.rem(lax.div(dp, 2), 2), "y": lax.div(dp, 4)}
        self.partner = {name: dp + step - 2 * step * self.spot[name] for name, step in (("core", 1), ("x", 2), ("y", 4))}

    def others(self):
        return [lax.rem(self.expert + k, self.experts) for k in range(1, self.experts)]

    def greet(self):
        barrier = pltpu.get_barrier_semaphore()
        targets = [(self.partner[name], self.expert) for name in ("core", "x", "y")] + [(self.dp, e) for e in self.others()]
        for target in targets:
            pl.semaphore_signal(barrier, inc=1, device_id=target, device_id_type=pl.DeviceIdType.MESH)
        pl.semaphore_wait(barrier, len(targets))

    def send(self, source, target, dp, expert):
        copy = pltpu.make_async_remote_copy(
            src_ref=source, dst_ref=target, send_sem=self.send_sems.at[self.count], recv_sem=self.recv_sems.at[self.count],
            device_id=(dp, expert), device_id_type=pl.DeviceIdType.MESH,
        )
        self.count += 1
        copy.start()
        return copy

    def cross(self, name, source, target):
        return self.send(source, target, self.partner[name], self.expert)


def span(start, size):
    return pl.ds(pl.multiple_of(start, size), size)


def add_into(ref, rows, lanes, others):
    step = 48 if rows.size % 64 else 64
    for i in range(rows.size // step):
        here = pl.ds(pl.multiple_of(rows.start + i * step, 16), step)
        total = ref[here, lanes].astype(F32)
        for other in others:
            total = total + other[i * step : (i + 1) * step, :].astype(F32)
        ref[here, lanes] = total.astype(BF16)


def reduce_matrix(ring, local, result, landing, first, second, copy_sem):
    size = local.shape[0]
    half, quarter, eighth = size // 2, size // 4, size // 4 // ring.experts
    half_land, quarter_land, eighth_land, part_land = landing
    core = ring.spot["core"]
    mine, other = span(core * half, half), span((1 - core) * half, half)
    copy = ring.cross("core", local.at[:, other], half_land)
    yield
    copy.wait()
    add_into(local, pl.ds(0, size), mine, [half_land])
    place = ring.spot[first] * half
    copy = ring.cross(first, local.at[span(half - place, half), mine], quarter_land)
    yield
    copy.wait()
    add_into(local, span(place, half), mine, [quarter_land])
    step = ring.spot[second] * quarter
    copy = ring.cross(second, local.at[span(place + quarter - step, quarter), mine], eighth_land)
    yield
    copy.wait()
    base = place + step
    add_into(local, span(base, quarter), mine, [eighth_land])
    copies = [
        ring.send(local.at[pl.ds(pl.multiple_of(base + e * eighth, 16), eighth), mine], part_land.at[k], ring.dp, e)
        for k, e in enumerate(ring.others())
    ]
    yield
    for copy in copies:
        copy.wait()
    part = pl.ds(pl.multiple_of(base + ring.expert * eighth, 16), eighth)
    add_into(local, part, mine, [part_land.at[k] for k in range(ring.experts - 1)])
    own = pltpu.make_async_copy(local.at[part, mine], result.at[part, mine], copy_sem)
    own.start()
    copies = [ring.send(local.at[part, mine], result.at[part, mine], ring.dp, e) for e in ring.others()]
    yield
    own.wait()
    for copy in copies:
        copy.wait()
    here = span(base, quarter)
    copy = ring.cross(second, result.at[here, mine], result.at[here, mine])
    yield
    copy.wait()
    here = span(place, half)
    copy = ring.cross(first, result.at[here, mine], result.at[here, mine])
    yield
    copy.wait()
    copy = ring.cross("core", result.at[:, mine], result.at[:, mine])
    yield
    copy.wait()


def reduce_small(ring, local, landing):
    for k, name in enumerate(("core", "x", "y")):
        copy = ring.cross(name, local, landing.at[k])
        yield
        copy.wait()
        local[...] += landing[k]
    copies = [ring.send(local, landing.at[3 + ring.expert], ring.dp, e) for e in ring.others()]
    landing[3 + ring.expert] = local[...]
    yield
    for copy in copies:
        copy.wait()
    total = landing[3]
    for e in range(1, ring.experts):
        total = total + landing[3 + e]
    local[...] = total


class Running:
    def __init__(self):
        self.steps = []

    def add(self, steps):
        next(steps)
        self.steps.append(steps)

    def tick(self):
        self.steps = [s for s in self.steps if next(s, self) is not self]

    def drain(self):
        while self.steps:
            self.tick()


def backward_kernel(
    targets, length, memory_length, heads, remote,
    dh_rows, ret_rows, place_column, mask, buckets, gains, grad_router, cotangent, tokens, h1, q1, k1, v1, c1, h2, q2, c2, x1, x2, p1, p2,
    k2, v2, memory, wq, wk, wv, wo, cq, ck, cv, co,
    *rest,
):
    grad_refs, rest = rest[:8], rest[8:]
    (
        output_out, grad_tokens_out, grad_memory_out, small,
        rows_v, ret_v, first_v, ctx_v, norm_v, q2_v, q1_v, k1_v, v1_v, x2_v, p1_v, weights_v,
        p2_v, kv_v, wide, do, dctx2, dctx1, dq, dk, dv, grads, dscores, ds, dsum, gain_acc, table_v, half_land, quarter_land, eighth_land,
        part_land, small_land, in_sems, out_sems, ring_sems, send_sems, recv_sems, own_sems,
    ) = rest
    rows, width = first_v.shape
    pairs = heads // 2
    x1_v, du, dx = wide.at[0:rows, :], wide.at[rows : 2 * rows, :], wide.at[2 * rows : 3 * rows, :]
    gk, gv = wide.at[0:width, :], wide.at[width : 2 * width, :]
    spare = (dctx1, dq)
    loads, stores, running = Loads(in_sems), Loads(out_sems), Running()
    loads.start("rows", dh_rows, rows_v)
    loads.start("cot", cotangent, first_v)
    loads.start("x2", x2, x2_v)
    loads.start("c2", c2, ctx_v)
    loads.start("co", co, weights_v.at[0])

    def fetch(t, sources):
        slot = t % 2
        m = pl.ds(t * memory_length, memory_length)
        for index, source in enumerate(sources):
            target = p2_v.at[slot] if index == 0 else kv_v.at[index - 1, slot]
            copy = pltpu.make_async_copy(source.at[t] if index == 0 else source.at[m, :], target, ring_sems.at[index, slot])
            copy.start()
            yield copy

    fetched = list(fetch(0, (p2, k2, v2)))
    for name, source, target in (
        ("q2", q2, q2_v), ("cq", cq, weights_v.at[1]), ("h2", h2, norm_v), ("x1", x1, x1_v), ("wo", wo, weights_v.at[2]),
        ("p1", p1, p1_v), ("q1", q1, q1_v), ("k1", k1, k1_v), ("v1", v1, v1_v), ("ck", ck, weights_v.at[3]),
        ("cv", cv, weights_v.at[4]),
    ):
        loads.start(name, source, target)
    if remote:
        ring = Ring(send_sems, recv_sems)
        ring.greet()
        capacity = rows_v.shape[0] // ring.experts
        block = lambda e: pl.ds(pl.multiple_of(e * capacity, 16), capacity)
        mine = block(ring.expert)
        ret_copies = [ring.send(ret_rows.at[block(e), :], ret_v.at[mine, :], ring.dp, e) for e in ring.others()]
        loads.start("ret", ret_rows.at[mine, :], ret_v.at[mine, :])
    else:
        ret_copies = []
        loads.start("ret", ret_rows, ret_v)

    gain = [gains[i : i + 1, :] for i in range(3)]
    low_lane, low, high = half_masks()
    gain_acc[...] = jnp.zeros_like(gain_acc)
    axes = ("x", "y")
    started = []

    def total_of(index):
        if remote:
            way = len(started) % 2
            landing = [land.at[index] for land in (half_land, quarter_land, eighth_land, part_land)]
            running.add(reduce_matrix(ring, grads.at[index], grad_refs[index], landing, axes[way], axes[1 - way], own_sems.at[index]))
        else:
            stores.start(("grad", index), grads.at[index], grad_refs[index])
        started.append(index)

    def inner_grad(index, left, right):
        for c in range(width // 256):
            cols = slice(c * 256, (c + 1) * 256)
            grads[index, cols, :] = dot_tn(left[:, cols], right[...]).astype(BF16)
        total_of(index)

    def back_through(values, index, base, target):
        def one(r):
            back, gain_rows = norm_back(values[r, :].astype(F32), gain[index], du[r, :])
            total = base[r, :].astype(F32) + back
            target[r, :] = total
            do[r, :] = total.astype(BF16)
            gain_acc[index] += gain_rows

        row_loop(rows, 32, one)

    loads.wait("rows", "cot", "x2")

    def gather(r):
        du[r, :] = collect(place_column, 128, r, rows_v)

    row_loop(rows, 128, gather)
    back_through(x2_v, 2, first_v, dx)
    loads.start("tokens", tokens, first_v)
    loads.wait("c2", "co")
    inner_grad(7, ctx_v, do)
    loads.start("c1", c1, ctx_v)

    def out_back(r, slot, target):
        target[r, :] = dot_nt(do[r, :], weights_v[slot]).astype(BF16)

    row_loop(rows, 256, functools.partial(out_back, slot=0, target=dctx2))
    loads.start("wq", wq, weights_v.at[0])
    loads.wait("q2")
    for t in range(targets):
        slot = t % 2
        ahead = list(fetch(t + 1, (p2, k2, v2))) if t + 1 < targets else []
        for copy in fetched:
            copy.wait()
        fetched = ahead
        r = slice(t * length, (t + 1) * length)
        for pair in range(pairs):
            lanes = slice(pair * LANES, (pair + 1) * LANES)
            side = pair % 2
            dscores[side] = dot_nt(stacked(dctx2[r, lanes], low, high), kv_v[1, slot, :, lanes])
            for chunk in range(2 * length // 32):
                part = slice(chunk * 32, (chunk + 1) * 32)
                prob = p2_v[slot, pair, part, :].astype(F32)
                dprob = dscores[side, part, :]
                inner = jnp.sum(prob * dprob, axis=-1, keepdims=True)
                ds[t, pair, part, :] = (prob * (dprob - inner)).astype(BF16)
            back = dot(ds[t, pair], kv_v[0, slot, :, lanes])
            dq[r, lanes] = jnp.where(low_lane, back[:length], back[length:]).astype(BF16)
        running.tick()
    fetched = list(fetch(0, (p2, memory)))
    loads.wait("h2", "cq", "x1")
    inner_grad(4, norm_v, dq)
    loads.start("h1", h1, norm_v)

    def query_back(r):
        du[r, :] = dot_nt(dq[r, :], weights_v[1])

    row_loop(rows, 256, query_back)
    loads.start("wk", wk, weights_v.at[1])
    back_through(x1_v, 1, dx, dx)
    running.tick()
    loads.wait("c1", "wo")
    inner_grad(3, ctx_v, do)
    row_loop(rows, 256, functools.partial(out_back, slot=2, target=dctx1))
    loads.start("wv", wv, weights_v.at[2])
    for copy in ret_copies:
        copy.wait()
    loads.wait("ret")

    def output_rows(r):
        dk[r, :] = (x2_v[r, :] + collect(place_column, 128, r, ret_v)).astype(BF16)

    row_loop(rows, 128, output_rows)
    stores.start("output", dk, output_out)
    running.tick()
    loads.wait("p1", "q1", "k1", "v1")
    stores.wait("output")
    for t in range(targets):
        r = slice(t * length, (t + 1) * length)
        allowed = allowed_of(mask[t : t + 1, :], length)
        for pair in range(pairs):
            lanes = slice(pair * LANES, (pair + 1) * LANES)
            side = pair % 2
            grad_rows = stacked(dctx1[r, lanes], low, high)
            both = dot_nt(grad_rows, v1_v[r, lanes])
            scratch = p2_v.at[1, side]
            for half in range(2):
                part = slice(half * length, (half + 1) * length)
                prob = p1_v[t, pair, part, :].astype(F32)
                dprob = both[part]
                inner = jnp.sum(prob * dprob, axis=-1, keepdims=True)
                score = jnp.where(allowed, prob * (dprob - inner), 0.0).astype(BF16)
                scratch[part, :length] = score
                wide_score = score.astype(F32)
                dsum[pair, part, :] = wide_score if t == 0 else dsum[pair, part, :] + wide_score
            dv[r, lanes] = dot_tn(p1_v[t, pair], grad_rows).astype(BF16)
            dk[r, lanes] = dot_tn(scratch[:, :length], stacked(q1_v[r, lanes], low, high)).astype(BF16)
            back = dot(scratch[:, :length], k1_v[r, lanes])
            dq[r, lanes] = jnp.where(low_lane, back[:length], back[length:]).astype(BF16)
        if t % 2:
            running.tick()
    loads.wait("h1", "wq", "wk", "wv", "tokens")
    for index, right in enumerate((dq, dk, dv)):
        inner_grad(index, norm_v, right)

    def self_back(r):
        du[r, :] = dot_nt(dq[r, :], weights_v[0]) + dot_nt(dk[r, :], weights_v[1]) + dot_nt(dv[r, :], weights_v[2])

    row_loop(rows, 256, self_back)
    running.tick()
    back_through(first_v, 0, dx, dx)
    stores.start("tokens", dx, grad_tokens_out)
    small[...] = jnp.zeros_like(small)
    for i in range(3):
        small[i : i + 1, :] = jnp.sum(gain_acc[i], axis=0, keepdims=True)
    small[8:16, :] = grad_router[0:8, :]
    table_v[...] = jnp.zeros_like(table_v)

    def table_rows(b, carry):
        hit = buckets[...] == b
        for head in range(heads):
            start = (head % 2) * length
            part = jnp.where(hit, dsum[head // 2, start : start + length, :], 0.0)
            table_v[pl.ds(head, 1), :] = jnp.sum(part, axis=0, keepdims=True)
        sums = jnp.sum(table_v[0:16, :], axis=-1, keepdims=True)
        eye = lax.broadcasted_iota(jnp.int32, (16, LANES), 0) == lax.broadcasted_iota(jnp.int32, (16, LANES), 1)
        table_v[pl.ds(16 + b, 1), :] = jnp.sum(jnp.where(eye, sums, 0.0), axis=0, keepdims=True)
        return carry

    lax.fori_loop(0, 32, table_rows, 0)
    for b in range(0, 32, 8):
        small[16:24, b // 8 * LANES : (b // 8 + 1) * LANES] = table_v[16 + b : 24 + b, :]
    if remote:
        running.add(reduce_small(ring, small, small_land))
    running.tick()
    loads.wait("ck", "cv")
    stores.wait("tokens")
    for t in range(targets):
        slot = t % 2
        ahead = list(fetch(t + 1, (p2, memory))) if t + 1 < targets else []
        for copy in fetched:
            copy.wait()
        fetched = ahead
        r = slice(t * length, (t + 1) * length)
        for pair in range(pairs):
            lanes = slice(pair * LANES, (pair + 1) * LANES)
            dv[:, lanes] = dot_tn(p2_v[slot, pair], stacked(dctx2[r, lanes], low, high)).astype(BF16)
            dk[:, lanes] = dot_tn(ds[t, pair], stacked(q2_v[r, lanes], low, high)).astype(BF16)
        last = t + 1 == targets
        for index, total, right in ((5, gk, dk), (6, gv, dv)):
            for c in range(width // 256):
                cols = slice(c * 256, (c + 1) * 256)
                part = dot_tn(kv_v[0, slot, :, cols], right[...])
                if t:
                    part = part + total[cols, :]
                if last:
                    grads[index, cols, :] = part.astype(BF16)
                else:
                    total[cols, :] = part
            if last:
                total_of(index)
        running.tick()
        buffer = spare[slot]
        if t >= 2:
            stores.wait(("memory", t - 2))

        def memory_rows(q, buffer=buffer):
            buffer[q, :] = (dot_nt(dk[q, :], weights_v[3]) + dot_nt(dv[q, :], weights_v[4])).astype(BF16)

        row_loop(memory_length, 256, memory_rows)
        stores.start(("memory", t), buffer, grad_memory_out.at[pl.ds(t * memory_length, memory_length), :])
    running.drain()
    stores.drain()


def params(**more):
    return pltpu.CompilerParams(vmem_limit_bytes=VMEM_LIMIT, **more)


def on_device(
    tokens, memory, target_mask, buckets, expert_ids, slots, gain_self, w_query, w_key, w_value, w_output, rel_table, gain_cross,
    c_query, c_key, c_value, c_output, gain_moe, router, expert_in, expert_out, cotangent,
):
    rows, width = tokens.shape
    targets, length = target_mask.shape
    bucket_count, heads = rel_table.shape
    memory_length = memory.shape[0] // targets
    pairs = heads // 2
    experts = lax.axis_size("expert")
    hidden = expert_in.shape[2]
    capacity = (5 * rows + 4 * experts - 1) // (4 * experts)
    slot_rows = experts * capacity
    place = jnp.where(slots < capacity, expert_ids * capacity + slots, -1)
    place_row, place_column = place.reshape(1, rows), place.reshape(rows, 1)
    gains = jnp.stack([gain_self, gain_cross, gain_moe]).astype(F32)
    weights = (w_query, w_key, w_value, w_output, c_query, c_key, c_value, c_output)

    def exchange(buffer):
        buffer = buffer.reshape(experts, capacity, width)
        return lax.all_to_all(buffer, "expert", split_axis=0, concat_axis=0, tiled=True).reshape(slot_rows, width)

    row_shape = jax.ShapeDtypeStruct((slot_rows, width), BF16)
    gsent = pl.pallas_call(
        dispatch_kernel, out_shape=row_shape, in_specs=[VMEM, VMEM], out_specs=VMEM, compiler_params=params(), name="dispatch"
    )(place_row, cotangent)
    grows = exchange(gsent)

    act_shape = ((rows, width), BF16)
    wide_shape = ((rows, width), F32)
    key_shape = ((targets * memory_length, width), BF16)
    kept = (
        [act_shape] * 8
        + [wide_shape] * 2
        + [((targets, pairs, 2 * length, length), BF16), ((targets, pairs, 2 * length, memory_length), BF16), key_shape, key_shape]
        + [((slot_rows, width), BF16)]
    )
    h1, q1, k1, v1, c1, h2, q2, c2, x1, x2, p1, p2, k2, v2, sent = pl.pallas_call(
        functools.partial(forward_kernel, targets, length, memory_length, heads),
        out_shape=[jax.ShapeDtypeStruct(*k) for k in kept],
        in_specs=[SMEM, ANY, ANY, VMEM, VMEM, VMEM, VMEM] + [ANY] * 8,
        out_specs=[ANY] * len(kept),
        scratch_shapes=[pltpu.VMEM((rows, width), BF16), pltpu.VMEM(*key_shape), pltpu.VMEM((8, width, width), BF16)]
        + [pltpu.VMEM(*k) for k in kept]
        + [
            pltpu.VMEM((pairs, 2 * length, length), F32),
            pltpu.VMEM((2, 2 * length, memory_length), F32),
            pltpu.SemaphoreType.DMA((10,)),
            pltpu.SemaphoreType.DMA((len(kept),)),
        ],
        compiler_params=params(),
        name="forward",
    )(rel_table.astype(F32), tokens, memory, target_mask, buckets, gains, place_row, *weights)

    inbound = exchange(sent)
    router_wide = jnp.pad(router, ((0, 0), (0, LANES - experts)))
    weight_grad = jax.ShapeDtypeStruct((width, hidden), BF16)
    ret, dh, grad_first, grad_second, grad_router = pl.pallas_call(
        functools.partial(expert_kernel, experts),
        out_shape=[row_shape, row_shape, weight_grad, weight_grad, jax.ShapeDtypeStruct((LANES, width), F32)],
        in_specs=[VMEM, VMEM, VMEM, ANY, ANY],
        out_specs=[VMEM, VMEM, ANY, ANY, VMEM],
        scratch_shapes=[
            pltpu.VMEM((width, hidden), BF16),
            pltpu.VMEM((hidden, width), BF16),
            pltpu.VMEM((width, slot_rows), BF16),
            pltpu.VMEM((slot_rows, width), BF16),
            pltpu.VMEM((width, slot_rows), BF16),
            pltpu.VMEM((slot_rows, LANES), F32),
            pltpu.VMEM((slot_rows, width), F32),
            pltpu.VMEM((slot_rows, width), F32),
            pltpu.VMEM((slot_rows, width), BF16),
            pltpu.VMEM((slot_rows, width), BF16),
            pltpu.VMEM((slot_rows, width), F32),
            pltpu.VMEM((slot_rows, width), F32),
            pltpu.VMEM((2, width, width), BF16),
            pltpu.VMEM((2, width, width), BF16),
            pltpu.SemaphoreType.DMA((2 * (hidden // width),)),
            pltpu.SemaphoreType.DMA((2 * (hidden // width),)),
        ],
        compiler_params=params(),
        name="experts",
    )(inbound, grows, router_wide, expert_in[0], expert_out[0])

    dh_rows = exchange(dh)
    remote = lax.axis_size("dp") == 8 and experts == 4
    ret_rows = ret if remote else exchange(ret)
    grad_first = lax.psum_scatter(grad_first, "dp", scatter_dimension=1, tiled=True)
    grad_second = lax.psum_scatter(grad_second, "dp", scatter_dimension=1, tiled=True)

    square = (width, width)
    act, wide = pltpu.VMEM(*act_shape), pltpu.VMEM(*wide_shape)
    small_shape = (24, width)
    lands = 8 if remote else 1
    half = width // 2
    copies = 8 * (6 + 2 * (experts - 1)) + 2 * experts + 1
    results = pl.pallas_call(
        functools.partial(backward_kernel, targets, length, memory_length, heads, remote),
        out_shape=[jax.ShapeDtypeStruct(square, BF16)] * 8
        + [
            jax.ShapeDtypeStruct((rows, width), BF16),
            jax.ShapeDtypeStruct((rows, width), F32),
            jax.ShapeDtypeStruct(memory.shape, BF16),
            jax.ShapeDtypeStruct(small_shape, F32),
        ],
        in_specs=[ANY, ANY, VMEM, VMEM, VMEM, VMEM, VMEM] + [ANY] * 25,
        out_specs=[ANY] * 11 + [VMEM],
        scratch_shapes=[pltpu.VMEM((slot_rows, width), BF16)] * 2
        + [act] * 7
        + [
            wide,
            pltpu.VMEM((targets, pairs, 2 * length, length), BF16),
            pltpu.VMEM((5,) + square, BF16),
            pltpu.VMEM((2, pairs, 2 * length, memory_length), BF16),
            pltpu.VMEM((2, 2, memory_length, width), BF16),
            pltpu.VMEM((3 * rows, width), F32),
        ]
        + [act] * 6
        + [
            pltpu.VMEM((8,) + square, BF16),
            pltpu.VMEM((2, 2 * length, memory_length), F32),
            pltpu.VMEM((targets, pairs, 2 * length, memory_length), BF16),
            pltpu.VMEM((pairs, 2 * length, length), F32),
            pltpu.VMEM((3, 8, width), F32),
            pltpu.VMEM((48, LANES), F32),
            pltpu.VMEM((lands, width, half), BF16),
            pltpu.VMEM((lands, half, half), BF16),
            pltpu.VMEM((lands, half // 2, half), BF16),
            pltpu.VMEM((lands, experts - 1, half // 2 // experts, half), BF16),
            pltpu.VMEM((experts + 3,) + small_shape, F32),
            pltpu.SemaphoreType.DMA((23,)),
            pltpu.SemaphoreType.DMA((16,)),
            pltpu.SemaphoreType.DMA((3, 2)),
            pltpu.SemaphoreType.DMA((copies,)),
            pltpu.SemaphoreType.DMA((copies,)),
            pltpu.SemaphoreType.DMA((8,)),
        ],
        compiler_params=params(collective_id=0, has_side_effects=True) if remote else params(),
        name="backward",
    )(
        dh_rows, ret_rows, place_column, target_mask, buckets, gains, grad_router, cotangent, tokens, h1, q1, k1, v1, c1, h2, q2, c2, x1, x2,
        p1, p2, k2, v2, memory, *weights,
    )
    summed, (output, grad_tokens, grad_memory, small) = results[:8], results[8:]
    if not remote:
        summed, small = lax.psum((summed, small), ("dp", "expert"))
    summed = [g.astype(F32) for g in summed]
    table = small[16:24, : 4 * LANES].reshape(8, 4, LANES).transpose(1, 0, 2).reshape(32, LANES)[:bucket_count, :heads]
    return (
        output, grad_tokens, grad_memory, small[0], summed[0], summed[1], summed[2], summed[3], table, small[1], summed[4],
        summed[5], summed[6], summed[7], small[2], small[8 : 8 + experts].T, grad_first.astype(F32)[None],
        grad_second.astype(F32).T[None],
    )


def solution(mesh):
    both, spread = P(("dp", "expert")), P(("dp", "expert"), None)
    placed = (
        (spread, spread, spread, P(), both, both) + (P(),) * 13 + (P("expert", None, None), P("expert", None, None), spread)
    )
    return jax.shard_map(
        on_device,
        mesh=mesh,
        in_specs=placed,
        out_specs=(spread, spread, spread) + (P(),) * 13 + (P("expert", None, "dp"), P("expert", "dp", None)),
        check_vma=False,
    )
```

```python
import functools

import jax
import jax.numpy as jnp
from jax import lax
from jax.experimental import pallas as pl
from jax.experimental.pallas import tpu as pltpu
from jax.sharding import PartitionSpec as P

EPS = 1e-06
NEG = -1000000000.0
F32 = jnp.float32
BF16 = jnp.bfloat16
LANES = 128
VMEM_LIMIT = 60 * 1024 * 1024
ANY = pl.BlockSpec(memory_space=pl.ANY)
VMEM = pl.BlockSpec(memory_space=pltpu.VMEM)
SMEM = pl.BlockSpec(memory_space=pltpu.SMEM)


def dot(left, right):
    return lax.dot_general(left, right, (((1,), (0,)), ((), ())), preferred_element_type=F32)


def dot_nt(left, right):
    return lax.dot_general(left, right, (((1,), (1,)), ((), ())), preferred_element_type=F32)


def dot_tn(left, right):
    return lax.dot_general(left, right, (((0,), (0,)), ((), ())), preferred_element_type=F32)


def row_loop(count, step, body):
    def one(i, carry):
        body(pl.ds(pl.multiple_of(i * step, step), step))
        return carry

    lax.fori_loop(0, count // step, one, 0)


def half_masks():
    lane = lax.broadcasted_iota(jnp.int32, (1, LANES), 1)
    low = jnp.where(lane < LANES // 2, 1.0, 0.0).astype(BF16)
    high = jnp.where(lane < LANES // 2, 0.0, 1.0).astype(BF16)
    return lane < LANES // 2, low, high


def stacked(pair, low, high):
    return jnp.concatenate([pair * low, pair * high], axis=0)


def norm_rows(values, gain):
    return values * lax.rsqrt(jnp.mean(values * values, axis=-1, keepdims=True) + EPS) * gain


def norm_back(values, gain, grad):
    scale = lax.rsqrt(jnp.mean(values * values, axis=-1, keepdims=True) + EPS)
    scaled = grad * gain
    inner = jnp.mean(scaled * values, axis=-1, keepdims=True)
    back = scale * scaled - values * (scale * scale * scale * inner)
    gain_rows = grad * values * scale
    return back, jnp.sum(gain_rows.reshape(-1, 8, gain_rows.shape[-1]), axis=0)


def allowed_of(mask_row, length):
    row = lax.broadcasted_iota(jnp.int32, (length, length), 0)
    col = lax.broadcasted_iota(jnp.int32, (length, length), 1)
    return (col <= row) & (mask_row == 1)


class Loads:
    def __init__(self, sems):
        self.sems = sems
        self.count = 0
        self.open = {}

    def start(self, name, source, target):
        copy = pltpu.make_async_copy(source, target, self.sems.at[self.count])
        self.count += 1
        copy.start()
        self.open[name] = copy

    def wait(self, *names):
        for name in names:
            self.open.pop(name).wait()

    def drain(self):
        self.wait(*list(self.open))


class Ring:
    def __init__(self, send_sems, recv_sems):
        self.send_sems, self.recv_sems = send_sems, recv_sems
        self.count = 0
        dp, self.expert = lax.axis_index("dp"), lax.axis_index("expert")
        self.experts = lax.axis_size("expert")
        self.dp = dp
        self.spot = {"core": lax.rem(dp, 2), "x": lax.rem(lax.div(dp, 2), 2), "y": lax.div(dp, 4)}
        self.partner = {name: dp + step - 2 * step * self.spot[name] for name, step in (("core", 1), ("x", 2), ("y", 4))}

        low, high = lax.rem(self.expert, 2), lax.div(self.expert, 2)
        near, far = 1 - 2 * low, 2 - 4 * high
        self.peers = [self.expert, self.expert + near, self.expert + far, self.expert + near + far]

    def others(self):
        return self.peers[1:]

    def block(self, expert, capacity):
        return pl.ds(pl.multiple_of(expert * capacity, 16), capacity)

    def slot(self, k, capacity, sender=None):
        low = lax.rem(self.expert if sender is None else sender, 2)
        return pl.ds(pl.multiple_of((low + (2 if k >= 2 else 0)) * capacity, 16), capacity)

    def scatter(self, source, target):
        capacity = source.shape[0] // self.experts
        return [
            self.send(source.at[self.block(e, capacity), :], target.at[self.slot(k, capacity), :], self.dp, e)
            for k, e in enumerate(self.peers)
            if k
        ]

    def greet(self, names):
        barrier = pltpu.get_barrier_semaphore()
        targets = [(self.partner[name], self.expert) for name in names] + [(self.dp, e) for e in self.others()]
        for target in targets:
            pl.semaphore_signal(barrier, inc=1, device_id=target, device_id_type=pl.DeviceIdType.MESH)
        pl.semaphore_wait(barrier, len(targets))

    def send(self, source, target, dp, expert):
        copy = pltpu.make_async_remote_copy(
            src_ref=source, dst_ref=target, send_sem=self.send_sems.at[self.count], recv_sem=self.recv_sems.at[self.count],
            device_id=(dp, expert), device_id_type=pl.DeviceIdType.MESH,
        )
        self.count += 1
        copy.start()
        return copy

    def cross(self, name, source, target):
        return self.send(source, target, self.partner[name], self.expert)


def forward_kernel(
    targets, length, memory_length, heads, remote,
    table, tokens, memory, mask, buckets, gains, place, cotangent, wq, wk, wv, wo, cq, ck, cv, co,
    h1_out, q1_out, k1_out, v1_out, c1_out, h2_out, q2_out, c2_out, x1_out, x2_out, p1_out, p2_out, k2_out, v2_out, sent_out, grows_out,
    tokens_v, memory_v, weights_v, h1, q1, k1, v1, c1, h2, q2, c2, x1, x2, p1, p2, k2, v2, sent, gsent, bias, scores, in_sems, out_sems,
    send_sems, recv_sems,
):
    rows, width = tokens_v.shape
    pairs = heads // 2
    loads, stores = Loads(in_sems), Loads(out_sems)
    loads.start("cot", cotangent, c2)
    loads.start("tokens", tokens, tokens_v)
    for index, (name, ref) in enumerate(zip(("wq", "wk", "wv"), (wq, wk, wv))):
        loads.start(name, ref, weights_v.at[index])
    loads.start("ck", ck, weights_v.at[5])
    loads.start("memory", memory, memory_v)
    loads.start("cv", cv, weights_v.at[6])
    loads.start("wo", wo, weights_v.at[3])
    loads.start("cq", cq, weights_v.at[4])
    loads.start("co", co, weights_v.at[7])
    gain = [gains[i : i + 1, :] for i in range(3)]
    low_lane, low, high = half_masks()

    if remote:
        ring = Ring(send_sems, recv_sems)
        ring.greet(())
    loads.wait("cot")
    dispatch(place, c2, gsent)
    gsent_copies = []
    if remote:
        gsent_copies = ring.scatter(gsent, grows_out)
        block = ring.block(ring.expert, sent.shape[0] // ring.experts)
        stores.start("grows", gsent.at[block, :], grows_out.at[ring.slot(0, sent.shape[0] // ring.experts), :])
    else:
        stores.start("grows", gsent, grows_out)
    bucket_count = table.shape[0]

    def bias_rows(r):
        here = buckets[r, :]
        hits = [here == b for b in range(bucket_count)]
        for head in range(heads):
            total = jnp.zeros(here.shape, F32)
            for b in range(bucket_count):
                total = jnp.where(hits[b], table[b, head], total)
            start = (head % 2) * length
            bias[head // 2, pl.ds(pl.multiple_of(r.start + start, 8), r.size), :] = total

    row_loop(length, 16, bias_rows)

    loads.wait("tokens")

    def first_norm(r):
        h1[r, :] = norm_rows(tokens_v[r, :].astype(F32), gain[0]).astype(BF16)

    row_loop(rows, 32, first_norm)
    stores.start("h1", h1, h1_out)
    for index, (name, ref) in enumerate(zip(("wq", "wk", "wv"), (q1, k1, v1))):
        loads.wait(name)

        def project(r, index=index, ref=ref):
            ref[r, :] = dot(h1[r, :], weights_v[index]).astype(BF16)

        row_loop(rows, 256, project)
    stores.start("q1", q1, q1_out)
    stores.start("k1", k1, k1_out)
    stores.start("v1", v1, v1_out)

    def self_target(t, carry):
        r = pl.ds(pl.multiple_of(t * length, length), length)
        allowed = allowed_of(mask[pl.ds(t, 1), :], length)
        for pair in range(pairs):
            lanes = slice(pair * LANES, (pair + 1) * LANES)
            both = dot_nt(stacked(q1[r, lanes], low, high), k1[r, lanes])
            for half in range(2):
                part = slice(half * length, (half + 1) * length)
                score = jnp.where(allowed, both[part] + bias[pair, part, :], NEG)
                expo = jnp.exp(score - jnp.max(score, axis=-1, keepdims=True))
                total = jnp.sum(expo, axis=-1, keepdims=True)
                p1[t, pair, part, :] = (expo / total).astype(BF16)
            context = dot(p1[t, pair], v1[r, lanes])
            c1[r, lanes] = jnp.where(low_lane, context[:length], context[length:]).astype(BF16)
        return carry

    lax.fori_loop(0, targets, self_target, 0)
    stores.start("p1", p1, p1_out)
    stores.start("c1", c1, c1_out)
    loads.wait("wo")

    def self_out(r):
        x1[r, :] = tokens_v[r, :].astype(F32) + dot(c1[r, :], weights_v[3])

    row_loop(rows, 256, self_out)
    stores.start("x1", x1, x1_out)

    def second_norm(r):
        h2[r, :] = norm_rows(x1[r, :], gain[1]).astype(BF16)

    row_loop(rows, 32, second_norm)
    stores.start("h2", h2, h2_out)
    loads.wait("cq")

    def cross_query(r):
        q2[r, :] = dot(h2[r, :], weights_v[4]).astype(BF16)

    row_loop(rows, 256, cross_query)
    stores.start("q2", q2, q2_out)
    loads.wait("memory", "ck", "cv")

    def cross_keys(r):
        k2[r, :] = dot(memory_v[r, :], weights_v[5]).astype(BF16)
        v2[r, :] = dot(memory_v[r, :], weights_v[6]).astype(BF16)

    row_loop(targets * memory_length, 256, cross_keys)
    stores.start("k2", k2, k2_out)
    stores.start("v2", v2, v2_out)

    def cross_target(t, carry):
        r = pl.ds(pl.multiple_of(t * length, length), length)
        m = pl.ds(pl.multiple_of(t * memory_length, memory_length), memory_length)
        for pair in range(pairs):
            lanes = slice(pair * LANES, (pair + 1) * LANES)
            slot = pair % 2
            scores[slot] = dot_nt(stacked(q2[r, lanes], low, high), k2[m, lanes])
            for chunk in range(2 * length // 32):
                part = slice(chunk * 32, (chunk + 1) * 32)
                score = scores[slot, part, :]
                expo = jnp.exp(score - jnp.max(score, axis=-1, keepdims=True))
                total = jnp.sum(expo, axis=-1, keepdims=True)
                p2[t, pair, part, :] = (expo / total).astype(BF16)
            context = dot(p2[t, pair], v2[m, lanes])
            c2[r, lanes] = jnp.where(low_lane, context[:length], context[length:]).astype(BF16)
        return carry

    lax.fori_loop(0, targets, cross_target, 0)
    stores.start("p2", p2, p2_out)
    stores.start("c2", c2, c2_out)
    loads.wait("co")

    def cross_out(r):
        x2[r, :] = x1[r, :] + dot(c2[r, :], weights_v[7])

    row_loop(rows, 256, cross_out)
    stores.start("x2", x2, x2_out)

    def third_norm(r):
        tokens_v[r, :] = norm_rows(x2[r, :], gain[2]).astype(BF16)

    row_loop(rows, 32, third_norm)
    dispatch(place, tokens_v, sent)
    stores.start("sent", sent, sent_out)
    for copy in gsent_copies:
        copy.wait()
    stores.drain()


def dispatch(place, source, target):
    step = 128

    def one(r):
        spot = lax.broadcasted_iota(jnp.int32, (step, source.shape[0]), 0) + r.start
        hit = jnp.where(spot == place[...], 1.0, 0.0).astype(BF16)
        target[r, :] = dot(hit, source[...]).astype(target.dtype)

    row_loop(target.shape[0], step, one)


def collect(place_column, step, r, source):
    spot = lax.broadcasted_iota(jnp.int32, (step, source.shape[0]), 1)
    hit = jnp.where(spot == place_column[r, :], 1.0, 0.0).astype(BF16)
    return dot(hit, source[...])


def expert_kernel(
    experts, remote, inbound, grows, router, first, second,
    ret_out, dh_out, grad_first, grad_second, grad_router,
    first_v, second_v, inbound_v, grows_v, inbound_t, dret, dret_t, probs, pre, dact, act, dpre, ret, dinb, ret_v, dh_v, sums, landing,
    in_sems, out_sems, send_sems, recv_sems,
):
    rows, width = inbound_v.shape
    hidden = first.shape[1]
    step = width
    tiles = hidden // step
    loads, stores = Loads(in_sems), Loads(out_sems)
    capacity = rows // experts
    half_rows = rows // 2
    if remote:
        ring = Ring(send_sems, recv_sems)
        ring.greet(("core",))
        arriving = ring.scatter(inbound, inbound_v)
        loads.start("inbound", inbound.at[ring.block(ring.expert, capacity), :], inbound_v.at[ring.slot(0, capacity), :])
    else:
        loads.start("inbound", inbound, inbound_v)
        arriving = []
    loads.start("grows", grows, grows_v)
    for f in range(tiles):
        cols = slice(f * step, (f + 1) * step)
        loads.start(("first", f), first.at[:, cols], first_v.at[:, cols])
        loads.start(("second", f), second.at[cols, :], second_v.at[cols, :])
    me = lax.axis_index("expert")
    lane = lax.broadcasted_iota(jnp.int32, (1, LANES), 1)
    mine = lane == me
    root = (2.0 / jnp.pi) ** 0.5
    grad_router[...] = jnp.zeros_like(grad_router)
    loads.wait("inbound", "grows")
    returning = []
    for side in range(2):
        start = side * half_rows
        here = slice(start, start + half_rows)
        for copy in (arriving[:1], arriving[1:])[side]:
            copy.wait_recv()

        def route(r, start=start):
            r = pl.ds(pl.multiple_of(start + r.start, 16), r.size)
            logits = jnp.where(lane < experts, dot(inbound_v[r, :], router[...]), -1e30)
            expo = jnp.exp(logits - jnp.max(logits, axis=-1, keepdims=True))
            prob = expo / jnp.sum(expo, axis=-1, keepdims=True)
            probs[r, :] = prob
            gate = jnp.sum(jnp.where(mine, prob, 0.0), axis=-1, keepdims=True)
            dret[r, :] = (gate * grows_v[r, :].astype(F32)).astype(BF16)

        row_loop(half_rows, half_rows // 2, route)
        for f in range(tiles):
            cols = slice(f * step, (f + 1) * step)
            if side == 0:
                loads.wait(("first", f), ("second", f))
            for c in range(0, step, 256):
                tile = slice(f * step + c, f * step + c + 256)
                pre[:, c : c + 256] = dot(inbound_v[here, :], first_v[:, tile])
                dact[:, c : c + 256] = dot_nt(dret[here, :], second_v[tile, :])

            def middle(r, start=start, cols=cols):
                u = pre[r, :]
                square = u * u
                t = jnp.tanh(root * (u + 0.044715 * (square * u)))
                half = 0.5 * (1.0 + t)
                out = pl.ds(pl.multiple_of(start + r.start, 16), r.size)
                act[out, cols] = (u * half).astype(BF16)
                slope = half + (0.5 * root) * u * (1.0 - t * t) * (1.0 + (3 * 0.044715) * square)
                dpre[out, cols] = (dact[r, :] * slope).astype(BF16)

            row_loop(half_rows, 16, middle)
            for c in range(0, width, 256):
                tile = slice(c, c + 256)
                one, two = dot(act[here, cols], second_v[cols, tile]), dot_nt(dpre[here, cols], first_v[tile, cols])
                if f:
                    one, two = one + ret[:, tile], two + dinb[:, tile]
                ret[:, tile] = one
                dinb[:, tile] = two

        def finish(r, start=start):
            out = pl.ds(pl.multiple_of(start + r.start, 16), r.size)
            result = ret[r, :].astype(BF16).astype(F32)
            prob = probs[out, :]
            gate = jnp.sum(jnp.where(mine, prob, 0.0), axis=-1, keepdims=True)
            dgate = jnp.sum(result * grows_v[out, :].astype(F32), axis=-1, keepdims=True)
            dlogits = (prob * (jnp.where(mine, 1.0, 0.0) - gate) * dgate).astype(BF16)
            ret_v[out, :] = (gate * result).astype(BF16)
            dh_v[out, :] = (dinb[r, :].astype(BF16).astype(F32) + dot_nt(dlogits, router[...])).astype(BF16)
            grad_router[...] += dot_tn(dlogits, inbound_v[out, :])

        row_loop(half_rows, half_rows // 2, finish)
        if remote:
            target = dh_out.at[ring.block(ring.expert, capacity), :]
            for k in ((1,), (2, 3))[side]:
                source = dh_v.at[ring.slot(k, capacity, ring.peers[k]), :]
                returning.append(ring.send(source, target, ring.dp, ring.peers[k]))
            if side == 0:
                stores.start("dh", dh_v.at[ring.slot(0, capacity), :], target)
        elif side:
            stores.start("dh", dh_v, dh_out)
    stores.start("ret", ret_v, ret_out)
    for copy in arriving:
        copy.wait_send()
    for c in range(width // LANES):
        cols = slice(c * LANES, (c + 1) * LANES)
        inbound_t[cols, :] = inbound_v[:, cols].T
        dret_t[cols, :] = dret[:, cols].T

    crossing = []

    def settle():
        f, copies = crossing.pop(0)
        for copy in copies:
            copy.wait()
        for j, out in enumerate((grad_first, grad_second)):

            def add(r, j=j, f=f):
                total = sums[j, ring.spot["core"], f, r, :].astype(F32) + landing[j, f, r, :].astype(F32)
                landing[j, f, r, :] = total.astype(BF16)

            row_loop(width, 64, add)
            stores.start(("sum", j, f), landing.at[j, f], out.at[f])

    for f in range(tiles):
        for j, (left, right) in enumerate(((inbound_t, dpre), (dret_t, act))):
            for b in range(2):
                cols = slice(f * step + b * (step // 2), f * step + (b + 1) * (step // 2))

                def weights(r, j=j, b=b, f=f, left=left, right=right, cols=cols):
                    sums[j, b, f, r, :] = dot(left[r, :], right[:, cols]).astype(BF16)

                row_loop(width, 256, weights)
                if not remote:
                    stores.start(("sum", j, b, f), sums.at[j, b, f], (grad_first, grad_second)[j].at[:, cols])
        if remote:
            other = 1 - ring.spot["core"]
            crossing.append((f, [ring.cross("core", sums.at[j, other, f], landing.at[j, f]) for j in range(2)]))
            if f:
                settle()
    if remote:
        settle()
        for copy in returning:
            copy.wait()
    stores.drain()


def span(start, size):
    return pl.ds(pl.multiple_of(start, size), size)


def add_into(ref, rows, lanes, others):
    step = 48 if rows.size % 64 else 64
    for i in range(rows.size // step):
        here = pl.ds(pl.multiple_of(rows.start + i * step, 16), step)
        total = ref[here, lanes].astype(F32)
        for other in others:
            total = total + other[i * step : (i + 1) * step, :].astype(F32)
        ref[here, lanes] = total.astype(BF16)


def reduce_matrix(ring, local, result, landing, first, second, copy_sem):
    size = local.shape[0]
    half, quarter, eighth = size // 2, size // 4, size // 4 // ring.experts
    half_land, quarter_land, eighth_land, part_land = landing
    core = ring.spot["core"]
    mine, other = span(core * half, half), span((1 - core) * half, half)
    copy = ring.cross("core", local.at[:, other], half_land)
    yield 1
    copy.wait()
    add_into(local, pl.ds(0, size), mine, [half_land])
    place = ring.spot[first] * half
    copy = ring.cross(first, local.at[span(half - place, half), mine], quarter_land)
    yield 2
    copy.wait()
    add_into(local, span(place, half), mine, [quarter_land])
    step = ring.spot[second] * quarter
    copy = ring.cross(second, local.at[span(place + quarter - step, quarter), mine], eighth_land)
    yield 1
    copy.wait()
    base = place + step
    add_into(local, span(base, quarter), mine, [eighth_land])
    copies = [
        ring.send(local.at[pl.ds(pl.multiple_of(base + e * eighth, 16), eighth), mine], part_land.at[k], ring.dp, e)
        for k, e in enumerate(ring.others())
    ]
    yield 1
    for copy in copies:
        copy.wait()
    part = pl.ds(pl.multiple_of(base + ring.expert * eighth, 16), eighth)
    add_into(local, part, mine, [part_land.at[k] for k in range(ring.experts - 1)])
    own = pltpu.make_async_copy(local.at[part, mine], result.at[part, mine], copy_sem)
    own.start()
    copies = [ring.send(local.at[part, mine], result.at[part, mine], ring.dp, e) for e in ring.others()]
    yield 1
    own.wait()
    for copy in copies:
        copy.wait()
    here = span(base, quarter)
    copy = ring.cross(second, result.at[here, mine], result.at[here, mine])
    yield 1
    copy.wait()
    here = span(place, half)
    copy = ring.cross(first, result.at[here, mine], result.at[here, mine])
    yield 2
    copy.wait()
    copy = ring.cross("core", result.at[:, mine], result.at[:, mine])
    yield 1
    copy.wait()


def reduce_expert(ring, part, near_land, far_land, keep, extra, first, result, sems):
    size, block = part.shape[1], part.shape[2]
    x, y = ring.spot["x"], ring.spot["y"]
    along_x = first == "x"
    stays = (x, 2 + x) if along_x else (2 * y, 2 * y + 1)
    leaves = (1 - x, 3 - x) if along_x else (2 - 2 * y, 3 - 2 * y)
    copies = [ring.cross(first, part.at[b], near_land.at[i]) for i, b in enumerate(leaves)]
    cols = [slice(i * block, (i + 1) * block) for i in range(2)]
    copies += [pltpu.make_async_copy(part.at[b], keep.at[:, cols[i]], sems.at[i]) for i, b in enumerate(stays)]
    for copy in copies[2:]:
        copy.start()
    yield 6
    for copy in copies:
        copy.wait()
    copies = [pltpu.make_async_copy(near_land.at[i], extra.at[:, cols[i]], sems.at[2 + i]) for i in range(2)]
    for copy in copies:
        copy.start()
    for copy in copies:
        copy.wait()
    for i in range(2):
        add_into(keep, pl.ds(0, size), cols[i], [extra.at[:, cols[i]]])
    spot = y if along_x else x
    copy = ring.cross("y" if along_x else "x", keep.at[:, span((1 - spot) * block, block)], far_land)
    yield 3
    copy.wait()
    copy = pltpu.make_async_copy(far_land, extra.at[:, cols[0]], sems.at[4])
    copy.start()
    copy.wait()
    stay = span(spot * block, block)
    add_into(keep, pl.ds(0, size), stay, [extra.at[:, cols[0]]])
    copy = pltpu.make_async_copy(keep.at[:, stay], result, sems.at[5])
    copy.start()
    copy.wait()


def reduce_small(ring, local, landing):
    for k, name in enumerate(("core", "x", "y")):
        copy = ring.cross(name, local, landing.at[k])
        yield 1
        copy.wait()
        local[...] += landing[k]
    copies = [ring.send(local, landing.at[3 + ring.expert], ring.dp, e) for e in ring.others()]
    landing[3 + ring.expert] = local[...]
    yield 1
    for copy in copies:
        copy.wait()
    total = landing[3]
    for e in range(1, ring.experts):
        total = total + landing[3 + e]
    local[...] = total


class Running:
    def __init__(self):
        self.steps = []

    def add(self, steps):
        self.steps.append([steps, next(steps)])

    def tick(self, patient=True):
        going = []
        for entry in self.steps:
            entry[1] -= 1
            if entry[1] <= 0 or not patient:
                entry[1] = next(entry[0], None)
            if entry[1] is not None:
                going.append(entry)
        self.steps = going

    def finish(self, steps):
        for entry in self.steps:
            if any(entry[0] is s for s in steps):
                for _ in entry[0]:
                    pass
                entry[1] = None
        self.steps = [e for e in self.steps if e[1] is not None]

    def drain(self):
        while self.steps:
            self.tick(False)


def backward_kernel(
    targets, length, memory_length, heads, remote,
    dh_rows, ret_rows, place_column, mask, buckets, gains, grad_router, cotangent, tokens, h1, q1, k1, v1, c1, h2, q2, c2, x1, x2, p1, p2,
    k2, v2, memory, wq, wk, wv, wo, cq, ck, cv, co, part_first, part_second,
    *rest,
):
    grad_refs, rest = rest[:8], rest[8:]
    (
        output_out, grad_tokens_out, grad_memory_out, sum_first, sum_second, near_first, near_second, far_first, far_second, small,
        rows_v, ret_v, first_v, ctx_v, norm_v, q2_v, q1_v, k1_v, v1_v, x2_v, p1_v, weights_v,
        p2_v, kv_v, wide, do, dctx2, dctx1, dq, dk, dv, grads, dscores, ds, dsum, gain_acc, table_v, half_land, quarter_land, eighth_land,
        part_land, small_land, in_sems, out_sems, ring_sems, send_sems, recv_sems, own_sems, expert_sems,
    ) = rest
    rows, width = first_v.shape
    pairs = heads // 2
    x1_v, du, dx = wide.at[0:rows, :], wide.at[rows : 2 * rows, :], wide.at[2 * rows : 3 * rows, :]
    gk, gv = wide.at[0:width, :], wide.at[width : 2 * width, :]
    spare = (dctx1, dq)
    loads, stores, running = Loads(in_sems), Loads(out_sems), Running()
    loads.start("rows", dh_rows, rows_v)
    loads.start("cot", cotangent, first_v)
    loads.start("x2", x2, x2_v)
    loads.start("c2", c2, ctx_v)
    loads.start("co", co, weights_v.at[0])

    def fetch(t, sources):
        slot = t % 2
        m = pl.ds(t * memory_length, memory_length)
        for index, source in enumerate(sources):
            target = p2_v.at[slot] if index == 0 else kv_v.at[index - 1, slot]
            copy = pltpu.make_async_copy(source.at[t] if index == 0 else source.at[m, :], target, ring_sems.at[index, slot])
            copy.start()
            yield copy

    fetched = list(fetch(0, (p2, k2, v2)))
    for name, source, target in (
        ("q2", q2, q2_v), ("cq", cq, weights_v.at[1]), ("h2", h2, norm_v), ("x1", x1, x1_v), ("wo", wo, weights_v.at[2]),
        ("p1", p1, p1_v), ("q1", q1, q1_v), ("k1", k1, k1_v), ("v1", v1, v1_v), ("ck", ck, weights_v.at[3]),
        ("cv", cv, weights_v.at[4]),
    ):
        loads.start(name, source, target)
    if remote:
        ring = Ring(send_sems, recv_sems)
        ring.greet(("core", "x", "y"))
        capacity = rows_v.shape[0] // ring.experts
        mine = ring.block(ring.expert, capacity)
        ret_copies = [
            ring.send(ret_rows.at[ring.slot(k, capacity, e), :], ret_v.at[mine, :], ring.dp, e) for k, e in enumerate(ring.peers) if k
        ]
        loads.start("ret", ret_rows.at[ring.slot(0, capacity), :], ret_v.at[mine, :])
        expert_sums = [
            reduce_expert(ring, part_first, near_first, far_first, grads.at[0], grads.at[2], "x", sum_first, expert_sems.at[0]),
            reduce_expert(ring, part_second, near_second, far_second, grads.at[1], grads.at[5], "y", sum_second, expert_sems.at[1]),
        ]
        for steps in expert_sums:
            running.add(steps)
    else:
        ret_copies, expert_sums = [], []
        loads.start("ret", ret_rows, ret_v)

    gain = [gains[i : i + 1, :] for i in range(3)]
    low_lane, low, high = half_masks()
    gain_acc[...] = jnp.zeros_like(gain_acc)
    axes = ("x", "y")
    started = []

    def total_of(index):
        if remote:
            way = len(started) % 2
            landing = [land.at[index] for land in (half_land, quarter_land, eighth_land, part_land)]
            running.add(reduce_matrix(ring, grads.at[index], grad_refs[index], landing, axes[way], axes[1 - way], own_sems.at[index]))
        else:
            stores.start(("grad", index), grads.at[index], grad_refs[index])
        started.append(index)

    def inner_grad(index, left, right):
        for c in range(width // 256):
            cols = slice(c * 256, (c + 1) * 256)
            grads[index, cols, :] = dot_tn(left[:, cols], right[...]).astype(BF16)
        total_of(index)

    def back_through(values, index, base, target):
        def one(r):
            back, gain_rows = norm_back(values[r, :].astype(F32), gain[index], du[r, :])
            total = base[r, :].astype(F32) + back
            target[r, :] = total
            do[r, :] = total.astype(BF16)
            gain_acc[index] += gain_rows

        row_loop(rows, 32, one)

    loads.wait("rows", "cot", "x2")

    def gather(r):
        du[r, :] = collect(place_column, 128, r, rows_v)

    row_loop(rows, 128, gather)
    back_through(x2_v, 2, first_v, dx)
    loads.start("tokens", tokens, first_v)
    loads.wait("c2", "co")
    inner_grad(7, ctx_v, do)
    loads.start("c1", c1, ctx_v)

    def out_back(r, slot, target):
        target[r, :] = dot_nt(do[r, :], weights_v[slot]).astype(BF16)

    row_loop(rows, 256, functools.partial(out_back, slot=0, target=dctx2))
    loads.start("wq", wq, weights_v.at[0])
    loads.wait("q2")
    for t in range(targets):
        slot = t % 2
        ahead = list(fetch(t + 1, (p2, k2, v2))) if t + 1 < targets else []
        for copy in fetched:
            copy.wait()
        fetched = ahead
        r = slice(t * length, (t + 1) * length)
        for pair in range(pairs):
            lanes = slice(pair * LANES, (pair + 1) * LANES)
            side = pair % 2
            dscores[side] = dot_nt(stacked(dctx2[r, lanes], low, high), kv_v[1, slot, :, lanes])
            for chunk in range(2 * length // 32):
                part = slice(chunk * 32, (chunk + 1) * 32)
                prob = p2_v[slot, pair, part, :].astype(F32)
                dprob = dscores[side, part, :]
                inner = jnp.sum(prob * dprob, axis=-1, keepdims=True)
                ds[t, pair, part, :] = (prob * (dprob - inner)).astype(BF16)
            back = dot(ds[t, pair], kv_v[0, slot, :, lanes])
            dq[r, lanes] = jnp.where(low_lane, back[:length], back[length:]).astype(BF16)
        running.tick()
    fetched = list(fetch(0, (p2, memory)))
    loads.wait("h2", "cq", "x1")
    inner_grad(4, norm_v, dq)
    loads.start("h1", h1, norm_v)

    def query_back(r):
        du[r, :] = dot_nt(dq[r, :], weights_v[1])

    row_loop(rows, 256, query_back)
    loads.start("wk", wk, weights_v.at[1])
    back_through(x1_v, 1, dx, dx)
    running.tick()
    loads.wait("c1", "wo")
    inner_grad(3, ctx_v, do)
    row_loop(rows, 256, functools.partial(out_back, slot=2, target=dctx1))
    loads.start("wv", wv, weights_v.at[2])
    for copy in ret_copies:
        copy.wait()
    loads.wait("ret")

    def output_rows(r):
        dk[r, :] = (x2_v[r, :] + collect(place_column, 128, r, ret_v)).astype(BF16)

    row_loop(rows, 128, output_rows)
    stores.start("output", dk, output_out)
    running.tick()
    loads.wait("p1", "q1", "k1", "v1")
    stores.wait("output")
    for t in range(targets):
        r = slice(t * length, (t + 1) * length)
        allowed = allowed_of(mask[t : t + 1, :], length)
        for pair in range(pairs):
            lanes = slice(pair * LANES, (pair + 1) * LANES)
            side = pair % 2
            grad_rows = stacked(dctx1[r, lanes], low, high)
            both = dot_nt(grad_rows, v1_v[r, lanes])
            scratch = p2_v.at[1, side]
            for half in range(2):
                part = slice(half * length, (half + 1) * length)
                prob = p1_v[t, pair, part, :].astype(F32)
                dprob = both[part]
                inner = jnp.sum(prob * dprob, axis=-1, keepdims=True)
                score = jnp.where(allowed, prob * (dprob - inner), 0.0).astype(BF16)
                scratch[part, :length] = score
                wide_score = score.astype(F32)
                dsum[pair, part, :] = wide_score if t == 0 else dsum[pair, part, :] + wide_score
            dv[r, lanes] = dot_tn(p1_v[t, pair], grad_rows).astype(BF16)
            dk[r, lanes] = dot_tn(scratch[:, :length], stacked(q1_v[r, lanes], low, high)).astype(BF16)
            back = dot(scratch[:, :length], k1_v[r, lanes])
            dq[r, lanes] = jnp.where(low_lane, back[:length], back[length:]).astype(BF16)
        if t % 2:
            running.tick()
    loads.wait("h1", "wq", "wk", "wv", "tokens")
    running.finish(expert_sums)
    for index, right in enumerate((dq, dk, dv)):
        inner_grad(index, norm_v, right)

    def self_back(r):
        du[r, :] = dot_nt(dq[r, :], weights_v[0]) + dot_nt(dk[r, :], weights_v[1]) + dot_nt(dv[r, :], weights_v[2])

    row_loop(rows, 256, self_back)
    running.tick()
    back_through(first_v, 0, dx, dx)
    stores.start("tokens", dx, grad_tokens_out)
    small[...] = jnp.zeros_like(small)
    for i in range(3):
        small[i : i + 1, :] = jnp.sum(gain_acc[i], axis=0, keepdims=True)
    small[8:16, :] = grad_router[0:8, :]
    table_v[...] = jnp.zeros_like(table_v)

    def table_rows(b, carry):
        hit = buckets[...] == b
        for head in range(heads):
            start = (head % 2) * length
            part = jnp.where(hit, dsum[head // 2, start : start + length, :], 0.0)
            table_v[pl.ds(head, 1), :] = jnp.sum(part, axis=0, keepdims=True)
        sums = jnp.sum(table_v[0:16, :], axis=-1, keepdims=True)
        eye = lax.broadcasted_iota(jnp.int32, (16, LANES), 0) == lax.broadcasted_iota(jnp.int32, (16, LANES), 1)
        table_v[pl.ds(16 + b, 1), :] = jnp.sum(jnp.where(eye, sums, 0.0), axis=0, keepdims=True)
        return carry

    lax.fori_loop(0, 32, table_rows, 0)
    for b in range(0, 32, 8):
        small[16:24, b // 8 * LANES : (b // 8 + 1) * LANES] = table_v[16 + b : 24 + b, :]
    if remote:
        running.add(reduce_small(ring, small, small_land))
    running.tick()
    loads.wait("ck", "cv")
    stores.wait("tokens")
    for t in range(targets):
        slot = t % 2
        ahead = list(fetch(t + 1, (p2, memory))) if t + 1 < targets else []
        for copy in fetched:
            copy.wait()
        fetched = ahead
        r = slice(t * length, (t + 1) * length)
        for pair in range(pairs):
            lanes = slice(pair * LANES, (pair + 1) * LANES)
            dv[:, lanes] = dot_tn(p2_v[slot, pair], stacked(dctx2[r, lanes], low, high)).astype(BF16)
            dk[:, lanes] = dot_tn(ds[t, pair], stacked(q2_v[r, lanes], low, high)).astype(BF16)
        last = t + 1 == targets
        for index, total, right in ((5, gk, dk), (6, gv, dv)):
            for c in range(width // 256):
                cols = slice(c * 256, (c + 1) * 256)
                part = dot_tn(kv_v[0, slot, :, cols], right[...])
                if t:
                    part = part + total[cols, :]
                if last:
                    grads[index, cols, :] = part.astype(BF16)
                else:
                    total[cols, :] = part
            if last:
                total_of(index)
        running.tick()
        buffer = spare[slot]
        if t >= 2:
            stores.wait(("memory", t - 2))

        def memory_rows(q, buffer=buffer):
            buffer[q, :] = (dot_nt(dk[q, :], weights_v[3]) + dot_nt(dv[q, :], weights_v[4])).astype(BF16)

        row_loop(memory_length, 256, memory_rows)
        stores.start(("memory", t), buffer, grad_memory_out.at[pl.ds(t * memory_length, memory_length), :])
    running.drain()
    stores.drain()


def params(**more):
    return pltpu.CompilerParams(vmem_limit_bytes=VMEM_LIMIT, **more)


def on_device(
    tokens, memory, target_mask, buckets, expert_ids, slots, gain_self, w_query, w_key, w_value, w_output, rel_table, gain_cross,
    c_query, c_key, c_value, c_output, gain_moe, router, expert_in, expert_out, cotangent,
):
    rows, width = tokens.shape
    targets, length = target_mask.shape
    bucket_count, heads = rel_table.shape
    memory_length = memory.shape[0] // targets
    pairs = heads // 2
    experts = lax.axis_size("expert")
    hidden = expert_in.shape[2]
    capacity = (5 * rows + 4 * experts - 1) // (4 * experts)
    slot_rows = experts * capacity
    place = jnp.where(slots < capacity, expert_ids * capacity + slots, -1)
    place_row, place_column = place.reshape(1, rows), place.reshape(rows, 1)
    gains = jnp.stack([gain_self, gain_cross, gain_moe]).astype(F32)
    weights = (w_query, w_key, w_value, w_output, c_query, c_key, c_value, c_output)

    remote = lax.axis_size("dp") == 8 and experts == 4 and hidden == 4 * width

    def exchange(buffer):
        if remote:
            return buffer
        buffer = buffer.reshape(experts, capacity, width)
        return lax.all_to_all(buffer, "expert", split_axis=0, concat_axis=0, tiled=True).reshape(slot_rows, width)

    def remote_params(collective_id):
        return params(collective_id=collective_id, has_side_effects=True) if remote else params()

    row_shape = jax.ShapeDtypeStruct((slot_rows, width), BF16)
    act_shape = ((rows, width), BF16)
    wide_shape = ((rows, width), F32)
    key_shape = ((targets * memory_length, width), BF16)
    kept = (
        [act_shape] * 8
        + [wide_shape] * 2
        + [((targets, pairs, 2 * length, length), BF16), ((targets, pairs, 2 * length, memory_length), BF16), key_shape, key_shape]
        + [((slot_rows, width), BF16)] * 2
    )
    h1, q1, k1, v1, c1, h2, q2, c2, x1, x2, p1, p2, k2, v2, sent, grows = pl.pallas_call(
        functools.partial(forward_kernel, targets, length, memory_length, heads, remote),
        out_shape=[jax.ShapeDtypeStruct(*k) for k in kept],
        in_specs=[SMEM, ANY, ANY, VMEM, VMEM, VMEM, VMEM, ANY] + [ANY] * 8,
        out_specs=[ANY] * len(kept),
        scratch_shapes=[pltpu.VMEM((rows, width), BF16), pltpu.VMEM(*key_shape), pltpu.VMEM((8, width, width), BF16)]
        + [pltpu.VMEM(*k) for k in kept]
        + [
            pltpu.VMEM((pairs, 2 * length, length), F32),
            pltpu.VMEM((2, 2 * length, memory_length), F32),
            pltpu.SemaphoreType.DMA((11,)),
            pltpu.SemaphoreType.DMA((len(kept),)),
            pltpu.SemaphoreType.DMA((experts - 1,)),
            pltpu.SemaphoreType.DMA((experts - 1,)),
        ],
        compiler_params=remote_params(1),
        name="forward",
    )(rel_table.astype(F32), tokens, memory, target_mask, buckets, gains, place_row, cotangent, *weights)

    sent, grows = exchange(sent), exchange(grows)
    router_wide = jnp.pad(router, ((0, 0), (0, LANES - experts)))
    tiles = hidden // width
    half = width // 2
    weight_grad = jax.ShapeDtypeStruct((tiles, width, half) if remote else (width, hidden), BF16)
    row_scratch, half_scratch = pltpu.VMEM((slot_rows, width), BF16), pltpu.VMEM((slot_rows // 2, width), F32)
    ret, dh, grad_first, grad_second, grad_router = pl.pallas_call(
        functools.partial(expert_kernel, experts, remote),
        out_shape=[row_shape, row_shape, weight_grad, weight_grad, jax.ShapeDtypeStruct((LANES, width), F32)],
        in_specs=[ANY, ANY, VMEM, ANY, ANY],
        out_specs=[ANY, ANY, ANY, ANY, VMEM],
        scratch_shapes=[
            pltpu.VMEM((width, hidden), BF16),
            pltpu.VMEM((hidden, width), BF16),
            row_scratch,
            row_scratch,
            pltpu.VMEM((width, slot_rows), BF16),
            row_scratch,
            pltpu.VMEM((width, slot_rows), BF16),
            pltpu.VMEM((slot_rows, LANES), F32),
            half_scratch,
            half_scratch,
            pltpu.VMEM((slot_rows, hidden), BF16),
            pltpu.VMEM((slot_rows, hidden), BF16),
            half_scratch,
            half_scratch,
            row_scratch,
            row_scratch,
            pltpu.VMEM((2, 2, tiles, width, half), BF16),
            pltpu.VMEM((2, tiles, width, half), BF16),
            pltpu.SemaphoreType.DMA((2 * tiles + 2,)),
            pltpu.SemaphoreType.DMA((4 * tiles + 2,)),
            pltpu.SemaphoreType.DMA((2 * experts - 2 + 2 * tiles,)),
            pltpu.SemaphoreType.DMA((2 * experts - 2 + 2 * tiles,)),
        ],
        compiler_params=remote_params(2),
        name="experts",
    )(sent, grows, router_wide, expert_in[0], expert_out[0])
    dh_rows, ret_rows = exchange(dh), exchange(ret)
    parts = (grad_first, grad_second)
    if not remote:
        parts = (ret, ret)

    square = (width, width)
    act, wide = pltpu.VMEM(*act_shape), pltpu.VMEM(*wide_shape)
    small_shape = (24, width)
    lands = 8 if remote else 1
    copies = 8 * (6 + 2 * (experts - 1)) + 2 * experts + 1 + 6
    block = jax.ShapeDtypeStruct((width, half), BF16)
    two_blocks = jax.ShapeDtypeStruct((2, width, half), BF16)
    results = pl.pallas_call(
        functools.partial(backward_kernel, targets, length, memory_length, heads, remote),
        out_shape=[jax.ShapeDtypeStruct(square, BF16)] * 8
        + [
            jax.ShapeDtypeStruct((rows, width), BF16),
            jax.ShapeDtypeStruct((rows, width), F32),
            jax.ShapeDtypeStruct(memory.shape, BF16),
            block,
            block,
            two_blocks,
            two_blocks,
            block,
            block,
            jax.ShapeDtypeStruct(small_shape, F32),
        ],
        in_specs=[ANY, ANY, VMEM, VMEM, VMEM, VMEM, VMEM] + [ANY] * 27,
        out_specs=[ANY] * 17 + [VMEM],
        scratch_shapes=[pltpu.VMEM((slot_rows, width), BF16)] * 2
        + [act] * 7
        + [
            wide,
            pltpu.VMEM((targets, pairs, 2 * length, length), BF16),
            pltpu.VMEM((5,) + square, BF16),
            pltpu.VMEM((2, pairs, 2 * length, memory_length), BF16),
            pltpu.VMEM((2, 2, memory_length, width), BF16),
            pltpu.VMEM((3 * rows, width), F32),
        ]
        + [act] * 6
        + [
            pltpu.VMEM((8,) + square, BF16),
            pltpu.VMEM((2, 2 * length, memory_length), F32),
            pltpu.VMEM((targets, pairs, 2 * length, memory_length), BF16),
            pltpu.VMEM((pairs, 2 * length, length), F32),
            pltpu.VMEM((3, 8, width), F32),
            pltpu.VMEM((48, LANES), F32),
            pltpu.VMEM((lands, width, half), BF16),
            pltpu.VMEM((lands, half, half), BF16),
            pltpu.VMEM((lands, half // 2, half), BF16),
            pltpu.VMEM((lands, experts - 1, half // 2 // experts, half), BF16),
            pltpu.VMEM((experts + 3,) + small_shape, F32),
            pltpu.SemaphoreType.DMA((23,)),
            pltpu.SemaphoreType.DMA((16,)),
            pltpu.SemaphoreType.DMA((3, 2)),
            pltpu.SemaphoreType.DMA((copies,)),
            pltpu.SemaphoreType.DMA((copies,)),
            pltpu.SemaphoreType.DMA((8,)),
            pltpu.SemaphoreType.DMA((2, 6)),
        ],
        compiler_params=remote_params(0),
        name="backward",
    )(
        dh_rows, ret_rows, place_column, target_mask, buckets, gains, grad_router, cotangent, tokens, h1, q1, k1, v1, c1, h2, q2, c2, x1, x2,
        p1, p2, k2, v2, memory, *weights, *parts,
    )
    summed, (output, grad_tokens, grad_memory, grad_first_sum, grad_second_sum), small = results[:8], results[8:13], results[-1]
    if not remote:
        summed, small = lax.psum((summed, small), ("dp", "expert"))
        grad_first_sum, grad_second_sum = (
            lax.psum_scatter(g, "dp", scatter_dimension=1, tiled=True) for g in (grad_first, grad_second)
        )
    summed = [g.astype(F32) for g in summed]
    table = small[16:24, : 4 * LANES].reshape(8, 4, LANES).transpose(1, 0, 2).reshape(32, LANES)[:bucket_count, :heads]
    return (
        output, grad_tokens, grad_memory, small[0], summed[0], summed[1], summed[2], summed[3], table, small[1], summed[4],
        summed[5], summed[6], summed[7], small[2], small[8 : 8 + experts].T, grad_first_sum.astype(F32)[None],
        grad_second_sum.astype(F32).T[None],
    )


def solution(mesh):
    both, spread = P(("dp", "expert")), P(("dp", "expert"), None)
    placed = (
        (spread, spread, spread, P(), both, both) + (P(),) * 13 + (P("expert", None, None), P("expert", None, None), spread)
    )
    return jax.shard_map(
        on_device,
        mesh=mesh,
        in_specs=placed,
        out_specs=(spread, spread, spread) + (P(),) * 13 + (P("expert", None, "dp"), P("expert", "dp", None)),
        check_vma=False,
    )
```

```python
import functools

import jax
import jax.numpy as jnp
from jax import lax
from jax.experimental import pallas as pl
from jax.experimental.pallas import tpu as pltpu
from jax.sharding import PartitionSpec as P

EPS = 1e-06
NEG = -1000000000.0
F32 = jnp.float32
BF16 = jnp.bfloat16
LANES = 128
VMEM_LIMIT = 60 * 1024 * 1024
ANY = pl.BlockSpec(memory_space=pl.ANY)
VMEM = pl.BlockSpec(memory_space=pltpu.VMEM)
SMEM = pl.BlockSpec(memory_space=pltpu.SMEM)


def dot(left, right):
    return lax.dot_general(left, right, (((1,), (0,)), ((), ())), preferred_element_type=F32)


def dot_nt(left, right):
    return lax.dot_general(left, right, (((1,), (1,)), ((), ())), preferred_element_type=F32)


def dot_tn(left, right):
    return lax.dot_general(left, right, (((0,), (0,)), ((), ())), preferred_element_type=F32)


def row_loop(count, step, body):
    def one(i, carry):
        body(pl.ds(pl.multiple_of(i * step, step), step))
        return carry

    lax.fori_loop(0, count // step, one, 0)


def half_masks():
    lane = lax.broadcasted_iota(jnp.int32, (1, LANES), 1)
    low = jnp.where(lane < LANES // 2, 1.0, 0.0).astype(BF16)
    high = jnp.where(lane < LANES // 2, 0.0, 1.0).astype(BF16)
    return lane < LANES // 2, low, high


def stacked(pair, low, high):
    return jnp.concatenate([pair * low, pair * high], axis=0)


def norm_rows(values, gain):
    return values * lax.rsqrt(jnp.mean(values * values, axis=-1, keepdims=True) + EPS) * gain


def norm_back(values, gain, grad):
    scale = lax.rsqrt(jnp.mean(values * values, axis=-1, keepdims=True) + EPS)
    scaled = grad * gain
    inner = jnp.mean(scaled * values, axis=-1, keepdims=True)
    back = scale * scaled - values * (scale * scale * scale * inner)
    gain_rows = grad * values * scale
    return back, jnp.sum(gain_rows.reshape(-1, 8, gain_rows.shape[-1]), axis=0)


def allowed_of(mask_row, length):
    row = lax.broadcasted_iota(jnp.int32, (length, length), 0)
    col = lax.broadcasted_iota(jnp.int32, (length, length), 1)
    return (col <= row) & (mask_row == 1)


class Loads:
    def __init__(self, sems):
        self.sems = sems
        self.count = 0
        self.open = {}

    def start(self, name, source, target):
        copy = pltpu.make_async_copy(source, target, self.sems.at[self.count])
        self.count += 1
        copy.start()
        self.open[name] = copy

    def wait(self, *names):
        for name in names:
            self.open.pop(name).wait()

    def drain(self):
        self.wait(*list(self.open))


class Ring:
    def __init__(self, send_sems, recv_sems):
        self.send_sems, self.recv_sems = send_sems, recv_sems
        self.count = 0
        dp, self.expert = lax.axis_index("dp"), lax.axis_index("expert")
        self.experts = lax.axis_size("expert")
        self.dp = dp
        self.spot = {"core": lax.rem(dp, 2), "x": lax.rem(lax.div(dp, 2), 2), "y": lax.div(dp, 4)}
        self.partner = {name: dp + step - 2 * step * self.spot[name] for name, step in (("core", 1), ("x", 2), ("y", 4))}

        low, high = lax.rem(self.expert, 2), lax.div(self.expert, 2)
        near, far = 1 - 2 * low, 2 - 4 * high
        self.peers = [self.expert, self.expert + near, self.expert + far, self.expert + near + far]

    def others(self):
        return self.peers[1:]

    def block(self, expert, capacity):
        return pl.ds(pl.multiple_of(expert * capacity, 16), capacity)

    def slot(self, k, capacity, sender=None):
        low = lax.rem(self.expert if sender is None else sender, 2)
        return pl.ds(pl.multiple_of((low + (2 if k >= 2 else 0)) * capacity, 16), capacity)

    def scatter(self, source, target):
        capacity = source.shape[0] // self.experts
        return [
            self.send(source.at[self.block(e, capacity), :], target.at[self.slot(k, capacity), :], self.dp, e)
            for k, e in enumerate(self.peers)
            if k
        ]

    def greet(self, names):
        barrier = pltpu.get_barrier_semaphore()
        targets = [(self.partner[name], self.expert) for name in names] + [(self.dp, e) for e in self.others()]
        for target in targets:
            pl.semaphore_signal(barrier, inc=1, device_id=target, device_id_type=pl.DeviceIdType.MESH)
        pl.semaphore_wait(barrier, len(targets))

    def send(self, source, target, dp, expert):
        copy = pltpu.make_async_remote_copy(
            src_ref=source, dst_ref=target, send_sem=self.send_sems.at[self.count], recv_sem=self.recv_sems.at[self.count],
            device_id=(dp, expert), device_id_type=pl.DeviceIdType.MESH,
        )
        self.count += 1
        copy.start()
        return copy

    def cross(self, name, source, target):
        return self.send(source, target, self.partner[name], self.expert)


def forward_kernel(
    targets, length, memory_length, heads, remote,
    table, tokens, memory, mask, buckets, gains, place, cotangent, wq, wk, wv, wo, cq, ck, cv, co,
    h1_out, q1_out, k1_out, v1_out, c1_out, h2_out, q2_out, c2_out, x1_out, x2_out, p1_out, p2_out, k2_out, v2_out, sent_out, grows_out,
    tokens_v, memory_v, weights_v, h1, q1, k1, v1, c1, h2, q2, c2, x1, x2, p1, p2, k2, v2, sent, gsent, bias, scores, in_sems, out_sems,
    send_sems, recv_sems,
):
    rows, width = tokens_v.shape
    pairs = heads // 2
    loads, stores = Loads(in_sems), Loads(out_sems)
    loads.start("cot", cotangent, c2)
    loads.start("tokens", tokens, tokens_v)
    for index, (name, ref) in enumerate(zip(("wq", "wk", "wv"), (wq, wk, wv))):
        loads.start(name, ref, weights_v.at[index])
    loads.start("ck", ck, weights_v.at[5])
    loads.start("memory", memory, memory_v)
    loads.start("cv", cv, weights_v.at[6])
    loads.start("wo", wo, weights_v.at[3])
    loads.start("cq", cq, weights_v.at[4])
    loads.start("co", co, weights_v.at[7])
    gain = [gains[i : i + 1, :] for i in range(3)]
    low_lane, low, high = half_masks()

    if remote:
        ring = Ring(send_sems, recv_sems)
        ring.greet(())
    loads.wait("cot")
    dispatch(place, c2, gsent)
    gsent_copies = []
    if remote:
        gsent_copies = ring.scatter(gsent, grows_out)
        block = ring.block(ring.expert, sent.shape[0] // ring.experts)
        stores.start("grows", gsent.at[block, :], grows_out.at[ring.slot(0, sent.shape[0] // ring.experts), :])
    else:
        stores.start("grows", gsent, grows_out)
    bucket_count = table.shape[0]

    def bias_rows(r):
        here = buckets[r, :]
        hits = [here == b for b in range(bucket_count)]
        for head in range(heads):
            total = jnp.zeros(here.shape, F32)
            for b in range(bucket_count):
                total = jnp.where(hits[b], table[b, head], total)
            start = (head % 2) * length
            bias[head // 2, pl.ds(pl.multiple_of(r.start + start, 8), r.size), :] = total

    row_loop(length, 16, bias_rows)

    loads.wait("tokens")

    def first_norm(r):
        h1[r, :] = norm_rows(tokens_v[r, :].astype(F32), gain[0]).astype(BF16)

    row_loop(rows, 32, first_norm)
    stores.start("h1", h1, h1_out)
    for index, (name, ref) in enumerate(zip(("wq", "wk", "wv"), (q1, k1, v1))):
        loads.wait(name)

        def project(r, index=index, ref=ref):
            ref[r, :] = dot(h1[r, :], weights_v[index]).astype(BF16)

        row_loop(rows, 256, project)
    stores.start("q1", q1, q1_out)
    stores.start("k1", k1, k1_out)
    stores.start("v1", v1, v1_out)

    def self_target(t, carry):
        r = pl.ds(pl.multiple_of(t * length, length), length)
        allowed = allowed_of(mask[pl.ds(t, 1), :], length)
        for pair in range(pairs):
            lanes = slice(pair * LANES, (pair + 1) * LANES)
            both = dot_nt(stacked(q1[r, lanes], low, high), k1[r, lanes])
            for half in range(2):
                part = slice(half * length, (half + 1) * length)
                score = jnp.where(allowed, both[part] + bias[pair, part, :], NEG)
                expo = jnp.exp(score - jnp.max(score, axis=-1, keepdims=True))
                total = jnp.sum(expo, axis=-1, keepdims=True)
                p1[t, pair, part, :] = (expo / total).astype(BF16)
            context = dot(p1[t, pair], v1[r, lanes])
            c1[r, lanes] = jnp.where(low_lane, context[:length], context[length:]).astype(BF16)
        return carry

    lax.fori_loop(0, targets, self_target, 0)
    stores.start("p1", p1, p1_out)
    stores.start("c1", c1, c1_out)
    loads.wait("wo")

    def self_out(r):
        x1[r, :] = tokens_v[r, :].astype(F32) + dot(c1[r, :], weights_v[3])

    row_loop(rows, 256, self_out)
    stores.start("x1", x1, x1_out)

    def second_norm(r):
        h2[r, :] = norm_rows(x1[r, :], gain[1]).astype(BF16)

    row_loop(rows, 32, second_norm)
    stores.start("h2", h2, h2_out)
    loads.wait("cq")

    def cross_query(r):
        q2[r, :] = dot(h2[r, :], weights_v[4]).astype(BF16)

    row_loop(rows, 256, cross_query)
    stores.start("q2", q2, q2_out)
    loads.wait("memory", "ck", "cv")

    def cross_keys(r):
        k2[r, :] = dot(memory_v[r, :], weights_v[5]).astype(BF16)
        v2[r, :] = dot(memory_v[r, :], weights_v[6]).astype(BF16)

    row_loop(targets * memory_length, 256, cross_keys)
    stores.start("k2", k2, k2_out)
    stores.start("v2", v2, v2_out)

    def cross_target(t, carry):
        r = pl.ds(pl.multiple_of(t * length, length), length)
        m = pl.ds(pl.multiple_of(t * memory_length, memory_length), memory_length)
        for pair in range(pairs):
            lanes = slice(pair * LANES, (pair + 1) * LANES)
            slot = pair % 2
            scores[slot] = dot_nt(stacked(q2[r, lanes], low, high), k2[m, lanes])
            for chunk in range(2 * length // 32):
                part = slice(chunk * 32, (chunk + 1) * 32)
                score = scores[slot, part, :]
                expo = jnp.exp(score - jnp.max(score, axis=-1, keepdims=True))
                total = jnp.sum(expo, axis=-1, keepdims=True)
                p2[t, pair, part, :] = (expo / total).astype(BF16)
            context = dot(p2[t, pair], v2[m, lanes])
            c2[r, lanes] = jnp.where(low_lane, context[:length], context[length:]).astype(BF16)
        return carry

    lax.fori_loop(0, targets, cross_target, 0)
    stores.start("p2", p2, p2_out)
    stores.start("c2", c2, c2_out)
    loads.wait("co")

    def cross_out(r):
        x2[r, :] = x1[r, :] + dot(c2[r, :], weights_v[7])

    row_loop(rows, 256, cross_out)
    stores.start("x2", x2, x2_out)

    def third_norm(r):
        tokens_v[r, :] = norm_rows(x2[r, :], gain[2]).astype(BF16)

    row_loop(rows, 32, third_norm)
    dispatch(place, tokens_v, sent)
    stores.start("sent", sent, sent_out)
    for copy in gsent_copies:
        copy.wait()
    stores.drain()


def dispatch(place, source, target):
    step = 128

    def one(r):
        spot = lax.broadcasted_iota(jnp.int32, (step, source.shape[0]), 0) + r.start
        hit = jnp.where(spot == place[...], 1.0, 0.0).astype(BF16)
        target[r, :] = dot(hit, source[...]).astype(target.dtype)

    row_loop(target.shape[0], step, one)


def collect(place_column, step, r, source):
    spot = lax.broadcasted_iota(jnp.int32, (step, source.shape[0]), 1)
    hit = jnp.where(spot == place_column[r, :], 1.0, 0.0).astype(BF16)
    return dot(hit, source[...])


def expert_kernel(
    experts, remote, inbound, grows, router, first, second,
    ret_out, dh_out, grad_first, grad_second, grad_router,
    first_v, second_v, inbound_v, grows_v, inbound_t, dret, dret_t, probs, pre, dact, act, dpre, ret, dinb, ret_v, dh_v, sums, landing,
    in_sems, out_sems, send_sems, recv_sems,
):
    rows, width = inbound_v.shape
    hidden = first.shape[1]
    step = width
    tiles = hidden // step
    loads, stores = Loads(in_sems), Loads(out_sems)
    capacity = rows // experts
    half_rows = rows // 2
    if remote:
        ring = Ring(send_sems, recv_sems)
        ring.greet(("core",))
        arriving = ring.scatter(inbound, inbound_v)
        loads.start("inbound", inbound.at[ring.block(ring.expert, capacity), :], inbound_v.at[ring.slot(0, capacity), :])
    else:
        loads.start("inbound", inbound, inbound_v)
        arriving = []
    loads.start("grows", grows, grows_v)
    for f in range(tiles):
        cols = slice(f * step, (f + 1) * step)
        loads.start(("first", f), first.at[:, cols], first_v.at[:, cols])
        loads.start(("second", f), second.at[cols, :], second_v.at[cols, :])
    me = lax.axis_index("expert")
    lane = lax.broadcasted_iota(jnp.int32, (1, LANES), 1)
    mine = lane == me
    root = (2.0 / jnp.pi) ** 0.5
    grad_router[...] = jnp.zeros_like(grad_router)
    loads.wait("inbound", "grows")
    returning = []
    for side in range(2):
        start = side * half_rows
        here = slice(start, start + half_rows)
        for copy in (arriving[:1], arriving[1:])[side]:
            copy.wait_recv()

        def route(r, start=start):
            r = pl.ds(pl.multiple_of(start + r.start, 16), r.size)
            logits = jnp.where(lane < experts, dot(inbound_v[r, :], router[...]), -1e30)
            expo = jnp.exp(logits - jnp.max(logits, axis=-1, keepdims=True))
            prob = expo / jnp.sum(expo, axis=-1, keepdims=True)
            probs[r, :] = prob
            gate = jnp.sum(jnp.where(mine, prob, 0.0), axis=-1, keepdims=True)
            dret[r, :] = (gate * grows_v[r, :].astype(F32)).astype(BF16)

        row_loop(half_rows, half_rows // 2, route)
        for f in range(tiles):
            cols = slice(f * step, (f + 1) * step)
            if side == 0:
                loads.wait(("first", f), ("second", f))
            for c in range(0, step, 256):
                tile = slice(f * step + c, f * step + c + 256)
                pre[:, c : c + 256] = dot(inbound_v[here, :], first_v[:, tile])
                dact[:, c : c + 256] = dot_nt(dret[here, :], second_v[tile, :])

            def middle(r, start=start, cols=cols):
                u = pre[r, :]
                square = u * u
                t = jnp.tanh(root * (u + 0.044715 * (square * u)))
                half = 0.5 * (1.0 + t)
                out = pl.ds(pl.multiple_of(start + r.start, 16), r.size)
                act[out, cols] = (u * half).astype(BF16)
                slope = half + (0.5 * root) * u * (1.0 - t * t) * (1.0 + (3 * 0.044715) * square)
                dpre[out, cols] = (dact[r, :] * slope).astype(BF16)

            row_loop(half_rows, 16, middle)
            for c in range(0, width, 256):
                tile = slice(c, c + 256)
                one, two = dot(act[here, cols], second_v[cols, tile]), dot_nt(dpre[here, cols], first_v[tile, cols])
                if f:
                    one, two = one + ret[:, tile], two + dinb[:, tile]
                ret[:, tile] = one
                dinb[:, tile] = two

        def finish(r, start=start):
            out = pl.ds(pl.multiple_of(start + r.start, 16), r.size)
            result = ret[r, :].astype(BF16).astype(F32)
            prob = probs[out, :]
            gate = jnp.sum(jnp.where(mine, prob, 0.0), axis=-1, keepdims=True)
            dgate = jnp.sum(result * grows_v[out, :].astype(F32), axis=-1, keepdims=True)
            dlogits = (prob * (jnp.where(mine, 1.0, 0.0) - gate) * dgate).astype(BF16)
            ret_v[out, :] = (gate * result).astype(BF16)
            dh_v[out, :] = (dinb[r, :].astype(BF16).astype(F32) + dot_nt(dlogits, router[...])).astype(BF16)
            grad_router[...] += dot_tn(dlogits, inbound_v[out, :])

        row_loop(half_rows, half_rows // 2, finish)
        if remote:
            target = dh_out.at[ring.block(ring.expert, capacity), :]
            for k in ((1,), (2, 3))[side]:
                source = dh_v.at[ring.slot(k, capacity, ring.peers[k]), :]
                returning.append(ring.send(source, target, ring.dp, ring.peers[k]))
            if side == 0:
                stores.start("dh", dh_v.at[ring.slot(0, capacity), :], target)
        elif side:
            stores.start("dh", dh_v, dh_out)
    stores.start("ret", ret_v, ret_out)
    for copy in arriving:
        copy.wait_send()
    for c in range(width // LANES):
        cols = slice(c * LANES, (c + 1) * LANES)
        inbound_t[cols, :] = inbound_v[:, cols].T
        dret_t[cols, :] = dret[:, cols].T

    crossing = []

    def settle():
        f, copies = crossing.pop(0)
        for copy in copies:
            copy.wait()
        for j, out in enumerate((grad_first, grad_second)):

            def add(r, j=j, f=f):
                total = sums[j, ring.spot["core"], f, r, :].astype(F32) + landing[j, f, r, :].astype(F32)
                landing[j, f, r, :] = total.astype(BF16)

            row_loop(width, 64, add)
            stores.start(("sum", j, f), landing.at[j, f], out.at[f])

    for f in range(tiles):
        for j, (left, right) in enumerate(((inbound_t, dpre), (dret_t, act))):
            for b in range(2):
                cols = slice(f * step + b * (step // 2), f * step + (b + 1) * (step // 2))

                def weights(r, j=j, b=b, f=f, left=left, right=right, cols=cols):
                    sums[j, b, f, r, :] = dot(left[r, :], right[:, cols]).astype(BF16)

                row_loop(width, 256, weights)
                if not remote:
                    stores.start(("sum", j, b, f), sums.at[j, b, f], (grad_first, grad_second)[j].at[:, cols])
        if remote:
            other = 1 - ring.spot["core"]
            crossing.append((f, [ring.cross("core", sums.at[j, other, f], landing.at[j, f]) for j in range(2)]))
            if f:
                settle()
    if remote:
        settle()
        for copy in returning:
            copy.wait()
    stores.drain()


def span(start, size):
    return pl.ds(pl.multiple_of(start, size), size)


def add_into(ref, rows, lanes, others):
    step = 48 if rows.size % 64 else 64
    for i in range(rows.size // step):
        here = pl.ds(pl.multiple_of(rows.start + i * step, 16), step)
        total = ref[here, lanes].astype(F32)
        for other in others:
            total = total + other[i * step : (i + 1) * step, :].astype(F32)
        ref[here, lanes] = total.astype(BF16)


def reduce_matrix(ring, local, result, landing, first, second, copy_sem):
    size = local.shape[0]
    half, quarter, eighth = size // 2, size // 4, size // 4 // ring.experts
    half_land, quarter_land, eighth_land, part_land = landing
    core = ring.spot["core"]
    mine, other = span(core * half, half), span((1 - core) * half, half)
    copy = ring.cross("core", local.at[:, other], half_land)
    yield link_time("core", size, half)
    copy.wait()
    add_into(local, pl.ds(0, size), mine, [half_land])
    place = ring.spot[first] * half
    copy = ring.cross(first, local.at[span(half - place, half), mine], quarter_land)
    yield link_time(first, half, half)
    copy.wait()
    add_into(local, span(place, half), mine, [quarter_land])
    step = ring.spot[second] * quarter
    copy = ring.cross(second, local.at[span(place + quarter - step, quarter), mine], eighth_land)
    yield link_time(second, quarter, half)
    copy.wait()
    base = place + step
    add_into(local, span(base, quarter), mine, [eighth_land])
    copies = [
        ring.send(local.at[pl.ds(pl.multiple_of(base + e * eighth, 16), eighth), mine], part_land.at[k], ring.dp, e)
        for k, e in enumerate(ring.others())
    ]
    yield link_time("z", eighth, half)
    for copy in copies:
        copy.wait()
    part = pl.ds(pl.multiple_of(base + ring.expert * eighth, 16), eighth)
    add_into(local, part, mine, [part_land.at[k] for k in range(ring.experts - 1)])
    own = pltpu.make_async_copy(local.at[part, mine], result.at[part, mine], copy_sem)
    own.start()
    copies = [ring.send(local.at[part, mine], result.at[part, mine], ring.dp, e) for e in ring.others()]
    yield link_time("z", eighth, half)
    own.wait()
    for copy in copies:
        copy.wait()
    here = span(base, quarter)
    copy = ring.cross(second, result.at[here, mine], result.at[here, mine])
    yield link_time(second, quarter, half)
    copy.wait()
    here = span(place, half)
    copy = ring.cross(first, result.at[here, mine], result.at[here, mine])
    yield link_time(first, half, half)
    copy.wait()
    copy = ring.cross("core", result.at[:, mine], result.at[:, mine])
    yield link_time("core", size, half)
    copy.wait()


def reduce_expert(ring, part, near_land, far_land, keep, extra, first, result, sems):
    size, block = part.shape[1], part.shape[2]
    x, y = ring.spot["x"], ring.spot["y"]
    along_x = first == "x"
    stays = (x, 2 + x) if along_x else (2 * y, 2 * y + 1)
    leaves = (1 - x, 3 - x) if along_x else (2 - 2 * y, 3 - 2 * y)
    copies = [ring.cross(first, part.at[b], near_land.at[i]) for i, b in enumerate(leaves)]
    cols = [slice(i * block, (i + 1) * block) for i in range(2)]
    copies += [pltpu.make_async_copy(part.at[b], keep.at[:, cols[i]], sems.at[i]) for i, b in enumerate(stays)]
    for copy in copies[2:]:
        copy.start()
    yield link_time(first, size, 2 * block)
    for copy in copies:
        copy.wait()
    copies = [pltpu.make_async_copy(near_land.at[i], extra.at[:, cols[i]], sems.at[2 + i]) for i in range(2)]
    for copy in copies:
        copy.start()
    for copy in copies:
        copy.wait()
    for i in range(2):
        add_into(keep, pl.ds(0, size), cols[i], [extra.at[:, cols[i]]])
    spot = y if along_x else x
    copy = ring.cross("y" if along_x else "x", keep.at[:, span((1 - spot) * block, block)], far_land)
    yield link_time("y" if along_x else "x", size, block)
    copy.wait()
    copy = pltpu.make_async_copy(far_land, extra.at[:, cols[0]], sems.at[4])
    copy.start()
    copy.wait()
    stay = span(spot * block, block)
    add_into(keep, pl.ds(0, size), stay, [extra.at[:, cols[0]]])
    copy = pltpu.make_async_copy(keep.at[:, stay], result, sems.at[5])
    copy.start()
    copy.wait()


def reduce_small(ring, local, landing):
    for k, name in enumerate(("core", "x", "y")):
        copy = ring.cross(name, local, landing.at[k])
        yield link_time(name, *local.shape, 4)
        copy.wait()
        local[...] += landing[k]
    copies = [ring.send(local, landing.at[3 + ring.expert], ring.dp, e) for e in ring.others()]
    landing[3 + ring.expert] = local[...]
    yield link_time("z", *local.shape, 4)
    for copy in copies:
        copy.wait()
    total = landing[3]
    for e in range(1, ring.experts):
        total = total + landing[3 + e]
    local[...] = total


class Running:
    DELAY = 1.5

    def __init__(self):
        self.steps = []
        self.now = 0.0
        self.free = {}

    def land(self, entry, use):
        if use is None:
            self.steps = [e for e in self.steps if e is not entry]
            return
        link, time = use
        self.free[link] = max(self.now, self.free.get(link, 0.0)) + time
        entry[1] = self.free[link] + self.DELAY

    def add(self, steps):
        entry = [steps, 0.0]
        self.steps.append(entry)
        self.land(entry, next(steps))

    def advance(self, entry):
        self.now = max(self.now, entry[1]) + 0.3
        self.land(entry, next(entry[0], None))

    def tick(self, time):
        self.now += time
        while self.steps:
            entry = min(self.steps, key=lambda e: e[1])
            if entry[1] > self.now:
                break
            self.advance(entry)

    def finish(self, steps):
        while any(e[0] is s for e in self.steps for s in steps):
            self.advance(min(self.steps, key=lambda e: e[1]))

    def drain(self):
        while self.steps:
            self.advance(min(self.steps, key=lambda e: e[1]))


def link_time(name, rows, columns, itemsize=2):
    rate = {"core": 300e3, "x": 50e3, "y": 50e3, "z": 12.5e3}[name]
    return name, rows * columns * itemsize / rate


def backward_kernel(
    targets, length, memory_length, heads, remote,
    dh_rows, ret_rows, place_column, mask, buckets, gains, grad_router, cotangent, tokens, h1, q1, k1, v1, c1, h2, q2, c2, x1, x2, p1, p2,
    k2, v2, memory, wq, wk, wv, wo, cq, ck, cv, co, part_first, part_second,
    *rest,
):
    grad_refs, rest = rest[:8], rest[8:]
    (
        output_out, grad_tokens_out, grad_memory_out, sum_first, sum_second, near_first, near_second, far_first, far_second, small,
        rows_v, ret_v, first_v, ctx_v, norm_v, q2_v, q1_v, k1_v, v1_v, x2_v, p1_v, weights_v,
        p2_v, kv_v, wide, do, dctx2, dctx1, dq, dk, dv, grads, dscores, ds, dsum, gain_acc, table_v, half_land, quarter_land, eighth_land,
        part_land, small_land, in_sems, out_sems, ring_sems, send_sems, recv_sems, own_sems, expert_sems,
    ) = rest
    rows, width = first_v.shape
    pairs = heads // 2
    x1_v, du, dx = wide.at[0:rows, :], wide.at[rows : 2 * rows, :], wide.at[2 * rows : 3 * rows, :]
    gk, gv = wide.at[0:width, :], wide.at[width : 2 * width, :]
    spare = (dctx1, dq)
    loads, stores, running = Loads(in_sems), Loads(out_sems), Running()
    loads.start("rows", dh_rows, rows_v)
    loads.start("cot", cotangent, first_v)
    loads.start("x2", x2, x2_v)
    loads.start("c2", c2, ctx_v)
    loads.start("co", co, weights_v.at[0])

    def fetch(t, sources):
        slot = t % 2
        m = pl.ds(t * memory_length, memory_length)
        for index, source in enumerate(sources):
            target = p2_v.at[slot] if index == 0 else kv_v.at[index - 1, slot]
            copy = pltpu.make_async_copy(source.at[t] if index == 0 else source.at[m, :], target, ring_sems.at[index, slot])
            copy.start()
            yield copy

    fetched = list(fetch(0, (p2, k2, v2)))
    for name, source, target in (
        ("q2", q2, q2_v), ("cq", cq, weights_v.at[1]), ("h2", h2, norm_v), ("x1", x1, x1_v), ("wo", wo, weights_v.at[2]),
        ("p1", p1, p1_v), ("q1", q1, q1_v), ("k1", k1, k1_v), ("v1", v1, v1_v), ("ck", ck, weights_v.at[3]),
        ("cv", cv, weights_v.at[4]),
    ):
        loads.start(name, source, target)
    if remote:
        ring = Ring(send_sems, recv_sems)
        ring.greet(("core", "x", "y"))
        capacity = rows_v.shape[0] // ring.experts
        mine = ring.block(ring.expert, capacity)
        ret_copies = [
            ring.send(ret_rows.at[ring.slot(k, capacity, e), :], ret_v.at[mine, :], ring.dp, e) for k, e in enumerate(ring.peers) if k
        ]
        loads.start("ret", ret_rows.at[ring.slot(0, capacity), :], ret_v.at[mine, :])
        expert_sums = [
            reduce_expert(ring, part_first, near_first, far_first, grads.at[0], grads.at[2], "x", sum_first, expert_sems.at[0]),
            reduce_expert(ring, part_second, near_second, far_second, grads.at[1], grads.at[5], "y", sum_second, expert_sems.at[1]),
        ]
        for steps in expert_sums:
            running.add(steps)
    else:
        ret_copies, expert_sums = [], []
        loads.start("ret", ret_rows, ret_v)

    gain = [gains[i : i + 1, :] for i in range(3)]
    low_lane, low, high = half_masks()
    gain_acc[...] = jnp.zeros_like(gain_acc)
    axes = ("x", "y")
    started = []

    def total_of(index):
        if remote:
            way = len(started) % 2
            landing = [land.at[index] for land in (half_land, quarter_land, eighth_land, part_land)]
            running.add(reduce_matrix(ring, grads.at[index], grad_refs[index], landing, axes[way], axes[1 - way], own_sems.at[index]))
        else:
            stores.start(("grad", index), grads.at[index], grad_refs[index])
        started.append(index)

    def inner_grad(index, left, right):
        for c in range(width // 256):
            cols = slice(c * 256, (c + 1) * 256)
            grads[index, cols, :] = dot_tn(left[:, cols], right[...]).astype(BF16)
        total_of(index)

    def back_through(values, index, base, target):
        def one(r):
            back, gain_rows = norm_back(values[r, :].astype(F32), gain[index], du[r, :])
            total = base[r, :].astype(F32) + back
            target[r, :] = total
            do[r, :] = total.astype(BF16)
            gain_acc[index] += gain_rows

        row_loop(rows, 32, one)

    loads.wait("rows", "cot", "x2")

    def gather(r):
        du[r, :] = collect(place_column, 128, r, rows_v)

    row_loop(rows, 128, gather)
    back_through(x2_v, 2, first_v, dx)
    loads.start("tokens", tokens, first_v)
    loads.wait("c2", "co")
    inner_grad(7, ctx_v, do)
    loads.start("c1", c1, ctx_v)

    def out_back(r, slot, target):
        target[r, :] = dot_nt(do[r, :], weights_v[slot]).astype(BF16)

    row_loop(rows, 256, functools.partial(out_back, slot=0, target=dctx2))
    running.tick(7.0)
    loads.start("wq", wq, weights_v.at[0])
    loads.wait("q2")
    for t in range(targets):
        slot = t % 2
        ahead = list(fetch(t + 1, (p2, k2, v2))) if t + 1 < targets else []
        for copy in fetched:
            copy.wait()
        fetched = ahead
        r = slice(t * length, (t + 1) * length)
        for pair in range(pairs):
            lanes = slice(pair * LANES, (pair + 1) * LANES)
            side = pair % 2
            dscores[side] = dot_nt(stacked(dctx2[r, lanes], low, high), kv_v[1, slot, :, lanes])
            for chunk in range(2 * length // 32):
                part = slice(chunk * 32, (chunk + 1) * 32)
                prob = p2_v[slot, pair, part, :].astype(F32)
                dprob = dscores[side, part, :]
                inner = jnp.sum(prob * dprob, axis=-1, keepdims=True)
                ds[t, pair, part, :] = (prob * (dprob - inner)).astype(BF16)
            back = dot(ds[t, pair], kv_v[0, slot, :, lanes])
            dq[r, lanes] = jnp.where(low_lane, back[:length], back[length:]).astype(BF16)
            if side:
                running.tick(1.4)
    fetched = list(fetch(0, (p2, memory)))
    loads.wait("h2", "cq", "x1")
    inner_grad(4, norm_v, dq)
    loads.start("h1", h1, norm_v)

    def query_back(r):
        du[r, :] = dot_nt(dq[r, :], weights_v[1])

    row_loop(rows, 256, query_back)
    loads.start("wk", wk, weights_v.at[1])
    running.tick(2.5)
    back_through(x1_v, 1, dx, dx)
    running.tick(1.5)
    loads.wait("c1", "wo")
    inner_grad(3, ctx_v, do)
    row_loop(rows, 256, functools.partial(out_back, slot=2, target=dctx1))
    loads.start("wv", wv, weights_v.at[2])
    running.tick(2.5)
    for copy in ret_copies:
        copy.wait()
    loads.wait("ret")

    def output_rows(r):
        dk[r, :] = (x2_v[r, :] + collect(place_column, 128, r, ret_v)).astype(BF16)

    row_loop(rows, 128, output_rows)
    stores.start("output", dk, output_out)
    running.tick(2.0)
    loads.wait("p1", "q1", "k1", "v1")
    stores.wait("output")
    for t in range(targets):
        r = slice(t * length, (t + 1) * length)
        allowed = allowed_of(mask[t : t + 1, :], length)
        for pair in range(pairs):
            lanes = slice(pair * LANES, (pair + 1) * LANES)
            side = pair % 2
            grad_rows = stacked(dctx1[r, lanes], low, high)
            both = dot_nt(grad_rows, v1_v[r, lanes])
            scratch = p2_v.at[1, side]
            for half in range(2):
                part = slice(half * length, (half + 1) * length)
                prob = p1_v[t, pair, part, :].astype(F32)
                dprob = both[part]
                inner = jnp.sum(prob * dprob, axis=-1, keepdims=True)
                score = jnp.where(allowed, prob * (dprob - inner), 0.0).astype(BF16)
                scratch[part, :length] = score
                wide_score = score.astype(F32)
                dsum[pair, part, :] = wide_score if t == 0 else dsum[pair, part, :] + wide_score
            dv[r, lanes] = dot_tn(p1_v[t, pair], grad_rows).astype(BF16)
            dk[r, lanes] = dot_tn(scratch[:, :length], stacked(q1_v[r, lanes], low, high)).astype(BF16)
            back = dot(scratch[:, :length], k1_v[r, lanes])
            dq[r, lanes] = jnp.where(low_lane, back[:length], back[length:]).astype(BF16)
        running.tick(2.5)
    loads.wait("h1", "wq", "wk", "wv", "tokens")
    running.finish(expert_sums)
    for index, right in enumerate((dq, dk, dv)):
        inner_grad(index, norm_v, right)
        running.tick(1.2)

    def self_back(r):
        du[r, :] = dot_nt(dq[r, :], weights_v[0]) + dot_nt(dk[r, :], weights_v[1]) + dot_nt(dv[r, :], weights_v[2])

    row_loop(rows, 256, self_back)
    running.tick(2.5)
    back_through(first_v, 0, dx, dx)
    stores.start("tokens", dx, grad_tokens_out)
    small[...] = jnp.zeros_like(small)
    for i in range(3):
        small[i : i + 1, :] = jnp.sum(gain_acc[i], axis=0, keepdims=True)
    small[8:16, :] = grad_router[0:8, :]
    table_v[...] = jnp.zeros_like(table_v)

    def table_rows(b, carry):
        hit = buckets[...] == b
        for head in range(heads):
            start = (head % 2) * length
            part = jnp.where(hit, dsum[head // 2, start : start + length, :], 0.0)
            table_v[pl.ds(head, 1), :] = jnp.sum(part, axis=0, keepdims=True)
        sums = jnp.sum(table_v[0:16, :], axis=-1, keepdims=True)
        eye = lax.broadcasted_iota(jnp.int32, (16, LANES), 0) == lax.broadcasted_iota(jnp.int32, (16, LANES), 1)
        table_v[pl.ds(16 + b, 1), :] = jnp.sum(jnp.where(eye, sums, 0.0), axis=0, keepdims=True)
        return carry

    lax.fori_loop(0, 32, table_rows, 0)
    for b in range(0, 32, 8):
        small[16:24, b // 8 * LANES : (b // 8 + 1) * LANES] = table_v[16 + b : 24 + b, :]
    if remote:
        running.tick(4.0)
        running.add(reduce_small(ring, small, small_land))
    loads.wait("ck", "cv")
    stores.wait("tokens")
    for t in range(targets):
        slot = t % 2
        ahead = list(fetch(t + 1, (p2, memory))) if t + 1 < targets else []
        for copy in fetched:
            copy.wait()
        fetched = ahead
        r = slice(t * length, (t + 1) * length)
        for pair in range(pairs):
            lanes = slice(pair * LANES, (pair + 1) * LANES)
            dv[:, lanes] = dot_tn(p2_v[slot, pair], stacked(dctx2[r, lanes], low, high)).astype(BF16)
            dk[:, lanes] = dot_tn(ds[t, pair], stacked(q2_v[r, lanes], low, high)).astype(BF16)
            if pair % 3 == 2:
                running.tick(1.2)
        last = t + 1 == targets
        for index, total, right in ((5, gk, dk), (6, gv, dv)):
            for c in range(width // 256):
                cols = slice(c * 256, (c + 1) * 256)
                part = dot_tn(kv_v[0, slot, :, cols], right[...])
                if t:
                    part = part + total[cols, :]
                if last:
                    grads[index, cols, :] = part.astype(BF16)
                else:
                    total[cols, :] = part
            if last:
                total_of(index)
            running.tick(1.0)
        buffer = spare[slot]
        if t >= 2:
            stores.wait(("memory", t - 2))

        def memory_rows(q, buffer=buffer):
            buffer[q, :] = (dot_nt(dk[q, :], weights_v[3]) + dot_nt(dv[q, :], weights_v[4])).astype(BF16)

        row_loop(memory_length, 256, memory_rows)
        running.tick(1.2)
        stores.start(("memory", t), buffer, grad_memory_out.at[pl.ds(t * memory_length, memory_length), :])
    running.drain()
    stores.drain()


def params(**more):
    return pltpu.CompilerParams(vmem_limit_bytes=VMEM_LIMIT, **more)


def on_device(
    tokens, memory, target_mask, buckets, expert_ids, slots, gain_self, w_query, w_key, w_value, w_output, rel_table, gain_cross,
    c_query, c_key, c_value, c_output, gain_moe, router, expert_in, expert_out, cotangent,
):
    rows, width = tokens.shape
    targets, length = target_mask.shape
    bucket_count, heads = rel_table.shape
    memory_length = memory.shape[0] // targets
    pairs = heads // 2
    experts = lax.axis_size("expert")
    hidden = expert_in.shape[2]
    capacity = (5 * rows + 4 * experts - 1) // (4 * experts)
    slot_rows = experts * capacity
    place = jnp.where(slots < capacity, expert_ids * capacity + slots, -1)
    place_row, place_column = place.reshape(1, rows), place.reshape(rows, 1)
    gains = jnp.stack([gain_self, gain_cross, gain_moe]).astype(F32)
    weights = (w_query, w_key, w_value, w_output, c_query, c_key, c_value, c_output)

    remote = lax.axis_size("dp") == 8 and experts == 4 and hidden == 4 * width

    def exchange(buffer):
        if remote:
            return buffer
        buffer = buffer.reshape(experts, capacity, width)
        return lax.all_to_all(buffer, "expert", split_axis=0, concat_axis=0, tiled=True).reshape(slot_rows, width)

    def remote_params(collective_id):
        return params(collective_id=collective_id, has_side_effects=True) if remote else params()

    row_shape = jax.ShapeDtypeStruct((slot_rows, width), BF16)
    act_shape = ((rows, width), BF16)
    wide_shape = ((rows, width), F32)
    key_shape = ((targets * memory_length, width), BF16)
    kept = (
        [act_shape] * 8
        + [wide_shape] * 2
        + [((targets, pairs, 2 * length, length), BF16), ((targets, pairs, 2 * length, memory_length), BF16), key_shape, key_shape]
        + [((slot_rows, width), BF16)] * 2
    )
    h1, q1, k1, v1, c1, h2, q2, c2, x1, x2, p1, p2, k2, v2, sent, grows = pl.pallas_call(
        functools.partial(forward_kernel, targets, length, memory_length, heads, remote),
        out_shape=[jax.ShapeDtypeStruct(*k) for k in kept],
        in_specs=[SMEM, ANY, ANY, VMEM, VMEM, VMEM, VMEM, ANY] + [ANY] * 8,
        out_specs=[ANY] * len(kept),
        scratch_shapes=[pltpu.VMEM((rows, width), BF16), pltpu.VMEM(*key_shape), pltpu.VMEM((8, width, width), BF16)]
        + [pltpu.VMEM(*k) for k in kept]
        + [
            pltpu.VMEM((pairs, 2 * length, length), F32),
            pltpu.VMEM((2, 2 * length, memory_length), F32),
            pltpu.SemaphoreType.DMA((11,)),
            pltpu.SemaphoreType.DMA((len(kept),)),
            pltpu.SemaphoreType.DMA((experts - 1,)),
            pltpu.SemaphoreType.DMA((experts - 1,)),
        ],
        compiler_params=remote_params(1),
        name="forward",
    )(rel_table.astype(F32), tokens, memory, target_mask, buckets, gains, place_row, cotangent, *weights)

    sent, grows = exchange(sent), exchange(grows)
    router_wide = jnp.pad(router, ((0, 0), (0, LANES - experts)))
    tiles = hidden // width
    half = width // 2
    weight_grad = jax.ShapeDtypeStruct((tiles, width, half) if remote else (width, hidden), BF16)
    row_scratch, half_scratch = pltpu.VMEM((slot_rows, width), BF16), pltpu.VMEM((slot_rows // 2, width), F32)
    ret, dh, grad_first, grad_second, grad_router = pl.pallas_call(
        functools.partial(expert_kernel, experts, remote),
        out_shape=[row_shape, row_shape, weight_grad, weight_grad, jax.ShapeDtypeStruct((LANES, width), F32)],
        in_specs=[ANY, ANY, VMEM, ANY, ANY],
        out_specs=[ANY, ANY, ANY, ANY, VMEM],
        scratch_shapes=[
            pltpu.VMEM((width, hidden), BF16),
            pltpu.VMEM((hidden, width), BF16),
            row_scratch,
            row_scratch,
            pltpu.VMEM((width, slot_rows), BF16),
            row_scratch,
            pltpu.VMEM((width, slot_rows), BF16),
            pltpu.VMEM((slot_rows, LANES), F32),
            half_scratch,
            half_scratch,
            pltpu.VMEM((slot_rows, hidden), BF16),
            pltpu.VMEM((slot_rows, hidden), BF16),
            half_scratch,
            half_scratch,
            row_scratch,
            row_scratch,
            pltpu.VMEM((2, 2, tiles, width, half), BF16),
            pltpu.VMEM((2, tiles, width, half), BF16),
            pltpu.SemaphoreType.DMA((2 * tiles + 2,)),
            pltpu.SemaphoreType.DMA((4 * tiles + 2,)),
            pltpu.SemaphoreType.DMA((2 * experts - 2 + 2 * tiles,)),
            pltpu.SemaphoreType.DMA((2 * experts - 2 + 2 * tiles,)),
        ],
        compiler_params=remote_params(2),
        name="experts",
    )(sent, grows, router_wide, expert_in[0], expert_out[0])
    dh_rows, ret_rows = exchange(dh), exchange(ret)
    parts = (grad_first, grad_second)
    if not remote:
        parts = (ret, ret)

    square = (width, width)
    act, wide = pltpu.VMEM(*act_shape), pltpu.VMEM(*wide_shape)
    small_shape = (24, width)
    lands = 8 if remote else 1
    copies = 8 * (6 + 2 * (experts - 1)) + 2 * experts + 1 + 6
    block = jax.ShapeDtypeStruct((width, half), BF16)
    two_blocks = jax.ShapeDtypeStruct((2, width, half), BF16)
    results = pl.pallas_call(
        functools.partial(backward_kernel, targets, length, memory_length, heads, remote),
        out_shape=[jax.ShapeDtypeStruct(square, BF16)] * 8
        + [
            jax.ShapeDtypeStruct((rows, width), BF16),
            jax.ShapeDtypeStruct((rows, width), F32),
            jax.ShapeDtypeStruct(memory.shape, BF16),
            block,
            block,
            two_blocks,
            two_blocks,
            block,
            block,
            jax.ShapeDtypeStruct(small_shape, F32),
        ],
        in_specs=[ANY, ANY, VMEM, VMEM, VMEM, VMEM, VMEM] + [ANY] * 27,
        out_specs=[ANY] * 17 + [VMEM],
        scratch_shapes=[pltpu.VMEM((slot_rows, width), BF16)] * 2
        + [act] * 7
        + [
            wide,
            pltpu.VMEM((targets, pairs, 2 * length, length), BF16),
            pltpu.VMEM((5,) + square, BF16),
            pltpu.VMEM((2, pairs, 2 * length, memory_length), BF16),
            pltpu.VMEM((2, 2, memory_length, width), BF16),
            pltpu.VMEM((3 * rows, width), F32),
        ]
        + [act] * 6
        + [
            pltpu.VMEM((8,) + square, BF16),
            pltpu.VMEM((2, 2 * length, memory_length), F32),
            pltpu.VMEM((targets, pairs, 2 * length, memory_length), BF16),
            pltpu.VMEM((pairs, 2 * length, length), F32),
            pltpu.VMEM((3, 8, width), F32),
            pltpu.VMEM((48, LANES), F32),
            pltpu.VMEM((lands, width, half), BF16),
            pltpu.VMEM((lands, half, half), BF16),
            pltpu.VMEM((lands, half // 2, half), BF16),
            pltpu.VMEM((lands, experts - 1, half // 2 // experts, half), BF16),
            pltpu.VMEM((experts + 3,) + small_shape, F32),
            pltpu.SemaphoreType.DMA((23,)),
            pltpu.SemaphoreType.DMA((16,)),
            pltpu.SemaphoreType.DMA((3, 2)),
            pltpu.SemaphoreType.DMA((copies,)),
            pltpu.SemaphoreType.DMA((copies,)),
            pltpu.SemaphoreType.DMA((8,)),
            pltpu.SemaphoreType.DMA((2, 6)),
        ],
        compiler_params=remote_params(0),
        name="backward",
    )(
        dh_rows, ret_rows, place_column, target_mask, buckets, gains, grad_router, cotangent, tokens, h1, q1, k1, v1, c1, h2, q2, c2, x1, x2,
        p1, p2, k2, v2, memory, *weights, *parts,
    )
    summed, (output, grad_tokens, grad_memory, grad_first_sum, grad_second_sum), small = results[:8], results[8:13], results[-1]
    if not remote:
        summed, small = lax.psum((summed, small), ("dp", "expert"))
        grad_first_sum, grad_second_sum = (
            lax.psum_scatter(g, "dp", scatter_dimension=1, tiled=True) for g in (grad_first, grad_second)
        )
    summed = [g.astype(F32) for g in summed]
    table = small[16:24, : 4 * LANES].reshape(8, 4, LANES).transpose(1, 0, 2).reshape(32, LANES)[:bucket_count, :heads]
    return (
        output, grad_tokens, grad_memory, small[0], summed[0], summed[1], summed[2], summed[3], table, small[1], summed[4],
        summed[5], summed[6], summed[7], small[2], small[8 : 8 + experts].T, grad_first_sum.astype(F32)[None],
        grad_second_sum.astype(F32).T[None],
    )


def solution(mesh):
    both, spread = P(("dp", "expert")), P(("dp", "expert"), None)
    placed = (
        (spread, spread, spread, P(), both, both) + (P(),) * 13 + (P("expert", None, None), P("expert", None, None), spread)
    )
    return jax.shard_map(
        on_device,
        mesh=mesh,
        in_specs=placed,
        out_specs=(spread, spread, spread) + (P(),) * 13 + (P("expert", None, "dp"), P("expert", "dp", None)),
        check_vma=False,
    )
```

```python
import functools

import jax
import jax.numpy as jnp
from jax import lax
from jax.experimental import pallas as pl
from jax.experimental.pallas import tpu as pltpu
from jax.sharding import PartitionSpec as P

EPS = 1e-06
NEG = -1000000000.0
F32 = jnp.float32
BF16 = jnp.bfloat16
LANES = 128
VMEM_LIMIT = 60 * 1024 * 1024
ANY = pl.BlockSpec(memory_space=pl.ANY)
VMEM = pl.BlockSpec(memory_space=pltpu.VMEM)
SMEM = pl.BlockSpec(memory_space=pltpu.SMEM)


def dot(left, right):
    return lax.dot_general(left, right, (((1,), (0,)), ((), ())), preferred_element_type=F32)


def dot_nt(left, right):
    return lax.dot_general(left, right, (((1,), (1,)), ((), ())), preferred_element_type=F32)


def dot_tn(left, right):
    return lax.dot_general(left, right, (((0,), (0,)), ((), ())), preferred_element_type=F32)


def row_loop(count, step, body):
    def one(i, carry):
        body(pl.ds(pl.multiple_of(i * step, step), step))
        return carry

    lax.fori_loop(0, count // step, one, 0)


def half_masks():
    lane = lax.broadcasted_iota(jnp.int32, (1, LANES), 1)
    low = jnp.where(lane < LANES // 2, 1.0, 0.0).astype(BF16)
    high = jnp.where(lane < LANES // 2, 0.0, 1.0).astype(BF16)
    return lane < LANES // 2, low, high


def stacked(pair, low, high):
    return jnp.concatenate([pair * low, pair * high], axis=0)


def norm_rows(values, gain):
    return values * lax.rsqrt(jnp.mean(values * values, axis=-1, keepdims=True) + EPS) * gain


def norm_back(values, gain, grad):
    scale = lax.rsqrt(jnp.mean(values * values, axis=-1, keepdims=True) + EPS)
    scaled = grad * gain
    inner = jnp.mean(scaled * values, axis=-1, keepdims=True)
    back = scale * scaled - values * (scale * scale * scale * inner)
    gain_rows = grad * values * scale
    return back, jnp.sum(gain_rows.reshape(-1, 8, gain_rows.shape[-1]), axis=0)


def allowed_of(mask_row, length):
    row = lax.broadcasted_iota(jnp.int32, (length, length), 0)
    col = lax.broadcasted_iota(jnp.int32, (length, length), 1)
    return (col <= row) & (mask_row == 1)


class Loads:
    def __init__(self, sems):
        self.sems = sems
        self.count = 0
        self.open = {}

    def start(self, name, source, target):
        copy = pltpu.make_async_copy(source, target, self.sems.at[self.count])
        self.count += 1
        copy.start()
        self.open[name] = copy

    def wait(self, *names):
        for name in names:
            self.open.pop(name).wait()

    def drain(self):
        self.wait(*list(self.open))


class Ring:
    def __init__(self, send_sems, recv_sems):
        self.send_sems, self.recv_sems = send_sems, recv_sems
        self.count = 0
        dp, self.expert = lax.axis_index("dp"), lax.axis_index("expert")
        self.experts = lax.axis_size("expert")
        self.dp = dp
        self.spot = {"core": lax.rem(dp, 2), "x": lax.rem(lax.div(dp, 2), 2), "y": lax.div(dp, 4)}
        self.partner = {name: dp + step - 2 * step * self.spot[name] for name, step in (("core", 1), ("x", 2), ("y", 4))}

        low, high = lax.rem(self.expert, 2), lax.div(self.expert, 2)
        near, far = 1 - 2 * low, 2 - 4 * high
        self.peers = [self.expert, self.expert + near, self.expert + far, self.expert + near + far]

    def others(self):
        return self.peers[1:]

    def block(self, expert, capacity):
        return pl.ds(pl.multiple_of(expert * capacity, 16), capacity)

    def slot(self, k, capacity, sender=None):
        low = lax.rem(self.expert if sender is None else sender, 2)
        return pl.ds(pl.multiple_of((low + (2 if k >= 2 else 0)) * capacity, 16), capacity)

    def scatter(self, source, target):
        capacity = source.shape[0] // self.experts
        return [
            self.send(source.at[self.block(e, capacity), :], target.at[self.slot(k, capacity), :], self.dp, e)
            for k, e in enumerate(self.peers)
            if k
        ]

    def greet(self, names):
        barrier = pltpu.get_barrier_semaphore()
        targets = [(self.partner[name], self.expert) for name in names] + [(self.dp, e) for e in self.others()]
        for target in targets:
            pl.semaphore_signal(barrier, inc=1, device_id=target, device_id_type=pl.DeviceIdType.MESH)
        pl.semaphore_wait(barrier, len(targets))

    def send(self, source, target, dp, expert):
        copy = pltpu.make_async_remote_copy(
            src_ref=source, dst_ref=target, send_sem=self.send_sems.at[self.count], recv_sem=self.recv_sems.at[self.count],
            device_id=(dp, expert), device_id_type=pl.DeviceIdType.MESH,
        )
        self.count += 1
        copy.start()
        return copy

    def cross(self, name, source, target):
        return self.send(source, target, self.partner[name], self.expert)


def forward_kernel(
    targets, length, memory_length, heads, remote,
    table, tokens, memory, mask, buckets, gains, place, cotangent, wq, wk, wv, wo, cq, ck, cv, co,
    h1_out, q1_out, k1_out, v1_out, c1_out, h2_out, q2_out, c2_out, x1_out, x2_out, p1_out, p2_out, k2_out, v2_out, sent_out, grows_out,
    tokens_v, memory_v, weights_v, h1, q1, k1, v1, c1, h2, q2, c2, x1, x2, p1, p2, k2, v2, sent, gsent, bias, scores, in_sems, out_sems,
    send_sems, recv_sems,
):
    rows, width = tokens_v.shape
    pairs = heads // 2
    loads, stores = Loads(in_sems), Loads(out_sems)
    loads.start("cot", cotangent, c2)
    loads.start("tokens", tokens, tokens_v)
    for index, (name, ref) in enumerate(zip(("wq", "wk", "wv"), (wq, wk, wv))):
        loads.start(name, ref, weights_v.at[index])
    loads.start("ck", ck, weights_v.at[5])
    loads.start("memory", memory, memory_v)
    loads.start("cv", cv, weights_v.at[6])
    loads.start("wo", wo, weights_v.at[3])
    loads.start("cq", cq, weights_v.at[4])
    loads.start("co", co, weights_v.at[7])
    gain = [gains[i : i + 1, :] for i in range(3)]
    low_lane, low, high = half_masks()

    if remote:
        ring = Ring(send_sems, recv_sems)
        ring.greet(())
    loads.wait("cot")
    dispatch(place, c2, gsent)
    gsent_copies = []
    if remote:
        gsent_copies = ring.scatter(gsent, grows_out)
        block = ring.block(ring.expert, sent.shape[0] // ring.experts)
        stores.start("grows", gsent.at[block, :], grows_out.at[ring.slot(0, sent.shape[0] // ring.experts), :])
    else:
        stores.start("grows", gsent, grows_out)
    bucket_count = table.shape[0]

    def bias_rows(r):
        here = buckets[r, :]
        hits = [here == b for b in range(bucket_count)]
        for head in range(heads):
            total = jnp.zeros(here.shape, F32)
            for b in range(bucket_count):
                total = jnp.where(hits[b], table[b, head], total)
            start = (head % 2) * length
            bias[head // 2, pl.ds(pl.multiple_of(r.start + start, 8), r.size), :] = total

    row_loop(length, 16, bias_rows)

    loads.wait("tokens")

    def first_norm(r):
        h1[r, :] = norm_rows(tokens_v[r, :].astype(F32), gain[0]).astype(BF16)

    row_loop(rows, 32, first_norm)
    stores.start("h1", h1, h1_out)
    for index, (name, ref) in enumerate(zip(("wq", "wk", "wv"), (q1, k1, v1))):
        loads.wait(name)

        def project(r, index=index, ref=ref):
            ref[r, :] = dot(h1[r, :], weights_v[index]).astype(BF16)

        row_loop(rows, 256, project)
    stores.start("q1", q1, q1_out)
    stores.start("k1", k1, k1_out)
    stores.start("v1", v1, v1_out)

    def self_target(t, carry):
        r = pl.ds(pl.multiple_of(t * length, length), length)
        allowed = allowed_of(mask[pl.ds(t, 1), :], length)
        for pair in range(pairs):
            lanes = slice(pair * LANES, (pair + 1) * LANES)
            both = dot_nt(stacked(q1[r, lanes], low, high), k1[r, lanes])
            for half in range(2):
                part = slice(half * length, (half + 1) * length)
                score = jnp.where(allowed, both[part] + bias[pair, part, :], NEG)
                expo = jnp.exp(score - jnp.max(score, axis=-1, keepdims=True))
                total = jnp.sum(expo, axis=-1, keepdims=True)
                p1[t, pair, part, :] = (expo / total).astype(BF16)
            context = dot(p1[t, pair], v1[r, lanes])
            c1[r, lanes] = jnp.where(low_lane, context[:length], context[length:]).astype(BF16)
        return carry

    lax.fori_loop(0, targets, self_target, 0)
    stores.start("p1", p1, p1_out)
    stores.start("c1", c1, c1_out)
    loads.wait("wo")

    def self_out(r):
        x1[r, :] = tokens_v[r, :].astype(F32) + dot(c1[r, :], weights_v[3])

    row_loop(rows, 256, self_out)
    stores.start("x1", x1, x1_out)

    def second_norm(r):
        h2[r, :] = norm_rows(x1[r, :], gain[1]).astype(BF16)

    row_loop(rows, 32, second_norm)
    stores.start("h2", h2, h2_out)
    loads.wait("cq")

    def cross_query(r):
        q2[r, :] = dot(h2[r, :], weights_v[4]).astype(BF16)

    row_loop(rows, 256, cross_query)
    stores.start("q2", q2, q2_out)
    loads.wait("memory", "ck", "cv")

    def cross_keys(r):
        k2[r, :] = dot(memory_v[r, :], weights_v[5]).astype(BF16)
        v2[r, :] = dot(memory_v[r, :], weights_v[6]).astype(BF16)

    row_loop(targets * memory_length, 256, cross_keys)
    stores.start("k2", k2, k2_out)
    stores.start("v2", v2, v2_out)

    def cross_target(t, carry):
        r = pl.ds(pl.multiple_of(t * length, length), length)
        m = pl.ds(pl.multiple_of(t * memory_length, memory_length), memory_length)
        for pair in range(pairs):
            lanes = slice(pair * LANES, (pair + 1) * LANES)
            slot = pair % 2
            scores[slot] = dot_nt(stacked(q2[r, lanes], low, high), k2[m, lanes])
            for chunk in range(2 * length // 32):
                part = slice(chunk * 32, (chunk + 1) * 32)
                score = scores[slot, part, :]
                expo = jnp.exp(score - jnp.max(score, axis=-1, keepdims=True))
                total = jnp.sum(expo, axis=-1, keepdims=True)
                p2[t, pair, part, :] = (expo / total).astype(BF16)
            context = dot(p2[t, pair], v2[m, lanes])
            c2[r, lanes] = jnp.where(low_lane, context[:length], context[length:]).astype(BF16)
        return carry

    lax.fori_loop(0, targets, cross_target, 0)
    stores.start("p2", p2, p2_out)
    stores.start("c2", c2, c2_out)
    loads.wait("co")

    def cross_out(r):
        x2[r, :] = x1[r, :] + dot(c2[r, :], weights_v[7])

    row_loop(rows, 256, cross_out)
    stores.start("x2", x2, x2_out)

    def third_norm(r):
        tokens_v[r, :] = norm_rows(x2[r, :], gain[2]).astype(BF16)

    row_loop(rows, 32, third_norm)
    dispatch(place, tokens_v, sent)
    stores.start("sent", sent, sent_out)
    for copy in gsent_copies:
        copy.wait()
    stores.drain()


def dispatch(place, source, target):
    step = 128

    def one(r):
        spot = lax.broadcasted_iota(jnp.int32, (step, source.shape[0]), 0) + r.start
        hit = jnp.where(spot == place[...], 1.0, 0.0).astype(BF16)
        target[r, :] = dot(hit, source[...]).astype(target.dtype)

    row_loop(target.shape[0], step, one)


def collect(place_column, step, r, source):
    spot = lax.broadcasted_iota(jnp.int32, (step, source.shape[0]), 1)
    hit = jnp.where(spot == place_column[r, :], 1.0, 0.0).astype(BF16)
    return dot(hit, source[...])


class ExpertSum:
    def __init__(self, ring, running, tiles, core_land, near_land, first, result, stores):
        self.ring, self.running, self.tiles, self.first = ring, running, tiles, first
        self.core_land, self.near_land = core_land, near_land
        self.result, self.stores = result, stores
        self.order = (0, 1, 2, 3) if first == "x" else (0, 2, 1, 3)
        self.ready, self.started = set(), False
        self.place = (lambda one, two: one + 2 * two) if first == "x" else (lambda one, two: 2 * one + two)

    def add(self, tile, other):
        core = self.ring.spot["core"]

        def rows(r):
            total = self.tiles[core, tile, r, :].astype(F32) + other[r, :].astype(F32)
            self.tiles[core, tile, r, :] = total.astype(BF16)

        row_loop(self.tiles.shape[2], 64, rows)

    def start(self, tile):
        self.running.add(self.between_cores(tile))

    def between_cores(self, tile):
        core = self.ring.spot["core"]
        copy = self.ring.cross("core", self.tiles.at[1 - core, tile], self.core_land.at[tile])
        yield link_time("core", *self.tiles.shape[2:])
        copy.wait()
        self.add(tile, self.core_land.at[tile])
        self.ready.add(tile)
        if {self.place(0, 0), self.place(1, 0)} <= self.ready and not self.started:
            self.started = True
            self.running.add(self.near())
        if {self.place(0, 1), self.place(1, 1)} <= self.ready:
            spot = self.ring.spot[self.first]
            self.keep(1, self.place(spot, 1))
            self.keep(2, self.place(1 - spot, 1))

    def near(self):
        spot = self.ring.spot[self.first]
        source = self.tiles.at[self.ring.spot["core"], self.place(1 - spot, 0)]
        copy = self.ring.cross(self.first, source, self.near_land)
        yield link_time(self.first, *self.tiles.shape[2:])
        copy.wait()
        self.keep(0, self.place(spot, 0), self.near_land)

    def keep(self, index, tile, other=None):
        if other is not None:
            self.add(tile, other)
        source = self.tiles.at[self.ring.spot["core"], tile]
        self.stores.start(("sum", self.first, index), source, self.result.at[index])


def expert_kernel(
    experts, remote, inbound, grows, router, first, second,
    ret_out, dh_out, grad_first, grad_second, grad_router,
    first_v, second_v, inbound_v, grows_v, inbound_t, dret, dret_t, probs, pre, dact, act, dpre, ret, dinb, ret_v, dh_v, sums, core_land, near_land,
    in_sems, out_sems, send_sems, recv_sems,
):
    rows, width = inbound_v.shape
    hidden = first.shape[1]
    step = width
    tiles = hidden // step
    loads, stores = Loads(in_sems), Loads(out_sems)
    capacity = rows // experts
    half_rows = rows // 2
    if remote:
        ring = Ring(send_sems, recv_sems)
        ring.greet(("core", "x", "y"))
        arriving = ring.scatter(inbound, inbound_v)
        loads.start("inbound", inbound.at[ring.block(ring.expert, capacity), :], inbound_v.at[ring.slot(0, capacity), :])
    else:
        loads.start("inbound", inbound, inbound_v)
        arriving = []
    loads.start("grows", grows, grows_v)
    for f in range(tiles):
        cols = slice(f * step, (f + 1) * step)
        loads.start(("first", f), first.at[:, cols], first_v.at[:, cols])
        loads.start(("second", f), second.at[cols, :], second_v.at[cols, :])
    me = lax.axis_index("expert")
    lane = lax.broadcasted_iota(jnp.int32, (1, LANES), 1)
    mine = lane == me
    root = (2.0 / jnp.pi) ** 0.5
    grad_router[...] = jnp.zeros_like(grad_router)
    loads.wait("inbound", "grows")
    returning = []
    for side in range(2):
        start = side * half_rows
        here = slice(start, start + half_rows)
        for copy in (arriving[:1], arriving[1:])[side]:
            copy.wait_recv()

        def route(r, start=start):
            r = pl.ds(pl.multiple_of(start + r.start, 16), r.size)
            logits = jnp.where(lane < experts, dot(inbound_v[r, :], router[...]), -1e30)
            expo = jnp.exp(logits - jnp.max(logits, axis=-1, keepdims=True))
            prob = expo / jnp.sum(expo, axis=-1, keepdims=True)
            probs[r, :] = prob
            gate = jnp.sum(jnp.where(mine, prob, 0.0), axis=-1, keepdims=True)
            dret[r, :] = (gate * grows_v[r, :].astype(F32)).astype(BF16)

        row_loop(half_rows, half_rows // 2, route)
        for f in range(tiles):
            cols = slice(f * step, (f + 1) * step)
            if side == 0:
                loads.wait(("first", f), ("second", f))
            for c in range(0, step, 256):
                tile = slice(f * step + c, f * step + c + 256)
                pre[:, c : c + 256] = dot(inbound_v[here, :], first_v[:, tile])
                dact[:, c : c + 256] = dot_nt(dret[here, :], second_v[tile, :])

            def middle(r, start=start, cols=cols):
                u = pre[r, :]
                square = u * u
                t = jnp.tanh(u * (root + (root * 0.044715) * square))
                half = 0.5 + 0.5 * t
                out = pl.ds(pl.multiple_of(start + r.start, 16), r.size)
                act[out, cols] = (u * half).astype(BF16)
                slope = half + (u * (0.5 * root + (1.5 * root * 0.044715) * square)) * (1.0 - t * t)
                dpre[out, cols] = (dact[r, :] * slope).astype(BF16)

            row_loop(half_rows, 16, middle)
            for c in range(0, width, 256):
                tile = slice(c, c + 256)
                one, two = dot(act[here, cols], second_v[cols, tile]), dot_nt(dpre[here, cols], first_v[tile, cols])
                if f:
                    one, two = one + ret[:, tile], two + dinb[:, tile]
                ret[:, tile] = one
                dinb[:, tile] = two

        def finish(r, start=start):
            out = pl.ds(pl.multiple_of(start + r.start, 16), r.size)
            result = ret[r, :].astype(BF16).astype(F32)
            prob = probs[out, :]
            gate = jnp.sum(jnp.where(mine, prob, 0.0), axis=-1, keepdims=True)
            dgate = jnp.sum(result * grows_v[out, :].astype(F32), axis=-1, keepdims=True)
            dlogits = (prob * (jnp.where(mine, 1.0, 0.0) - gate) * dgate).astype(BF16)
            ret_v[out, :] = (gate * result).astype(BF16)
            dh_v[out, :] = (dinb[r, :].astype(BF16).astype(F32) + dot_nt(dlogits, router[...])).astype(BF16)
            grad_router[...] += dot_tn(dlogits, inbound_v[out, :])

        row_loop(half_rows, half_rows // 2, finish)
        if remote:
            target = dh_out.at[ring.block(ring.expert, capacity), :]
            for k in ((1,), (2, 3))[side]:
                source = dh_v.at[ring.slot(k, capacity, ring.peers[k]), :]
                returning.append(ring.send(source, target, ring.dp, ring.peers[k]))
            if side == 0:
                stores.start("dh", dh_v.at[ring.slot(0, capacity), :], target)
        elif side:
            stores.start("dh", dh_v, dh_out)
    stores.start("ret", ret_v, ret_out)
    for copy in arriving:
        copy.wait_send()
    for c in range(width // LANES):
        cols = slice(c * LANES, (c + 1) * LANES)
        inbound_t[cols, :] = inbound_v[:, cols].T
        dret_t[cols, :] = dret[:, cols].T

    running = Running()
    if remote:
        expert_sums = [
            ExpertSum(ring, running, sums.at[j], core_land.at[j], near_land.at[j], axis, out, stores)
            for j, (axis, out) in enumerate((("x", grad_first), ("y", grad_second)))
        ]
    for i in range(tiles):
        for j, (left, right) in enumerate(((inbound_t, dpre), (dret_t, act))):
            f = expert_sums[j].order[i] if remote else i
            for b in range(2):
                cols = slice(f * step + b * (step // 2), f * step + (b + 1) * (step // 2))

                def weights(r, j=j, b=b, f=f, left=left, right=right, cols=cols):
                    sums[j, b, f, r, :] = dot(left[r, :], right[:, cols]).astype(BF16)

                row_loop(width, 256, weights)
                if not remote:
                    stores.start(("sum", j, b, f), sums.at[j, b, f], (grad_first, grad_second)[j].at[:, cols])
            running.tick(1.6)
            if remote:
                expert_sums[j].start(f)
    running.drain()
    for copy in returning:
        copy.wait()
    stores.drain()


def span(start, size):
    return pl.ds(pl.multiple_of(start, size), size)


def add_into(ref, rows, lanes, others):
    step = 48 if rows.size % 64 else 64
    for i in range(rows.size // step):
        here = pl.ds(pl.multiple_of(rows.start + i * step, 16), step)
        total = ref[here, lanes].astype(F32)
        for other in others:
            total = total + other[i * step : (i + 1) * step, :].astype(F32)
        ref[here, lanes] = total.astype(BF16)


def reduce_matrix(ring, local, result, landing, first, second, copy_sem):
    size = local.shape[0]
    half, quarter, eighth = size // 2, size // 4, size // 4 // ring.experts
    half_land, quarter_land, eighth_land, part_land = landing
    core = ring.spot["core"]
    mine, other = span(core * half, half), span((1 - core) * half, half)
    copy = ring.cross("core", local.at[:, other], half_land)
    yield link_time("core", size, half)
    copy.wait()
    add_into(local, pl.ds(0, size), mine, [half_land])
    place = ring.spot[first] * half
    copy = ring.cross(first, local.at[span(half - place, half), mine], quarter_land)
    yield link_time(first, half, half)
    copy.wait()
    add_into(local, span(place, half), mine, [quarter_land])
    step = ring.spot[second] * quarter
    copy = ring.cross(second, local.at[span(place + quarter - step, quarter), mine], eighth_land)
    yield link_time(second, quarter, half)
    copy.wait()
    base = place + step
    add_into(local, span(base, quarter), mine, [eighth_land])
    copies = [
        ring.send(local.at[pl.ds(pl.multiple_of(base + e * eighth, 16), eighth), mine], part_land.at[k], ring.dp, e)
        for k, e in enumerate(ring.others())
    ]
    yield link_time("z", eighth, half)
    for copy in copies:
        copy.wait()
    part = pl.ds(pl.multiple_of(base + ring.expert * eighth, 16), eighth)
    add_into(local, part, mine, [part_land.at[k] for k in range(ring.experts - 1)])
    own = pltpu.make_async_copy(local.at[part, mine], result.at[part, mine], copy_sem)
    own.start()
    copies = [ring.send(local.at[part, mine], result.at[part, mine], ring.dp, e) for e in ring.others()]
    yield link_time("z", eighth, half)
    own.wait()
    for copy in copies:
        copy.wait()
    here = span(base, quarter)
    copy = ring.cross(second, result.at[here, mine], result.at[here, mine])
    yield link_time(second, quarter, half)
    copy.wait()
    here = span(place, half)
    copy = ring.cross(first, result.at[here, mine], result.at[here, mine])
    yield link_time(first, half, half)
    copy.wait()
    copy = ring.cross("core", result.at[:, mine], result.at[:, mine])
    yield link_time("core", size, half)
    copy.wait()


def reduce_expert(ring, part, near_land, far_land, keep, extra, first, result, sems):
    size, block = part.shape[1], part.shape[2]
    second = "y" if first == "x" else "x"
    cols = [slice(i * block, (i + 1) * block) for i in range(2)]
    copies = [ring.cross(first, part.at[2], near_land)]
    copies += [pltpu.make_async_copy(part.at[i], keep.at[:, cols[i]], sems.at[i]) for i in range(2)]
    for copy in copies[1:]:
        copy.start()
    yield link_time(first, size, block)
    for copy in copies:
        copy.wait()
    copy = pltpu.make_async_copy(near_land, extra.at[:, cols[1]], sems.at[2])
    copy.start()
    copy.wait()
    add_into(keep, pl.ds(0, size), cols[1], [extra.at[:, cols[1]]])
    spot = ring.spot[second]
    copy = ring.cross(second, keep.at[:, span((1 - spot) * block, block)], far_land)
    yield link_time(second, size, block)
    copy.wait()
    copy = pltpu.make_async_copy(far_land, extra.at[:, cols[0]], sems.at[3])
    copy.start()
    copy.wait()
    stay = span(spot * block, block)
    add_into(keep, pl.ds(0, size), stay, [extra.at[:, cols[0]]])
    copy = pltpu.make_async_copy(keep.at[:, stay], result, sems.at[4])
    copy.start()
    copy.wait()


def reduce_small(ring, local, landing):
    for k, name in enumerate(("core", "x", "y")):
        copy = ring.cross(name, local, landing.at[k])
        yield link_time(name, *local.shape, 4)
        copy.wait()
        local[...] += landing[k]
    copies = [ring.send(local, landing.at[3 + ring.expert], ring.dp, e) for e in ring.others()]
    landing[3 + ring.expert] = local[...]
    yield link_time("z", *local.shape, 4)
    for copy in copies:
        copy.wait()
    total = landing[3]
    for e in range(1, ring.experts):
        total = total + landing[3 + e]
    local[...] = total


class Running:
    DELAY = 1.5

    def __init__(self):
        self.steps = []
        self.now = 0.0
        self.free = {}

    def land(self, entry, use):
        if use is None:
            self.steps = [e for e in self.steps if e is not entry]
            return
        link, time = use
        self.free[link] = max(self.now, self.free.get(link, 0.0)) + time
        entry[1] = self.free[link] + self.DELAY

    def add(self, steps):
        entry = [steps, 0.0]
        self.steps.append(entry)
        self.land(entry, next(steps))

    def advance(self, entry):
        self.now = max(self.now, entry[1]) + 0.3
        self.land(entry, next(entry[0], None))

    def tick(self, time):
        self.now += time
        while self.steps:
            entry = min(self.steps, key=lambda e: e[1])
            if entry[1] > self.now:
                break
            self.advance(entry)

    def finish(self, steps):
        while any(e[0] is s for e in self.steps for s in steps):
            self.advance(min(self.steps, key=lambda e: e[1]))

    def drain(self):
        while self.steps:
            self.advance(min(self.steps, key=lambda e: e[1]))


def link_time(name, rows, columns, itemsize=2):
    rate = {"core": 300e3, "x": 50e3, "y": 50e3, "z": 12.5e3}[name]
    return name, rows * columns * itemsize / rate


def backward_kernel(
    targets, length, memory_length, heads, remote,
    dh_rows, ret_rows, place_column, mask, buckets, gains, grad_router, cotangent, tokens, h1, q1, k1, v1, c1, h2, q2, c2, x1, x2, p1, p2,
    k2, v2, memory, wq, wk, wv, wo, cq, ck, cv, co, part_first, part_second,
    *rest,
):
    grad_refs, rest = rest[:8], rest[8:]
    (
        output_out, grad_tokens_out, grad_memory_out, sum_first, sum_second, near_first, near_second, far_first, far_second, small,
        rows_v, ret_v, acts, x2_v, p1_v, weights_v, p2_v, kv_v, wide, grads, dscores, ds, dsum, gain_acc, table_v, half_land, quarter_land, eighth_land,
        part_land, small_land, in_sems, out_sems, ring_sems, send_sems, recv_sems, own_sems, expert_sems,
    ) = rest
    rows, width = x2_v.shape
    pairs = heads // 2
    first_v, q2_v, dctx2, dq, dk, dv, q1_v, k1_v, v1_v, ctx_v, norm_v, do, dctx1, _ = [acts.at[i * rows : (i + 1) * rows, :] for i in range(14)]
    dv2, dk2 = acts.at[6 * rows : 10 * rows, :], acts.at[10 * rows : 14 * rows, :]
    x1_v, du, dx = wide.at[0:rows, :], wide.at[rows : 2 * rows, :], wide.at[2 * rows : 3 * rows, :]
    spare = (dctx2, q2_v)
    loads, stores, running = Loads(in_sems), Loads(out_sems), Running()
    loads.start("rows", dh_rows, rows_v)
    loads.start("cot", cotangent, first_v)
    loads.start("x2", x2, x2_v)
    loads.start("c2", c2, ctx_v)
    loads.start("co", co, weights_v.at[0])

    def fetch(t, sources):
        slot = t % 2
        m = pl.ds(t * memory_length, memory_length)
        for index, source in enumerate(sources):
            target = p2_v.at[slot] if index == 0 else kv_v.at[index - 1, slot]
            copy = pltpu.make_async_copy(source.at[t] if index == 0 else source.at[m, :], target, ring_sems.at[index, slot])
            copy.start()
            yield copy

    fetched = list(fetch(0, (p2, k2, v2)))
    for name, source, target in (
        ("q2", q2, q2_v), ("cq", cq, weights_v.at[1]), ("h2", h2, norm_v), ("x1", x1, x1_v), ("wo", wo, weights_v.at[2]),
        ("p1", p1, p1_v), ("q1", q1, q1_v), ("k1", k1, k1_v), ("v1", v1, v1_v), ("ck", ck, weights_v.at[3]),
        ("cv", cv, weights_v.at[4]),
    ):
        loads.start(name, source, target)
    if remote:
        ring = Ring(send_sems, recv_sems)
        ring.greet(("core", "x", "y"))
        capacity = rows_v.shape[0] // ring.experts
        mine = ring.block(ring.expert, capacity)
        ret_copies = [
            ring.send(ret_rows.at[ring.slot(k, capacity, e), :], ret_v.at[mine, :], ring.dp, e) for k, e in enumerate(ring.peers) if k
        ]
        loads.start("ret", ret_rows.at[ring.slot(0, capacity), :], ret_v.at[mine, :])
        expert_sums = [
            reduce_expert(ring, part_first, near_first, far_first, grads.at[0], grads.at[2], "x", sum_first, expert_sems.at[0]),
            reduce_expert(ring, part_second, near_second, far_second, grads.at[1], grads.at[5], "y", sum_second, expert_sems.at[1]),
        ]
        for steps in expert_sums:
            running.add(steps)
    else:
        ret_copies, expert_sums = [], []
        loads.start("ret", ret_rows, ret_v)

    gain = [gains[i : i + 1, :] for i in range(3)]
    low_lane, low, high = half_masks()
    gain_acc[...] = jnp.zeros_like(gain_acc)
    axes = ("x", "y")
    started = []

    def total_of(index):
        if remote:
            way = len(started) % 2
            landing = [land.at[index] for land in (half_land, quarter_land, eighth_land, part_land)]
            running.add(reduce_matrix(ring, grads.at[index], grad_refs[index], landing, axes[way], axes[1 - way], own_sems.at[index]))
        else:
            stores.start(("grad", index), grads.at[index], grad_refs[index])
        started.append(index)

    def inner_grad(index, left, right):
        for c in range(width // 256):
            cols = slice(c * 256, (c + 1) * 256)
            grads[index, cols, :] = dot_tn(left[:, cols], right[...]).astype(BF16)
        total_of(index)

    def back_through(values, index, base, target):
        def one(r):
            back, gain_rows = norm_back(values[r, :].astype(F32), gain[index], du[r, :])
            total = base[r, :].astype(F32) + back
            target[r, :] = total
            if index:
                do[r, :] = total.astype(BF16)
            gain_acc[index] += gain_rows

        row_loop(rows, 32, one)

    loads.wait("rows", "cot", "x2")

    def gather(r):
        du[r, :] = collect(place_column, 128, r, rows_v)

    row_loop(rows, 128, gather)
    back_through(x2_v, 2, first_v, dx)
    loads.start("tokens", tokens, first_v)
    loads.wait("c2", "co")
    inner_grad(7, ctx_v, do)
    loads.start("c1", c1, ctx_v)

    def out_back(r, slot, target):
        target[r, :] = dot_nt(do[r, :], weights_v[slot]).astype(BF16)

    row_loop(rows, 256, functools.partial(out_back, slot=0, target=dctx2))
    running.tick(7.0)
    loads.start("wq", wq, weights_v.at[0])
    loads.wait("q2")
    for t in range(targets):
        slot = t % 2
        ahead = list(fetch(t + 1, (p2, k2, v2))) if t + 1 < targets else []
        for copy in fetched:
            copy.wait()
        fetched = ahead
        r = slice(t * length, (t + 1) * length)
        for pair in range(pairs):
            lanes = slice(pair * LANES, (pair + 1) * LANES)
            side = pair % 2
            dscores[side] = dot_nt(stacked(dctx2[r, lanes], low, high), kv_v[1, slot, :, lanes])
            for chunk in range(2 * length // 32):
                part = slice(chunk * 32, (chunk + 1) * 32)
                prob = p2_v[slot, pair, part, :].astype(F32)
                dprob = dscores[side, part, :]
                inner = jnp.sum(prob * dprob, axis=-1, keepdims=True)
                ds[t, pair, part, :] = (prob * (dprob - inner)).astype(BF16)
            back = dot(ds[t, pair], kv_v[0, slot, :, lanes])
            dq[r, lanes] = jnp.where(low_lane, back[:length], back[length:]).astype(BF16)
            if side:
                running.tick(1.4)
    memory_copies = []
    for t in range(targets):
        source = memory.at[pl.ds(t * memory_length, memory_length), :]
        memory_copies.append(pltpu.make_async_copy(source, kv_v.at[t // 2, t % 2], ring_sems.at[1 + t // 2, t % 2]))
        memory_copies[-1].start()
    fetched = list(fetch(0, (p2,)))
    loads.wait("h2", "cq", "x1")
    inner_grad(4, norm_v, dq)
    loads.start("h1", h1, norm_v)

    def query_back(r):
        du[r, :] = dot_nt(dq[r, :], weights_v[1])

    row_loop(rows, 256, query_back)
    loads.start("wk", wk, weights_v.at[1])
    running.tick(2.5)
    back_through(x1_v, 1, dx, dx)
    running.tick(1.5)
    loads.wait("c1", "wo")
    inner_grad(3, ctx_v, do)
    row_loop(rows, 256, functools.partial(out_back, slot=2, target=dctx1))
    loads.start("wv", wv, weights_v.at[2])
    running.tick(2.5)
    for copy in ret_copies:
        copy.wait()
    loads.wait("ret")

    def output_rows(r):
        dk[r, :] = (x2_v[r, :] + collect(place_column, 128, r, ret_v)).astype(BF16)

    row_loop(rows, 128, output_rows)
    stores.start("output", dk, output_out)
    running.tick(2.0)
    loads.wait("p1", "q1", "k1", "v1")
    stores.wait("output")
    for t in range(targets):
        r = slice(t * length, (t + 1) * length)
        allowed = allowed_of(mask[t : t + 1, :], length)
        for pair in range(pairs):
            lanes = slice(pair * LANES, (pair + 1) * LANES)
            side = pair % 2
            grad_rows = stacked(dctx1[r, lanes], low, high)
            both = dot_nt(grad_rows, v1_v[r, lanes])
            scratch = p2_v.at[1, side]
            for half in range(2):
                part = slice(half * length, (half + 1) * length)
                prob = p1_v[t, pair, part, :].astype(F32)
                dprob = both[part]
                inner = jnp.sum(prob * dprob, axis=-1, keepdims=True)
                score = jnp.where(allowed, prob * (dprob - inner), 0.0).astype(BF16)
                scratch[part, :length] = score
                wide_score = score.astype(F32)
                dsum[pair, part, :] = wide_score if t == 0 else dsum[pair, part, :] + wide_score
            dv[r, lanes] = dot_tn(p1_v[t, pair], grad_rows).astype(BF16)
            dk[r, lanes] = dot_tn(scratch[:, :length], stacked(q1_v[r, lanes], low, high)).astype(BF16)
            back = dot(scratch[:, :length], k1_v[r, lanes])
            dq[r, lanes] = jnp.where(low_lane, back[:length], back[length:]).astype(BF16)
        running.tick(2.5)
    loads.wait("h1", "wq", "wk", "wv", "tokens")
    running.finish(expert_sums)
    for index, right in enumerate((dq, dk, dv)):
        inner_grad(index, norm_v, right)
        running.tick(1.2)

    loads.wait("ck", "cv")
    for t in range(targets):
        slot = t % 2
        ahead = list(fetch(t + 1, (p2,))) if t + 1 < targets else []
        for copy in fetched:
            copy.wait()
        fetched = ahead
        r = slice(t * length, (t + 1) * length)
        m = slice(t * memory_length, (t + 1) * memory_length)
        for pair in range(pairs):
            lanes = slice(pair * LANES, (pair + 1) * LANES)
            dv2[m, lanes] = dot_tn(p2_v[slot, pair], stacked(dctx2[r, lanes], low, high)).astype(BF16)
            dk2[m, lanes] = dot_tn(ds[t, pair], stacked(q2_v[r, lanes], low, high)).astype(BF16)
            if pair % 3 == 2:
                running.tick(1.2)
    for copy in memory_copies:
        copy.wait()
    for index, right in ((5, dk2), (6, dv2)):
        for c in range(width // 256):
            cols = slice(c * 256, (c + 1) * 256)
            total = 0.0
            for t in range(targets):
                m = slice(t * memory_length, (t + 1) * memory_length)
                total = total + dot_tn(kv_v[t // 2, t % 2, :, cols], right[m, :])
            grads[index, cols, :] = total.astype(BF16)
            running.tick(1.3)
        total_of(index)

    def self_back(r):
        du[r, :] = dot_nt(dq[r, :], weights_v[0]) + dot_nt(dk[r, :], weights_v[1]) + dot_nt(dv[r, :], weights_v[2])

    row_loop(rows, 256, self_back)
    running.tick(2.5)
    back_through(first_v, 0, dx, dx)
    stores.start("tokens", dx, grad_tokens_out)
    running.tick(1.5)
    small[...] = jnp.zeros_like(small)
    for i in range(3):
        small[i : i + 1, :] = jnp.sum(gain_acc[i], axis=0, keepdims=True)
    small[8:16, :] = grad_router[0:8, :]
    table_v[...] = jnp.zeros_like(table_v)

    def table_rows(b, carry):
        hit = buckets[...] == b
        for head in range(heads):
            start = (head % 2) * length
            part = jnp.where(hit, dsum[head // 2, start : start + length, :], 0.0)
            table_v[pl.ds(head, 1), :] = jnp.sum(part, axis=0, keepdims=True)
        sums = jnp.sum(table_v[0:16, :], axis=-1, keepdims=True)
        eye = lax.broadcasted_iota(jnp.int32, (16, LANES), 0) == lax.broadcasted_iota(jnp.int32, (16, LANES), 1)
        table_v[pl.ds(16 + b, 1), :] = jnp.sum(jnp.where(eye, sums, 0.0), axis=0, keepdims=True)
        return carry

    for b in range(0, 32, 16):
        lax.fori_loop(b, b + 16, table_rows, 0)
        running.tick(2.0)
    for b in range(0, 32, 8):
        small[16:24, b // 8 * LANES : (b // 8 + 1) * LANES] = table_v[16 + b : 24 + b, :]
    if remote:
        running.add(reduce_small(ring, small, small_land))
    for t in range(targets):
        buffer = spare[t % 2]
        if t >= 2:
            stores.wait(("memory", t - 2))
        for half in range(2):
            q = slice(half * memory_length // 2, (half + 1) * memory_length // 2)
            m = slice(t * memory_length + q.start, t * memory_length + q.stop)
            buffer[q, :] = (dot_nt(dk2[m, :], weights_v[3]) + dot_nt(dv2[m, :], weights_v[4])).astype(BF16)
            running.tick(1.2)
        stores.start(("memory", t), buffer, grad_memory_out.at[pl.ds(t * memory_length, memory_length), :])
    running.drain()
    stores.drain()


def params(**more):
    return pltpu.CompilerParams(vmem_limit_bytes=VMEM_LIMIT, **more)


def on_device(
    tokens, memory, target_mask, buckets, expert_ids, slots, gain_self, w_query, w_key, w_value, w_output, rel_table, gain_cross,
    c_query, c_key, c_value, c_output, gain_moe, router, expert_in, expert_out, cotangent,
):
    rows, width = tokens.shape
    targets, length = target_mask.shape
    bucket_count, heads = rel_table.shape
    memory_length = memory.shape[0] // targets
    pairs = heads // 2
    experts = lax.axis_size("expert")
    hidden = expert_in.shape[2]
    capacity = (5 * rows + 4 * experts - 1) // (4 * experts)
    slot_rows = experts * capacity
    place = jnp.where(slots < capacity, expert_ids * capacity + slots, -1)
    place_row, place_column = place.reshape(1, rows), place.reshape(rows, 1)
    gains = jnp.stack([gain_self, gain_cross, gain_moe]).astype(F32)
    weights = (w_query, w_key, w_value, w_output, c_query, c_key, c_value, c_output)

    remote = lax.axis_size("dp") == 8 and experts == 4 and hidden == 4 * width

    def exchange(buffer):
        if remote:
            return buffer
        buffer = buffer.reshape(experts, capacity, width)
        return lax.all_to_all(buffer, "expert", split_axis=0, concat_axis=0, tiled=True).reshape(slot_rows, width)

    def remote_params(collective_id):
        return params(collective_id=collective_id, has_side_effects=True) if remote else params()

    row_shape = jax.ShapeDtypeStruct((slot_rows, width), BF16)
    act_shape = ((rows, width), BF16)
    wide_shape = ((rows, width), F32)
    key_shape = ((targets * memory_length, width), BF16)
    kept = (
        [act_shape] * 8
        + [wide_shape] * 2
        + [((targets, pairs, 2 * length, length), BF16), ((targets, pairs, 2 * length, memory_length), BF16), key_shape, key_shape]
        + [((slot_rows, width), BF16)] * 2
    )
    h1, q1, k1, v1, c1, h2, q2, c2, x1, x2, p1, p2, k2, v2, sent, grows = pl.pallas_call(
        functools.partial(forward_kernel, targets, length, memory_length, heads, remote),
        out_shape=[jax.ShapeDtypeStruct(*k) for k in kept],
        in_specs=[SMEM, ANY, ANY, VMEM, VMEM, VMEM, VMEM, ANY] + [ANY] * 8,
        out_specs=[ANY] * len(kept),
        scratch_shapes=[pltpu.VMEM((rows, width), BF16), pltpu.VMEM(*key_shape), pltpu.VMEM((8, width, width), BF16)]
        + [pltpu.VMEM(*k) for k in kept]
        + [
            pltpu.VMEM((pairs, 2 * length, length), F32),
            pltpu.VMEM((2, 2 * length, memory_length), F32),
            pltpu.SemaphoreType.DMA((11,)),
            pltpu.SemaphoreType.DMA((len(kept),)),
            pltpu.SemaphoreType.DMA((experts - 1,)),
            pltpu.SemaphoreType.DMA((experts - 1,)),
        ],
        compiler_params=remote_params(1),
        name="forward",
    )(rel_table.astype(F32), tokens, memory, target_mask, buckets, gains, place_row, cotangent, *weights)

    sent, grows = exchange(sent), exchange(grows)
    router_wide = jnp.pad(router, ((0, 0), (0, LANES - experts)))
    tiles = hidden // width
    half = width // 2
    weight_grad = jax.ShapeDtypeStruct((3, width, half) if remote else (width, hidden), BF16)
    row_scratch, half_scratch = pltpu.VMEM((slot_rows, width), BF16), pltpu.VMEM((slot_rows // 2, width), F32)
    ret, dh, grad_first, grad_second, grad_router = pl.pallas_call(
        functools.partial(expert_kernel, experts, remote),
        out_shape=[row_shape, row_shape, weight_grad, weight_grad, jax.ShapeDtypeStruct((LANES, width), F32)],
        in_specs=[ANY, ANY, VMEM, ANY, ANY],
        out_specs=[ANY, ANY, ANY, ANY, VMEM],
        scratch_shapes=[
            pltpu.VMEM((width, hidden), BF16),
            pltpu.VMEM((hidden, width), BF16),
            row_scratch,
            row_scratch,
            pltpu.VMEM((width, slot_rows), BF16),
            row_scratch,
            pltpu.VMEM((width, slot_rows), BF16),
            pltpu.VMEM((slot_rows, LANES), F32),
            half_scratch,
            half_scratch,
            pltpu.VMEM((slot_rows, hidden), BF16),
            pltpu.VMEM((slot_rows, hidden), BF16),
            half_scratch,
            half_scratch,
            row_scratch,
            row_scratch,
            pltpu.VMEM((2, 2, tiles, width, half), BF16),
            pltpu.VMEM((2, tiles, width, half), BF16),
            pltpu.VMEM((2, width, half), BF16),
            pltpu.SemaphoreType.DMA((2 * tiles + 2,)),
            pltpu.SemaphoreType.DMA((4 * tiles + 2,)),
            pltpu.SemaphoreType.DMA((2 * experts + 2 * tiles,)),
            pltpu.SemaphoreType.DMA((2 * experts + 2 * tiles,)),
        ],
        compiler_params=remote_params(2),
        name="experts",
    )(sent, grows, router_wide, expert_in[0], expert_out[0])
    dh_rows, ret_rows = exchange(dh), exchange(ret)
    parts = (grad_first, grad_second)
    if not remote:
        parts = (ret, ret)

    square = (width, width)
    wide = pltpu.VMEM(*wide_shape)
    small_shape = (24, width)
    lands = 8 if remote else 1
    copies = 8 * (6 + 2 * (experts - 1)) + 2 * experts + 1 + 4
    block = jax.ShapeDtypeStruct((width, half), BF16)
    results = pl.pallas_call(
        functools.partial(backward_kernel, targets, length, memory_length, heads, remote),
        out_shape=[jax.ShapeDtypeStruct(square, BF16)] * 8
        + [
            jax.ShapeDtypeStruct((rows, width), BF16),
            jax.ShapeDtypeStruct((rows, width), F32),
            jax.ShapeDtypeStruct(memory.shape, BF16),
            block,
            block,
            block,
            block,
            block,
            block,
            jax.ShapeDtypeStruct(small_shape, F32),
        ],
        in_specs=[ANY, ANY, VMEM, VMEM, VMEM, VMEM, VMEM] + [ANY] * 27,
        out_specs=[ANY] * 17 + [VMEM],
        scratch_shapes=[pltpu.VMEM((slot_rows, width), BF16)] * 2
        + [
            pltpu.VMEM((14 * rows, width), BF16),
            wide,
            pltpu.VMEM((targets, pairs, 2 * length, length), BF16),
            pltpu.VMEM((5,) + square, BF16),
            pltpu.VMEM((2, pairs, 2 * length, memory_length), BF16),
            pltpu.VMEM((2, 2, memory_length, width), BF16),
            pltpu.VMEM((3 * rows, width), F32),
            pltpu.VMEM((8,) + square, BF16),
            pltpu.VMEM((2, 2 * length, memory_length), F32),
            pltpu.VMEM((targets, pairs, 2 * length, memory_length), BF16),
            pltpu.VMEM((pairs, 2 * length, length), F32),
            pltpu.VMEM((3, 8, width), F32),
            pltpu.VMEM((48, LANES), F32),
            pltpu.VMEM((lands, width, half), BF16),
            pltpu.VMEM((lands, half, half), BF16),
            pltpu.VMEM((lands, half // 2, half), BF16),
            pltpu.VMEM((lands, experts - 1, half // 2 // experts, half), BF16),
            pltpu.VMEM((experts + 3,) + small_shape, F32),
            pltpu.SemaphoreType.DMA((23,)),
            pltpu.SemaphoreType.DMA((16,)),
            pltpu.SemaphoreType.DMA((3, 2)),
            pltpu.SemaphoreType.DMA((copies,)),
            pltpu.SemaphoreType.DMA((copies,)),
            pltpu.SemaphoreType.DMA((8,)),
            pltpu.SemaphoreType.DMA((2, 6)),
        ],
        compiler_params=remote_params(0),
        name="backward",
    )(
        dh_rows, ret_rows, place_column, target_mask, buckets, gains, grad_router, cotangent, tokens, h1, q1, k1, v1, c1, h2, q2, c2, x1, x2,
        p1, p2, k2, v2, memory, *weights, *parts,
    )
    summed, (output, grad_tokens, grad_memory, grad_first_sum, grad_second_sum), small = results[:8], results[8:13], results[-1]
    if not remote:
        summed, small = lax.psum((summed, small), ("dp", "expert"))
        grad_first_sum, grad_second_sum = (
            lax.psum_scatter(g, "dp", scatter_dimension=1, tiled=True) for g in (grad_first, grad_second)
        )
    summed = [g.astype(F32) for g in summed]
    table = small[16:24, : 4 * LANES].reshape(8, 4, LANES).transpose(1, 0, 2).reshape(32, LANES)[:bucket_count, :heads]
    return (
        output, grad_tokens, grad_memory, small[0], summed[0], summed[1], summed[2], summed[3], table, small[1], summed[4],
        summed[5], summed[6], summed[7], small[2], small[8 : 8 + experts].T, grad_first_sum.astype(F32)[None],
        grad_second_sum.astype(F32).T[None],
    )


def solution(mesh):
    both, spread = P(("dp", "expert")), P(("dp", "expert"), None)
    placed = (
        (spread, spread, spread, P(), both, both) + (P(),) * 13 + (P("expert", None, None), P("expert", None, None), spread)
    )
    return jax.shard_map(
        on_device,
        mesh=mesh,
        in_specs=placed,
        out_specs=(spread, spread, spread) + (P(),) * 13 + (P("expert", None, "dp"), P("expert", "dp", None)),
        check_vma=False,
    )
```

```python
import functools

import jax
import jax.numpy as jnp
from jax import lax
from jax.experimental import pallas as pl
from jax.experimental.pallas import tpu as pltpu
from jax.sharding import PartitionSpec as P

EPS = 1e-06
NEG = -1000000000.0
F32 = jnp.float32
BF16 = jnp.bfloat16
LANES = 128
VMEM_LIMIT = 63_400_000
ANY = pl.BlockSpec(memory_space=pl.ANY)
VMEM = pl.BlockSpec(memory_space=pltpu.VMEM)
SMEM = pl.BlockSpec(memory_space=pltpu.SMEM)


def dot(left, right):
    return lax.dot_general(left, right, (((1,), (0,)), ((), ())), preferred_element_type=F32)


def dot_nt(left, right):
    return lax.dot_general(left, right, (((1,), (1,)), ((), ())), preferred_element_type=F32)


def dot_tn(left, right):
    return lax.dot_general(left, right, (((0,), (0,)), ((), ())), preferred_element_type=F32)


def row_loop(count, step, body):
    def one(i, carry):
        body(pl.ds(pl.multiple_of(i * step, step), step))
        return carry

    lax.fori_loop(0, count // step, one, 0)


def half_masks():
    lane = lax.broadcasted_iota(jnp.int32, (1, LANES), 1)
    low = jnp.where(lane < LANES // 2, 1.0, 0.0).astype(BF16)
    high = jnp.where(lane < LANES // 2, 0.0, 1.0).astype(BF16)
    return lane < LANES // 2, low, high


def stacked(pair, low, high):
    return jnp.concatenate([pair * low, pair * high], axis=0)


def norm_rows(values, gain):
    return values * lax.rsqrt(jnp.mean(values * values, axis=-1, keepdims=True) + EPS) * gain


def norm_back(values, gain, grad):
    scale = lax.rsqrt(jnp.mean(values * values, axis=-1, keepdims=True) + EPS)
    scaled = grad * gain
    inner = jnp.mean(scaled * values, axis=-1, keepdims=True)
    back = scale * scaled - values * (scale * scale * scale * inner)
    gain_rows = grad * values * scale
    return back, jnp.sum(gain_rows.reshape(-1, 8, gain_rows.shape[-1]), axis=0)


def allowed_of(mask_row, length):
    row = lax.broadcasted_iota(jnp.int32, (length, length), 0)
    col = lax.broadcasted_iota(jnp.int32, (length, length), 1)
    return (col <= row) & (mask_row == 1)


class Loads:
    def __init__(self, sems):
        self.sems = sems
        self.count = 0
        self.open = {}

    def start(self, name, source, target):
        copy = pltpu.make_async_copy(source, target, self.sems.at[self.count])
        self.count += 1
        copy.start()
        self.open[name] = copy

    def wait(self, *names):
        for name in names:
            self.open.pop(name).wait()

    def drain(self):
        self.wait(*list(self.open))


class Ring:
    def __init__(self, send_sems, recv_sems):
        self.send_sems, self.recv_sems = send_sems, recv_sems
        self.count = 0
        dp, self.expert = lax.axis_index("dp"), lax.axis_index("expert")
        self.experts = lax.axis_size("expert")
        self.dp = dp
        self.spot = {"core": lax.rem(dp, 2), "x": lax.rem(lax.div(dp, 2), 2), "y": lax.div(dp, 4)}
        self.partner = {name: dp + step - 2 * step * self.spot[name] for name, step in (("core", 1), ("x", 2), ("y", 4))}

        low, high = lax.rem(self.expert, 2), lax.div(self.expert, 2)
        near, far = 1 - 2 * low, 2 - 4 * high
        self.peers = [self.expert, self.expert + near, self.expert + far, self.expert + near + far]

    def others(self):
        return self.peers[1:]

    def block(self, expert, capacity):
        return pl.ds(pl.multiple_of(expert * capacity, 16), capacity)

    def slot(self, k, capacity, sender=None):
        low = lax.rem(self.expert if sender is None else sender, 2)
        return pl.ds(pl.multiple_of((low + (2 if k >= 2 else 0)) * capacity, 16), capacity)

    def scatter(self, source, target):
        capacity = source.shape[0] // self.experts
        return [
            self.send(source.at[self.block(e, capacity), :], target.at[self.slot(k, capacity), :], self.dp, e)
            for k, e in enumerate(self.peers)
            if k
        ]

    def greet(self, names):
        barrier = pltpu.get_barrier_semaphore()
        targets = [(self.partner[name], self.expert) for name in names] + [(self.dp, e) for e in self.others()]
        for target in targets:
            pl.semaphore_signal(barrier, inc=1, device_id=target, device_id_type=pl.DeviceIdType.MESH)
        pl.semaphore_wait(barrier, len(targets))

    def send(self, source, target, dp, expert):
        copy = pltpu.make_async_remote_copy(
            src_ref=source, dst_ref=target, send_sem=self.send_sems.at[self.count], recv_sem=self.recv_sems.at[self.count],
            device_id=(dp, expert), device_id_type=pl.DeviceIdType.MESH,
        )
        self.count += 1
        copy.start()
        return copy

    def cross(self, name, source, target):
        return self.send(source, target, self.partner[name], self.expert)


def forward_kernel(
    targets, length, memory_length, heads, remote,
    table, tokens, memory, mask, buckets, gain_one, gain_two, gain_three, place, cotangent, wq, wk, wv, wo, cq, ck, cv, co,
    h1_out, q1_out, k1_out, v1_out, c1_out, h2_out, q2_out, c2_out, x1_out, x2_out, p1_out, p2_out, k2_out, v2_out, sent_out, grows_out,
    tokens_v, memory_v, weights_v, h1, q1, k1, v1, c1, h2, q2, c2, x1, x2, p1, p2, k2, v2, sent, gsent, bias, spread, scores, in_sems, out_sems,
    send_sems, recv_sems,
):
    rows, width = tokens_v.shape
    pairs = heads // 2
    loads, stores = Loads(in_sems), Loads(out_sems)
    loads.start("cot", cotangent, c2)
    loads.start("tokens", tokens, tokens_v)
    for index, (name, ref) in enumerate(zip(("wq", "wk", "wv"), (wq, wk, wv))):
        loads.start(name, ref, weights_v.at[index])
    loads.start("ck", ck, weights_v.at[5])
    loads.start("memory", memory, memory_v)
    loads.start("cv", cv, weights_v.at[6])
    loads.start("wo", wo, weights_v.at[3])
    loads.start("cq", cq, weights_v.at[4])
    loads.start("co", co, weights_v.at[7])
    gain = [g[...].astype(F32) for g in (gain_one, gain_two, gain_three)]
    low_lane, low, high = half_masks()

    if remote:
        ring = Ring(send_sems, recv_sems)
        ring.greet(())
    loads.wait("cot")
    dispatch(place, c2, gsent)
    gsent_copies = []
    if remote:
        gsent_copies = ring.scatter(gsent, grows_out)
        block = ring.block(ring.expert, sent.shape[0] // ring.experts)
        stores.start("grows", gsent.at[block, :], grows_out.at[ring.slot(0, sent.shape[0] // ring.experts), :])
    else:
        stores.start("grows", gsent, grows_out)
    bucket_count = table.shape[0]
    for head in range(heads):
        column = table[:, head : head + 1].astype(F32)
        spread[head * bucket_count : (head + 1) * bucket_count, :] = jnp.broadcast_to(column, (bucket_count, LANES))

    def bias_rows(r):
        here = buckets[r, :]
        hits = [here == b for b in range(bucket_count)]
        for head in range(heads):
            total = jnp.zeros(here.shape, F32)
            for b in range(bucket_count):
                at = head * bucket_count + b
                total = jnp.where(hits[b], spread[at : at + 1, :], total)
            start = (head % 2) * length
            bias[head // 2, pl.ds(pl.multiple_of(r.start + start, 8), r.size), :] = total

    row_loop(length, 16, bias_rows)

    loads.wait("tokens")

    def first_norm(r):
        h1[r, :] = norm_rows(tokens_v[r, :].astype(F32), gain[0]).astype(BF16)

    row_loop(rows, 32, first_norm)
    stores.start("h1", h1, h1_out)
    for index, (name, ref) in enumerate(zip(("wq", "wk", "wv"), (q1, k1, v1))):
        loads.wait(name)

        def project(r, index=index, ref=ref):
            ref[r, :] = dot(h1[r, :], weights_v[index]).astype(BF16)

        row_loop(rows, 256, project)
    stores.start("q1", q1, q1_out)
    stores.start("k1", k1, k1_out)
    stores.start("v1", v1, v1_out)

    def self_target(t, carry):
        r = pl.ds(pl.multiple_of(t * length, length), length)
        allowed = allowed_of(mask[pl.ds(t, 1), :], length)
        for pair in range(pairs):
            lanes = slice(pair * LANES, (pair + 1) * LANES)
            both = dot_nt(stacked(q1[r, lanes], low, high), k1[r, lanes])
            for half in range(2):
                part = slice(half * length, (half + 1) * length)
                score = jnp.where(allowed, both[part] + bias[pair, part, :], NEG)
                expo = jnp.exp(score - jnp.max(score, axis=-1, keepdims=True))
                total = jnp.sum(expo, axis=-1, keepdims=True)
                p1[t, pair, part, :] = (expo / total).astype(BF16)
            context = dot(p1[t, pair], v1[r, lanes])
            c1[r, lanes] = jnp.where(low_lane, context[:length], context[length:]).astype(BF16)
        return carry

    lax.fori_loop(0, targets, self_target, 0)
    stores.start("p1", p1, p1_out)
    stores.start("c1", c1, c1_out)
    loads.wait("wo")

    def self_out(r):
        x1[r, :] = tokens_v[r, :].astype(F32) + dot(c1[r, :], weights_v[3])

    row_loop(rows, 256, self_out)
    stores.start("x1", x1, x1_out)

    def second_norm(r):
        h2[r, :] = norm_rows(x1[r, :], gain[1]).astype(BF16)

    row_loop(rows, 32, second_norm)
    stores.start("h2", h2, h2_out)
    loads.wait("cq")

    def cross_query(r):
        q2[r, :] = dot(h2[r, :], weights_v[4]).astype(BF16)

    row_loop(rows, 256, cross_query)
    stores.start("q2", q2, q2_out)
    loads.wait("memory", "ck", "cv")

    def cross_keys(r):
        k2[r, :] = dot(memory_v[r, :], weights_v[5]).astype(BF16)
        v2[r, :] = dot(memory_v[r, :], weights_v[6]).astype(BF16)

    row_loop(targets * memory_length, 256, cross_keys)
    stores.start("k2", k2, k2_out)
    stores.start("v2", v2, v2_out)

    def cross_target(t, carry):
        r = pl.ds(pl.multiple_of(t * length, length), length)
        m = pl.ds(pl.multiple_of(t * memory_length, memory_length), memory_length)
        for pair in range(pairs):
            lanes = slice(pair * LANES, (pair + 1) * LANES)
            slot = pair % 2
            scores[slot] = dot_nt(stacked(q2[r, lanes], low, high), k2[m, lanes])
            for chunk in range(2 * length // 32):
                part = slice(chunk * 32, (chunk + 1) * 32)
                score = scores[slot, part, :]
                expo = jnp.exp(score - jnp.max(score, axis=-1, keepdims=True))
                total = jnp.sum(expo, axis=-1, keepdims=True)
                p2[t, pair, part, :] = (expo / total).astype(BF16)
            context = dot(p2[t, pair], v2[m, lanes])
            c2[r, lanes] = jnp.where(low_lane, context[:length], context[length:]).astype(BF16)
        return carry

    lax.fori_loop(0, targets, cross_target, 0)
    stores.start("p2", p2, p2_out)
    stores.start("c2", c2, c2_out)
    loads.wait("co")

    def cross_out(r):
        x2[r, :] = x1[r, :] + dot(c2[r, :], weights_v[7])

    row_loop(rows, 256, cross_out)
    stores.start("x2", x2, x2_out)

    def third_norm(r):
        tokens_v[r, :] = norm_rows(x2[r, :], gain[2]).astype(BF16)

    row_loop(rows, 32, third_norm)
    dispatch(place, tokens_v, sent)
    stores.start("sent", sent, sent_out)
    for copy in gsent_copies:
        copy.wait()
    stores.drain()


def dispatch(place, source, target):
    step = 128

    def one(r):
        spot = lax.broadcasted_iota(jnp.int32, (step, source.shape[0]), 0) + r.start
        hit = jnp.where(spot == place[...], 1.0, 0.0).astype(BF16)
        target[r, :] = dot(hit, source[...]).astype(target.dtype)

    row_loop(target.shape[0], step, one)


def collect(place_column, step, r, source):
    spot = lax.broadcasted_iota(jnp.int32, (step, source.shape[0]), 1)
    hit = jnp.where(spot == place_column[r, :], 1.0, 0.0).astype(BF16)
    return dot(hit, source[...])


class ExpertSum:
    def __init__(self, ring, running, tiles, core_land, near_land, first, result, stores):
        self.ring, self.running, self.tiles, self.first = ring, running, tiles, first
        self.core_land, self.near_land = core_land, near_land
        self.result, self.stores = result, stores
        self.order = (0, 1, 2, 3) if first == "x" else (0, 2, 1, 3)
        self.ready, self.started = set(), False
        self.place = (lambda one, two: one + 2 * two) if first == "x" else (lambda one, two: 2 * one + two)

    def add(self, tile, other):
        core = self.ring.spot["core"]

        def rows(r):
            total = self.tiles[core, tile, r, :].astype(F32) + other[r, :].astype(F32)
            self.tiles[core, tile, r, :] = total.astype(BF16)

        row_loop(self.tiles.shape[2], 64, rows)

    def start(self, tile):
        self.running.add(self.between_cores(tile))

    def between_cores(self, tile):
        core = self.ring.spot["core"]
        copy = self.ring.cross("core", self.tiles.at[1 - core, tile], self.core_land.at[tile])
        yield link_time("core", *self.tiles.shape[2:])
        copy.wait()
        self.add(tile, self.core_land.at[tile])
        self.ready.add(tile)
        if {self.place(0, 0), self.place(1, 0)} <= self.ready and not self.started:
            self.started = True
            self.running.add(self.near())
        if {self.place(0, 1), self.place(1, 1)} <= self.ready:
            spot = self.ring.spot[self.first]
            self.keep(1, self.place(spot, 1))
            self.keep(2, self.place(1 - spot, 1))

    def near(self):
        spot = self.ring.spot[self.first]
        source = self.tiles.at[self.ring.spot["core"], self.place(1 - spot, 0)]
        copy = self.ring.cross(self.first, source, self.near_land)
        yield link_time(self.first, *self.tiles.shape[2:])
        copy.wait()
        self.keep(0, self.place(spot, 0), self.near_land)

    def keep(self, index, tile, other=None):
        if other is not None:
            self.add(tile, other)
        source = self.tiles.at[self.ring.spot["core"], tile]
        self.stores.start(("sum", self.first, index), source, self.result.at[index])


def expert_kernel(
    experts, remote, inbound, grows, router_rows, first, second,
    ret_out, dh_out, grad_first, grad_second, grad_router,
    router, router_sum, first_v, second_v, inbound_v, grows_v, inbound_t, dret, dret_t, probs, pre, dact, act, dpre, ret, dinb, ret_v, dh_v, sums, core_land, near_land,
    in_sems, out_sems, send_sems, recv_sems,
):
    rows, width = inbound_v.shape
    hidden = first.shape[1]
    step = width
    tiles = hidden // step
    loads, stores = Loads(in_sems), Loads(out_sems)
    capacity = rows // experts
    half_rows = rows // 2
    if remote:
        ring = Ring(send_sems, recv_sems)
        ring.greet(("core", "x", "y"))
        arriving = ring.scatter(inbound, inbound_v)
        loads.start("inbound", inbound.at[ring.block(ring.expert, capacity), :], inbound_v.at[ring.slot(0, capacity), :])
    else:
        loads.start("inbound", inbound, inbound_v)
        arriving = []
    loads.start("grows", grows, grows_v)
    for f in range(tiles):
        cols = slice(f * step, (f + 1) * step)
        loads.start(("first", f), first.at[:, cols], first_v.at[:, cols])
        loads.start(("second", f), second.at[cols, :], second_v.at[cols, :])
    me = lax.axis_index("expert")
    lane = lax.broadcasted_iota(jnp.int32, (1, LANES), 1)
    mine = lane == me
    root = (2.0 / jnp.pi) ** 0.5
    router_sum[...] = jnp.zeros_like(router_sum)
    router[...] = jnp.zeros_like(router)
    router[0:experts, :] = router_rows[...]
    loads.wait("inbound", "grows")
    returning = []
    for side in range(2):
        start = side * half_rows
        here = slice(start, start + half_rows)
        for copy in (arriving[:1], arriving[1:])[side]:
            copy.wait_recv()

        def route(r, start=start):
            r = pl.ds(pl.multiple_of(start + r.start, 16), r.size)
            logits = jnp.where(lane < experts, dot_nt(inbound_v[r, :], router[...]), -1e30)
            expo = jnp.exp(logits - jnp.max(logits, axis=-1, keepdims=True))
            prob = expo / jnp.sum(expo, axis=-1, keepdims=True)
            probs[r, :] = prob
            gate = jnp.sum(jnp.where(mine, prob, 0.0), axis=-1, keepdims=True)
            dret[r, :] = (gate * grows_v[r, :].astype(F32)).astype(BF16)

        row_loop(half_rows, half_rows // 2, route)
        for f in range(tiles):
            cols = slice(f * step, (f + 1) * step)
            if side == 0:
                loads.wait(("first", f), ("second", f))
            for c in range(0, step, 256):
                tile = slice(f * step + c, f * step + c + 256)
                pre[:, c : c + 256] = dot(inbound_v[here, :], first_v[:, tile])
                dact[:, c : c + 256] = dot_nt(dret[here, :], second_v[tile, :])

            def middle(r, start=start, cols=cols):
                u = pre[r, :]
                square = u * u
                t = jnp.tanh(u * (root + (root * 0.044715) * square))
                half = 0.5 + 0.5 * t
                out = pl.ds(pl.multiple_of(start + r.start, 16), r.size)
                act[out, cols] = (u * half).astype(BF16)
                slope = half + (u * (0.5 * root + (1.5 * root * 0.044715) * square)) * (1.0 - t * t)
                dpre[out, cols] = (dact[r, :] * slope).astype(BF16)

            row_loop(half_rows, 16, middle)
            for c in range(0, width, 256):
                tile = slice(c, c + 256)
                one, two = dot(act[here, cols], second_v[cols, tile]), dot_nt(dpre[here, cols], first_v[tile, cols])
                if f:
                    one, two = one + ret[:, tile], two + dinb[:, tile]
                ret[:, tile] = one
                dinb[:, tile] = two

        def finish(r, start=start):
            out = pl.ds(pl.multiple_of(start + r.start, 16), r.size)
            result = ret[r, :].astype(BF16).astype(F32)
            prob = probs[out, :]
            gate = jnp.sum(jnp.where(mine, prob, 0.0), axis=-1, keepdims=True)
            dgate = jnp.sum(result * grows_v[out, :].astype(F32), axis=-1, keepdims=True)
            dlogits = (prob * (jnp.where(mine, 1.0, 0.0) - gate) * dgate).astype(BF16)
            ret_v[out, :] = (gate * result).astype(BF16)
            dh_v[out, :] = (dinb[r, :].astype(BF16).astype(F32) + dot(dlogits, router[...])).astype(BF16)
            router_sum[...] += dot_tn(dlogits, inbound_v[out, :])

        row_loop(half_rows, half_rows // 2, finish)
        if remote:
            target = dh_out.at[ring.block(ring.expert, capacity), :]
            for k in ((1,), (2, 3))[side]:
                source = dh_v.at[ring.slot(k, capacity, ring.peers[k]), :]
                returning.append(ring.send(source, target, ring.dp, ring.peers[k]))
            if side == 0:
                stores.start("dh", dh_v.at[ring.slot(0, capacity), :], target)
        elif side:
            stores.start("dh", dh_v, dh_out)
    stores.start("ret", ret_v, ret_out)
    grad_router[...] = router_sum[0:8, :]
    for copy in arriving:
        copy.wait_send()
    for c in range(width // LANES):
        cols = slice(c * LANES, (c + 1) * LANES)
        inbound_t[cols, :] = inbound_v[:, cols].T
        dret_t[cols, :] = dret[:, cols].T

    running = Running()
    if remote:
        expert_sums = [
            ExpertSum(ring, running, sums.at[j], core_land.at[j], near_land.at[j], axis, out, stores)
            for j, (axis, out) in enumerate((("x", grad_first), ("y", grad_second)))
        ]
    for i in range(tiles):
        for j, (left, right) in enumerate(((inbound_t, dpre), (dret_t, act))):
            f = expert_sums[j].order[i] if remote else i
            for b in range(2):
                cols = slice(f * step + b * (step // 2), f * step + (b + 1) * (step // 2))

                def weights(r, j=j, b=b, f=f, left=left, right=right, cols=cols):
                    sums[j, b, f, r, :] = dot(left[r, :], right[:, cols]).astype(BF16)

                row_loop(width, 256, weights)
                if not remote:
                    stores.start(("sum", j, b, f), sums.at[j, b, f], (grad_first, grad_second)[j].at[:, cols])
            running.tick(1.6)
            if remote:
                expert_sums[j].start(f)
    running.drain()
    for copy in returning:
        copy.wait()
    stores.drain()


def span(start, size):
    return pl.ds(pl.multiple_of(start, size), size)


def add_into(ref, rows, lanes, others):
    step = 48 if rows.size % 64 else 64
    for i in range(rows.size // step):
        here = pl.ds(pl.multiple_of(rows.start + i * step, 16), step)
        total = ref[here, lanes].astype(F32)
        for other in others:
            total = total + other[i * step : (i + 1) * step, :].astype(F32)
        ref[here, lanes] = total.astype(BF16)


def reduce_matrix(ring, local, result, core_land, landing, axes, copy_sem):
    size = local.shape[0]
    half = size // 2
    core = ring.spot["core"]
    mine, other = span(core * half, half), span((1 - core) * half, half)
    copy = ring.cross("core", local.at[:, other], core_land)
    yield link_time("core", size, half)
    copy.wait()
    add_into(local, pl.ds(0, size), mine, [core_land])
    base, count, row, trail = 0, size, 0, []
    for axis in axes:
        parts = ring.experts if axis == "z" else 2
        part = count // parts
        lands = [landing.at[row + k * part : row + (k + 1) * part, :] for k in range(parts - 1)]
        if axis == "z":
            spot = ring.expert
            copies = [ring.send(local.at[span(base + e * part, part), mine], lands[k], ring.dp, e) for k, e in enumerate(ring.others())]
        else:
            spot = ring.spot[axis]
            copies = [ring.cross(axis, local.at[span(base + (1 - spot) * part, part), mine], lands[0])]
        yield link_time(axis, part, half)
        for copy in copies:
            copy.wait()
        base, count, row = base + spot * part, part, row + (parts - 1) * part
        here = span(base, count)
        add_into(local, here, mine, lands)
        trail.append((axis, here))
    own = pltpu.make_async_copy(local.at[here, mine], result.at[here, mine], copy_sem)
    own.start()
    source = local
    for axis, here in reversed(trail):
        block, target = source.at[here, mine], result.at[here, mine]
        if axis == "z":
            copies = [ring.send(block, target, ring.dp, e) for e in ring.others()]
        else:
            copies = [ring.cross(axis, block, target)]
        yield link_time(axis, here.size, half)
        if source is local:
            own.wait()
        for copy in copies:
            copy.wait()
        source = result
    copy = ring.cross("core", result.at[:, mine], result.at[:, mine])
    yield link_time("core", size, half)
    copy.wait()


def reduce_expert(ring, part, near_land, far_land, keep, extra, first, result, sems):
    size, block = part.shape[1], part.shape[2]
    second = "y" if first == "x" else "x"
    cols = [slice(i * block, (i + 1) * block) for i in range(2)]
    copies = [ring.cross(first, part.at[2], near_land)]
    copies += [pltpu.make_async_copy(part.at[i], keep.at[:, cols[i]], sems.at[i]) for i in range(2)]
    for copy in copies[1:]:
        copy.start()
    yield link_time(first, size, block)
    for copy in copies:
        copy.wait()
    copy = pltpu.make_async_copy(near_land, extra.at[:, cols[1]], sems.at[2])
    copy.start()
    copy.wait()
    add_into(keep, pl.ds(0, size), cols[1], [extra.at[:, cols[1]]])
    spot = ring.spot[second]
    copy = ring.cross(second, keep.at[:, span((1 - spot) * block, block)], far_land)
    yield link_time(second, size, block)
    copy.wait()
    copy = pltpu.make_async_copy(far_land, extra.at[:, cols[0]], sems.at[3])
    copy.start()
    copy.wait()
    stay = span(spot * block, block)
    add_into(keep, pl.ds(0, size), stay, [extra.at[:, cols[0]]])
    copy = pltpu.make_async_copy(keep.at[:, stay], result, sems.at[4])
    copy.start()
    copy.wait()


def reduce_small(ring, local, landing):
    for k, name in enumerate(("core", "x", "y")):
        copy = ring.cross(name, local, landing.at[k])
        yield link_time(name, *local.shape, 4)
        copy.wait()
        local[...] += landing[k]
    copies = [ring.send(local, landing.at[3 + ring.expert], ring.dp, e) for e in ring.others()]
    landing[3 + ring.expert] = local[...]
    yield link_time("z", *local.shape, 4)
    for copy in copies:
        copy.wait()
    total = landing[3]
    for e in range(1, ring.experts):
        total = total + landing[3 + e]
    local[...] = total


class Running:
    DELAY = 1.5

    def __init__(self):
        self.steps = []
        self.now = 0.0
        self.free = {}

    def land(self, entry, use):
        if use is None:
            self.steps = [e for e in self.steps if e is not entry]
            return
        link, time = use
        self.free[link] = max(self.now, self.free.get(link, 0.0)) + time
        entry[1] = self.free[link] + self.DELAY

    def add(self, steps):
        entry = [steps, 0.0]
        self.steps.append(entry)
        self.land(entry, next(steps))

    def advance(self, entry):
        self.now = max(self.now, entry[1]) + 0.3
        self.land(entry, next(entry[0], None))

    def tick(self, time):
        self.now += time
        while self.steps:
            entry = min(self.steps, key=lambda e: e[1])
            if entry[1] > self.now:
                break
            self.advance(entry)

    def finish(self, steps):
        while any(e[0] is s for e in self.steps for s in steps):
            self.advance(min(self.steps, key=lambda e: e[1]))

    def drain(self):
        while self.steps:
            self.advance(min(self.steps, key=lambda e: e[1]))


def link_time(name, rows, columns, itemsize=2):
    rate = {"core": 300e3, "x": 50e3, "y": 50e3, "z": 12.5e3}[name]
    return name, rows * columns * itemsize / rate


def backward_kernel(
    targets, length, memory_length, heads, remote,
    dh_rows, ret_rows, place_column, mask, buckets, gain_one, gain_two, gain_three, grad_router, cotangent, tokens, h1, q1, k1, v1, c1, h2, q2, c2, x1, x2, p1, p2,
    k2, v2, memory, wq, wk, wv, wo, cq, ck, cv, co, part_first, part_second,
    *rest,
):
    grad_refs, rest = rest[:8], rest[8:]
    (
        output_out, grad_tokens_out, grad_memory_out, dv2_out, sum_first, sum_second, near_first, near_second, far_first, far_second, small,
        rows_v, ret_v, acts, x2_v, p1_v, weights_v, p2_v, kv_v, wide, grads, dscores, ds, dsum, gain_acc, table_v, core_land, landing, small_land, in_sems, out_sems, ring_sems, send_sems, recv_sems, own_sems, expert_sems,
    ) = rest
    rows, width = x2_v.shape
    pairs = heads // 2
    first_v, q2_v, dctx2, dq, dk, dv, q1_v, k1_v, v1_v, ctx_v, norm_v, do, dctx1, _ = [acts.at[i * rows : (i + 1) * rows, :] for i in range(14)]
    dv2, dk2 = acts.at[6 * rows : 10 * rows, :], acts.at[10 * rows : 14 * rows, :]
    x1_v, du, dx = wide.at[0:rows, :], wide.at[rows : 2 * rows, :], wide.at[2 * rows : 3 * rows, :]
    spare = (dctx2, q2_v)
    gv = wide.at[0:width, :]
    memory_slots, dv2_slots = (rows_v.at[0:memory_length, :], dk2.at[3 * rows : 4 * rows, :]), (do, dctx1)
    loads, stores, running = Loads(in_sems), Loads(out_sems), Running()
    loads.start("rows", dh_rows, rows_v)
    loads.start("cot", cotangent, first_v)
    loads.start("x2", x2, x2_v)
    loads.start("c2", c2, ctx_v)
    loads.start("co", co, weights_v.at[0])

    def fetch(t, sources, first=0):
        slot = t % 2
        m = pl.ds(t * memory_length, memory_length)
        for index, source in enumerate(sources, first):
            target = (p2_v.at[slot], kv_v.at[0, slot], kv_v.at[1, slot], memory_slots[slot])[index]
            copy = pltpu.make_async_copy(source.at[t] if index == 0 else source.at[m, :], target, ring_sems.at[index, slot])
            copy.start()
            yield copy

    fetched = list(fetch(0, (p2, k2, v2)))
    for name, source, target in (
        ("q2", q2, q2_v), ("cq", cq, weights_v.at[1]), ("h2", h2, norm_v), ("wo", wo, weights_v.at[2]),
        ("p1", p1, p1_v), ("q1", q1, q1_v), ("k1", k1, k1_v), ("v1", v1, v1_v), ("ck", ck, weights_v.at[3]),
        ("cv", cv, weights_v.at[4]),
    ):
        loads.start(name, source, target)
    if remote:
        ring = Ring(send_sems, recv_sems)
        ring.greet(("core", "x", "y"))
        capacity = rows_v.shape[0] // ring.experts
        mine = ring.block(ring.expert, capacity)
        ret_copies = [
            ring.send(ret_rows.at[ring.slot(k, capacity, e), :], ret_v.at[mine, :], ring.dp, e) for k, e in enumerate(ring.peers) if k
        ]
        loads.start("ret", ret_rows.at[ring.slot(0, capacity), :], ret_v.at[mine, :])
        expert_sums = [
            reduce_expert(ring, part_first, near_first, far_first, grads.at[0], grads.at[2], "x", sum_first, expert_sems.at[0]),
            reduce_expert(ring, part_second, near_second, far_second, grads.at[1], grads.at[5], "y", sum_second, expert_sems.at[1]),
        ]
        for steps in expert_sums:
            running.add(steps)
    else:
        ret_copies, expert_sums = [], []
        loads.start("ret", ret_rows, ret_v)

    gain = [g[...].astype(F32) for g in (gain_one, gain_two, gain_three)]
    low_lane, low, high = half_masks()
    gain_acc[...] = jnp.zeros_like(gain_acc)
    started = []

    def total_of(index):
        if remote:
            axes = (("x", "y", "z"), ("y", "x", "z"))[len(started) % 2]
            running.add(reduce_matrix(ring, grads.at[index], grad_refs[index], core_land.at[index], landing.at[index], axes, own_sems.at[index]))
        else:
            stores.start(("grad", index), grads.at[index], grad_refs[index])
        started.append(index)

    def inner_grad(index, left, right):
        for c in range(width // 256):
            cols = slice(c * 256, (c + 1) * 256)
            grads[index, cols, :] = dot_tn(left[:, cols], right[...]).astype(BF16)
        total_of(index)

    def back_through(values, index, base, target):
        def one(r):
            back, gain_rows = norm_back(values[r, :].astype(F32), gain[index], du[r, :])
            total = base[r, :].astype(F32) + back
            target[r, :] = total
            if index:
                do[r, :] = total.astype(BF16)
            gain_acc[index] += gain_rows

        row_loop(rows, 32, one)

    loads.wait("rows", "cot", "x2")

    def gather(r):
        du[r, :] = collect(place_column, 128, r, rows_v)

    row_loop(rows, 128, gather)
    fetched += list(fetch(0, (memory,), 3))
    back_through(x2_v, 2, first_v, dx)
    loads.start("tokens", tokens, first_v)
    loads.wait("c2", "co")
    inner_grad(7, ctx_v, do)
    loads.start("c1", c1, ctx_v)

    def out_back(r, slot, target):
        target[r, :] = dot_nt(do[r, :], weights_v[slot]).astype(BF16)

    row_loop(rows, 256, functools.partial(out_back, slot=0, target=dctx2))
    running.tick(7.0)
    loads.start("wq", wq, weights_v.at[0])
    loads.wait("q2")
    for t in range(targets):
        slot = t % 2
        ahead = list(fetch(t + 1, (p2, k2, v2, memory))) if t + 1 < targets else []
        if t >= 2:
            stores.wait(("dv2", t - 2))
        for copy in fetched:
            copy.wait()
        fetched = ahead
        r = slice(t * length, (t + 1) * length)
        for pair in range(pairs):
            lanes = slice(pair * LANES, (pair + 1) * LANES)
            side = pair % 2
            grad_rows = stacked(dctx2[r, lanes], low, high)
            dscores[side] = dot_nt(grad_rows, kv_v[1, slot, :, lanes])
            dv2_slots[slot][:, lanes] = dot_tn(p2_v[slot, pair], grad_rows).astype(BF16)
            for chunk in range(2 * length // 32):
                part = slice(chunk * 32, (chunk + 1) * 32)
                prob = p2_v[slot, pair, part, :].astype(F32)
                dprob = dscores[side, part, :]
                inner = jnp.sum(prob * dprob, axis=-1, keepdims=True)
                ds[t, pair, part, :] = (prob * (dprob - inner)).astype(BF16)
            back = dot(ds[t, pair], kv_v[0, slot, :, lanes])
            dq[r, lanes] = jnp.where(low_lane, back[:length], back[length:]).astype(BF16)
            if side:
                running.tick(1.8)
        stores.start(("dv2", t), dv2_slots[slot], dv2_out.at[pl.ds(t * memory_length, memory_length), :])
        for c in range(width // 256):
            cols = slice(c * 256, (c + 1) * 256)
            part = dot_tn(memory_slots[slot][:, cols], dv2_slots[slot][...])
            if t:
                part = part + gv[cols, :]
            if t + 1 < targets:
                gv[cols, :] = part
            else:
                grads[6, cols, :] = part.astype(BF16)
        running.tick(1.2)
    total_of(6)
    loads.start("x1", x1, x1_v)
    memory_copies = []
    for t in range(targets):
        source = memory.at[pl.ds(t * memory_length, memory_length), :]
        memory_copies.append(pltpu.make_async_copy(source, kv_v.at[t // 2, t % 2], ring_sems.at[1 + t // 2, t % 2]))
        memory_copies[-1].start()
    for t in range(max(0, targets - 2), targets):
        stores.wait(("dv2", t))
    loads.wait("h2", "cq", "x1")
    inner_grad(4, norm_v, dq)
    loads.start("h1", h1, norm_v)

    def query_back(r):
        du[r, :] = dot_nt(dq[r, :], weights_v[1])

    row_loop(rows, 256, query_back)
    loads.start("wk", wk, weights_v.at[1])
    running.tick(2.5)
    back_through(x1_v, 1, dx, dx)
    running.tick(1.5)
    loads.wait("c1", "wo")
    inner_grad(3, ctx_v, do)
    row_loop(rows, 256, functools.partial(out_back, slot=2, target=dctx1))
    loads.start("wv", wv, weights_v.at[2])
    running.tick(2.5)
    for copy in ret_copies:
        copy.wait()
    loads.wait("ret")

    def output_rows(r):
        dk[r, :] = (x2_v[r, :] + collect(place_column, 128, r, ret_v)).astype(BF16)

    row_loop(rows, 128, output_rows)
    stores.start("output", dk, output_out)
    running.tick(2.0)
    loads.wait("p1", "q1", "k1", "v1")
    stores.wait("output")
    for t in range(targets):
        r = slice(t * length, (t + 1) * length)
        allowed = allowed_of(mask[t : t + 1, :], length)
        for pair in range(pairs):
            lanes = slice(pair * LANES, (pair + 1) * LANES)
            side = pair % 2
            grad_rows = stacked(dctx1[r, lanes], low, high)
            both = dot_nt(grad_rows, v1_v[r, lanes])
            scratch = p2_v.at[1, side]
            for half in range(2):
                part = slice(half * length, (half + 1) * length)
                prob = p1_v[t, pair, part, :].astype(F32)
                dprob = both[part]
                inner = jnp.sum(prob * dprob, axis=-1, keepdims=True)
                score = jnp.where(allowed, prob * (dprob - inner), 0.0).astype(BF16)
                scratch[part, :length] = score
                wide_score = score.astype(F32)
                dsum[pair, part, :] = wide_score if t == 0 else dsum[pair, part, :] + wide_score
            dv[r, lanes] = dot_tn(p1_v[t, pair], grad_rows).astype(BF16)
            dk[r, lanes] = dot_tn(scratch[:, :length], stacked(q1_v[r, lanes], low, high)).astype(BF16)
            back = dot(scratch[:, :length], k1_v[r, lanes])
            dq[r, lanes] = jnp.where(low_lane, back[:length], back[length:]).astype(BF16)
        running.tick(2.5)
    loads.wait("h1", "wq", "wk", "wv", "tokens")
    running.finish(expert_sums)
    for index, right in enumerate((dq, dk, dv)):
        inner_grad(index, norm_v, right)
        running.tick(1.2)
    loads.start("dv2", dv2_out, dv2)

    for t in range(targets):
        r = slice(t * length, (t + 1) * length)
        m = slice(t * memory_length, (t + 1) * memory_length)
        for pair in range(pairs):
            lanes = slice(pair * LANES, (pair + 1) * LANES)
            dk2[m, lanes] = dot_tn(ds[t, pair], stacked(q2_v[r, lanes], low, high)).astype(BF16)
        running.tick(1.2)
    for copy in memory_copies:
        copy.wait()
    for c in range(width // 256):
        cols = slice(c * 256, (c + 1) * 256)
        total = 0.0
        for t in range(targets):
            m = slice(t * memory_length, (t + 1) * memory_length)
            total = total + dot_tn(kv_v[t // 2, t % 2, :, cols], dk2[m, :])
        grads[5, cols, :] = total.astype(BF16)
        running.tick(1.3)
    total_of(5)

    def self_back(r):
        du[r, :] = dot_nt(dq[r, :], weights_v[0]) + dot_nt(dk[r, :], weights_v[1]) + dot_nt(dv[r, :], weights_v[2])

    row_loop(rows, 256, self_back)
    running.tick(2.5)
    back_through(first_v, 0, dx, dx)
    stores.start("tokens", dx, grad_tokens_out)
    running.tick(1.5)
    small[...] = jnp.zeros_like(small)
    for i in range(3):
        small[i : i + 1, :] = jnp.sum(gain_acc[i], axis=0, keepdims=True)
    small[8:16, :] = grad_router[0:8, :]
    table_v[...] = jnp.zeros_like(table_v)

    def table_rows(b, carry):
        hit = buckets[...] == b
        for head in range(heads):
            start = (head % 2) * length
            part = jnp.where(hit, dsum[head // 2, start : start + length, :], 0.0)
            table_v[pl.ds(head, 1), :] = jnp.sum(part, axis=0, keepdims=True)
        sums = jnp.sum(table_v[0:16, :], axis=-1, keepdims=True)
        eye = lax.broadcasted_iota(jnp.int32, (16, LANES), 0) == lax.broadcasted_iota(jnp.int32, (16, LANES), 1)
        table_v[pl.ds(16 + b, 1), :] = jnp.sum(jnp.where(eye, sums, 0.0), axis=0, keepdims=True)
        return carry

    for b in range(0, 32, 16):
        lax.fori_loop(b, b + 16, table_rows, 0)
        running.tick(2.0)
    for b in range(0, 32, 8):
        small[16:24, b // 8 * LANES : (b // 8 + 1) * LANES] = table_v[16 + b : 24 + b, :]
    if remote:
        running.add(reduce_small(ring, small, small_land))
    loads.wait("ck", "cv", "dv2")
    for t in range(targets):
        buffer = spare[t % 2]
        if t >= 2:
            stores.wait(("memory", t - 2))
        for half in range(2):
            q = slice(half * memory_length // 2, (half + 1) * memory_length // 2)
            m = slice(t * memory_length + q.start, t * memory_length + q.stop)
            buffer[q, :] = (dot_nt(dk2[m, :], weights_v[3]) + dot_nt(dv2[m, :], weights_v[4])).astype(BF16)
            running.tick(1.2)
        stores.start(("memory", t), buffer, grad_memory_out.at[pl.ds(t * memory_length, memory_length), :])
    running.drain()
    stores.drain()


def finish_kernel(*refs):
    sources, small, targets, table, routed = refs[:13], refs[13], refs[14:27], refs[27], refs[28]
    narrow, wide, parts, first, second, in_sems, out_sems = refs[29:]
    loads, stores = Loads(in_sems), Loads(out_sems)
    for i in range(8):
        loads.start(i, sources[i], narrow.at[i])
    for i in range(2):
        loads.start(8 + i, sources[8 + i], parts.at[i])
    for i in range(10, 13):
        loads.start(i, sources[i], targets[i])
    for i in range(8):
        loads.wait(i)

        def widen(r, i=i):
            wide[i, r, :] = narrow[i, r, :].astype(F32)

        row_loop(wide.shape[1], 64, widen)
        stores.start(i, wide.at[i], targets[i])
    loads.wait(8, 9)

    def widen_part(r):
        first[r, :] = parts[0, r, :].astype(F32)

    row_loop(first.shape[0], 64, widen_part)
    stores.start(8, first, targets[8])
    for c in range(0, first.shape[0], LANES):
        second[:, c : c + LANES] = parts[1, c : c + LANES, :].astype(F32).T
    stores.start(9, second, targets[9])
    count, heads = table.shape
    for b in range(0, count, 8):
        table[b : b + 8, :] = small[16:24, b // 8 * LANES : b // 8 * LANES + heads]
    routed[...] = small[8:16, :].T[:, : routed.shape[1]]
    loads.drain()
    stores.drain()


def params(**more):
    return pltpu.CompilerParams(vmem_limit_bytes=VMEM_LIMIT, **more)


def on_device(
    tokens, memory, target_mask, buckets, expert_ids, slots, gain_self, w_query, w_key, w_value, w_output, rel_table, gain_cross,
    c_query, c_key, c_value, c_output, gain_moe, router, expert_in, expert_out, cotangent,
):
    rows, width = tokens.shape
    targets, length = target_mask.shape
    bucket_count, heads = rel_table.shape
    memory_length = memory.shape[0] // targets
    pairs = heads // 2
    experts = lax.axis_size("expert")
    hidden = expert_in.shape[2]
    capacity = (5 * rows + 4 * experts - 1) // (4 * experts)
    slot_rows = experts * capacity
    place = jnp.where(slots < capacity, expert_ids * capacity + slots, -1)
    place_row, place_column = place.reshape(1, rows), place.reshape(rows, 1)
    gains = [g.reshape(1, width) for g in (gain_self, gain_cross, gain_moe)]
    weights = (w_query, w_key, w_value, w_output, c_query, c_key, c_value, c_output)

    remote = lax.axis_size("dp") == 8 and experts == 4 and hidden == 4 * width

    def exchange(buffer):
        if remote:
            return buffer
        buffer = buffer.reshape(experts, capacity, width)
        return lax.all_to_all(buffer, "expert", split_axis=0, concat_axis=0, tiled=True).reshape(slot_rows, width)

    def remote_params(collective_id):
        return params(collective_id=collective_id, has_side_effects=True) if remote else params()

    row_shape = jax.ShapeDtypeStruct((slot_rows, width), BF16)
    act_shape = ((rows, width), BF16)
    wide_shape = ((rows, width), F32)
    key_shape = ((targets * memory_length, width), BF16)
    kept = (
        [act_shape] * 8
        + [wide_shape] * 2
        + [((targets, pairs, 2 * length, length), BF16), ((targets, pairs, 2 * length, memory_length), BF16), key_shape, key_shape]
        + [((slot_rows, width), BF16)] * 2
    )
    h1, q1, k1, v1, c1, h2, q2, c2, x1, x2, p1, p2, k2, v2, sent, grows = pl.pallas_call(
        functools.partial(forward_kernel, targets, length, memory_length, heads, remote),
        out_shape=[jax.ShapeDtypeStruct(*k) for k in kept],
        in_specs=[VMEM, ANY, ANY, VMEM, VMEM, VMEM, VMEM, VMEM, VMEM, ANY] + [ANY] * 8,
        out_specs=[ANY] * len(kept),
        scratch_shapes=[pltpu.VMEM((rows, width), BF16), pltpu.VMEM(*key_shape), pltpu.VMEM((8, width, width), BF16)]
        + [pltpu.VMEM(*k) for k in kept]
        + [
            pltpu.VMEM((pairs, 2 * length, length), F32),
            pltpu.VMEM((heads * bucket_count, length), F32),
            pltpu.VMEM((2, 2 * length, memory_length), F32),
            pltpu.SemaphoreType.DMA((11,)),
            pltpu.SemaphoreType.DMA((len(kept),)),
            pltpu.SemaphoreType.DMA((experts - 1,)),
            pltpu.SemaphoreType.DMA((experts - 1,)),
        ],
        compiler_params=remote_params(1),
        name="forward",
    )(rel_table, tokens, memory, target_mask, buckets, *gains, place_row, cotangent, *weights)

    sent, grows = exchange(sent), exchange(grows)
    tiles = hidden // width
    half = width // 2
    weight_grad = jax.ShapeDtypeStruct((3, width, half) if remote else (width, hidden), BF16)
    row_scratch, half_scratch = pltpu.VMEM((slot_rows, width), BF16), pltpu.VMEM((slot_rows // 2, width), F32)
    ret, dh, grad_first, grad_second, grad_router = pl.pallas_call(
        functools.partial(expert_kernel, experts, remote),
        out_shape=[row_shape, row_shape, weight_grad, weight_grad, jax.ShapeDtypeStruct((8, width), F32)],
        in_specs=[ANY, ANY, VMEM, ANY, ANY],
        out_specs=[ANY, ANY, ANY, ANY, VMEM],
        scratch_shapes=[
            pltpu.VMEM((LANES, width), BF16),
            pltpu.VMEM((LANES, width), F32),
            pltpu.VMEM((width, hidden), BF16),
            pltpu.VMEM((hidden, width), BF16),
            row_scratch,
            row_scratch,
            pltpu.VMEM((width, slot_rows), BF16),
            row_scratch,
            pltpu.VMEM((width, slot_rows), BF16),
            pltpu.VMEM((slot_rows, LANES), F32),
            half_scratch,
            half_scratch,
            pltpu.VMEM((slot_rows, hidden), BF16),
            pltpu.VMEM((slot_rows, hidden), BF16),
            half_scratch,
            half_scratch,
            row_scratch,
            row_scratch,
            pltpu.VMEM((2, 2, tiles, width, half), BF16),
            pltpu.VMEM((2, tiles, width, half), BF16),
            pltpu.VMEM((2, width, half), BF16),
            pltpu.SemaphoreType.DMA((2 * tiles + 2,)),
            pltpu.SemaphoreType.DMA((4 * tiles + 2,)),
            pltpu.SemaphoreType.DMA((2 * experts + 2 * tiles,)),
            pltpu.SemaphoreType.DMA((2 * experts + 2 * tiles,)),
        ],
        compiler_params=remote_params(2),
        name="experts",
    )(sent, grows, router.T, expert_in[0], expert_out[0])
    dh_rows, ret_rows = exchange(dh), exchange(ret)
    parts = (grad_first, grad_second)
    if not remote:
        parts = (ret, ret)

    square = (width, width)
    wide = pltpu.VMEM(*wide_shape)
    small_shape = (24, width)
    lands = 8 if remote else 1
    copies = 8 * (6 + 2 * (experts - 1)) + 2 * experts + 1 + 4
    block = jax.ShapeDtypeStruct((width, half), BF16)
    results = pl.pallas_call(
        functools.partial(backward_kernel, targets, length, memory_length, heads, remote),
        out_shape=[jax.ShapeDtypeStruct(square, BF16)] * 8
        + [
            jax.ShapeDtypeStruct((rows, width), BF16),
            jax.ShapeDtypeStruct((rows, width), F32),
            jax.ShapeDtypeStruct(memory.shape, BF16),
            jax.ShapeDtypeStruct(memory.shape, BF16),
            block,
            block,
            block,
            block,
            block,
            block,
            jax.ShapeDtypeStruct(small_shape, F32),
        ],
        in_specs=[ANY, ANY] + [VMEM] * 7 + [ANY] * 27,
        out_specs=[ANY] * 18 + [VMEM],
        scratch_shapes=[pltpu.VMEM((slot_rows, width), BF16)] * 2
        + [
            pltpu.VMEM((14 * rows, width), BF16),
            wide,
            pltpu.VMEM((targets, pairs, 2 * length, length), BF16),
            pltpu.VMEM((5,) + square, BF16),
            pltpu.VMEM((2, pairs, 2 * length, memory_length), BF16),
            pltpu.VMEM((2, 2, memory_length, width), BF16),
            pltpu.VMEM((3 * rows, width), F32),
            pltpu.VMEM((8,) + square, BF16),
            pltpu.VMEM((2, 2 * length, memory_length), F32),
            pltpu.VMEM((targets, pairs, 2 * length, memory_length), BF16),
            pltpu.VMEM((pairs, 2 * length, length), F32),
            pltpu.VMEM((3, 8, width), F32),
            pltpu.VMEM((48, LANES), F32),
            pltpu.VMEM((lands, width, half), BF16),
            pltpu.VMEM((lands, width - width // (4 * experts), half), BF16),
            pltpu.VMEM((experts + 3,) + small_shape, F32),
            pltpu.SemaphoreType.DMA((24,)),
            pltpu.SemaphoreType.DMA((20,)),
            pltpu.SemaphoreType.DMA((4, 2)),
            pltpu.SemaphoreType.DMA((copies,)),
            pltpu.SemaphoreType.DMA((copies,)),
            pltpu.SemaphoreType.DMA((8,)),
            pltpu.SemaphoreType.DMA((2, 6)),
        ],
        compiler_params=remote_params(0),
        name="backward",
    )(
        dh_rows, ret_rows, place_column, target_mask, buckets, *gains, grad_router, cotangent, tokens, h1, q1, k1, v1, c1, h2, q2, c2, x1, x2,
        p1, p2, k2, v2, memory, *weights, *parts,
    )
    summed, (output, grad_tokens, grad_memory, _, grad_first_sum, grad_second_sum), small = results[:8], results[8:14], results[-1]
    if not remote:
        summed, small = lax.psum((summed, small), ("dp", "expert"))
        grad_first_sum, grad_second_sum = (
            lax.psum_scatter(g, "dp", scatter_dimension=1, tiled=True) for g in (grad_first, grad_second)
        )
    wide_square = jax.ShapeDtypeStruct(square, F32)
    part_shape = grad_first_sum.shape
    finished = pl.pallas_call(
        finish_kernel,
        out_shape=[wide_square] * 8
        + [
            jax.ShapeDtypeStruct(part_shape, F32),
            jax.ShapeDtypeStruct(part_shape[::-1], F32),
            jax.ShapeDtypeStruct(output.shape, BF16),
            jax.ShapeDtypeStruct(grad_tokens.shape, F32),
            jax.ShapeDtypeStruct(grad_memory.shape, BF16),
            jax.ShapeDtypeStruct((bucket_count, heads), F32),
            jax.ShapeDtypeStruct((width, experts), F32),
        ],
        in_specs=[ANY] * 13 + [VMEM],
        out_specs=[ANY] * 8 + [ANY] * 5 + [VMEM] * 2,
        scratch_shapes=[
            pltpu.VMEM((8,) + square, BF16),
            pltpu.VMEM((8,) + square, F32),
            pltpu.VMEM((2,) + part_shape, BF16),
            pltpu.VMEM(part_shape, F32),
            pltpu.VMEM(part_shape[::-1], F32),
            pltpu.SemaphoreType.DMA((13,)),
            pltpu.SemaphoreType.DMA((10,)),
        ],
        compiler_params=params(),
        name="finish",
    )(*summed, grad_first_sum, grad_second_sum, output, grad_tokens, grad_memory, small)
    wq_grad, wk_grad, wv_grad, wo_grad, cq_grad, ck_grad, cv_grad, co_grad, first, second, output, grad_tokens, grad_memory, table, routed = finished
    return (
        output, grad_tokens, grad_memory, small[0], wq_grad, wk_grad, wv_grad, wo_grad, table, small[1], cq_grad, ck_grad, cv_grad, co_grad,
        small[2], routed, first[None], second[None],
    )


def solution(mesh):
    both, spread = P(("dp", "expert")), P(("dp", "expert"), None)
    placed = (
        (spread, spread, spread, P(), both, both) + (P(),) * 13 + (P("expert", None, None), P("expert", None, None), spread)
    )
    return jax.shard_map(
        on_device,
        mesh=mesh,
        in_specs=placed,
        out_specs=(spread, spread, spread) + (P(),) * 13 + (P("expert", None, "dp"), P("expert", "dp", None)),
        check_vma=False,
    )
```

```python
import functools

import jax
import jax.numpy as jnp
from jax import lax
from jax.experimental import pallas as pl
from jax.experimental.pallas import tpu as pltpu
from jax.sharding import PartitionSpec as P

EPS = 1e-06
NEG = -1000000000.0
F32 = jnp.float32
BF16 = jnp.bfloat16
LANES = 128
VMEM_LIMIT = 63_400_000
ANY = pl.BlockSpec(memory_space=pl.ANY)
VMEM = pl.BlockSpec(memory_space=pltpu.VMEM)
SMEM = pl.BlockSpec(memory_space=pltpu.SMEM)


def dot(left, right):
    return lax.dot_general(left, right, (((1,), (0,)), ((), ())), preferred_element_type=F32)


def dot_nt(left, right):
    return lax.dot_general(left, right, (((1,), (1,)), ((), ())), preferred_element_type=F32)


def dot_tn(left, right):
    return lax.dot_general(left, right, (((0,), (0,)), ((), ())), preferred_element_type=F32)


def row_loop(count, step, body):
    def one(i, carry):
        body(pl.ds(pl.multiple_of(i * step, step), step))
        return carry

    lax.fori_loop(0, count // step, one, 0)


def half_masks():
    lane = lax.broadcasted_iota(jnp.int32, (1, LANES), 1)
    low = jnp.where(lane < LANES // 2, 1.0, 0.0).astype(BF16)
    high = jnp.where(lane < LANES // 2, 0.0, 1.0).astype(BF16)
    return lane < LANES // 2, low, high


def stacked(pair, low, high):
    return jnp.concatenate([pair * low, pair * high], axis=0)


def norm_rows(values, gain):
    return values * lax.rsqrt(jnp.mean(values * values, axis=-1, keepdims=True) + EPS) * gain


def norm_back(values, gain, grad):
    scale = lax.rsqrt(jnp.mean(values * values, axis=-1, keepdims=True) + EPS)
    scaled = grad * gain
    inner = jnp.mean(scaled * values, axis=-1, keepdims=True)
    back = scale * scaled - values * (scale * scale * scale * inner)
    gain_rows = grad * values * scale
    return back, jnp.sum(gain_rows.reshape(-1, 8, gain_rows.shape[-1]), axis=0)


def allowed_of(mask_row, length):
    row = lax.broadcasted_iota(jnp.int32, (length, length), 0)
    col = lax.broadcasted_iota(jnp.int32, (length, length), 1)
    return (col <= row) & (mask_row == 1)


class Loads:
    def __init__(self, sems):
        self.sems = sems
        self.count = 0
        self.open = {}

    def start(self, name, source, target):
        copy = pltpu.make_async_copy(source, target, self.sems.at[self.count])
        self.count += 1
        copy.start()
        self.open[name] = copy

    def wait(self, *names):
        for name in names:
            self.open.pop(name).wait()

    def drain(self):
        self.wait(*list(self.open))


class Ring:
    def __init__(self, send_sems, recv_sems):
        self.send_sems, self.recv_sems = send_sems, recv_sems
        self.count = 0
        dp, self.expert = lax.axis_index("dp"), lax.axis_index("expert")
        self.experts = lax.axis_size("expert")
        self.dp = dp
        self.spot = {"core": lax.rem(dp, 2), "x": lax.rem(lax.div(dp, 2), 2), "y": lax.div(dp, 4)}
        self.partner = {name: dp + step - 2 * step * self.spot[name] for name, step in (("core", 1), ("x", 2), ("y", 4))}

        low, high = lax.rem(self.expert, 2), lax.div(self.expert, 2)
        near, far = 1 - 2 * low, 2 - 4 * high
        self.peers = [self.expert, self.expert + near, self.expert + far, self.expert + near + far]

    def others(self):
        return self.peers[1:]

    def block(self, expert, capacity):
        return pl.ds(pl.multiple_of(expert * capacity, 16), capacity)

    def slot(self, k, capacity, sender=None):
        low = lax.rem(self.expert if sender is None else sender, 2)
        return pl.ds(pl.multiple_of((low + (2 if k >= 2 else 0)) * capacity, 16), capacity)

    def scatter(self, source, target):
        capacity = source.shape[0] // self.experts
        return [
            self.send(source.at[self.block(e, capacity), :], target.at[self.slot(k, capacity), :], self.dp, e)
            for k, e in enumerate(self.peers)
            if k
        ]

    def greet(self, names):
        barrier = pltpu.get_barrier_semaphore()
        targets = [(self.partner[name], self.expert) for name in names] + [(self.dp, e) for e in self.others()]
        for target in targets:
            pl.semaphore_signal(barrier, inc=1, device_id=target, device_id_type=pl.DeviceIdType.MESH)
        pl.semaphore_wait(barrier, len(targets))

    def send(self, source, target, dp, expert):
        copy = pltpu.make_async_remote_copy(
            src_ref=source, dst_ref=target, send_sem=self.send_sems.at[self.count], recv_sem=self.recv_sems.at[self.count],
            device_id=(dp, expert), device_id_type=pl.DeviceIdType.MESH,
        )
        self.count += 1
        copy.start()
        return copy

    def cross(self, name, source, target):
        return self.send(source, target, self.partner[name], self.expert)


def forward_kernel(
    targets, length, memory_length, heads, remote,
    table, tokens, memory, mask, buckets, gain_one, gain_two, gain_three, place, cotangent, wq, wk, wv, wo, cq, ck, cv, co,
    h1_out, q1_out, k1_out, v1_out, c1_out, h2_out, q2_out, c2_out, x1_out, x2_out, p1_out, p2_out, k2_out, v2_out, sent_out, grows_out,
    tokens_v, memory_v, weights_v, h1, q1, k1, v1, c1, h2, q2, c2, x1, x2, p1, p2, k2, v2, sent, gsent, bias, spread, scores, in_sems, out_sems,
    send_sems, recv_sems,
):
    rows, width = tokens_v.shape
    pairs = heads // 2
    loads, stores = Loads(in_sems), Loads(out_sems)
    loads.start("cot", cotangent, c2)
    loads.start("tokens", tokens, tokens_v)
    for index, (name, ref) in enumerate(zip(("wq", "wk", "wv"), (wq, wk, wv))):
        loads.start(name, ref, weights_v.at[index])
    loads.start("ck", ck, weights_v.at[5])
    loads.start("memory", memory, memory_v)
    loads.start("cv", cv, weights_v.at[6])
    loads.start("wo", wo, weights_v.at[3])
    loads.start("cq", cq, weights_v.at[4])
    loads.start("co", co, weights_v.at[7])
    gain = [g[...].astype(F32).reshape(1, -1) for g in (gain_one, gain_two, gain_three)]
    low_lane, low, high = half_masks()

    if remote:
        ring = Ring(send_sems, recv_sems)
        ring.greet(())
    loads.wait("cot")
    dispatch(place, c2, gsent)
    gsent_copies = []
    if remote:
        gsent_copies = ring.scatter(gsent, grows_out)
        block = ring.block(ring.expert, sent.shape[0] // ring.experts)
        stores.start("grows", gsent.at[block, :], grows_out.at[ring.slot(0, sent.shape[0] // ring.experts), :])
    else:
        stores.start("grows", gsent, grows_out)
    bucket_count = table.shape[0]
    for head in range(heads):
        column = table[:, head : head + 1].astype(F32)
        spread[head * bucket_count : (head + 1) * bucket_count, :] = jnp.broadcast_to(column, (bucket_count, LANES))

    def bias_rows(r):
        here = buckets[r, :]
        hits = [here == b for b in range(bucket_count)]
        for head in range(heads):
            total = jnp.zeros(here.shape, F32)
            for b in range(bucket_count):
                at = head * bucket_count + b
                total = jnp.where(hits[b], spread[at : at + 1, :], total)
            start = (head % 2) * length
            bias[head // 2, pl.ds(pl.multiple_of(r.start + start, 8), r.size), :] = total

    row_loop(length, 16, bias_rows)

    loads.wait("tokens")

    def first_norm(r):
        h1[r, :] = norm_rows(tokens_v[r, :].astype(F32), gain[0]).astype(BF16)

    row_loop(rows, 32, first_norm)
    stores.start("h1", h1, h1_out)
    for index, (name, ref) in enumerate(zip(("wq", "wk", "wv"), (q1, k1, v1))):
        loads.wait(name)

        def project(r, index=index, ref=ref):
            ref[r, :] = dot(h1[r, :], weights_v[index]).astype(BF16)

        row_loop(rows, 256, project)
    stores.start("q1", q1, q1_out)
    stores.start("k1", k1, k1_out)
    stores.start("v1", v1, v1_out)

    def self_target(t, carry):
        r = pl.ds(pl.multiple_of(t * length, length), length)
        allowed = allowed_of(mask[pl.ds(t, 1), :], length)
        for pair in range(pairs):
            lanes = slice(pair * LANES, (pair + 1) * LANES)
            both = dot_nt(stacked(q1[r, lanes], low, high), k1[r, lanes])
            for half in range(2):
                part = slice(half * length, (half + 1) * length)
                score = jnp.where(allowed, both[part] + bias[pair, part, :], NEG)
                expo = jnp.exp(score - jnp.max(score, axis=-1, keepdims=True))
                total = jnp.sum(expo, axis=-1, keepdims=True)
                p1[t, pair, part, :] = (expo / total).astype(BF16)
            context = dot(p1[t, pair], v1[r, lanes])
            c1[r, lanes] = jnp.where(low_lane, context[:length], context[length:]).astype(BF16)
        return carry

    lax.fori_loop(0, targets, self_target, 0)
    stores.start("p1", p1, p1_out)
    stores.start("c1", c1, c1_out)
    loads.wait("wo")

    def self_out(r):
        x1[r, :] = tokens_v[r, :].astype(F32) + dot(c1[r, :], weights_v[3])

    row_loop(rows, 256, self_out)
    stores.start("x1", x1, x1_out)

    def second_norm(r):
        h2[r, :] = norm_rows(x1[r, :], gain[1]).astype(BF16)

    row_loop(rows, 32, second_norm)
    stores.start("h2", h2, h2_out)
    loads.wait("cq")

    def cross_query(r):
        q2[r, :] = dot(h2[r, :], weights_v[4]).astype(BF16)

    row_loop(rows, 256, cross_query)
    stores.start("q2", q2, q2_out)
    loads.wait("memory", "ck", "cv")

    def cross_keys(r):
        k2[r, :] = dot(memory_v[r, :], weights_v[5]).astype(BF16)
        v2[r, :] = dot(memory_v[r, :], weights_v[6]).astype(BF16)

    row_loop(targets * memory_length, 256, cross_keys)
    stores.start("k2", k2, k2_out)
    stores.start("v2", v2, v2_out)

    def cross_target(t, carry):
        r = pl.ds(pl.multiple_of(t * length, length), length)
        m = pl.ds(pl.multiple_of(t * memory_length, memory_length), memory_length)
        for pair in range(pairs):
            lanes = slice(pair * LANES, (pair + 1) * LANES)
            slot = pair % 2
            scores[slot] = dot_nt(stacked(q2[r, lanes], low, high), k2[m, lanes])
            for chunk in range(2 * length // 32):
                part = slice(chunk * 32, (chunk + 1) * 32)
                score = scores[slot, part, :]
                expo = jnp.exp(score - jnp.max(score, axis=-1, keepdims=True))
                total = jnp.sum(expo, axis=-1, keepdims=True)
                p2[t, pair, part, :] = (expo / total).astype(BF16)
            context = dot(p2[t, pair], v2[m, lanes])
            c2[r, lanes] = jnp.where(low_lane, context[:length], context[length:]).astype(BF16)
        return carry

    lax.fori_loop(0, targets, cross_target, 0)
    stores.start("p2", p2, p2_out)
    stores.start("c2", c2, c2_out)
    loads.wait("co")

    def cross_out(r):
        x2[r, :] = x1[r, :] + dot(c2[r, :], weights_v[7])

    row_loop(rows, 256, cross_out)
    stores.start("x2", x2, x2_out)

    def third_norm(r):
        tokens_v[r, :] = norm_rows(x2[r, :], gain[2]).astype(BF16)

    row_loop(rows, 32, third_norm)
    dispatch(place, tokens_v, sent)
    stores.start("sent", sent, sent_out)
    for copy in gsent_copies:
        copy.wait()
    stores.drain()


def dispatch(place, source, target):
    step = 128

    def one(r):
        spot = lax.broadcasted_iota(jnp.int32, (step, source.shape[0]), 0) + r.start
        hit = jnp.where(spot == place[...], 1.0, 0.0).astype(BF16)
        target[r, :] = dot(hit, source[...]).astype(target.dtype)

    row_loop(target.shape[0], step, one)


def collect(place_column, step, r, source):
    spot = lax.broadcasted_iota(jnp.int32, (step, source.shape[0]), 1)
    hit = jnp.where(spot == place_column[r, :], 1.0, 0.0).astype(BF16)
    return dot(hit, source[...])


class ExpertSum:
    def __init__(self, ring, running, tiles, core_land, near_land, first, result, stores):
        self.ring, self.running, self.tiles, self.first = ring, running, tiles, first
        self.core_land, self.near_land = core_land, near_land
        self.result, self.stores = result, stores
        self.order = (0, 1, 2, 3) if first == "x" else (0, 2, 1, 3)
        self.ready, self.started = set(), False
        self.place = (lambda one, two: one + 2 * two) if first == "x" else (lambda one, two: 2 * one + two)

    def add(self, tile, other):
        core = self.ring.spot["core"]

        def rows(r):
            total = self.tiles[core, tile, r, :].astype(F32) + other[r, :].astype(F32)
            self.tiles[core, tile, r, :] = total.astype(BF16)

        row_loop(self.tiles.shape[2], 64, rows)

    def start(self, tile):
        self.running.add(self.between_cores(tile))

    def between_cores(self, tile):
        core = self.ring.spot["core"]
        copy = self.ring.cross("core", self.tiles.at[1 - core, tile], self.core_land.at[tile])
        yield link_time("core", *self.tiles.shape[2:])
        copy.wait()
        self.add(tile, self.core_land.at[tile])
        self.ready.add(tile)
        if {self.place(0, 0), self.place(1, 0)} <= self.ready and not self.started:
            self.started = True
            self.running.add(self.near())
        if {self.place(0, 1), self.place(1, 1)} <= self.ready:
            spot = self.ring.spot[self.first]
            self.keep(1, self.place(spot, 1))
            self.keep(2, self.place(1 - spot, 1))

    def near(self):
        spot = self.ring.spot[self.first]
        source = self.tiles.at[self.ring.spot["core"], self.place(1 - spot, 0)]
        copy = self.ring.cross(self.first, source, self.near_land)
        yield link_time(self.first, *self.tiles.shape[2:])
        copy.wait()
        self.keep(0, self.place(spot, 0), self.near_land)

    def keep(self, index, tile, other=None):
        if other is not None:
            self.add(tile, other)
        source = self.tiles.at[self.ring.spot["core"], tile]
        self.stores.start(("sum", self.first, index), source, self.result.at[index])


def expert_kernel(
    experts, remote, inbound, grows, router_rows, first, second,
    ret_out, dh_out, grad_first, grad_second, grad_router,
    router, router_sum, first_v, second_v, inbound_v, grows_v, inbound_t, dret, dret_t, probs, pre, dact, act, dpre, ret, dinb, ret_v, dh_v, sums, core_land, near_land,
    in_sems, out_sems, send_sems, recv_sems,
):
    rows, width = inbound_v.shape
    hidden = first.shape[1]
    step = width
    tiles = hidden // step
    loads, stores = Loads(in_sems), Loads(out_sems)
    capacity = rows // experts
    half_rows = rows // 2
    if remote:
        ring = Ring(send_sems, recv_sems)
        ring.greet(("core", "x", "y"))
        arriving = ring.scatter(inbound, inbound_v)
        loads.start("inbound", inbound.at[ring.block(ring.expert, capacity), :], inbound_v.at[ring.slot(0, capacity), :])
    else:
        loads.start("inbound", inbound, inbound_v)
        arriving = []
    loads.start("grows", grows, grows_v)
    for f in range(tiles):
        cols = slice(f * step, (f + 1) * step)
        loads.start(("first", f), first.at[:, cols], first_v.at[:, cols])
        loads.start(("second", f), second.at[cols, :], second_v.at[cols, :])
    me = lax.axis_index("expert")
    lane = lax.broadcasted_iota(jnp.int32, (1, LANES), 1)
    mine = lane == me
    root = (2.0 / jnp.pi) ** 0.5
    router_sum[...] = jnp.zeros_like(router_sum)
    router[...] = jnp.zeros_like(router)
    router[0:experts, :] = router_rows[...]
    loads.wait("inbound", "grows")
    returning = []
    for side in range(2):
        start = side * half_rows
        here = slice(start, start + half_rows)
        for copy in (arriving[:1], arriving[1:])[side]:
            copy.wait_recv()

        def route(r, start=start):
            r = pl.ds(pl.multiple_of(start + r.start, 16), r.size)
            logits = jnp.where(lane < experts, dot_nt(inbound_v[r, :], router[...]), -1e30)
            expo = jnp.exp(logits - jnp.max(logits, axis=-1, keepdims=True))
            prob = expo / jnp.sum(expo, axis=-1, keepdims=True)
            probs[r, :] = prob
            gate = jnp.sum(jnp.where(mine, prob, 0.0), axis=-1, keepdims=True)
            dret[r, :] = (gate * grows_v[r, :].astype(F32)).astype(BF16)

        row_loop(half_rows, half_rows // 2, route)
        for f in range(tiles):
            cols = slice(f * step, (f + 1) * step)
            if side == 0:
                loads.wait(("first", f), ("second", f))
            for c in range(0, step, 256):
                tile = slice(f * step + c, f * step + c + 256)
                pre[:, c : c + 256] = dot(inbound_v[here, :], first_v[:, tile])
                dact[:, c : c + 256] = dot_nt(dret[here, :], second_v[tile, :])

            def middle(r, start=start, cols=cols):
                u = pre[r, :]
                square = u * u
                t = jnp.tanh(u * (root + (root * 0.044715) * square))
                half = 0.5 + 0.5 * t
                out = pl.ds(pl.multiple_of(start + r.start, 16), r.size)
                act[out, cols] = (u * half).astype(BF16)
                slope = half + (u * (0.5 * root + (1.5 * root * 0.044715) * square)) * (1.0 - t * t)
                dpre[out, cols] = (dact[r, :] * slope).astype(BF16)

            row_loop(half_rows, 16, middle)
            for c in range(0, width, 256):
                tile = slice(c, c + 256)
                one, two = dot(act[here, cols], second_v[cols, tile]), dot_nt(dpre[here, cols], first_v[tile, cols])
                if f:
                    one, two = one + ret[:, tile], two + dinb[:, tile]
                ret[:, tile] = one
                dinb[:, tile] = two

        def finish(r, start=start):
            out = pl.ds(pl.multiple_of(start + r.start, 16), r.size)
            result = ret[r, :].astype(BF16).astype(F32)
            prob = probs[out, :]
            gate = jnp.sum(jnp.where(mine, prob, 0.0), axis=-1, keepdims=True)
            dgate = jnp.sum(result * grows_v[out, :].astype(F32), axis=-1, keepdims=True)
            dlogits = (prob * (jnp.where(mine, 1.0, 0.0) - gate) * dgate).astype(BF16)
            ret_v[out, :] = (gate * result).astype(BF16)
            dh_v[out, :] = (dinb[r, :].astype(BF16).astype(F32) + dot(dlogits, router[...])).astype(BF16)
            router_sum[...] += dot_tn(dlogits, inbound_v[out, :])

        row_loop(half_rows, half_rows // 2, finish)
        if remote:
            target = dh_out.at[ring.block(ring.expert, capacity), :]
            for k in ((1,), (2, 3))[side]:
                source = dh_v.at[ring.slot(k, capacity, ring.peers[k]), :]
                returning.append(ring.send(source, target, ring.dp, ring.peers[k]))
            if side == 0:
                stores.start("dh", dh_v.at[ring.slot(0, capacity), :], target)
        elif side:
            stores.start("dh", dh_v, dh_out)
    stores.start("ret", ret_v, ret_out)
    grad_router[...] = router_sum[0:8, :]
    for copy in arriving:
        copy.wait_send()
    for c in range(width // LANES):
        cols = slice(c * LANES, (c + 1) * LANES)
        inbound_t[cols, :] = inbound_v[:, cols].T
        dret_t[cols, :] = dret[:, cols].T

    running = Running()
    if remote:
        expert_sums = [
            ExpertSum(ring, running, sums.at[j], core_land.at[j], near_land.at[j], axis, out, stores)
            for j, (axis, out) in enumerate((("x", grad_first), ("y", grad_second)))
        ]
    for i in range(tiles):
        for j, (left, right) in enumerate(((inbound_t, dpre), (dret_t, act))):
            f = expert_sums[j].order[i] if remote else i
            for b in range(2):
                cols = slice(f * step + b * (step // 2), f * step + (b + 1) * (step // 2))

                def weights(r, j=j, b=b, f=f, left=left, right=right, cols=cols):
                    sums[j, b, f, r, :] = dot(left[r, :], right[:, cols]).astype(BF16)

                row_loop(width, 256, weights)
                if not remote:
                    stores.start(("sum", j, b, f), sums.at[j, b, f], (grad_first, grad_second)[j].at[:, cols])
            running.tick(1.6)
            if remote:
                expert_sums[j].start(f)
    running.drain()
    for copy in returning:
        copy.wait()
    stores.drain()


def span(start, size):
    return pl.ds(pl.multiple_of(start, size), size)


def add_into(ref, rows, lanes, others, target=None):
    step = 48 if rows.size % 64 else 64
    for i in range(rows.size // step):
        here = pl.ds(pl.multiple_of(rows.start + i * step, 16), step)
        total = ref[here, lanes].astype(F32)
        for other in others:
            total = total + other[i * step : (i + 1) * step, :].astype(F32)
        if target is None:
            ref[here, lanes] = total.astype(BF16)
        else:
            target[here, :] = total.astype(BF16)


def reduce_matrix(ring, local, result, core_land, landing, axes, stores, ready):
    size = local.shape[0]
    half = size // 2
    core = ring.spot["core"]
    mine, other = span(core * half, half), span((1 - core) * half, half)
    copy = ring.cross("core", local.at[:, other], core_land)
    yield link_time("core", size, half)
    copy.wait()
    pl.semaphore_signal(ready, inc=1, device_id=(ring.partner["core"], ring.expert), device_id_type=pl.DeviceIdType.MESH)
    add_into(local, pl.ds(0, size), mine, [core_land])
    base, count, row, trail = 0, size, 0, []
    for axis in axes:
        parts = ring.experts if axis == "z" else 2
        part = count // parts
        lands = [landing.at[row + k * part : row + (k + 1) * part, :] for k in range(parts - 1)]
        if axis == "z":
            spot = ring.expert
            copies = [ring.send(local.at[span(base + e * part, part), mine], lands[k], ring.dp, e) for k, e in enumerate(ring.others())]
        else:
            spot = ring.spot[axis]
            copies = [ring.cross(axis, local.at[span(base + (1 - spot) * part, part), mine], lands[0])]
        yield link_time(axis, part, half)
        for copy in copies:
            copy.wait()
        base, count, row = base + spot * part, part, row + (parts - 1) * part
        here = span(base, count)
        add_into(local, here, mine, lands, core_land if axis == axes[-1] else None)
        trail.append((axis, here))
    for axis, here in reversed(trail):
        block = core_land.at[here, :]
        if axis == "z":
            copies = [ring.send(block, block, ring.dp, e) for e in ring.others()]
        else:
            copies = [ring.cross(axis, block, block)]
        yield link_time(axis, here.size, half)
        for copy in copies:
            copy.wait()
    pl.semaphore_wait(ready, 1)
    copy = ring.cross("core", core_land, local.at[:, mine])
    yield link_time("core", size, half)
    copy.wait()
    stores.start(("mine", stores.count), core_land, result.at[:, mine])
    stores.start(("other", stores.count), local.at[:, other], result.at[:, other])


def reduce_expert(ring, part, keep, extra, first, result, sems):
    size, block = part.shape[1], part.shape[2]
    second = "y" if first == "x" else "x"
    cols = [slice(i * block, (i + 1) * block) for i in range(2)]
    copies = [ring.cross(first, part.at[2], extra.at[:, cols[1]])]
    copies += [pltpu.make_async_copy(part.at[i], keep.at[:, cols[i]], sems.at[i]) for i in range(2)]
    for copy in copies[1:]:
        copy.start()
    yield link_time(first, size, block)
    for copy in copies:
        copy.wait()
    add_into(keep, pl.ds(0, size), cols[1], [extra.at[:, cols[1]]])
    spot = ring.spot[second]
    copy = ring.cross(second, keep.at[:, span((1 - spot) * block, block)], extra.at[:, cols[0]])
    yield link_time(second, size, block)
    copy.wait()
    stay = span(spot * block, block)
    add_into(keep, pl.ds(0, size), stay, [extra.at[:, cols[0]]])
    copy = pltpu.make_async_copy(keep.at[:, stay], result, sems.at[2])
    copy.start()
    copy.wait()


def reduce_small(ring, local, landing):
    for k, name in enumerate(("core", "x", "y")):
        copy = ring.cross(name, local, landing.at[k])
        yield link_time(name, *local.shape, 4)
        copy.wait()
        local[...] += landing[k]
    copies = [ring.send(local, landing.at[3 + ring.expert], ring.dp, e) for e in ring.others()]
    landing[3 + ring.expert] = local[...]
    yield link_time("z", *local.shape, 4)
    for copy in copies:
        copy.wait()
    total = landing[3]
    for e in range(1, ring.experts):
        total = total + landing[3 + e]
    local[...] = total


class Running:
    DELAY = 1.5

    def __init__(self):
        self.steps = []
        self.now = 0.0
        self.free = {}

    def land(self, entry, use):
        if use is None:
            self.steps = [e for e in self.steps if e is not entry]
            return
        link, time = use
        self.free[link] = max(self.now, self.free.get(link, 0.0)) + time
        entry[1] = self.free[link] + self.DELAY

    def add(self, steps):
        entry = [steps, 0.0]
        self.steps.append(entry)
        self.land(entry, next(steps))

    def advance(self, entry):
        self.now = max(self.now, entry[1]) + 0.3
        self.land(entry, next(entry[0], None))

    def tick(self, time):
        self.now += time
        while self.steps:
            entry = min(self.steps, key=lambda e: e[1])
            if entry[1] > self.now:
                break
            self.advance(entry)

    def finish(self, steps):
        while any(e[0] is s for e in self.steps for s in steps):
            self.advance(min(self.steps, key=lambda e: e[1]))

    def drain(self):
        while self.steps:
            self.advance(min(self.steps, key=lambda e: e[1]))


def link_time(name, rows, columns, itemsize=2):
    rate = {"core": 300e3, "x": 50e3, "y": 50e3, "z": 12.5e3}[name]
    return name, rows * columns * itemsize / rate


def backward_kernel(
    targets, length, memory_length, heads, remote,
    dh_rows, ret_rows, place_column, mask, buckets, gain_one, gain_two, gain_three, grad_router, cotangent, tokens, h1, q1, k1, v1, c1, h2, q2, c2, x1, x2, p1, p2,
    k2, v2, memory, wq, wk, wv, wo, cq, ck, cv, co, part_first, part_second,
    *rest,
):
    grad_refs, rest = rest[:8], rest[8:]
    (
        output_out, grad_tokens_out, grad_memory_out, dv2_out, sum_first, sum_second, small,
        rows_v, ret_v, acts, x2_v, p1_v, weights_v, p2_v, kv_v, wide, grads, dscores, ds, dsum, gain_acc, table_v, core_land, landing, small_land, in_sems, out_sems, ring_sems, send_sems, recv_sems, expert_sems, ready,
    ) = rest
    rows, width = x2_v.shape
    pairs = heads // 2
    first_v, q2_v, dctx2, dq, dk, dv, q1_v, k1_v, v1_v, ctx_v, norm_v, do, dctx1, _ = [acts.at[i * rows : (i + 1) * rows, :] for i in range(14)]
    dv2, dk2 = acts.at[6 * rows : 10 * rows, :], acts.at[10 * rows : 14 * rows, :]
    x1_v, du, dx = wide.at[0:rows, :], wide.at[rows : 2 * rows, :], wide.at[2 * rows : 3 * rows, :]
    spare = (dctx2, q2_v)
    gv = wide.at[0:width, :]
    memory_slots, dv2_slots = (rows_v.at[0:memory_length, :], dk2.at[3 * rows : 4 * rows, :]), (do, dctx1)
    loads, stores, running = Loads(in_sems), Loads(out_sems), Running()
    loads.start("rows", dh_rows, rows_v)
    loads.start("cot", cotangent, first_v)
    loads.start("x2", x2, x2_v)
    loads.start("c2", c2, ctx_v)
    loads.start("co", co, weights_v.at[0])

    def fetch(t, sources, first=0):
        slot = t % 2
        m = pl.ds(t * memory_length, memory_length)
        for index, source in enumerate(sources, first):
            target = (p2_v.at[slot], kv_v.at[0, slot], kv_v.at[1, slot], memory_slots[slot])[index]
            copy = pltpu.make_async_copy(source.at[t] if index == 0 else source.at[m, :], target, ring_sems.at[index, slot])
            copy.start()
            yield copy

    fetched = list(fetch(0, (p2, k2, v2)))
    for name, source, target in (
        ("q2", q2, q2_v), ("cq", cq, weights_v.at[1]), ("h2", h2, norm_v), ("wo", wo, weights_v.at[2]),
        ("p1", p1, p1_v), ("q1", q1, q1_v), ("k1", k1, k1_v), ("v1", v1, v1_v), ("ck", ck, weights_v.at[3]),
        ("cv", cv, weights_v.at[4]),
    ):
        loads.start(name, source, target)
    if remote:
        ring = Ring(send_sems, recv_sems)
        ring.greet(("core", "x", "y"))
        capacity = rows_v.shape[0] // ring.experts
        mine = ring.block(ring.expert, capacity)
        ret_copies = [
            ring.send(ret_rows.at[ring.slot(k, capacity, e), :], ret_v.at[mine, :], ring.dp, e) for k, e in enumerate(ring.peers) if k
        ]
        loads.start("ret", ret_rows.at[ring.slot(0, capacity), :], ret_v.at[mine, :])
        expert_sums = [
            reduce_expert(ring, part_first, grads.at[0], grads.at[2], "x", sum_first, expert_sems.at[0]),
            reduce_expert(ring, part_second, grads.at[1], grads.at[5], "y", sum_second, expert_sems.at[1]),
        ]
        for steps in expert_sums:
            running.add(steps)
    else:
        ret_copies, expert_sums = [], []
        loads.start("ret", ret_rows, ret_v)

    gain = [g[...].astype(F32).reshape(1, -1) for g in (gain_one, gain_two, gain_three)]
    low_lane, low, high = half_masks()
    gain_acc[...] = jnp.zeros_like(gain_acc)
    started = []

    def total_of(index):
        if remote:
            axes = (("x", "y", "z"), ("y", "x", "z"))[len(started) % 2]
            running.add(reduce_matrix(ring, grads.at[index], grad_refs[index], core_land.at[index], landing.at[index], axes, stores, ready.at[index]))
        else:
            stores.start(("grad", index), grads.at[index], grad_refs[index])
        started.append(index)

    def inner_grad(index, left, right):
        for c in range(width // 256):
            cols = slice(c * 256, (c + 1) * 256)
            grads[index, cols, :] = dot_tn(left[:, cols], right[...]).astype(BF16)
        total_of(index)

    def back_through(values, index, base, target):
        def one(r):
            back, gain_rows = norm_back(values[r, :].astype(F32), gain[index], du[r, :])
            total = base[r, :].astype(F32) + back
            target[r, :] = total
            if index:
                do[r, :] = total.astype(BF16)
            gain_acc[index] += gain_rows

        row_loop(rows, 32, one)

    loads.wait("rows", "cot", "x2")

    def gather(r):
        du[r, :] = collect(place_column, 128, r, rows_v)

    row_loop(rows, 128, gather)
    fetched += list(fetch(0, (memory,), 3))
    back_through(x2_v, 2, first_v, dx)
    loads.start("tokens", tokens, first_v)
    loads.wait("c2", "co")
    inner_grad(7, ctx_v, do)
    loads.start("c1", c1, ctx_v)

    def out_back(r, slot, target):
        target[r, :] = dot_nt(do[r, :], weights_v[slot]).astype(BF16)

    row_loop(rows, 256, functools.partial(out_back, slot=0, target=dctx2))
    running.tick(7.0)
    loads.start("wq", wq, weights_v.at[0])
    loads.wait("q2")
    for t in range(targets):
        slot = t % 2
        ahead = list(fetch(t + 1, (p2, k2, v2, memory))) if t + 1 < targets else []
        if t >= 2:
            stores.wait(("dv2", t - 2))
        for copy in fetched:
            copy.wait()
        fetched = ahead
        r = slice(t * length, (t + 1) * length)
        for pair in range(pairs):
            lanes = slice(pair * LANES, (pair + 1) * LANES)
            side = pair % 2
            grad_rows = stacked(dctx2[r, lanes], low, high)
            dscores[side] = dot_nt(grad_rows, kv_v[1, slot, :, lanes])
            dv2_slots[slot][:, lanes] = dot_tn(p2_v[slot, pair], grad_rows).astype(BF16)
            for chunk in range(2 * length // 32):
                part = slice(chunk * 32, (chunk + 1) * 32)
                prob = p2_v[slot, pair, part, :].astype(F32)
                dprob = dscores[side, part, :]
                inner = jnp.sum(prob * dprob, axis=-1, keepdims=True)
                ds[t, pair, part, :] = (prob * (dprob - inner)).astype(BF16)
            back = dot(ds[t, pair], kv_v[0, slot, :, lanes])
            dq[r, lanes] = jnp.where(low_lane, back[:length], back[length:]).astype(BF16)
            if side:
                running.tick(1.8)
        stores.start(("dv2", t), dv2_slots[slot], dv2_out.at[pl.ds(t * memory_length, memory_length), :])
        for c in range(width // 256):
            cols = slice(c * 256, (c + 1) * 256)
            part = dot_tn(memory_slots[slot][:, cols], dv2_slots[slot][...])
            if t:
                part = part + gv[cols, :]
            if t + 1 < targets:
                gv[cols, :] = part
            else:
                grads[6, cols, :] = part.astype(BF16)
        running.tick(1.2)
    total_of(6)
    loads.start("x1", x1, x1_v)
    memory_copies = []
    for t in range(targets):
        source = memory.at[pl.ds(t * memory_length, memory_length), :]
        memory_copies.append(pltpu.make_async_copy(source, kv_v.at[t // 2, t % 2], ring_sems.at[1 + t // 2, t % 2]))
        memory_copies[-1].start()
    for t in range(max(0, targets - 2), targets):
        stores.wait(("dv2", t))
    loads.wait("h2", "cq", "x1")
    inner_grad(4, norm_v, dq)
    loads.start("h1", h1, norm_v)

    def query_back(r):
        du[r, :] = dot_nt(dq[r, :], weights_v[1])

    row_loop(rows, 256, query_back)
    loads.start("wk", wk, weights_v.at[1])
    running.tick(2.5)
    back_through(x1_v, 1, dx, dx)
    running.tick(1.5)
    loads.wait("c1", "wo")
    inner_grad(3, ctx_v, do)
    row_loop(rows, 256, functools.partial(out_back, slot=2, target=dctx1))
    loads.start("wv", wv, weights_v.at[2])
    running.tick(2.5)
    for copy in ret_copies:
        copy.wait()
    loads.wait("ret")

    def output_rows(r):
        dk[r, :] = (x2_v[r, :] + collect(place_column, 128, r, ret_v)).astype(BF16)

    row_loop(rows, 128, output_rows)
    stores.start("output", dk, output_out)
    running.tick(2.0)
    loads.wait("p1", "q1", "k1", "v1")
    stores.wait("output")
    for t in range(targets):
        r = slice(t * length, (t + 1) * length)
        allowed = allowed_of(mask[t : t + 1, :], length)
        for pair in range(pairs):
            lanes = slice(pair * LANES, (pair + 1) * LANES)
            side = pair % 2
            grad_rows = stacked(dctx1[r, lanes], low, high)
            both = dot_nt(grad_rows, v1_v[r, lanes])
            scratch = p2_v.at[1, side]
            for half in range(2):
                part = slice(half * length, (half + 1) * length)
                prob = p1_v[t, pair, part, :].astype(F32)
                dprob = both[part]
                inner = jnp.sum(prob * dprob, axis=-1, keepdims=True)
                score = jnp.where(allowed, prob * (dprob - inner), 0.0).astype(BF16)
                scratch[part, :length] = score
                wide_score = score.astype(F32)
                dsum[pair, part, :] = wide_score if t == 0 else dsum[pair, part, :] + wide_score
            dv[r, lanes] = dot_tn(p1_v[t, pair], grad_rows).astype(BF16)
            dk[r, lanes] = dot_tn(scratch[:, :length], stacked(q1_v[r, lanes], low, high)).astype(BF16)
            back = dot(scratch[:, :length], k1_v[r, lanes])
            dq[r, lanes] = jnp.where(low_lane, back[:length], back[length:]).astype(BF16)
        running.tick(2.5)
    loads.wait("h1", "wq", "wk", "wv", "tokens")
    running.finish(expert_sums)
    for index, right in enumerate((dq, dk, dv)):
        inner_grad(index, norm_v, right)
        running.tick(1.2)
    loads.start("dv2", dv2_out, dv2)

    for t in range(targets):
        r = slice(t * length, (t + 1) * length)
        m = slice(t * memory_length, (t + 1) * memory_length)
        for pair in range(pairs):
            lanes = slice(pair * LANES, (pair + 1) * LANES)
            dk2[m, lanes] = dot_tn(ds[t, pair], stacked(q2_v[r, lanes], low, high)).astype(BF16)
        running.tick(1.2)
    for copy in memory_copies:
        copy.wait()
    for c in range(width // 256):
        cols = slice(c * 256, (c + 1) * 256)
        total = 0.0
        for t in range(targets):
            m = slice(t * memory_length, (t + 1) * memory_length)
            total = total + dot_tn(kv_v[t // 2, t % 2, :, cols], dk2[m, :])
        grads[5, cols, :] = total.astype(BF16)
        running.tick(1.3)
    total_of(5)

    def self_back(r):
        du[r, :] = dot_nt(dq[r, :], weights_v[0]) + dot_nt(dk[r, :], weights_v[1]) + dot_nt(dv[r, :], weights_v[2])

    row_loop(rows, 256, self_back)
    running.tick(2.5)
    back_through(first_v, 0, dx, dx)
    stores.start("tokens", dx, grad_tokens_out)
    running.tick(1.5)
    small[...] = jnp.zeros_like(small)
    for i in range(3):
        small[i : i + 1, :] = jnp.sum(gain_acc[i], axis=0, keepdims=True)
    small[8:16, :] = grad_router[0:8, :]
    table_v[...] = jnp.zeros_like(table_v)

    def table_rows(b, carry):
        hit = buckets[...] == b
        for head in range(heads):
            start = (head % 2) * length
            part = jnp.where(hit, dsum[head // 2, start : start + length, :], 0.0)
            table_v[pl.ds(head, 1), :] = jnp.sum(part, axis=0, keepdims=True)
        sums = jnp.sum(table_v[0:16, :], axis=-1, keepdims=True)
        eye = lax.broadcasted_iota(jnp.int32, (16, LANES), 0) == lax.broadcasted_iota(jnp.int32, (16, LANES), 1)
        table_v[pl.ds(16 + b, 1), :] = jnp.sum(jnp.where(eye, sums, 0.0), axis=0, keepdims=True)
        return carry

    for b in range(0, 32, 16):
        lax.fori_loop(b, b + 16, table_rows, 0)
        running.tick(2.0)
    for b in range(0, 32, 8):
        small[16:24, b // 8 * LANES : (b // 8 + 1) * LANES] = table_v[16 + b : 24 + b, :]
    if remote:
        running.add(reduce_small(ring, small, small_land))
    loads.wait("ck", "cv", "dv2")
    for t in range(targets):
        buffer = spare[t % 2]
        if t >= 2:
            stores.wait(("memory", t - 2))
        for half in range(2):
            q = slice(half * memory_length // 2, (half + 1) * memory_length // 2)
            m = slice(t * memory_length + q.start, t * memory_length + q.stop)
            buffer[q, :] = (dot_nt(dk2[m, :], weights_v[3]) + dot_nt(dv2[m, :], weights_v[4])).astype(BF16)
            running.tick(1.2)
        stores.start(("memory", t), buffer, grad_memory_out.at[pl.ds(t * memory_length, memory_length), :])
    running.drain()
    stores.drain()


def finish_kernel(*refs):
    sources, small, targets, table, routed = refs[:13], refs[13], refs[14:27], refs[27], refs[28]
    narrow, wide, parts, first, second, *passed, in_sems, out_sems = refs[29:]
    loads, stores = Loads(in_sems), Loads(out_sems)
    for i in range(8):
        loads.start(i, sources[i], narrow.at[i])
    for i in range(2):
        loads.start(8 + i, sources[8 + i], parts.at[i])
    for i in range(10, 13):
        loads.start(i, sources[i], passed[i - 10])
    for i in range(8):
        loads.wait(i)

        def widen(r, i=i):
            wide[i, r, :] = narrow[i, r, :].astype(F32)

        row_loop(wide.shape[1], 64, widen)
        stores.start(i, wide.at[i], targets[i])
    loads.wait(8, 9)

    def widen_part(r):
        first[r, :] = parts[0, r, :].astype(F32)

    row_loop(first.shape[0], 64, widen_part)
    stores.start(8, first, targets[8])
    for c in range(0, first.shape[0], LANES):
        second[:, c : c + LANES] = parts[1, c : c + LANES, :].astype(F32).T
    stores.start(9, second, targets[9])
    count, heads = table.shape
    for b in range(0, count, 8):
        table[b : b + 8, :] = small[16:24, b // 8 * LANES : b // 8 * LANES + heads]
    routed[...] = small[8:16, :].T[:, : routed.shape[1]]
    for i in range(10, 13):
        loads.wait(i)
        stores.start(i, passed[i - 10], targets[i])
    stores.drain()


def params(**more):
    return pltpu.CompilerParams(vmem_limit_bytes=VMEM_LIMIT, **more)


def on_device(
    tokens, memory, target_mask, buckets, expert_ids, slots, gain_self, w_query, w_key, w_value, w_output, rel_table, gain_cross,
    c_query, c_key, c_value, c_output, gain_moe, router, expert_in, expert_out, cotangent,
):
    rows, width = tokens.shape
    targets, length = target_mask.shape
    bucket_count, heads = rel_table.shape
    memory_length = memory.shape[0] // targets
    pairs = heads // 2
    experts = lax.axis_size("expert")
    hidden = expert_in.shape[2]
    capacity = (5 * rows + 4 * experts - 1) // (4 * experts)
    slot_rows = experts * capacity
    place = jnp.where(slots < capacity, expert_ids * capacity + slots, -1)
    place_row, place_column = place.reshape(1, rows), place.reshape(rows, 1)
    gains = [gain_self, gain_cross, gain_moe]
    weights = (w_query, w_key, w_value, w_output, c_query, c_key, c_value, c_output)

    remote = lax.axis_size("dp") == 8 and experts == 4 and hidden == 4 * width

    def exchange(buffer):
        if remote:
            return buffer
        buffer = buffer.reshape(experts, capacity, width)
        return lax.all_to_all(buffer, "expert", split_axis=0, concat_axis=0, tiled=True).reshape(slot_rows, width)

    def remote_params(collective_id):
        return params(collective_id=collective_id, has_side_effects=True) if remote else params()

    row_shape = jax.ShapeDtypeStruct((slot_rows, width), BF16)
    act_shape = ((rows, width), BF16)
    wide_shape = ((rows, width), F32)
    key_shape = ((targets * memory_length, width), BF16)
    kept = (
        [act_shape] * 8
        + [wide_shape] * 2
        + [((targets, pairs, 2 * length, length), BF16), ((targets, pairs, 2 * length, memory_length), BF16), key_shape, key_shape]
        + [((slot_rows, width), BF16)] * 2
    )
    h1, q1, k1, v1, c1, h2, q2, c2, x1, x2, p1, p2, k2, v2, sent, grows = pl.pallas_call(
        functools.partial(forward_kernel, targets, length, memory_length, heads, remote),
        out_shape=[jax.ShapeDtypeStruct(*k) for k in kept],
        in_specs=[VMEM, ANY, ANY, VMEM, VMEM, VMEM, VMEM, VMEM, VMEM, ANY] + [ANY] * 8,
        out_specs=[ANY] * len(kept),
        scratch_shapes=[pltpu.VMEM((rows, width), BF16), pltpu.VMEM(*key_shape), pltpu.VMEM((8, width, width), BF16)]
        + [pltpu.VMEM(*k) for k in kept]
        + [
            pltpu.VMEM((pairs, 2 * length, length), F32),
            pltpu.VMEM((heads * bucket_count, length), F32),
            pltpu.VMEM((2, 2 * length, memory_length), F32),
            pltpu.SemaphoreType.DMA((11,)),
            pltpu.SemaphoreType.DMA((len(kept),)),
            pltpu.SemaphoreType.DMA((experts - 1,)),
            pltpu.SemaphoreType.DMA((experts - 1,)),
        ],
        compiler_params=remote_params(1),
        name="forward",
    )(rel_table, tokens, memory, target_mask, buckets, *gains, place_row, cotangent, *weights)

    sent, grows = exchange(sent), exchange(grows)
    tiles = hidden // width
    half = width // 2
    weight_grad = jax.ShapeDtypeStruct((3, width, half) if remote else (width, hidden), BF16)
    row_scratch, half_scratch = pltpu.VMEM((slot_rows, width), BF16), pltpu.VMEM((slot_rows // 2, width), F32)
    ret, dh, grad_first, grad_second, grad_router = pl.pallas_call(
        functools.partial(expert_kernel, experts, remote),
        out_shape=[row_shape, row_shape, weight_grad, weight_grad, jax.ShapeDtypeStruct((8, width), F32)],
        in_specs=[ANY, ANY, VMEM, ANY, ANY],
        out_specs=[ANY, ANY, ANY, ANY, VMEM],
        scratch_shapes=[
            pltpu.VMEM((LANES, width), BF16),
            pltpu.VMEM((LANES, width), F32),
            pltpu.VMEM((width, hidden), BF16),
            pltpu.VMEM((hidden, width), BF16),
            row_scratch,
            row_scratch,
            pltpu.VMEM((width, slot_rows), BF16),
            row_scratch,
            pltpu.VMEM((width, slot_rows), BF16),
            pltpu.VMEM((slot_rows, LANES), F32),
            half_scratch,
            half_scratch,
            pltpu.VMEM((slot_rows, hidden), BF16),
            pltpu.VMEM((slot_rows, hidden), BF16),
            half_scratch,
            half_scratch,
            row_scratch,
            row_scratch,
            pltpu.VMEM((2, 2, tiles, width, half), BF16),
            pltpu.VMEM((2, tiles, width, half), BF16),
            pltpu.VMEM((2, width, half), BF16),
            pltpu.SemaphoreType.DMA((2 * tiles + 2,)),
            pltpu.SemaphoreType.DMA((4 * tiles + 2,)),
            pltpu.SemaphoreType.DMA((2 * experts + 2 * tiles,)),
            pltpu.SemaphoreType.DMA((2 * experts + 2 * tiles,)),
        ],
        compiler_params=remote_params(2),
        name="experts",
    )(sent, grows, router.T, expert_in[0], expert_out[0])
    dh_rows, ret_rows = exchange(dh), exchange(ret)
    parts = (grad_first, grad_second)
    if not remote:
        parts = (ret, ret)

    square = (width, width)
    wide = pltpu.VMEM(*wide_shape)
    small_shape = (24, width)
    lands = 8 if remote else 1
    copies = 8 * (6 + 2 * (experts - 1)) + 2 * experts + 1 + 4
    block = jax.ShapeDtypeStruct((width, half), BF16)
    results = pl.pallas_call(
        functools.partial(backward_kernel, targets, length, memory_length, heads, remote),
        out_shape=[jax.ShapeDtypeStruct(square, BF16)] * 8
        + [
            jax.ShapeDtypeStruct((rows, width), BF16),
            jax.ShapeDtypeStruct((rows, width), F32),
            jax.ShapeDtypeStruct(memory.shape, BF16),
            jax.ShapeDtypeStruct(memory.shape, BF16),
            block,
            block,
            jax.ShapeDtypeStruct(small_shape, F32),
        ],
        in_specs=[ANY, ANY] + [VMEM] * 7 + [ANY] * 27,
        out_specs=[ANY] * 14 + [VMEM],
        scratch_shapes=[pltpu.VMEM((slot_rows, width), BF16)] * 2
        + [
            pltpu.VMEM((14 * rows, width), BF16),
            wide,
            pltpu.VMEM((targets, pairs, 2 * length, length), BF16),
            pltpu.VMEM((5,) + square, BF16),
            pltpu.VMEM((2, pairs, 2 * length, memory_length), BF16),
            pltpu.VMEM((2, 2, memory_length, width), BF16),
            pltpu.VMEM((3 * rows, width), F32),
            pltpu.VMEM((8,) + square, BF16),
            pltpu.VMEM((2, 2 * length, memory_length), F32),
            pltpu.VMEM((targets, pairs, 2 * length, memory_length), BF16),
            pltpu.VMEM((pairs, 2 * length, length), F32),
            pltpu.VMEM((3, 8, width), F32),
            pltpu.VMEM((48, LANES), F32),
            pltpu.VMEM((lands, width, half), BF16),
            pltpu.VMEM((lands, width - width // (4 * experts), half), BF16),
            pltpu.VMEM((experts + 3,) + small_shape, F32),
            pltpu.SemaphoreType.DMA((24,)),
            pltpu.SemaphoreType.DMA((28,)),
            pltpu.SemaphoreType.DMA((4, 2)),
            pltpu.SemaphoreType.DMA((copies,)),
            pltpu.SemaphoreType.DMA((copies,)),
            pltpu.SemaphoreType.DMA((2, 3)),
            pltpu.SemaphoreType.REGULAR((8,)),
        ],
        compiler_params=remote_params(0),
        name="backward",
    )(
        dh_rows, ret_rows, place_column, target_mask, buckets, *gains, grad_router, cotangent, tokens, h1, q1, k1, v1, c1, h2, q2, c2, x1, x2,
        p1, p2, k2, v2, memory, *weights, *parts,
    )
    summed, (output, grad_tokens, grad_memory, _, grad_first_sum, grad_second_sum), small = results[:8], results[8:14], results[-1]
    if not remote:
        summed, small = lax.psum((summed, small), ("dp", "expert"))
        grad_first_sum, grad_second_sum = (
            lax.psum_scatter(g, "dp", scatter_dimension=1, tiled=True) for g in (grad_first, grad_second)
        )
    wide_square = jax.ShapeDtypeStruct(square, F32)
    part_shape = grad_first_sum.shape
    finished = pl.pallas_call(
        finish_kernel,
        out_shape=[wide_square] * 8
        + [
            jax.ShapeDtypeStruct(part_shape, F32),
            jax.ShapeDtypeStruct(part_shape[::-1], F32),
            jax.ShapeDtypeStruct(output.shape, BF16),
            jax.ShapeDtypeStruct(grad_tokens.shape, F32),
            jax.ShapeDtypeStruct(grad_memory.shape, BF16),
            jax.ShapeDtypeStruct((bucket_count, heads), F32),
            jax.ShapeDtypeStruct((width, experts), F32),
        ],
        in_specs=[ANY] * 13 + [VMEM],
        out_specs=[ANY] * 8 + [ANY] * 5 + [VMEM] * 2,
        scratch_shapes=[
            pltpu.VMEM((8,) + square, BF16),
            pltpu.VMEM((8,) + square, F32),
            pltpu.VMEM((2,) + part_shape, BF16),
            pltpu.VMEM(part_shape, F32),
            pltpu.VMEM(part_shape[::-1], F32),
            pltpu.VMEM(output.shape, BF16),
            pltpu.VMEM(grad_tokens.shape, F32),
            pltpu.VMEM(grad_memory.shape, BF16),
            pltpu.SemaphoreType.DMA((13,)),
            pltpu.SemaphoreType.DMA((13,)),
        ],
        compiler_params=params(),
        name="finish",
    )(*summed, grad_first_sum, grad_second_sum, output, grad_tokens, grad_memory, small)
    wq_grad, wk_grad, wv_grad, wo_grad, cq_grad, ck_grad, cv_grad, co_grad, first, second, output, grad_tokens, grad_memory, table, routed = finished
    return (
        output, grad_tokens, grad_memory, small[0], wq_grad, wk_grad, wv_grad, wo_grad, table, small[1], cq_grad, ck_grad, cv_grad, co_grad,
        small[2], routed, first[None], second[None],
    )


def solution(mesh):
    both, spread = P(("dp", "expert")), P(("dp", "expert"), None)
    placed = (
        (spread, spread, spread, P(), both, both) + (P(),) * 13 + (P("expert", None, None), P("expert", None, None), spread)
    )
    return jax.shard_map(
        on_device,
        mesh=mesh,
        in_specs=placed,
        out_specs=(spread, spread, spread) + (P(),) * 13 + (P("expert", None, "dp"), P("expert", "dp", None)),
        check_vma=False,
    )
```

```python
import functools

import jax
import jax.numpy as jnp
from jax import lax
from jax.experimental import pallas as pl
from jax.experimental.pallas import tpu as pltpu
from jax.sharding import PartitionSpec as P

EPS = 1e-06
NEG = -1000000000.0
F32 = jnp.float32
BF16 = jnp.bfloat16
LANES = 128
VMEM_LIMIT = 63_400_000
ANY = pl.BlockSpec(memory_space=pl.ANY)
VMEM = pl.BlockSpec(memory_space=pltpu.VMEM)
SMEM = pl.BlockSpec(memory_space=pltpu.SMEM)


def dot(left, right):
    return lax.dot_general(left, right, (((1,), (0,)), ((), ())), preferred_element_type=F32)


def dot_nt(left, right):
    return lax.dot_general(left, right, (((1,), (1,)), ((), ())), preferred_element_type=F32)


def dot_tn(left, right):
    return lax.dot_general(left, right, (((0,), (0,)), ((), ())), preferred_element_type=F32)


def column_tiles(width, step=256):
    return [slice(c, c + step) for c in range(0, width, step)]


def row_loop(count, step, body):
    def one(i, carry):
        body(pl.ds(pl.multiple_of(i * step, step), step))
        return carry

    lax.fori_loop(0, count // step, one, 0)


def half_masks():
    lane = lax.broadcasted_iota(jnp.int32, (1, LANES), 1)
    low = jnp.where(lane < LANES // 2, 1.0, 0.0).astype(BF16)
    high = jnp.where(lane < LANES // 2, 0.0, 1.0).astype(BF16)
    return lane < LANES // 2, low, high


def stacked(pair, low, high):
    return jnp.concatenate([pair * low, pair * high], axis=0)


def norm_rows(values, gain):
    return values * lax.rsqrt(jnp.mean(values * values, axis=-1, keepdims=True) + EPS) * gain


def norm_back(values, gain, grad):
    scale = lax.rsqrt(jnp.mean(values * values, axis=-1, keepdims=True) + EPS)
    scaled = grad * gain
    inner = jnp.mean(scaled * values, axis=-1, keepdims=True)
    back = scale * scaled - values * (scale * scale * scale * inner)
    gain_rows = grad * values * scale
    return back, jnp.sum(gain_rows.reshape(-1, 8, gain_rows.shape[-1]), axis=0)


def allowed_of(mask_row, length):
    row = lax.broadcasted_iota(jnp.int32, (length, length), 0)
    col = lax.broadcasted_iota(jnp.int32, (length, length), 1)
    return (col <= row) & (mask_row == 1)


class Loads:
    def __init__(self, sems):
        self.sems = sems
        self.count = 0
        self.open = {}

    def start(self, name, source, target):
        copy = pltpu.make_async_copy(source, target, self.sems.at[self.count])
        self.count += 1
        copy.start()
        self.open[name] = copy

    def wait(self, *names):
        for name in names:
            self.open.pop(name).wait()

    def drain(self):
        self.wait(*list(self.open))


class Ring:
    def __init__(self, send_sems, recv_sems):
        self.send_sems, self.recv_sems = send_sems, recv_sems
        self.count = 0
        dp, self.expert = lax.axis_index("dp"), lax.axis_index("expert")
        self.experts = lax.axis_size("expert")
        self.dp = dp
        self.spot = {"core": lax.rem(dp, 2), "x": lax.rem(lax.div(dp, 2), 2), "y": lax.div(dp, 4)}
        self.partner = {name: dp + step - 2 * step * self.spot[name] for name, step in (("core", 1), ("x", 2), ("y", 4))}

        low, high = lax.rem(self.expert, 2), lax.div(self.expert, 2)
        near, far = 1 - 2 * low, 2 - 4 * high
        self.peers = [self.expert, self.expert + near, self.expert + far, self.expert + near + far]

    def others(self):
        return self.peers[1:]

    def block(self, expert, capacity):
        return pl.ds(pl.multiple_of(expert * capacity, 16), capacity)

    def slot(self, k, capacity, sender=None):
        low = lax.rem(self.expert if sender is None else sender, 2)
        return pl.ds(pl.multiple_of((low + (2 if k >= 2 else 0)) * capacity, 16), capacity)

    def scatter(self, source, target):
        capacity = source.shape[0] // self.experts
        return [
            self.send(source.at[self.block(e, capacity), :], target.at[self.slot(k, capacity), :], self.dp, e)
            for k, e in enumerate(self.peers)
            if k
        ]

    def greet(self, names):
        barrier = pltpu.get_barrier_semaphore()
        targets = [(self.partner[name], self.expert) for name in names] + [(self.dp, e) for e in self.others()]
        for target in targets:
            pl.semaphore_signal(barrier, inc=1, device_id=target, device_id_type=pl.DeviceIdType.MESH)
        pl.semaphore_wait(barrier, len(targets))

    def send(self, source, target, dp, expert):
        copy = pltpu.make_async_remote_copy(
            src_ref=source, dst_ref=target, send_sem=self.send_sems.at[self.count], recv_sem=self.recv_sems.at[self.count],
            device_id=(dp, expert), device_id_type=pl.DeviceIdType.MESH,
        )
        self.count += 1
        copy.start()
        return copy

    def cross(self, name, source, target):
        return self.send(source, target, self.partner[name], self.expert)


def forward_kernel(
    targets, length, memory_length, heads, remote,
    table, tokens, memory, mask, buckets, gain_one, gain_two, gain_three, place, cotangent, wq, wk, wv, wo, cq, ck, cv, co,
    h1_out, q1_out, k1_out, v1_out, c1_out, h2_out, q2_out, c2_out, x1_out, x2_out, p1_out, p2_out, k2_out, v2_out, sent_out, grows_out,
    tokens_v, memory_v, weights_v, h1, q1, k1, v1, c1, h2, q2, c2, x1, x2, p1, p2, k2, v2, sent, gsent, bias, spread, scores, in_sems, out_sems,
    send_sems, recv_sems,
):
    rows, width = tokens_v.shape
    pairs = heads // 2
    loads, stores = Loads(in_sems), Loads(out_sems)
    loads.start("cot", cotangent, c2)
    loads.start("tokens", tokens, tokens_v)
    for index, (name, ref) in enumerate(zip(("wq", "wk", "wv"), (wq, wk, wv))):
        loads.start(name, ref, weights_v.at[index])
    loads.start("ck", ck, weights_v.at[5])
    loads.start("memory", memory, memory_v)
    loads.start("cv", cv, weights_v.at[6])
    loads.start("wo", wo, weights_v.at[3])
    loads.start("cq", cq, weights_v.at[4])
    loads.start("co", co, weights_v.at[7])
    gain = [g[...].astype(F32).reshape(1, -1) for g in (gain_one, gain_two, gain_three)]
    low_lane, low, high = half_masks()

    if remote:
        ring = Ring(send_sems, recv_sems)
        ring.greet(())
    loads.wait("cot")
    dispatch(place, c2, gsent)
    gsent_copies = []
    if remote:
        gsent_copies = ring.scatter(gsent, grows_out)
        block = ring.block(ring.expert, sent.shape[0] // ring.experts)
        stores.start("grows", gsent.at[block, :], grows_out.at[ring.slot(0, sent.shape[0] // ring.experts), :])
    else:
        stores.start("grows", gsent, grows_out)
    bucket_count = table.shape[1]
    by_head = table[...].astype(F32)
    for head in range(heads):
        row = jnp.broadcast_to(by_head[head : head + 1, :], (LANES, bucket_count))
        spread[head * bucket_count : (head + 1) * bucket_count, :] = row.T

    def bias_rows(r):
        here = buckets[r, :]
        hits = [here == b for b in range(bucket_count)]
        for head in range(heads):
            total = jnp.zeros(here.shape, F32)
            for b in range(bucket_count):
                at = head * bucket_count + b
                total = jnp.where(hits[b], spread[at : at + 1, :], total)
            start = (head % 2) * length
            bias[head // 2, pl.ds(pl.multiple_of(r.start + start, 8), r.size), :] = total

    row_loop(length, 16, bias_rows)

    loads.wait("tokens")

    def first_norm(r):
        h1[r, :] = norm_rows(tokens_v[r, :].astype(F32), gain[0]).astype(BF16)

    row_loop(rows, 32, first_norm)
    stores.start("h1", h1, h1_out)
    for index, (name, ref) in enumerate(zip(("wq", "wk", "wv"), (q1, k1, v1))):
        loads.wait(name)

        for cols in column_tiles(width):
            ref[:, cols] = dot(h1[...], weights_v[index, :, cols]).astype(BF16)
    stores.start("q1", q1, q1_out)
    stores.start("k1", k1, k1_out)
    stores.start("v1", v1, v1_out)

    def self_target(t, carry):
        r = pl.ds(pl.multiple_of(t * length, length), length)
        allowed = allowed_of(mask[pl.ds(t, 1), :], length)
        for pair in range(pairs):
            lanes = slice(pair * LANES, (pair + 1) * LANES)
            both = dot_nt(stacked(q1[r, lanes], low, high), k1[r, lanes])
            for half in range(2):
                part = slice(half * length, (half + 1) * length)
                score = jnp.where(allowed, both[part] + bias[pair, part, :], NEG)
                expo = jnp.exp(score - jnp.max(score, axis=-1, keepdims=True))
                total = jnp.sum(expo, axis=-1, keepdims=True)
                p1[t, pair, part, :] = (expo * (1.0 / total)).astype(BF16)
            context = dot(p1[t, pair], v1[r, lanes])
            c1[r, lanes] = jnp.where(low_lane, context[:length], context[length:]).astype(BF16)
        return carry

    lax.fori_loop(0, targets, self_target, 0)
    stores.start("p1", p1, p1_out)
    stores.start("c1", c1, c1_out)
    loads.wait("wo")

    for cols in column_tiles(width):
        x1[:, cols] = tokens_v[:, cols].astype(F32) + dot(c1[...], weights_v[3, :, cols])
    stores.start("x1", x1, x1_out)

    def second_norm(r):
        h2[r, :] = norm_rows(x1[r, :], gain[1]).astype(BF16)

    row_loop(rows, 32, second_norm)
    stores.start("h2", h2, h2_out)
    loads.wait("cq")

    for cols in column_tiles(width):
        q2[:, cols] = dot(h2[...], weights_v[4, :, cols]).astype(BF16)
    stores.start("q2", q2, q2_out)
    loads.wait("memory", "ck", "cv")

    def cross_keys(r):
        for cols in column_tiles(width):
            k2[r, cols] = dot(memory_v[r, :], weights_v[5, :, cols]).astype(BF16)
            v2[r, cols] = dot(memory_v[r, :], weights_v[6, :, cols]).astype(BF16)

    row_loop(targets * memory_length, memory_length, cross_keys)
    stores.start("k2", k2, k2_out)
    stores.start("v2", v2, v2_out)

    def cross_target(t, carry):
        r = pl.ds(pl.multiple_of(t * length, length), length)
        m = pl.ds(pl.multiple_of(t * memory_length, memory_length), memory_length)
        for pair in range(pairs):
            lanes = slice(pair * LANES, (pair + 1) * LANES)
            slot = pair % 2
            scores[slot] = dot_nt(stacked(q2[r, lanes], low, high), k2[m, lanes])
            for chunk in range(2 * length // 32):
                part = slice(chunk * 32, (chunk + 1) * 32)
                score = scores[slot, part, :]
                expo = jnp.exp(score - jnp.max(score, axis=-1, keepdims=True))
                total = jnp.sum(expo, axis=-1, keepdims=True)
                p2[t, pair, part, :] = (expo * (1.0 / total)).astype(BF16)
            context = dot(p2[t, pair], v2[m, lanes])
            c2[r, lanes] = jnp.where(low_lane, context[:length], context[length:]).astype(BF16)
        return carry

    lax.fori_loop(0, targets, cross_target, 0)
    stores.start("p2", p2, p2_out)
    stores.start("c2", c2, c2_out)
    loads.wait("co")

    for cols in column_tiles(width):
        x2[:, cols] = x1[:, cols] + dot(c2[...], weights_v[7, :, cols])
    stores.start("x2", x2, x2_out)

    def third_norm(r):
        tokens_v[r, :] = norm_rows(x2[r, :], gain[2]).astype(BF16)

    row_loop(rows, 32, third_norm)
    dispatch(place, tokens_v, sent)
    stores.start("sent", sent, sent_out)
    for copy in gsent_copies:
        copy.wait()
    stores.drain()


def dispatch(place, source, target):
    step = target.shape[0] // 2

    def one(r):
        spot = lax.broadcasted_iota(jnp.int32, (step, source.shape[0]), 0) + r.start
        hit = jnp.where(spot == place[...], 1.0, 0.0).astype(BF16)
        for cols in column_tiles(source.shape[1]):
            target[r, cols] = dot(hit, source[:, cols]).astype(target.dtype)

    row_loop(target.shape[0], step, one)


def collect(place_column, source, put):
    spot = lax.broadcasted_iota(jnp.int32, (place_column.shape[0], source.shape[0]), 1)
    hit = jnp.where(spot == place_column[...], 1.0, 0.0).astype(BF16)
    for cols in column_tiles(source.shape[1]):
        put(cols, dot(hit, source[:, cols]))


class ExpertSum:
    def __init__(self, ring, running, tiles, core_land, near_land, first, result, stores):
        self.ring, self.running, self.tiles, self.first = ring, running, tiles, first
        self.core_land, self.near_land = core_land, near_land
        self.result, self.stores = result, stores
        self.order = (0, 1, 2, 3) if first == "x" else (0, 2, 1, 3)
        self.ready, self.started = set(), False
        self.place = (lambda one, two: one + 2 * two) if first == "x" else (lambda one, two: 2 * one + two)

    def add(self, tile, other):
        core = self.ring.spot["core"]

        def rows(r):
            total = self.tiles[core, tile, r, :].astype(F32) + other[r, :].astype(F32)
            self.tiles[core, tile, r, :] = total.astype(BF16)

        row_loop(self.tiles.shape[2], 64, rows)

    def start(self, tile):
        self.running.add(self.between_cores(tile))

    def between_cores(self, tile):
        core = self.ring.spot["core"]
        copy = self.ring.cross("core", self.tiles.at[1 - core, tile], self.core_land.at[tile])
        yield link_time("core", *self.tiles.shape[2:])
        copy.wait()
        self.add(tile, self.core_land.at[tile])
        self.ready.add(tile)
        if {self.place(0, 0), self.place(1, 0)} <= self.ready and not self.started:
            self.started = True
            self.running.add(self.near())
        if {self.place(0, 1), self.place(1, 1)} <= self.ready:
            spot = self.ring.spot[self.first]
            self.keep(1, self.place(spot, 1))
            self.keep(2, self.place(1 - spot, 1))

    def near(self):
        spot = self.ring.spot[self.first]
        source = self.tiles.at[self.ring.spot["core"], self.place(1 - spot, 0)]
        copy = self.ring.cross(self.first, source, self.near_land)
        yield link_time(self.first, *self.tiles.shape[2:])
        copy.wait()
        self.keep(0, self.place(spot, 0), self.near_land)

    def keep(self, index, tile, other=None):
        if other is not None:
            self.add(tile, other)
        source = self.tiles.at[self.ring.spot["core"], tile]
        self.stores.start(("sum", self.first, index), source, self.result.at[index])


def expert_kernel(
    experts, remote, inbound, grows, router_rows, first, second,
    ret_out, dh_out, grad_first, grad_second, grad_router,
    router, router_turned, router_sum, first_v, second_v, inbound_v, grows_v, inbound_t, dret, dret_t, probs, pre, dact, act, dpre, ret, dinb, ret_v, dh_v, sums, core_land, near_land,
    in_sems, out_sems, send_sems, recv_sems,
):
    rows, width = inbound_v.shape
    hidden = first.shape[1]
    step = width
    tiles = hidden // step
    loads, stores = Loads(in_sems), Loads(out_sems)
    capacity = rows // experts
    half_rows = rows // 2
    if remote:
        ring = Ring(send_sems, recv_sems)
        ring.greet(("core", "x", "y"))
        arriving = ring.scatter(inbound, inbound_v)
        loads.start("inbound", inbound.at[ring.block(ring.expert, capacity), :], inbound_v.at[ring.slot(0, capacity), :])
    else:
        loads.start("inbound", inbound, inbound_v)
        arriving = []
    loads.start("grows", grows, grows_v)
    for f in range(tiles):
        cols = slice(f * step, (f + 1) * step)
        loads.start(("first", f), first.at[:, cols], first_v.at[:, cols])
        loads.start(("second", f), second.at[cols, :], second_v.at[cols, :])
    me = lax.axis_index("expert")
    lane = lax.broadcasted_iota(jnp.int32, (1, LANES), 1)
    mine = lane == me
    root = (2.0 / jnp.pi) ** 0.5
    router_sum[...] = jnp.zeros_like(router_sum)
    router[...] = jnp.zeros_like(router)
    router[0:experts, :] = router_rows[...]
    for cols in column_tiles(width, LANES):
        router_turned[cols, :] = router[:, cols].T
    loads.wait("inbound", "grows")
    returning = []
    for side in range(2):
        start = side * half_rows
        here = slice(start, start + half_rows)
        for copy in (arriving[:1], arriving[1:])[side]:
            copy.wait_recv()

        def route(r, start=start):
            r = pl.ds(pl.multiple_of(start + r.start, 16), r.size)
            logits = jnp.where(lane < experts, dot(inbound_v[r, :], router_turned[...]), -1e30)
            expo = jnp.exp(logits - jnp.max(logits, axis=-1, keepdims=True))
            prob = expo / jnp.sum(expo, axis=-1, keepdims=True)
            probs[r, :] = prob
            gate = jnp.sum(jnp.where(mine, prob, 0.0), axis=-1, keepdims=True)
            dret[r, :] = (gate * grows_v[r, :].astype(F32)).astype(BF16)

        row_loop(half_rows, half_rows // 2, route)
        for f in range(tiles):
            cols = slice(f * step, (f + 1) * step)
            if side == 0:
                loads.wait(("first", f), ("second", f))
            for c in range(0, step, 256):
                tile = slice(f * step + c, f * step + c + 256)
                pre[:, c : c + 256] = dot(inbound_v[here, :], first_v[:, tile])
                dact[:, c : c + 256] = dot_nt(dret[here, :], second_v[tile, :])

            def middle(r, start=start, cols=cols):
                u = pre[r, :]
                square = u * u
                t = jnp.tanh(u * (root + (root * 0.044715) * square))
                half = 0.5 + 0.5 * t
                out = pl.ds(pl.multiple_of(start + r.start, 16), r.size)
                act[out, cols] = (u * half).astype(BF16)
                slope = half + (u * (0.5 * root + (1.5 * root * 0.044715) * square)) * (1.0 - t * t)
                dpre[out, cols] = (dact[r, :] * slope).astype(BF16)

            row_loop(half_rows, 16, middle)
            for c in range(0, width, 256):
                tile = slice(c, c + 256)
                one, two = dot(act[here, cols], second_v[cols, tile]), dot_nt(dpre[here, cols], first_v[tile, cols])
                if f:
                    one, two = one + ret[:, tile], two + dinb[:, tile]
                ret[:, tile] = one
                dinb[:, tile] = two

        def finish(r, start=start):
            out = pl.ds(pl.multiple_of(start + r.start, 16), r.size)
            result = ret[r, :].astype(BF16).astype(F32)
            prob = probs[out, :]
            gate = jnp.sum(jnp.where(mine, prob, 0.0), axis=-1, keepdims=True)
            dgate = jnp.sum(result * grows_v[out, :].astype(F32), axis=-1, keepdims=True)
            dlogits = (prob * (jnp.where(mine, 1.0, 0.0) - gate) * dgate).astype(BF16)
            ret_v[out, :] = (gate * result).astype(BF16)
            dh_v[out, :] = (dinb[r, :].astype(BF16).astype(F32) + dot(dlogits, router[...])).astype(BF16)
            router_sum[...] += dot_tn(dlogits, inbound_v[out, :])

        row_loop(half_rows, half_rows // 2, finish)
        if remote:
            target = dh_out.at[ring.block(ring.expert, capacity), :]
            for k in ((1,), (2, 3))[side]:
                source = dh_v.at[ring.slot(k, capacity, ring.peers[k]), :]
                returning.append(ring.send(source, target, ring.dp, ring.peers[k]))
            if side == 0:
                stores.start("dh", dh_v.at[ring.slot(0, capacity), :], target)
        elif side:
            stores.start("dh", dh_v, dh_out)
    stores.start("ret", ret_v, ret_out)
    grad_router[...] = router_sum[0:8, :]
    for copy in arriving:
        copy.wait_send()
    for c in range(width // LANES):
        cols = slice(c * LANES, (c + 1) * LANES)
        inbound_t[cols, :] = inbound_v[:, cols].T
        dret_t[cols, :] = dret[:, cols].T

    running = Running()
    if remote:
        expert_sums = [
            ExpertSum(ring, running, sums.at[j], core_land.at[j], near_land.at[j], axis, out, stores)
            for j, (axis, out) in enumerate((("x", grad_first), ("y", grad_second)))
        ]
    for i in range(tiles):
        for j, (left, right) in enumerate(((inbound_t, dpre), (dret_t, act))):
            f = expert_sums[j].order[i] if remote else i
            for cols in column_tiles(step):
                total = dot(left[...], right[:, f * step + cols.start : f * step + cols.stop]).astype(BF16)
                for c in range(cols.start, cols.stop, LANES):
                    b, at = divmod(c, step // 2)
                    sums[j, b, f, :, at : at + LANES] = total[:, c - cols.start : c - cols.start + LANES]
            if not remote:
                for b in range(2):
                    cols = slice(f * step + b * (step // 2), f * step + (b + 1) * (step // 2))
                    stores.start(("sum", j, b, f), sums.at[j, b, f], (grad_first, grad_second)[j].at[:, cols])
            running.tick(1.6)
            if remote:
                expert_sums[j].start(f)
    running.drain()
    for copy in returning:
        copy.wait()
    stores.drain()


def span(start, size):
    return pl.ds(pl.multiple_of(start, size), size)


def add_into(ref, rows, lanes, others, target=None):
    step = 48 if rows.size % 64 else 64
    for i in range(rows.size // step):
        here = pl.ds(pl.multiple_of(rows.start + i * step, 16), step)
        total = ref[here, lanes].astype(F32)
        for other in others:
            total = total + other[i * step : (i + 1) * step, :].astype(F32)
        if target is None:
            ref[here, lanes] = total.astype(BF16)
        else:
            target[here, :] = total.astype(BF16)


def reduce_matrix(ring, local, result, core_land, landing, axes, stores, ready):
    size = local.shape[0]
    half = size // 2
    core = ring.spot["core"]
    mine, other = span(core * half, half), span((1 - core) * half, half)
    copy = ring.cross("core", local.at[:, other], core_land)
    yield link_time("core", size, half)
    copy.wait()
    pl.semaphore_signal(ready, inc=1, device_id=(ring.partner["core"], ring.expert), device_id_type=pl.DeviceIdType.MESH)
    add_into(local, pl.ds(0, size), mine, [core_land])
    base, count, row, trail = 0, size, 0, []
    for axis in axes:
        parts = ring.experts if axis == "z" else 2
        part = count // parts
        lands = [landing.at[row + k * part : row + (k + 1) * part, :] for k in range(parts - 1)]
        if axis == "z":
            spot = ring.expert
            copies = [ring.send(local.at[span(base + e * part, part), mine], lands[k], ring.dp, e) for k, e in enumerate(ring.others())]
        else:
            spot = ring.spot[axis]
            copies = [ring.cross(axis, local.at[span(base + (1 - spot) * part, part), mine], lands[0])]
        yield link_time(axis, part, half)
        for copy in copies:
            copy.wait()
        base, count, row = base + spot * part, part, row + (parts - 1) * part
        here = span(base, count)
        add_into(local, here, mine, lands, core_land if axis == axes[-1] else None)
        trail.append((axis, here))
    for axis, here in reversed(trail):
        block = core_land.at[here, :]
        if axis == "z":
            copies = [ring.send(block, block, ring.dp, e) for e in ring.others()]
        else:
            copies = [ring.cross(axis, block, block)]
        yield link_time(axis, here.size, half)
        for copy in copies:
            copy.wait()
    pl.semaphore_wait(ready, 1)
    copy = ring.cross("core", core_land, local.at[:, mine])
    yield link_time("core", size, half)
    copy.wait()
    stores.start(("mine", stores.count), core_land, result.at[:, mine])
    stores.start(("other", stores.count), local.at[:, other], result.at[:, other])


def reduce_expert(ring, part, keep, extra, first, result, sems):
    size, block = part.shape[1], part.shape[2]
    second = "y" if first == "x" else "x"
    cols = [slice(i * block, (i + 1) * block) for i in range(2)]
    copies = [ring.cross(first, part.at[2], extra.at[:, cols[1]])]
    copies += [pltpu.make_async_copy(part.at[i], keep.at[:, cols[i]], sems.at[i]) for i in range(2)]
    for copy in copies[1:]:
        copy.start()
    yield link_time(first, size, block)
    for copy in copies:
        copy.wait()
    add_into(keep, pl.ds(0, size), cols[1], [extra.at[:, cols[1]]])
    spot = ring.spot[second]
    copy = ring.cross(second, keep.at[:, span((1 - spot) * block, block)], extra.at[:, cols[0]])
    yield link_time(second, size, block)
    copy.wait()
    stay = span(spot * block, block)
    add_into(keep, pl.ds(0, size), stay, [extra.at[:, cols[0]]])
    copy = pltpu.make_async_copy(keep.at[:, stay], result, sems.at[2])
    copy.start()
    copy.wait()


def reduce_small(ring, local, landing):
    for k, name in enumerate(("core", "x", "y")):
        copy = ring.cross(name, local, landing.at[k])
        yield link_time(name, *local.shape, 4)
        copy.wait()
        local[...] += landing[k]
    copies = [ring.send(local, landing.at[3 + ring.expert], ring.dp, e) for e in ring.others()]
    landing[3 + ring.expert] = local[...]
    yield link_time("z", *local.shape, 4)
    for copy in copies:
        copy.wait()
    total = landing[3]
    for e in range(1, ring.experts):
        total = total + landing[3 + e]
    local[...] = total


class Running:
    DELAY = 1.5

    def __init__(self):
        self.steps = []
        self.now = 0.0
        self.free = {}

    def land(self, entry, use):
        if use is None:
            self.steps = [e for e in self.steps if e is not entry]
            return
        link, time = use
        self.free[link] = max(self.now, self.free.get(link, 0.0)) + time
        entry[1] = self.free[link] + self.DELAY

    def add(self, steps):
        entry = [steps, 0.0]
        self.steps.append(entry)
        self.land(entry, next(steps))

    def advance(self, entry):
        self.now = max(self.now, entry[1]) + 0.3
        self.land(entry, next(entry[0], None))

    def tick(self, time):
        self.now += time
        while self.steps:
            entry = min(self.steps, key=lambda e: e[1])
            if entry[1] > self.now:
                break
            self.advance(entry)

    def finish(self, steps):
        while any(e[0] is s for e in self.steps for s in steps):
            self.advance(min(self.steps, key=lambda e: e[1]))

    def drain(self):
        while self.steps:
            self.advance(min(self.steps, key=lambda e: e[1]))


def link_time(name, rows, columns, itemsize=2):
    rate = {"core": 300e3, "x": 50e3, "y": 50e3, "z": 12.5e3}[name]
    return name, rows * columns * itemsize / rate


def backward_kernel(
    targets, length, memory_length, heads, remote,
    dh_rows, ret_rows, place_column, mask, buckets, gain_one, gain_two, gain_three, grad_router, cotangent, tokens, h1, q1, k1, v1, c1, h2, q2, c2, x1, x2, p1, p2,
    k2, v2, memory, wq, wk, wv, wo, cq, ck, cv, co, part_first, part_second,
    *rest,
):
    grad_refs, rest = rest[:8], rest[8:]
    (
        output_out, grad_tokens_out, grad_memory_out, dv2_out, sum_first, sum_second, small,
        rows_v, ret_v, acts, x2_v, p1_v, weights_v, p2_v, kv_v, wide, grads, dscores, ds, dsum, gain_acc, table_v, core_land, landing, small_land, in_sems, out_sems, ring_sems, send_sems, recv_sems, expert_sems, ready,
    ) = rest
    rows, width = x2_v.shape
    pairs = heads // 2
    first_v, q2_v, dctx2, dq, dk, dv, q1_v, k1_v, v1_v, ctx_v, norm_v, do, dctx1, _ = [acts.at[i * rows : (i + 1) * rows, :] for i in range(14)]
    dv2, dk2 = acts.at[6 * rows : 10 * rows, :], acts.at[10 * rows : 14 * rows, :]
    x1_v, du, dx = wide.at[0:rows, :], wide.at[rows : 2 * rows, :], wide.at[2 * rows : 3 * rows, :]
    spare = (dctx2, q2_v)
    gv = wide.at[0:width, :]
    memory_slots, dv2_slots = (rows_v.at[0:memory_length, :], dk2.at[3 * rows : 4 * rows, :]), (do, dctx1)
    loads, stores, running = Loads(in_sems), Loads(out_sems), Running()
    loads.start("rows", dh_rows, rows_v)
    loads.start("cot", cotangent, first_v)
    loads.start("x2", x2, x2_v)
    loads.start("c2", c2, ctx_v)
    loads.start("co", co, weights_v.at[0])

    def fetch(t, sources, first=0):
        slot = t % 2
        m = pl.ds(t * memory_length, memory_length)
        for index, source in enumerate(sources, first):
            target = (p2_v.at[slot], kv_v.at[0, slot], kv_v.at[1, slot], memory_slots[slot])[index]
            copy = pltpu.make_async_copy(source.at[t] if index == 0 else source.at[m, :], target, ring_sems.at[index, slot])
            copy.start()
            yield copy

    fetched = list(fetch(0, (p2, k2, v2)))
    for name, source, target in (
        ("q2", q2, q2_v), ("cq", cq, weights_v.at[1]), ("h2", h2, norm_v), ("wo", wo, weights_v.at[2]),
        ("p1", p1, p1_v), ("q1", q1, q1_v), ("k1", k1, k1_v), ("v1", v1, v1_v), ("ck", ck, weights_v.at[3]),
        ("cv", cv, weights_v.at[4]),
    ):
        loads.start(name, source, target)
    if remote:
        ring = Ring(send_sems, recv_sems)
        ring.greet(("core", "x", "y"))
        capacity = rows_v.shape[0] // ring.experts
        mine = ring.block(ring.expert, capacity)
        ret_copies = [
            ring.send(ret_rows.at[ring.slot(k, capacity, e), :], ret_v.at[mine, :], ring.dp, e) for k, e in enumerate(ring.peers) if k
        ]
        loads.start("ret", ret_rows.at[ring.slot(0, capacity), :], ret_v.at[mine, :])
        expert_sums = [
            reduce_expert(ring, part_first, grads.at[0], grads.at[2], "x", sum_first, expert_sems.at[0]),
            reduce_expert(ring, part_second, grads.at[1], grads.at[5], "y", sum_second, expert_sems.at[1]),
        ]
        for steps in expert_sums:
            running.add(steps)
    else:
        ret_copies, expert_sums = [], []
        loads.start("ret", ret_rows, ret_v)

    gain = [g[...].astype(F32).reshape(1, -1) for g in (gain_one, gain_two, gain_three)]
    low_lane, low, high = half_masks()
    gain_acc[...] = jnp.zeros_like(gain_acc)
    started = []

    def total_of(index):
        if remote:
            axes = (("x", "y", "z"), ("y", "x", "z"))[len(started) % 2]
            running.add(reduce_matrix(ring, grads.at[index], grad_refs[index], core_land.at[index], landing.at[index], axes, stores, ready.at[index]))
        else:
            stores.start(("grad", index), grads.at[index], grad_refs[index])
        started.append(index)

    def inner_grad(index, left, right):
        for c in range(width // 256):
            cols = slice(c * 256, (c + 1) * 256)
            grads[index, cols, :] = dot_tn(left[:, cols], right[...]).astype(BF16)
        total_of(index)

    def back_through(values, index, base, target):
        def one(r):
            back, gain_rows = norm_back(values[r, :].astype(F32), gain[index], du[r, :])
            total = base[r, :].astype(F32) + back
            target[r, :] = total
            if index:
                do[r, :] = total.astype(BF16)
            gain_acc[index] += gain_rows

        row_loop(rows, 32, one)

    loads.wait("rows", "cot", "x2")

    def gathered(cols, values):
        du[:, cols] = values

    collect(place_column, rows_v, gathered)
    fetched += list(fetch(0, (memory,), 3))
    back_through(x2_v, 2, first_v, dx)
    loads.start("tokens", tokens, first_v)
    loads.wait("c2", "co")
    inner_grad(7, ctx_v, do)
    loads.start("c1", c1, ctx_v)

    def out_back(slot, target):
        for cols in column_tiles(width):
            target[:, cols] = dot_nt(do[...], weights_v[slot, cols, :]).astype(BF16)

    out_back(0, dctx2)
    running.tick(7.0)
    loads.start("wq", wq, weights_v.at[0])
    loads.wait("q2")
    for t in range(targets):
        slot = t % 2
        ahead = list(fetch(t + 1, (p2, k2, v2, memory))) if t + 1 < targets else []
        if t >= 2:
            stores.wait(("dv2", t - 2))
        for copy in fetched:
            copy.wait()
        fetched = ahead
        r = slice(t * length, (t + 1) * length)
        for pair in range(pairs):
            lanes = slice(pair * LANES, (pair + 1) * LANES)
            side = pair % 2
            grad_rows = stacked(dctx2[r, lanes], low, high)
            dscores[side] = dot_nt(grad_rows, kv_v[1, slot, :, lanes])
            dv2_slots[slot][:, lanes] = dot_tn(p2_v[slot, pair], grad_rows).astype(BF16)
            for chunk in range(2 * length // 32):
                part = slice(chunk * 32, (chunk + 1) * 32)
                prob = p2_v[slot, pair, part, :].astype(F32)
                dprob = dscores[side, part, :]
                inner = jnp.sum(prob * dprob, axis=-1, keepdims=True)
                ds[t, pair, part, :] = (prob * (dprob - inner)).astype(BF16)
            back = dot(ds[t, pair], kv_v[0, slot, :, lanes])
            dq[r, lanes] = jnp.where(low_lane, back[:length], back[length:]).astype(BF16)
            if side:
                running.tick(1.8)
        stores.start(("dv2", t), dv2_slots[slot], dv2_out.at[pl.ds(t * memory_length, memory_length), :])
        for c in range(width // 256):
            cols = slice(c * 256, (c + 1) * 256)
            part = dot_tn(memory_slots[slot][:, cols], dv2_slots[slot][...])
            if t:
                part = part + gv[cols, :]
            if t + 1 < targets:
                gv[cols, :] = part
            else:
                grads[6, cols, :] = part.astype(BF16)
        running.tick(1.2)
    total_of(6)
    loads.start("x1", x1, x1_v)
    memory_copies = []
    for t in range(targets):
        source = memory.at[pl.ds(t * memory_length, memory_length), :]
        memory_copies.append(pltpu.make_async_copy(source, kv_v.at[t // 2, t % 2], ring_sems.at[1 + t // 2, t % 2]))
        memory_copies[-1].start()
    for t in range(max(0, targets - 2), targets):
        stores.wait(("dv2", t))
    loads.wait("h2", "cq", "x1")
    inner_grad(4, norm_v, dq)
    loads.start("h1", h1, norm_v)

    for cols in column_tiles(width):
        du[:, cols] = dot_nt(dq[...], weights_v[1, cols, :])
    loads.start("wk", wk, weights_v.at[1])
    running.tick(2.5)
    back_through(x1_v, 1, dx, dx)
    running.tick(1.5)
    loads.wait("c1", "wo")
    inner_grad(3, ctx_v, do)
    out_back(2, dctx1)
    loads.start("wv", wv, weights_v.at[2])
    running.tick(2.5)
    for copy in ret_copies:
        copy.wait()
    loads.wait("ret")

    def output_columns(cols, values):
        dk[:, cols] = (x2_v[:, cols] + values).astype(BF16)

    collect(place_column, ret_v, output_columns)
    stores.start("output", dk, output_out)
    running.tick(2.0)
    loads.wait("p1", "q1", "k1", "v1")
    stores.wait("output")
    for t in range(targets):
        r = slice(t * length, (t + 1) * length)
        allowed = allowed_of(mask[t : t + 1, :], length)
        for pair in range(pairs):
            lanes = slice(pair * LANES, (pair + 1) * LANES)
            side = pair % 2
            grad_rows = stacked(dctx1[r, lanes], low, high)
            both = dot_nt(grad_rows, v1_v[r, lanes])
            scratch = p2_v.at[1, side]
            for half in range(2):
                part = slice(half * length, (half + 1) * length)
                prob = p1_v[t, pair, part, :].astype(F32)
                dprob = both[part]
                inner = jnp.sum(prob * dprob, axis=-1, keepdims=True)
                score = jnp.where(allowed, prob * (dprob - inner), 0.0).astype(BF16)
                scratch[part, :length] = score
                wide_score = score.astype(F32)
                dsum[pair, part, :] = wide_score if t == 0 else dsum[pair, part, :] + wide_score
            dv[r, lanes] = dot_tn(p1_v[t, pair], grad_rows).astype(BF16)
            dk[r, lanes] = dot_tn(scratch[:, :length], stacked(q1_v[r, lanes], low, high)).astype(BF16)
            back = dot(scratch[:, :length], k1_v[r, lanes])
            dq[r, lanes] = jnp.where(low_lane, back[:length], back[length:]).astype(BF16)
        running.tick(2.5)
    loads.wait("h1", "wq", "wk", "wv", "tokens")
    running.finish(expert_sums)
    for index, right in enumerate((dq, dk, dv)):
        inner_grad(index, norm_v, right)
        running.tick(1.2)
    loads.start("dv2", dv2_out, dv2)

    for t in range(targets):
        r = slice(t * length, (t + 1) * length)
        m = slice(t * memory_length, (t + 1) * memory_length)
        for pair in range(pairs):
            lanes = slice(pair * LANES, (pair + 1) * LANES)
            dk2[m, lanes] = dot_tn(ds[t, pair], stacked(q2_v[r, lanes], low, high)).astype(BF16)
        running.tick(1.2)
    for copy in memory_copies:
        copy.wait()
    for c in range(width // 256):
        cols = slice(c * 256, (c + 1) * 256)
        total = 0.0
        for t in range(targets):
            m = slice(t * memory_length, (t + 1) * memory_length)
            total = total + dot_tn(kv_v[t // 2, t % 2, :, cols], dk2[m, :])
        grads[5, cols, :] = total.astype(BF16)
        running.tick(1.3)
    total_of(5)

    for cols in column_tiles(width):
        du[:, cols] = (
            dot_nt(dq[...], weights_v[0, cols, :]) + dot_nt(dk[...], weights_v[1, cols, :]) + dot_nt(dv[...], weights_v[2, cols, :])
        )
    running.tick(2.5)
    back_through(first_v, 0, dx, dx)
    stores.start("tokens", dx, grad_tokens_out)
    running.tick(1.5)
    small[...] = jnp.zeros_like(small)
    for i in range(3):
        small[i : i + 1, :] = jnp.sum(gain_acc[i], axis=0, keepdims=True)
    small[8:16, :] = grad_router[0:8, :]
    table_v[...] = jnp.zeros_like(table_v)

    def table_rows(b, carry):
        hit = buckets[...] == b
        for head in range(heads):
            start = (head % 2) * length
            part = jnp.where(hit, dsum[head // 2, start : start + length, :], 0.0)
            table_v[pl.ds(head, 1), :] = jnp.sum(part, axis=0, keepdims=True)
        sums = jnp.sum(table_v[0:16, :], axis=-1, keepdims=True)
        here = lax.broadcasted_iota(jnp.int32, (1, LANES), 1) == b
        table_v[16:32, :] += jnp.where(here, sums, 0.0)
        return carry

    for b in range(0, 32, 16):
        lax.fori_loop(b, b + 16, table_rows, 0)
        running.tick(2.0)
    small[16:24, 0:LANES] = table_v[16:24, :]
    small[16:24, LANES : 2 * LANES] = table_v[24:32, :]
    if remote:
        running.add(reduce_small(ring, small, small_land))
    loads.wait("ck", "cv", "dv2")
    for t in range(targets):
        buffer = spare[t % 2]
        if t >= 2:
            stores.wait(("memory", t - 2))
        m = slice(t * memory_length, (t + 1) * memory_length)
        for cols in column_tiles(width):
            buffer[:, cols] = (dot_nt(dk2[m, :], weights_v[3, cols, :]) + dot_nt(dv2[m, :], weights_v[4, cols, :])).astype(BF16)
            running.tick(0.8)
        stores.start(("memory", t), buffer, grad_memory_out.at[pl.ds(t * memory_length, memory_length), :])
    running.drain()
    stores.drain()


def finish_kernel(*refs):
    sources, small, targets, table, routed, gain_refs = refs[:13], refs[13], refs[14:27], refs[27], refs[28], refs[29:32]
    narrow, wide, parts, first, second, *passed, in_sems, out_sems = refs[32:]
    loads, stores = Loads(in_sems), Loads(out_sems)
    for i in range(8):
        loads.start(i, sources[i], narrow.at[i])
    for i in range(2):
        loads.start(8 + i, sources[8 + i], parts.at[i])
    for i in range(10, 13):
        loads.start(i, sources[i], passed[i - 10])
    for i in range(8):
        loads.wait(i)

        def widen(r, i=i):
            wide[i, r, :] = narrow[i, r, :].astype(F32)

        row_loop(wide.shape[1], 64, widen)
        stores.start(i, wide.at[i], targets[i])
    loads.wait(8, 9)

    def widen_part(r):
        first[r, :] = parts[0, r, :].astype(F32)

    row_loop(first.shape[0], 64, widen_part)
    stores.start(8, first, targets[8])
    for c in range(0, first.shape[0], LANES):
        second[:, c : c + LANES] = parts[1, c : c + LANES, :].astype(F32).T
    stores.start(9, second, targets[9])
    heads, count = table.shape
    table[0:8, :] = small[16:24, 0:count]
    table[8:heads, :] = small[16 : 16 + heads - 8, LANES : LANES + count]
    routed[...] = small[8 : 8 + routed.shape[0], :]
    for i, ref in enumerate(gain_refs):
        ref[...] = small[i : i + 1, :].reshape(-1)
    for i in range(10, 13):
        loads.wait(i)
        stores.start(i, passed[i - 10], targets[i])
    stores.drain()


def params(**more):
    return pltpu.CompilerParams(vmem_limit_bytes=VMEM_LIMIT, **more)


def on_device(
    tokens, memory, target_mask, buckets, expert_ids, slots, gain_self, w_query, w_key, w_value, w_output, rel_table, gain_cross,
    c_query, c_key, c_value, c_output, gain_moe, router, expert_in, expert_out, cotangent,
):
    rows, width = tokens.shape
    targets, length = target_mask.shape
    bucket_count, heads = rel_table.shape
    memory_length = memory.shape[0] // targets
    pairs = heads // 2
    experts = lax.axis_size("expert")
    hidden = expert_in.shape[2]
    capacity = (5 * rows + 4 * experts - 1) // (4 * experts)
    slot_rows = experts * capacity
    place = jnp.where(slots < capacity, expert_ids * capacity + slots, -1)
    place_row, place_column = place.reshape(1, rows), place.reshape(rows, 1)
    gains = [gain_self, gain_cross, gain_moe]
    weights = (w_query, w_key, w_value, w_output, c_query, c_key, c_value, c_output)

    remote = lax.axis_size("dp") == 8 and experts == 4 and hidden == 4 * width

    def exchange(buffer):
        if remote:
            return buffer
        buffer = buffer.reshape(experts, capacity, width)
        return lax.all_to_all(buffer, "expert", split_axis=0, concat_axis=0, tiled=True).reshape(slot_rows, width)

    def remote_params(collective_id):
        return params(collective_id=collective_id, has_side_effects=True) if remote else params()

    row_shape = jax.ShapeDtypeStruct((slot_rows, width), BF16)
    act_shape = ((rows, width), BF16)
    wide_shape = ((rows, width), F32)
    key_shape = ((targets * memory_length, width), BF16)
    kept = (
        [act_shape] * 8
        + [wide_shape] * 2
        + [((targets, pairs, 2 * length, length), BF16), ((targets, pairs, 2 * length, memory_length), BF16), key_shape, key_shape]
        + [((slot_rows, width), BF16)] * 2
    )
    h1, q1, k1, v1, c1, h2, q2, c2, x1, x2, p1, p2, k2, v2, sent, grows = pl.pallas_call(
        functools.partial(forward_kernel, targets, length, memory_length, heads, remote),
        out_shape=[jax.ShapeDtypeStruct(*k) for k in kept],
        in_specs=[VMEM, ANY, ANY, VMEM, VMEM, VMEM, VMEM, VMEM, VMEM, ANY] + [ANY] * 8,
        out_specs=[ANY] * len(kept),
        scratch_shapes=[pltpu.VMEM((rows, width), BF16), pltpu.VMEM(*key_shape), pltpu.VMEM((8, width, width), BF16)]
        + [pltpu.VMEM(*k) for k in kept]
        + [
            pltpu.VMEM((pairs, 2 * length, length), F32),
            pltpu.VMEM((heads * bucket_count, length), F32),
            pltpu.VMEM((2, 2 * length, memory_length), F32),
            pltpu.SemaphoreType.DMA((11,)),
            pltpu.SemaphoreType.DMA((len(kept),)),
            pltpu.SemaphoreType.DMA((experts - 1,)),
            pltpu.SemaphoreType.DMA((experts - 1,)),
        ],
        compiler_params=remote_params(1),
        name="forward",
    )(rel_table.T, tokens, memory, target_mask, buckets, *gains, place_row, cotangent, *weights)

    sent, grows = exchange(sent), exchange(grows)
    tiles = hidden // width
    half = width // 2
    weight_grad = jax.ShapeDtypeStruct((3, width, half) if remote else (width, hidden), BF16)
    row_scratch, half_scratch = pltpu.VMEM((slot_rows, width), BF16), pltpu.VMEM((slot_rows // 2, width), F32)
    ret, dh, grad_first, grad_second, grad_router = pl.pallas_call(
        functools.partial(expert_kernel, experts, remote),
        out_shape=[row_shape, row_shape, weight_grad, weight_grad, jax.ShapeDtypeStruct((8, width), F32)],
        in_specs=[ANY, ANY, VMEM, ANY, ANY],
        out_specs=[ANY, ANY, ANY, ANY, VMEM],
        scratch_shapes=[
            pltpu.VMEM((LANES, width), BF16),
            pltpu.VMEM((width, LANES), BF16),
            pltpu.VMEM((LANES, width), F32),
            pltpu.VMEM((width, hidden), BF16),
            pltpu.VMEM((hidden, width), BF16),
            row_scratch,
            row_scratch,
            pltpu.VMEM((width, slot_rows), BF16),
            row_scratch,
            pltpu.VMEM((width, slot_rows), BF16),
            pltpu.VMEM((slot_rows, LANES), F32),
            half_scratch,
            half_scratch,
            pltpu.VMEM((slot_rows, hidden), BF16),
            pltpu.VMEM((slot_rows, hidden), BF16),
            half_scratch,
            half_scratch,
            row_scratch,
            row_scratch,
            pltpu.VMEM((2, 2, tiles, width, half), BF16),
            pltpu.VMEM((2, tiles, width, half), BF16),
            pltpu.VMEM((2, width, half), BF16),
            pltpu.SemaphoreType.DMA((2 * tiles + 2,)),
            pltpu.SemaphoreType.DMA((4 * tiles + 2,)),
            pltpu.SemaphoreType.DMA((2 * experts + 2 * tiles,)),
            pltpu.SemaphoreType.DMA((2 * experts + 2 * tiles,)),
        ],
        compiler_params=remote_params(2),
        name="experts",
    )(sent, grows, router.T, expert_in[0], expert_out[0])
    dh_rows, ret_rows = exchange(dh), exchange(ret)
    parts = (grad_first, grad_second)
    if not remote:
        parts = (ret, ret)

    square = (width, width)
    wide = pltpu.VMEM(*wide_shape)
    small_shape = (24, width)
    lands = 8 if remote else 1
    copies = 8 * (6 + 2 * (experts - 1)) + 2 * experts + 1 + 4
    block = jax.ShapeDtypeStruct((width, half), BF16)
    results = pl.pallas_call(
        functools.partial(backward_kernel, targets, length, memory_length, heads, remote),
        out_shape=[jax.ShapeDtypeStruct(square, BF16)] * 8
        + [
            jax.ShapeDtypeStruct((rows, width), BF16),
            jax.ShapeDtypeStruct((rows, width), F32),
            jax.ShapeDtypeStruct(memory.shape, BF16),
            jax.ShapeDtypeStruct(memory.shape, BF16),
            block,
            block,
            jax.ShapeDtypeStruct(small_shape, F32),
        ],
        in_specs=[ANY, ANY] + [VMEM] * 7 + [ANY] * 27,
        out_specs=[ANY] * 14 + [VMEM],
        scratch_shapes=[pltpu.VMEM((slot_rows, width), BF16)] * 2
        + [
            pltpu.VMEM((14 * rows, width), BF16),
            wide,
            pltpu.VMEM((targets, pairs, 2 * length, length), BF16),
            pltpu.VMEM((5,) + square, BF16),
            pltpu.VMEM((2, pairs, 2 * length, memory_length), BF16),
            pltpu.VMEM((2, 2, memory_length, width), BF16),
            pltpu.VMEM((3 * rows, width), F32),
            pltpu.VMEM((8,) + square, BF16),
            pltpu.VMEM((2, 2 * length, memory_length), F32),
            pltpu.VMEM((targets, pairs, 2 * length, memory_length), BF16),
            pltpu.VMEM((pairs, 2 * length, length), F32),
            pltpu.VMEM((3, 8, width), F32),
            pltpu.VMEM((32, LANES), F32),
            pltpu.VMEM((lands, width, half), BF16),
            pltpu.VMEM((lands, width - width // (4 * experts), half), BF16),
            pltpu.VMEM((experts + 3,) + small_shape, F32),
            pltpu.SemaphoreType.DMA((24,)),
            pltpu.SemaphoreType.DMA((28,)),
            pltpu.SemaphoreType.DMA((4, 2)),
            pltpu.SemaphoreType.DMA((copies,)),
            pltpu.SemaphoreType.DMA((copies,)),
            pltpu.SemaphoreType.DMA((2, 3)),
            pltpu.SemaphoreType.REGULAR((8,)),
        ],
        compiler_params=remote_params(0),
        name="backward",
    )(
        dh_rows, ret_rows, place_column, target_mask, buckets, *gains, grad_router, cotangent, tokens, h1, q1, k1, v1, c1, h2, q2, c2, x1, x2,
        p1, p2, k2, v2, memory, *weights, *parts,
    )
    summed, (output, grad_tokens, grad_memory, _, grad_first_sum, grad_second_sum), small = results[:8], results[8:14], results[-1]
    if not remote:
        summed, small = lax.psum((summed, small), ("dp", "expert"))
        grad_first_sum, grad_second_sum = (
            lax.psum_scatter(g, "dp", scatter_dimension=1, tiled=True) for g in (grad_first, grad_second)
        )
    wide_square = jax.ShapeDtypeStruct(square, F32)
    part_shape = grad_first_sum.shape
    finished = pl.pallas_call(
        finish_kernel,
        out_shape=[wide_square] * 8
        + [
            jax.ShapeDtypeStruct(part_shape, F32),
            jax.ShapeDtypeStruct(part_shape[::-1], F32),
            jax.ShapeDtypeStruct(output.shape, BF16),
            jax.ShapeDtypeStruct(grad_tokens.shape, F32),
            jax.ShapeDtypeStruct(grad_memory.shape, BF16),
            jax.ShapeDtypeStruct((heads, bucket_count), F32),
            jax.ShapeDtypeStruct((experts, width), F32),
        ]
        + [jax.ShapeDtypeStruct((width,), F32)] * 3,
        in_specs=[ANY] * 13 + [VMEM],
        out_specs=[ANY] * 8 + [ANY] * 5 + [VMEM] * 5,
        scratch_shapes=[
            pltpu.VMEM((8,) + square, BF16),
            pltpu.VMEM((8,) + square, F32),
            pltpu.VMEM((2,) + part_shape, BF16),
            pltpu.VMEM(part_shape, F32),
            pltpu.VMEM(part_shape[::-1], F32),
            pltpu.VMEM(output.shape, BF16),
            pltpu.VMEM(grad_tokens.shape, F32),
            pltpu.VMEM(grad_memory.shape, BF16),
            pltpu.SemaphoreType.DMA((13,)),
            pltpu.SemaphoreType.DMA((13,)),
        ],
        compiler_params=params(),
        name="finish",
    )(*summed, grad_first_sum, grad_second_sum, output, grad_tokens, grad_memory, small)
    wq_grad, wk_grad, wv_grad, wo_grad, cq_grad, ck_grad, cv_grad, co_grad, first, second, output, grad_tokens, grad_memory, table, routed, *gain_grads = finished
    return (
        output, grad_tokens, grad_memory, gain_grads[0], wq_grad, wk_grad, wv_grad, wo_grad, table.T, gain_grads[1], cq_grad, ck_grad, cv_grad,
        co_grad, gain_grads[2], routed.T, first[None], second[None],
    )


def solution(mesh):
    both, spread = P(("dp", "expert")), P(("dp", "expert"), None)
    placed = (
        (spread, spread, spread, P(), both, both) + (P(),) * 13 + (P("expert", None, None), P("expert", None, None), spread)
    )
    return jax.shard_map(
        on_device,
        mesh=mesh,
        in_specs=placed,
        out_specs=(spread, spread, spread) + (P(),) * 13 + (P("expert", None, "dp"), P("expert", "dp", None)),
        check_vma=False,
    )
```

```python
import functools

import jax
import jax.numpy as jnp
from jax import lax
from jax.experimental import pallas as pl
from jax.experimental.pallas import tpu as pltpu
from jax.sharding import PartitionSpec as P

EPS = 1e-06
NEG = -1000000000.0
F32 = jnp.float32
BF16 = jnp.bfloat16
LANES = 128
VMEM_LIMIT = 63_400_000
ANY = pl.BlockSpec(memory_space=pl.ANY)
VMEM = pl.BlockSpec(memory_space=pltpu.VMEM)
SMEM = pl.BlockSpec(memory_space=pltpu.SMEM)


def dot(left, right):
    return lax.dot_general(left, right, (((1,), (0,)), ((), ())), preferred_element_type=F32)


def dot_nt(left, right):
    return lax.dot_general(left, right, (((1,), (1,)), ((), ())), preferred_element_type=F32)


def dot_tn(left, right):
    return lax.dot_general(left, right, (((0,), (0,)), ((), ())), preferred_element_type=F32)


def column_tiles(width, step=256):
    return [slice(c, c + step) for c in range(0, width, step)]


def row_loop(count, step, body):
    def one(i, carry):
        body(pl.ds(pl.multiple_of(i * step, step), step))
        return carry

    lax.fori_loop(0, count // step, one, 0)


def half_masks():
    lane = lax.broadcasted_iota(jnp.int32, (1, LANES), 1)
    low = jnp.where(lane < LANES // 2, 1.0, 0.0).astype(BF16)
    high = jnp.where(lane < LANES // 2, 0.0, 1.0).astype(BF16)
    return lane < LANES // 2, low, high


def stacked(pair, low, high):
    return jnp.concatenate([pair * low, pair * high], axis=0)


def norm_rows(values, gain):
    return values * lax.rsqrt(jnp.mean(values * values, axis=-1, keepdims=True) + EPS) * gain


def norm_back(values, gain, grad):
    scale = lax.rsqrt(jnp.mean(values * values, axis=-1, keepdims=True) + EPS)
    scaled = grad * gain
    inner = jnp.mean(scaled * values, axis=-1, keepdims=True)
    back = scale * scaled - values * (scale * scale * scale * inner)
    gain_rows = grad * values * scale
    return back, jnp.sum(gain_rows.reshape(-1, 8, gain_rows.shape[-1]), axis=0)


def allowed_of(mask_row, length):
    row = lax.broadcasted_iota(jnp.int32, (length, length), 0)
    col = lax.broadcasted_iota(jnp.int32, (length, length), 1)
    return (col <= row) & (mask_row == 1)


class Loads:
    def __init__(self, sems):
        self.sems = sems
        self.count = 0
        self.open = {}

    def start(self, name, source, target):
        copy = pltpu.make_async_copy(source, target, self.sems.at[self.count])
        self.count += 1
        copy.start()
        self.open[name] = copy

    def wait(self, *names):
        for name in names:
            self.open.pop(name).wait()

    def drain(self):
        self.wait(*list(self.open))


class Ring:
    def __init__(self, send_sems, recv_sems):
        self.send_sems, self.recv_sems = send_sems, recv_sems
        self.count = 0
        dp, self.expert = lax.axis_index("dp"), lax.axis_index("expert")
        self.experts = lax.axis_size("expert")
        self.dp = dp
        self.spot = {"core": lax.rem(dp, 2), "x": lax.rem(lax.div(dp, 2), 2), "y": lax.div(dp, 4)}
        self.partner = {name: dp + step - 2 * step * self.spot[name] for name, step in (("core", 1), ("x", 2), ("y", 4))}

        low, high = lax.rem(self.expert, 2), lax.div(self.expert, 2)
        near, far = 1 - 2 * low, 2 - 4 * high
        self.peers = [self.expert, self.expert + near, self.expert + far, self.expert + near + far]

    def others(self):
        return self.peers[1:]

    def block(self, expert, capacity):
        return pl.ds(pl.multiple_of(expert * capacity, 16), capacity)

    def slot(self, k, capacity, sender=None):
        low = lax.rem(self.expert if sender is None else sender, 2)
        return pl.ds(pl.multiple_of((low + (2 if k >= 2 else 0)) * capacity, 16), capacity)

    def scatter(self, source, target):
        capacity = source.shape[0] // self.experts
        return [
            self.send(source.at[self.block(e, capacity), :], target.at[self.slot(k, capacity), :], self.dp, e)
            for k, e in enumerate(self.peers)
            if k
        ]

    def greet(self, names):
        barrier = pltpu.get_barrier_semaphore()
        targets = [(self.partner[name], self.expert) for name in names] + [(self.dp, e) for e in self.others()]
        for target in targets:
            pl.semaphore_signal(barrier, inc=1, device_id=target, device_id_type=pl.DeviceIdType.MESH)
        pl.semaphore_wait(barrier, len(targets))

    def send(self, source, target, dp, expert):
        copy = pltpu.make_async_remote_copy(
            src_ref=source, dst_ref=target, send_sem=self.send_sems.at[self.count], recv_sem=self.recv_sems.at[self.count],
            device_id=(dp, expert), device_id_type=pl.DeviceIdType.MESH,
        )
        self.count += 1
        copy.start()
        return copy

    def cross(self, name, source, target):
        return self.send(source, target, self.partner[name], self.expert)


def forward_kernel(
    targets, length, memory_length, heads, remote,
    table, tokens, memory, mask, buckets, gain_one, gain_two, gain_three, place, cotangent, wq, wk, wv, wo, cq, ck, cv, co,
    h1_out, q1_out, k1_out, v1_out, c1_out, h2_out, q2_out, c2_out, x1_out, x2_out, p1_out, p2_out, k2_out, v2_out, sent_out, grows_out,
    tokens_v, memory_v, weights_v, h1, q1, k1, v1, c1, h2, q2, c2, x1, x2, p1, p2, k2, v2, sent, gsent, bias, spread, scores, in_sems, out_sems,
    send_sems, recv_sems,
):
    rows, width = tokens_v.shape
    pairs = heads // 2
    loads, stores = Loads(in_sems), Loads(out_sems)
    loads.start("cot", cotangent, c2)
    loads.start("tokens", tokens, tokens_v)
    for index, (name, ref) in enumerate(zip(("wq", "wk", "wv"), (wq, wk, wv))):
        loads.start(name, ref, weights_v.at[index])
    loads.start("ck", ck, weights_v.at[5])
    loads.start("memory", memory, memory_v)
    loads.start("cv", cv, weights_v.at[6])
    loads.start("wo", wo, weights_v.at[3])
    loads.start("cq", cq, weights_v.at[4])
    loads.start("co", co, weights_v.at[7])
    gain = [g[...].astype(F32).reshape(1, -1) for g in (gain_one, gain_two, gain_three)]
    low_lane, low, high = half_masks()

    if remote:
        ring = Ring(send_sems, recv_sems)
        ring.greet(())
    loads.wait("cot")
    dispatch(place, c2, gsent)
    gsent_copies = []
    if remote:
        gsent_copies = ring.scatter(gsent, grows_out)
        block = ring.block(ring.expert, sent.shape[0] // ring.experts)
        stores.start("grows", gsent.at[block, :], grows_out.at[ring.slot(0, sent.shape[0] // ring.experts), :])
    else:
        stores.start("grows", gsent, grows_out)
    bucket_count = table.shape[1]
    by_head = table[...].astype(F32)
    for head in range(heads):
        row = jnp.broadcast_to(by_head[head : head + 1, :], (LANES, bucket_count))
        spread[head * bucket_count : (head + 1) * bucket_count, :] = row.T

    def bias_rows(r):
        here = buckets[r, :]
        hits = [here == b for b in range(bucket_count)]
        for head in range(heads):
            total = jnp.zeros(here.shape, F32)
            for b in range(bucket_count):
                at = head * bucket_count + b
                total = jnp.where(hits[b], spread[at : at + 1, :], total)
            start = (head % 2) * length
            bias[head // 2, pl.ds(pl.multiple_of(r.start + start, 8), r.size), :] = total

    row_loop(length, 16, bias_rows)

    loads.wait("tokens")

    def first_norm(r):
        h1[r, :] = norm_rows(tokens_v[r, :].astype(F32), gain[0]).astype(BF16)

    row_loop(rows, 32, first_norm)
    stores.start("h1", h1, h1_out)
    for index, (name, ref) in enumerate(zip(("wq", "wk", "wv"), (q1, k1, v1))):
        loads.wait(name)

        for cols in column_tiles(width):
            ref[:, cols] = dot(h1[...], weights_v[index, :, cols]).astype(BF16)
    stores.start("q1", q1, q1_out)
    stores.start("k1", k1, k1_out)
    stores.start("v1", v1, v1_out)

    def self_target(t, carry):
        r = pl.ds(pl.multiple_of(t * length, length), length)
        allowed = allowed_of(mask[pl.ds(t, 1), :], length)
        for pair in range(pairs):
            lanes = slice(pair * LANES, (pair + 1) * LANES)
            both = dot_nt(stacked(q1[r, lanes], low, high), k1[r, lanes])
            for half in range(2):
                part = slice(half * length, (half + 1) * length)
                score = jnp.where(allowed, both[part] + bias[pair, part, :], NEG)
                expo = jnp.exp(score - jnp.max(score, axis=-1, keepdims=True))
                total = jnp.sum(expo, axis=-1, keepdims=True)
                p1[t, pair, part, :] = (expo * (1.0 / total)).astype(BF16)
            context = dot(p1[t, pair], v1[r, lanes])
            c1[r, lanes] = jnp.where(low_lane, context[:length], context[length:]).astype(BF16)
        return carry

    lax.fori_loop(0, targets, self_target, 0)
    stores.start("p1", p1, p1_out)
    stores.start("c1", c1, c1_out)
    loads.wait("wo")

    for cols in column_tiles(width):
        x1[:, cols] = tokens_v[:, cols].astype(F32) + dot(c1[...], weights_v[3, :, cols])
    stores.start("x1", x1, x1_out)

    def second_norm(r):
        h2[r, :] = norm_rows(x1[r, :], gain[1]).astype(BF16)

    row_loop(rows, 32, second_norm)
    stores.start("h2", h2, h2_out)
    loads.wait("cq")

    for cols in column_tiles(width):
        q2[:, cols] = dot(h2[...], weights_v[4, :, cols]).astype(BF16)
    stores.start("q2", q2, q2_out)
    loads.wait("memory", "ck", "cv")

    def cross_keys(r):
        for cols in column_tiles(width):
            k2[r, cols] = dot(memory_v[r, :], weights_v[5, :, cols]).astype(BF16)
            v2[r, cols] = dot(memory_v[r, :], weights_v[6, :, cols]).astype(BF16)

    row_loop(targets * memory_length, memory_length, cross_keys)
    stores.start("k2", k2, k2_out)
    stores.start("v2", v2, v2_out)

    def cross_target(t, carry):
        r = pl.ds(pl.multiple_of(t * length, length), length)
        m = pl.ds(pl.multiple_of(t * memory_length, memory_length), memory_length)
        for pair in range(pairs):
            lanes = slice(pair * LANES, (pair + 1) * LANES)
            slot = pair % 2
            scores[slot] = dot_nt(stacked(q2[r, lanes], low, high), k2[m, lanes])
            for chunk in range(2 * length // 32):
                part = slice(chunk * 32, (chunk + 1) * 32)
                score = scores[slot, part, :]
                expo = jnp.exp(score - jnp.max(score, axis=-1, keepdims=True))
                total = jnp.sum(expo, axis=-1, keepdims=True)
                p2[t, pair, part, :] = (expo * (1.0 / total)).astype(BF16)
            context = dot(p2[t, pair], v2[m, lanes])
            c2[r, lanes] = jnp.where(low_lane, context[:length], context[length:]).astype(BF16)
        return carry

    lax.fori_loop(0, targets, cross_target, 0)
    stores.start("p2", p2, p2_out)
    stores.start("c2", c2, c2_out)
    loads.wait("co")

    for cols in column_tiles(width):
        x2[:, cols] = x1[:, cols] + dot(c2[...], weights_v[7, :, cols])
    stores.start("x2", x2, x2_out)

    def third_norm(r):
        tokens_v[r, :] = norm_rows(x2[r, :], gain[2]).astype(BF16)

    row_loop(rows, 32, third_norm)
    dispatch(place, tokens_v, sent)
    stores.start("sent", sent, sent_out)
    for copy in gsent_copies:
        copy.wait()
    stores.drain()


def dispatch(place, source, target):
    step = target.shape[0] // 2

    def one(r):
        spot = lax.broadcasted_iota(jnp.int32, (step, source.shape[0]), 0) + r.start
        hit = jnp.where(spot == place[...], 1.0, 0.0).astype(BF16)
        for cols in column_tiles(source.shape[1]):
            target[r, cols] = dot(hit, source[:, cols]).astype(target.dtype)

    row_loop(target.shape[0], step, one)


def collect(place_column, source, put):
    spot = lax.broadcasted_iota(jnp.int32, (place_column.shape[0], source.shape[0]), 1)
    hit = jnp.where(spot == place_column[...], 1.0, 0.0).astype(BF16)
    for cols in column_tiles(source.shape[1]):
        put(cols, dot(hit, source[:, cols]))


class ExpertSum:
    def __init__(self, ring, running, tiles, core_land, near_land, first, result, stores):
        self.ring, self.running, self.tiles, self.first = ring, running, tiles, first
        self.core_land, self.near_land = core_land, near_land
        self.result, self.stores = result, stores
        self.order = (0, 1, 2, 3) if first == "x" else (0, 2, 1, 3)
        self.ready, self.started = set(), False
        self.place = (lambda one, two: one + 2 * two) if first == "x" else (lambda one, two: 2 * one + two)

    def add(self, tile, other):
        core = self.ring.spot["core"]

        def rows(r):
            total = self.tiles[core, tile, r, :].astype(F32) + other[r, :].astype(F32)
            self.tiles[core, tile, r, :] = total.astype(BF16)

        row_loop(self.tiles.shape[2], 64, rows)

    def start(self, tile):
        self.running.add(self.between_cores(tile))

    def between_cores(self, tile):
        core = self.ring.spot["core"]
        copy = self.ring.cross("core", self.tiles.at[1 - core, tile], self.core_land.at[tile])
        yield link_time("core", *self.tiles.shape[2:])
        copy.wait()
        self.add(tile, self.core_land.at[tile])
        self.ready.add(tile)
        if {self.place(0, 0), self.place(1, 0)} <= self.ready and not self.started:
            self.started = True
            self.running.add(self.near())
        if {self.place(0, 1), self.place(1, 1)} <= self.ready:
            spot = self.ring.spot[self.first]
            self.keep(1, self.place(spot, 1))
            self.keep(2, self.place(1 - spot, 1))

    def near(self):
        spot = self.ring.spot[self.first]
        source = self.tiles.at[self.ring.spot["core"], self.place(1 - spot, 0)]
        copy = self.ring.cross(self.first, source, self.near_land)
        yield link_time(self.first, *self.tiles.shape[2:])
        copy.wait()
        self.keep(0, self.place(spot, 0), self.near_land)

    def keep(self, index, tile, other=None):
        if other is not None:
            self.add(tile, other)
        source = self.tiles.at[self.ring.spot["core"], tile]
        self.stores.start(("sum", self.first, index), source, self.result.at[index])


def expert_kernel(
    experts, remote, inbound, grows, router_rows, first, second,
    ret_out, dh_out, grad_first, grad_second, grad_router,
    router, router_turned, router_sum, first_v, second_v, inbound_v, grows_v, inbound_t, dret, dret_t, probs, pre, dact, act, dpre, ret, dinb, ret_v, dh_v, sums, core_land, near_land,
    in_sems, out_sems, send_sems, recv_sems,
):
    rows, width = inbound_v.shape
    hidden = first.shape[1]
    step = width
    tiles = hidden // step
    loads, stores = Loads(in_sems), Loads(out_sems)
    capacity = rows // experts
    half_rows = rows // 2
    if remote:
        ring = Ring(send_sems, recv_sems)
        ring.greet(("core", "x", "y"))
        arriving = ring.scatter(inbound, inbound_v)
        loads.start("inbound", inbound.at[ring.block(ring.expert, capacity), :], inbound_v.at[ring.slot(0, capacity), :])
    else:
        loads.start("inbound", inbound, inbound_v)
        arriving = []
    loads.start("grows", grows, grows_v)
    for f in range(tiles):
        cols = slice(f * step, (f + 1) * step)
        loads.start(("first", f), first.at[:, cols], first_v.at[:, cols])
        loads.start(("second", f), second.at[cols, :], second_v.at[cols, :])
    me = lax.axis_index("expert")
    lane = lax.broadcasted_iota(jnp.int32, (1, LANES), 1)
    mine = lane == me
    root = (2.0 / jnp.pi) ** 0.5
    router_sum[...] = jnp.zeros_like(router_sum)
    router[...] = jnp.zeros_like(router)
    router[0:experts, :] = router_rows[...]
    for cols in column_tiles(width, LANES):
        router_turned[cols, :] = router[:, cols].T
    loads.wait("inbound", "grows")
    returning = []
    for side in range(2):
        start = side * half_rows
        here = slice(start, start + half_rows)
        for copy in (arriving[:1], arriving[1:])[side]:
            copy.wait_recv()

        def route(r, start=start):
            r = pl.ds(pl.multiple_of(start + r.start, 16), r.size)
            logits = jnp.where(lane < experts, dot(inbound_v[r, :], router_turned[...]), -1e30)
            expo = jnp.exp(logits - jnp.max(logits, axis=-1, keepdims=True))
            prob = expo / jnp.sum(expo, axis=-1, keepdims=True)
            probs[r, :] = prob
            gate = jnp.sum(jnp.where(mine, prob, 0.0), axis=-1, keepdims=True)
            dret[r, :] = (gate * grows_v[r, :].astype(F32)).astype(BF16)

        row_loop(half_rows, half_rows // 2, route)
        for f in range(tiles):
            cols = slice(f * step, (f + 1) * step)
            if side == 0:
                loads.wait(("first", f), ("second", f))
            for c in range(0, step, 256):
                tile = slice(f * step + c, f * step + c + 256)
                pre[:, c : c + 256] = dot(inbound_v[here, :], first_v[:, tile])
                dact[:, c : c + 256] = dot_nt(dret[here, :], second_v[tile, :])

            def middle(r, start=start, cols=cols):
                u = pre[r, :]
                square = u * u
                t = jnp.tanh(u * (root + (root * 0.044715) * square))
                half = 0.5 + 0.5 * t
                out = pl.ds(pl.multiple_of(start + r.start, 16), r.size)
                act[out, cols] = (u * half).astype(BF16)
                slope = half + (u * (0.5 * root + (1.5 * root * 0.044715) * square)) * (1.0 - t * t)
                dpre[out, cols] = (dact[r, :] * slope).astype(BF16)

            row_loop(half_rows, 16, middle)
            for c in range(0, width, 256):
                tile = slice(c, c + 256)
                one, two = dot(act[here, cols], second_v[cols, tile]), dot_nt(dpre[here, cols], first_v[tile, cols])
                if f:
                    one, two = one + ret[:, tile], two + dinb[:, tile]
                ret[:, tile] = one
                dinb[:, tile] = two

        def finish(r, start=start):
            out = pl.ds(pl.multiple_of(start + r.start, 16), r.size)
            result = ret[r, :].astype(BF16).astype(F32)
            prob = probs[out, :]
            gate = jnp.sum(jnp.where(mine, prob, 0.0), axis=-1, keepdims=True)
            dgate = jnp.sum(result * grows_v[out, :].astype(F32), axis=-1, keepdims=True)
            dlogits = (prob * (jnp.where(mine, 1.0, 0.0) - gate) * dgate).astype(BF16)
            ret_v[out, :] = (gate * result).astype(BF16)
            dh_v[out, :] = (dinb[r, :].astype(BF16).astype(F32) + dot(dlogits, router[...])).astype(BF16)
            router_sum[...] += dot_tn(dlogits, inbound_v[out, :])

        row_loop(half_rows, half_rows // 2, finish)
        if remote:
            target = dh_out.at[ring.block(ring.expert, capacity), :]
            for k in ((1,), (2, 3))[side]:
                source = dh_v.at[ring.slot(k, capacity, ring.peers[k]), :]
                returning.append(ring.send(source, target, ring.dp, ring.peers[k]))
            if side == 0:
                stores.start("dh", dh_v.at[ring.slot(0, capacity), :], target)
        elif side:
            stores.start("dh", dh_v, dh_out)
    stores.start("ret", ret_v, ret_out)
    grad_router[...] = router_sum[0:8, :]
    for copy in arriving:
        copy.wait_send()
    for c in range(width // LANES):
        cols = slice(c * LANES, (c + 1) * LANES)
        inbound_t[cols, :] = inbound_v[:, cols].T
        dret_t[cols, :] = dret[:, cols].T

    running = Running()
    if remote:
        expert_sums = [
            ExpertSum(ring, running, sums.at[j], core_land.at[j], near_land.at[j], axis, out, stores)
            for j, (axis, out) in enumerate((("x", grad_first), ("y", grad_second)))
        ]
    for i in range(tiles):
        for j, (left, right) in enumerate(((inbound_t, dpre), (dret_t, act))):
            f = expert_sums[j].order[i] if remote else i
            for cols in column_tiles(step):
                total = dot(left[...], right[:, f * step + cols.start : f * step + cols.stop]).astype(BF16)
                for c in range(cols.start, cols.stop, LANES):
                    b, at = divmod(c, step // 2)
                    sums[j, b, f, :, at : at + LANES] = total[:, c - cols.start : c - cols.start + LANES]
            if not remote:
                for b in range(2):
                    cols = slice(f * step + b * (step // 2), f * step + (b + 1) * (step // 2))
                    stores.start(("sum", j, b, f), sums.at[j, b, f], (grad_first, grad_second)[j].at[:, cols])
            running.tick(1.6)
            if remote:
                expert_sums[j].start(f)
    running.drain()
    for copy in returning:
        copy.wait()
    stores.drain()


def span(start, size):
    return pl.ds(pl.multiple_of(start, size), size)


def add_into(ref, rows, lanes, others, target=None):
    step = 48 if rows.size % 64 else 64
    for i in range(rows.size // step):
        here = pl.ds(pl.multiple_of(rows.start + i * step, 16), step)
        total = ref[here, lanes].astype(F32)
        for other in others:
            total = total + other[i * step : (i + 1) * step, :].astype(F32)
        if target is None:
            ref[here, lanes] = total.astype(BF16)
        else:
            target[here, :] = total.astype(BF16)


def reduce_matrix(ring, local, result, core_land, landing, axes, stores, ready):
    size = local.shape[0]
    half = size // 2
    core = ring.spot["core"]
    mine, other = span(core * half, half), span((1 - core) * half, half)
    copy = ring.cross("core", local.at[:, other], core_land)
    yield link_time("core", size, half)
    copy.wait()
    pl.semaphore_signal(ready, inc=1, device_id=(ring.partner["core"], ring.expert), device_id_type=pl.DeviceIdType.MESH)
    add_into(local, pl.ds(0, size), mine, [core_land])
    base, count, row, trail = 0, size, 0, []
    for axis in axes:
        parts = ring.experts if axis == "z" else 2
        part = count // parts
        lands = [landing.at[row + k * part : row + (k + 1) * part, :] for k in range(parts - 1)]
        if axis == "z":
            spot = ring.expert
            copies = [ring.send(local.at[span(base + e * part, part), mine], lands[k], ring.dp, e) for k, e in enumerate(ring.others())]
        else:
            spot = ring.spot[axis]
            copies = [ring.cross(axis, local.at[span(base + (1 - spot) * part, part), mine], lands[0])]
        yield link_time(axis, part, half)
        for copy in copies:
            copy.wait()
        base, count, row = base + spot * part, part, row + (parts - 1) * part
        here = span(base, count)
        add_into(local, here, mine, lands, core_land if axis == axes[-1] else None)
        trail.append((axis, here))
    for axis, here in reversed(trail):
        block = core_land.at[here, :]
        if axis == "z":
            copies = [ring.send(block, block, ring.dp, e) for e in ring.others()]
        else:
            copies = [ring.cross(axis, block, block)]
        yield link_time(axis, here.size, half)
        for copy in copies:
            copy.wait()
    pl.semaphore_wait(ready, 1)
    copy = ring.cross("core", core_land, local.at[:, mine])
    yield link_time("core", size, half)
    copy.wait()
    stores.start(("mine", stores.count), core_land, result.at[:, mine])
    stores.start(("other", stores.count), local.at[:, other], result.at[:, other])


def reduce_expert(ring, part, keep, extra, first, result, sems):
    size, block = part.shape[1], part.shape[2]
    second = "y" if first == "x" else "x"
    cols = [slice(i * block, (i + 1) * block) for i in range(2)]
    copies = [ring.cross(first, part.at[2], extra.at[:, cols[1]])]
    copies += [pltpu.make_async_copy(part.at[i], keep.at[:, cols[i]], sems.at[i]) for i in range(2)]
    for copy in copies[1:]:
        copy.start()
    yield link_time(first, size, block)
    for copy in copies:
        copy.wait()
    add_into(keep, pl.ds(0, size), cols[1], [extra.at[:, cols[1]]])
    spot = ring.spot[second]
    copy = ring.cross(second, keep.at[:, span((1 - spot) * block, block)], extra.at[:, cols[0]])
    yield link_time(second, size, block)
    copy.wait()
    stay = span(spot * block, block)
    add_into(keep, pl.ds(0, size), stay, [extra.at[:, cols[0]]])
    copy = pltpu.make_async_copy(keep.at[:, stay], result, sems.at[2])
    copy.start()
    copy.wait()


def reduce_small(ring, local, landing):
    for k, name in enumerate(("core", "x", "y")):
        copy = ring.cross(name, local, landing.at[k])
        yield link_time(name, *local.shape, 4)
        copy.wait()
        local[...] += landing[k]
    copies = [ring.send(local, landing.at[3 + ring.expert], ring.dp, e) for e in ring.others()]
    landing[3 + ring.expert] = local[...]
    yield link_time("z", *local.shape, 4)
    for copy in copies:
        copy.wait()
    total = landing[3]
    for e in range(1, ring.experts):
        total = total + landing[3 + e]
    local[...] = total


class Running:
    DELAY = 2.0

    def __init__(self):
        self.steps = []
        self.now = 0.0
        self.free = {}

    def land(self, entry, use):
        if use is None:
            self.steps = [e for e in self.steps if e is not entry]
            return
        link, time = use
        self.free[link] = max(self.now, self.free.get(link, 0.0)) + time
        entry[1] = self.free[link] + self.DELAY

    def add(self, steps, rank=0):
        entry = [steps, 0.0, rank]
        self.steps.append(entry)
        self.land(entry, next(steps))

    def advance(self, entry):
        self.now = max(self.now, entry[1]) + 0.3
        entry[2] += 1
        self.land(entry, next(entry[0], None))

    def tick(self, time):
        self.now += time
        while landed := [e for e in self.steps if e[1] <= self.now]:
            self.advance(min(landed, key=lambda e: (e[2], e[1])))

    def finish(self, steps):
        while any(e[0] is s for e in self.steps for s in steps):
            self.advance(min(self.steps, key=lambda e: e[1]))

    def drain(self):
        while self.steps:
            self.advance(min(self.steps, key=lambda e: e[1]))
            self.tick(0.0)


def link_time(name, rows, columns, itemsize=2):
    rate = 0.85 * {"core": 300e3, "x": 50e3, "y": 50e3, "z": 12.5e3}[name]
    return name, rows * columns * itemsize / rate


PLAN = (
    ("xyz", -6), ("xyz", -1), ("zxy", -4), ("yxz", -6), ("yxz", 3), ("yxz", -3), ("xyz", 6), ("yxz", -4),
)


def backward_kernel(
    targets, length, memory_length, heads, remote,
    dh_rows, ret_rows, place_column, mask, buckets, gain_one, gain_two, gain_three, grad_router, cotangent, tokens, h1, q1, k1, v1, c1, h2, q2, c2, x1, x2, p1, p2,
    k2, v2, memory, wq, wk, wv, wo, cq, ck, cv, co, part_first, part_second,
    *rest,
):
    grad_refs, rest = rest[:8], rest[8:]
    (
        output_out, grad_tokens_out, grad_memory_out, dv2_out, sum_first, sum_second, small,
        rows_v, ret_v, acts, x2_v, p1_v, weights_v, p2_v, kv_v, wide, grads, dscores, ds, dsum, gain_acc, table_v, core_land, landing, small_land, in_sems, out_sems, ring_sems, send_sems, recv_sems, expert_sems, ready,
    ) = rest
    rows, width = x2_v.shape
    pairs = heads // 2
    first_v, q2_v, dctx2, dq, dk, dv, q1_v, k1_v, v1_v, ctx_v, norm_v, do, dctx1, _ = [acts.at[i * rows : (i + 1) * rows, :] for i in range(14)]
    dv2, dk2 = acts.at[6 * rows : 10 * rows, :], acts.at[10 * rows : 14 * rows, :]
    x1_v, du, dx = wide.at[0:rows, :], wide.at[rows : 2 * rows, :], wide.at[2 * rows : 3 * rows, :]
    spare = (dctx2, q2_v)
    gv = wide.at[0:width, :]
    memory_slots, dv2_slots = (rows_v.at[0:memory_length, :], dk2.at[3 * rows : 4 * rows, :]), (do, dctx1)
    loads, stores, running = Loads(in_sems), Loads(out_sems), Running()
    loads.start("rows", dh_rows, rows_v)
    loads.start("cot", cotangent, first_v)
    loads.start("x2", x2, x2_v)
    loads.start("c2", c2, ctx_v)
    loads.start("co", co, weights_v.at[0])

    def fetch(t, sources, first=0):
        slot = t % 2
        m = pl.ds(t * memory_length, memory_length)
        for index, source in enumerate(sources, first):
            target = (p2_v.at[slot], kv_v.at[0, slot], kv_v.at[1, slot], memory_slots[slot])[index]
            copy = pltpu.make_async_copy(source.at[t] if index == 0 else source.at[m, :], target, ring_sems.at[index, slot])
            copy.start()
            yield copy

    fetched = list(fetch(0, (p2, k2, v2)))
    for name, source, target in (
        ("q2", q2, q2_v), ("cq", cq, weights_v.at[1]), ("h2", h2, norm_v), ("wo", wo, weights_v.at[2]),
        ("p1", p1, p1_v), ("q1", q1, q1_v), ("k1", k1, k1_v), ("v1", v1, v1_v), ("ck", ck, weights_v.at[3]),
        ("cv", cv, weights_v.at[4]),
    ):
        loads.start(name, source, target)
    if remote:
        ring = Ring(send_sems, recv_sems)
        ring.greet(("core", "x", "y"))
        capacity = rows_v.shape[0] // ring.experts
        mine = ring.block(ring.expert, capacity)
        ret_copies = [
            ring.send(ret_rows.at[ring.slot(k, capacity, e), :], ret_v.at[mine, :], ring.dp, e) for k, e in enumerate(ring.peers) if k
        ]
        loads.start("ret", ret_rows.at[ring.slot(0, capacity), :], ret_v.at[mine, :])
        expert_sums = [
            reduce_expert(ring, part_first, grads.at[0], grads.at[2], "x", sum_first, expert_sems.at[0]),
            reduce_expert(ring, part_second, grads.at[1], grads.at[5], "y", sum_second, expert_sems.at[1]),
        ]
        for steps in expert_sums:
            running.add(steps, -5)
        running.free["z"] = 20.0
    else:
        ret_copies, expert_sums = [], []
        loads.start("ret", ret_rows, ret_v)

    gain = [g[...].astype(F32).reshape(1, -1) for g in (gain_one, gain_two, gain_three)]
    low_lane, low, high = half_masks()
    gain_acc[...] = jnp.zeros_like(gain_acc)
    started = []

    def total_of(index):
        if remote:
            axes, rank = PLAN[len(started)]
            lands = core_land.at[index], landing.at[index]
            running.add(reduce_matrix(ring, grads.at[index], grad_refs[index], *lands, axes, stores, ready.at[index]), rank)
        else:
            stores.start(("grad", index), grads.at[index], grad_refs[index])
        started.append(index)

    def inner_grad(index, left, right):
        for c in range(width // 256):
            cols = slice(c * 256, (c + 1) * 256)
            grads[index, cols, :] = dot_tn(left[:, cols], right[...]).astype(BF16)
        total_of(index)

    def back_through(values, index, base, target):
        def one(r):
            back, gain_rows = norm_back(values[r, :].astype(F32), gain[index], du[r, :])
            total = base[r, :].astype(F32) + back
            target[r, :] = total
            if index:
                do[r, :] = total.astype(BF16)
            gain_acc[index] += gain_rows

        row_loop(rows, 32, one)

    loads.wait("rows", "cot", "x2")

    def gathered(cols, values):
        du[:, cols] = values

    collect(place_column, rows_v, gathered)
    fetched += list(fetch(0, (memory,), 3))
    back_through(x2_v, 2, first_v, dx)
    loads.start("tokens", tokens, first_v)
    loads.wait("c2", "co")
    inner_grad(7, ctx_v, do)
    loads.start("c1", c1, ctx_v)

    def out_back(slot, target):
        for cols in column_tiles(width):
            target[:, cols] = dot_nt(do[...], weights_v[slot, cols, :]).astype(BF16)

    out_back(0, dctx2)
    running.tick(4.9)
    loads.start("wq", wq, weights_v.at[0])
    loads.wait("q2")
    for t in range(targets):
        slot = t % 2
        ahead = list(fetch(t + 1, (p2, k2, v2, memory))) if t + 1 < targets else []
        if t >= 2:
            stores.wait(("dv2", t - 2))
        for copy in fetched:
            copy.wait()
        fetched = ahead
        r = slice(t * length, (t + 1) * length)
        for pair in range(pairs):
            lanes = slice(pair * LANES, (pair + 1) * LANES)
            side = pair % 2
            grad_rows = stacked(dctx2[r, lanes], low, high)
            dscores[side] = dot_nt(grad_rows, kv_v[1, slot, :, lanes])
            dv2_slots[slot][:, lanes] = dot_tn(p2_v[slot, pair], grad_rows).astype(BF16)
            for chunk in range(2 * length // 32):
                part = slice(chunk * 32, (chunk + 1) * 32)
                prob = p2_v[slot, pair, part, :].astype(F32)
                dprob = dscores[side, part, :]
                inner = jnp.sum(prob * dprob, axis=-1, keepdims=True)
                ds[t, pair, part, :] = (prob * (dprob - inner)).astype(BF16)
            back = dot(ds[t, pair], kv_v[0, slot, :, lanes])
            dq[r, lanes] = jnp.where(low_lane, back[:length], back[length:]).astype(BF16)
            if side:
                running.tick(1.26)
        stores.start(("dv2", t), dv2_slots[slot], dv2_out.at[pl.ds(t * memory_length, memory_length), :])
        for c in range(width // 256):
            cols = slice(c * 256, (c + 1) * 256)
            part = dot_tn(memory_slots[slot][:, cols], dv2_slots[slot][...])
            if t:
                part = part + gv[cols, :]
            if t + 1 < targets:
                gv[cols, :] = part
            else:
                grads[6, cols, :] = part.astype(BF16)
        running.tick(0.84)
    total_of(6)
    loads.start("x1", x1, x1_v)
    memory_copies = []
    for t in range(targets):
        source = memory.at[pl.ds(t * memory_length, memory_length), :]
        memory_copies.append(pltpu.make_async_copy(source, kv_v.at[t // 2, t % 2], ring_sems.at[1 + t // 2, t % 2]))
        memory_copies[-1].start()
    for t in range(max(0, targets - 2), targets):
        stores.wait(("dv2", t))
    loads.wait("h2", "cq", "x1")
    inner_grad(4, norm_v, dq)
    loads.start("h1", h1, norm_v)

    for cols in column_tiles(width):
        du[:, cols] = dot_nt(dq[...], weights_v[1, cols, :])
    loads.start("wk", wk, weights_v.at[1])
    running.tick(1.75)
    back_through(x1_v, 1, dx, dx)
    running.tick(1.05)
    loads.wait("c1", "wo")
    inner_grad(3, ctx_v, do)
    out_back(2, dctx1)
    loads.start("wv", wv, weights_v.at[2])
    running.tick(1.75)
    for copy in ret_copies:
        copy.wait()
    loads.wait("ret")

    def output_columns(cols, values):
        dk[:, cols] = (x2_v[:, cols] + values).astype(BF16)

    collect(place_column, ret_v, output_columns)
    stores.start("output", dk, output_out)
    running.tick(1.4)
    loads.wait("p1", "q1", "k1", "v1")
    stores.wait("output")
    for t in range(targets):
        r = slice(t * length, (t + 1) * length)
        allowed = allowed_of(mask[t : t + 1, :], length)
        for pair in range(pairs):
            lanes = slice(pair * LANES, (pair + 1) * LANES)
            side = pair % 2
            grad_rows = stacked(dctx1[r, lanes], low, high)
            both = dot_nt(grad_rows, v1_v[r, lanes])
            scratch = p2_v.at[1, side]
            for half in range(2):
                part = slice(half * length, (half + 1) * length)
                prob = p1_v[t, pair, part, :].astype(F32)
                dprob = both[part]
                inner = jnp.sum(prob * dprob, axis=-1, keepdims=True)
                score = jnp.where(allowed, prob * (dprob - inner), 0.0).astype(BF16)
                scratch[part, :length] = score
                wide_score = score.astype(F32)
                dsum[pair, part, :] = wide_score if t == 0 else dsum[pair, part, :] + wide_score
            dv[r, lanes] = dot_tn(p1_v[t, pair], grad_rows).astype(BF16)
            dk[r, lanes] = dot_tn(scratch[:, :length], stacked(q1_v[r, lanes], low, high)).astype(BF16)
            back = dot(scratch[:, :length], k1_v[r, lanes])
            dq[r, lanes] = jnp.where(low_lane, back[:length], back[length:]).astype(BF16)
        running.tick(1.75)
    loads.wait("h1", "wq", "wk", "wv", "tokens")
    running.finish(expert_sums)
    for index, right in enumerate((dq, dk, dv)):
        inner_grad(index, norm_v, right)
        running.tick(0.84)
    loads.start("dv2", dv2_out, dv2)

    for t in range(targets):
        r = slice(t * length, (t + 1) * length)
        m = slice(t * memory_length, (t + 1) * memory_length)
        for pair in range(pairs):
            lanes = slice(pair * LANES, (pair + 1) * LANES)
            dk2[m, lanes] = dot_tn(ds[t, pair], stacked(q2_v[r, lanes], low, high)).astype(BF16)
        running.tick(0.84)
    for copy in memory_copies:
        copy.wait()
    for c in range(width // 256):
        cols = slice(c * 256, (c + 1) * 256)
        total = 0.0
        for t in range(targets):
            m = slice(t * memory_length, (t + 1) * memory_length)
            total = total + dot_tn(kv_v[t // 2, t % 2, :, cols], dk2[m, :])
        grads[5, cols, :] = total.astype(BF16)
        running.tick(0.91)
    total_of(5)

    for cols in column_tiles(width):
        du[:, cols] = (
            dot_nt(dq[...], weights_v[0, cols, :]) + dot_nt(dk[...], weights_v[1, cols, :]) + dot_nt(dv[...], weights_v[2, cols, :])
        )
    running.tick(1.75)
    back_through(first_v, 0, dx, dx)
    stores.start("tokens", dx, grad_tokens_out)
    running.tick(1.05)
    small[...] = jnp.zeros_like(small)
    for i in range(3):
        small[i : i + 1, :] = jnp.sum(gain_acc[i], axis=0, keepdims=True)
    small[8:16, :] = grad_router[0:8, :]
    table_v[...] = jnp.zeros_like(table_v)

    def table_rows(b, carry):
        hit = buckets[...] == b
        for head in range(heads):
            start = (head % 2) * length
            part = jnp.where(hit, dsum[head // 2, start : start + length, :], 0.0)
            table_v[pl.ds(head, 1), :] = jnp.sum(part, axis=0, keepdims=True)
        sums = jnp.sum(table_v[0:16, :], axis=-1, keepdims=True)
        here = lax.broadcasted_iota(jnp.int32, (1, LANES), 1) == b
        table_v[16:32, :] += jnp.where(here, sums, 0.0)
        return carry

    for b in range(0, 32, 16):
        lax.fori_loop(b, b + 16, table_rows, 0)
        running.tick(1.4)
    small[16:24, 0:LANES] = table_v[16:24, :]
    small[16:24, LANES : 2 * LANES] = table_v[24:32, :]
    if remote:
        running.add(reduce_small(ring, small, small_land), 1)
    loads.wait("ck", "cv", "dv2")
    for t in range(targets):
        buffer = spare[t % 2]
        if t >= 2:
            stores.wait(("memory", t - 2))
        m = slice(t * memory_length, (t + 1) * memory_length)
        for cols in column_tiles(width):
            buffer[:, cols] = (dot_nt(dk2[m, :], weights_v[3, cols, :]) + dot_nt(dv2[m, :], weights_v[4, cols, :])).astype(BF16)
            running.tick(0.56)
        stores.start(("memory", t), buffer, grad_memory_out.at[pl.ds(t * memory_length, memory_length), :])
    running.drain()
    stores.drain()


def finish_kernel(*refs):
    sources, small, targets, table, routed, gain_refs = refs[:13], refs[13], refs[14:27], refs[27], refs[28], refs[29:32]
    narrow, wide, parts, first, second, *passed, in_sems, out_sems = refs[32:]
    loads, stores = Loads(in_sems), Loads(out_sems)
    landing = [narrow.at[i] for i in range(8)] + [parts.at[i] for i in range(2)] + passed
    order = [10, 11, 0, 1, 2, 12, 3, 4, 5, 6, 7, 8, 9]

    def ahead():
        if order:
            i = order.pop(0)
            loads.start(i, sources[i], landing[i])

    def arrive(*names):
        loads.wait(*names)
        for name in names:
            ahead()
            if name >= 10:
                stores.start(name, passed[name - 10], targets[name])

    for _ in range(4):
        ahead()
    for i in range(8):
        arrive(*{0: (10, 11, 0), 3: (12, 3)}.get(i, (i,)))

        def widen(r, i=i):
            wide[i, r, :] = narrow[i, r, :].astype(F32)

        row_loop(wide.shape[1], 64, widen)
        stores.start(i, wide.at[i], targets[i])
    arrive(8, 9)

    def widen_part(r):
        first[r, :] = parts[0, r, :].astype(F32)

    row_loop(first.shape[0], 64, widen_part)
    stores.start(8, first, targets[8])
    for c in range(0, first.shape[0], LANES):
        second[:, c : c + LANES] = parts[1, c : c + LANES, :].astype(F32).T
    stores.start(9, second, targets[9])
    heads, count = table.shape
    table[0:8, :] = small[16:24, 0:count]
    table[8:heads, :] = small[16 : 16 + heads - 8, LANES : LANES + count]
    routed[...] = small[8 : 8 + routed.shape[0], :]
    for i, ref in enumerate(gain_refs):
        ref[...] = small[i : i + 1, :].reshape(-1)
    stores.drain()


def params(**more):
    return pltpu.CompilerParams(vmem_limit_bytes=VMEM_LIMIT, **more)


def on_device(
    tokens, memory, target_mask, buckets, expert_ids, slots, gain_self, w_query, w_key, w_value, w_output, rel_table, gain_cross,
    c_query, c_key, c_value, c_output, gain_moe, router, expert_in, expert_out, cotangent,
):
    rows, width = tokens.shape
    targets, length = target_mask.shape
    bucket_count, heads = rel_table.shape
    memory_length = memory.shape[0] // targets
    pairs = heads // 2
    experts = lax.axis_size("expert")
    hidden = expert_in.shape[2]
    capacity = (5 * rows + 4 * experts - 1) // (4 * experts)
    slot_rows = experts * capacity
    place = jnp.where(slots < capacity, expert_ids * capacity + slots, -1)
    place_row, place_column = place.reshape(1, rows), place.reshape(rows, 1)
    gains = [gain_self, gain_cross, gain_moe]
    weights = (w_query, w_key, w_value, w_output, c_query, c_key, c_value, c_output)

    remote = lax.axis_size("dp") == 8 and experts == 4 and hidden == 4 * width

    def exchange(buffer):
        if remote:
            return buffer
        buffer = buffer.reshape(experts, capacity, width)
        return lax.all_to_all(buffer, "expert", split_axis=0, concat_axis=0, tiled=True).reshape(slot_rows, width)

    def remote_params(collective_id):
        return params(collective_id=collective_id, has_side_effects=True) if remote else params()

    row_shape = jax.ShapeDtypeStruct((slot_rows, width), BF16)
    act_shape = ((rows, width), BF16)
    wide_shape = ((rows, width), F32)
    key_shape = ((targets * memory_length, width), BF16)
    kept = (
        [act_shape] * 8
        + [wide_shape] * 2
        + [((targets, pairs, 2 * length, length), BF16), ((targets, pairs, 2 * length, memory_length), BF16), key_shape, key_shape]
        + [((slot_rows, width), BF16)] * 2
    )
    h1, q1, k1, v1, c1, h2, q2, c2, x1, x2, p1, p2, k2, v2, sent, grows = pl.pallas_call(
        functools.partial(forward_kernel, targets, length, memory_length, heads, remote),
        out_shape=[jax.ShapeDtypeStruct(*k) for k in kept],
        in_specs=[VMEM, ANY, ANY, VMEM, VMEM, VMEM, VMEM, VMEM, VMEM, ANY] + [ANY] * 8,
        out_specs=[ANY] * len(kept),
        scratch_shapes=[pltpu.VMEM((rows, width), BF16), pltpu.VMEM(*key_shape), pltpu.VMEM((8, width, width), BF16)]
        + [pltpu.VMEM(*k) for k in kept]
        + [
            pltpu.VMEM((pairs, 2 * length, length), F32),
            pltpu.VMEM((heads * bucket_count, length), F32),
            pltpu.VMEM((2, 2 * length, memory_length), F32),
            pltpu.SemaphoreType.DMA((11,)),
            pltpu.SemaphoreType.DMA((len(kept),)),
            pltpu.SemaphoreType.DMA((experts - 1,)),
            pltpu.SemaphoreType.DMA((experts - 1,)),
        ],
        compiler_params=remote_params(1),
        name="forward",
    )(rel_table.T, tokens, memory, target_mask, buckets, *gains, place_row, cotangent, *weights)

    sent, grows = exchange(sent), exchange(grows)
    tiles = hidden // width
    half = width // 2
    weight_grad = jax.ShapeDtypeStruct((3, width, half) if remote else (width, hidden), BF16)
    row_scratch, half_scratch = pltpu.VMEM((slot_rows, width), BF16), pltpu.VMEM((slot_rows // 2, width), F32)
    ret, dh, grad_first, grad_second, grad_router = pl.pallas_call(
        functools.partial(expert_kernel, experts, remote),
        out_shape=[row_shape, row_shape, weight_grad, weight_grad, jax.ShapeDtypeStruct((8, width), F32)],
        in_specs=[ANY, ANY, VMEM, ANY, ANY],
        out_specs=[ANY, ANY, ANY, ANY, VMEM],
        scratch_shapes=[
            pltpu.VMEM((LANES, width), BF16),
            pltpu.VMEM((width, LANES), BF16),
            pltpu.VMEM((LANES, width), F32),
            pltpu.VMEM((width, hidden), BF16),
            pltpu.VMEM((hidden, width), BF16),
            row_scratch,
            row_scratch,
            pltpu.VMEM((width, slot_rows), BF16),
            row_scratch,
            pltpu.VMEM((width, slot_rows), BF16),
            pltpu.VMEM((slot_rows, LANES), F32),
            half_scratch,
            half_scratch,
            pltpu.VMEM((slot_rows, hidden), BF16),
            pltpu.VMEM((slot_rows, hidden), BF16),
            half_scratch,
            half_scratch,
            row_scratch,
            row_scratch,
            pltpu.VMEM((2, 2, tiles, width, half), BF16),
            pltpu.VMEM((2, tiles, width, half), BF16),
            pltpu.VMEM((2, width, half), BF16),
            pltpu.SemaphoreType.DMA((2 * tiles + 2,)),
            pltpu.SemaphoreType.DMA((4 * tiles + 2,)),
            pltpu.SemaphoreType.DMA((2 * experts + 2 * tiles,)),
            pltpu.SemaphoreType.DMA((2 * experts + 2 * tiles,)),
        ],
        compiler_params=remote_params(2),
        name="experts",
    )(sent, grows, router.T, expert_in[0], expert_out[0])
    dh_rows, ret_rows = exchange(dh), exchange(ret)
    parts = (grad_first, grad_second)
    if not remote:
        parts = (ret, ret)

    square = (width, width)
    wide = pltpu.VMEM(*wide_shape)
    small_shape = (24, width)
    lands = 8 if remote else 1
    copies = 8 * (6 + 2 * (experts - 1)) + 2 * experts + 1 + 4
    block = jax.ShapeDtypeStruct((width, half), BF16)
    results = pl.pallas_call(
        functools.partial(backward_kernel, targets, length, memory_length, heads, remote),
        out_shape=[jax.ShapeDtypeStruct(square, BF16)] * 8
        + [
            jax.ShapeDtypeStruct((rows, width), BF16),
            jax.ShapeDtypeStruct((rows, width), F32),
            jax.ShapeDtypeStruct(memory.shape, BF16),
            jax.ShapeDtypeStruct(memory.shape, BF16),
            block,
            block,
            jax.ShapeDtypeStruct(small_shape, F32),
        ],
        in_specs=[ANY, ANY] + [VMEM] * 7 + [ANY] * 27,
        out_specs=[ANY] * 14 + [VMEM],
        scratch_shapes=[pltpu.VMEM((slot_rows, width), BF16)] * 2
        + [
            pltpu.VMEM((14 * rows, width), BF16),
            wide,
            pltpu.VMEM((targets, pairs, 2 * length, length), BF16),
            pltpu.VMEM((5,) + square, BF16),
            pltpu.VMEM((2, pairs, 2 * length, memory_length), BF16),
            pltpu.VMEM((2, 2, memory_length, width), BF16),
            pltpu.VMEM((3 * rows, width), F32),
            pltpu.VMEM((8,) + square, BF16),
            pltpu.VMEM((2, 2 * length, memory_length), F32),
            pltpu.VMEM((targets, pairs, 2 * length, memory_length), BF16),
            pltpu.VMEM((pairs, 2 * length, length), F32),
            pltpu.VMEM((3, 8, width), F32),
            pltpu.VMEM((32, LANES), F32),
            pltpu.VMEM((lands, width, half), BF16),
            pltpu.VMEM((lands, width - width // (4 * experts), half), BF16),
            pltpu.VMEM((experts + 3,) + small_shape, F32),
            pltpu.SemaphoreType.DMA((24,)),
            pltpu.SemaphoreType.DMA((28,)),
            pltpu.SemaphoreType.DMA((4, 2)),
            pltpu.SemaphoreType.DMA((copies,)),
            pltpu.SemaphoreType.DMA((copies,)),
            pltpu.SemaphoreType.DMA((2, 3)),
            pltpu.SemaphoreType.REGULAR((8,)),
        ],
        compiler_params=remote_params(0),
        name="backward",
    )(
        dh_rows, ret_rows, place_column, target_mask, buckets, *gains, grad_router, cotangent, tokens, h1, q1, k1, v1, c1, h2, q2, c2, x1, x2,
        p1, p2, k2, v2, memory, *weights, *parts,
    )
    summed, (output, grad_tokens, grad_memory, _, grad_first_sum, grad_second_sum), small = results[:8], results[8:14], results[-1]
    if not remote:
        summed, small = lax.psum((summed, small), ("dp", "expert"))
        grad_first_sum, grad_second_sum = (
            lax.psum_scatter(g, "dp", scatter_dimension=1, tiled=True) for g in (grad_first, grad_second)
        )
    wide_square = jax.ShapeDtypeStruct(square, F32)
    part_shape = grad_first_sum.shape
    finished = pl.pallas_call(
        finish_kernel,
        out_shape=[wide_square] * 8
        + [
            jax.ShapeDtypeStruct(part_shape, F32),
            jax.ShapeDtypeStruct(part_shape[::-1], F32),
            jax.ShapeDtypeStruct(output.shape, BF16),
            jax.ShapeDtypeStruct(grad_tokens.shape, F32),
            jax.ShapeDtypeStruct(grad_memory.shape, BF16),
            jax.ShapeDtypeStruct((heads, bucket_count), F32),
            jax.ShapeDtypeStruct((experts, width), F32),
        ]
        + [jax.ShapeDtypeStruct((width,), F32)] * 3,
        in_specs=[ANY] * 13 + [VMEM],
        out_specs=[ANY] * 8 + [ANY] * 5 + [VMEM] * 5,
        scratch_shapes=[
            pltpu.VMEM((8,) + square, BF16),
            pltpu.VMEM((8,) + square, F32),
            pltpu.VMEM((2,) + part_shape, BF16),
            pltpu.VMEM(part_shape, F32),
            pltpu.VMEM(part_shape[::-1], F32),
            pltpu.VMEM(output.shape, BF16),
            pltpu.VMEM(grad_tokens.shape, F32),
            pltpu.VMEM(grad_memory.shape, BF16),
            pltpu.SemaphoreType.DMA((13,)),
            pltpu.SemaphoreType.DMA((13,)),
        ],
        compiler_params=params(),
        name="finish",
    )(*summed, grad_first_sum, grad_second_sum, output, grad_tokens, grad_memory, small)
    wq_grad, wk_grad, wv_grad, wo_grad, cq_grad, ck_grad, cv_grad, co_grad, first, second, output, grad_tokens, grad_memory, table, routed, *gain_grads = finished
    return (
        output, grad_tokens, grad_memory, gain_grads[0], wq_grad, wk_grad, wv_grad, wo_grad, table.T, gain_grads[1], cq_grad, ck_grad, cv_grad,
        co_grad, gain_grads[2], routed.T, first[None], second[None],
    )


def solution(mesh):
    both, spread = P(("dp", "expert")), P(("dp", "expert"), None)
    placed = (
        (spread, spread, spread, P(), both, both) + (P(),) * 13 + (P("expert", None, None), P("expert", None, None), spread)
    )
    return jax.shard_map(
        on_device,
        mesh=mesh,
        in_specs=placed,
        out_specs=(spread, spread, spread) + (P(),) * 13 + (P("expert", None, "dp"), P("expert", "dp", None)),
        check_vma=False,
    )
```

```python
import functools

import jax
import jax.numpy as jnp
from jax import lax
from jax.experimental import pallas as pl
from jax.experimental.pallas import tpu as pltpu
from jax.sharding import PartitionSpec as P

EPS = 1e-06
NEG = -1000000000.0
F32 = jnp.float32
BF16 = jnp.bfloat16
LANES = 128
VMEM_LIMIT = 63_400_000
ANY = pl.BlockSpec(memory_space=pl.ANY)
VMEM = pl.BlockSpec(memory_space=pltpu.VMEM)
SMEM = pl.BlockSpec(memory_space=pltpu.SMEM)


def dot(left, right):
    return lax.dot_general(left, right, (((1,), (0,)), ((), ())), preferred_element_type=F32)


def dot_nt(left, right):
    return lax.dot_general(left, right, (((1,), (1,)), ((), ())), preferred_element_type=F32)


def dot_tn(left, right):
    return lax.dot_general(left, right, (((0,), (0,)), ((), ())), preferred_element_type=F32)


def column_tiles(width, step=256):
    return [slice(c, c + step) for c in range(0, width, step)]


def row_loop(count, step, body):
    def one(i, carry):
        body(pl.ds(pl.multiple_of(i * step, step), step))
        return carry

    lax.fori_loop(0, count // step, one, 0)


def half_masks():
    lane = lax.broadcasted_iota(jnp.int32, (1, LANES), 1)
    low = jnp.where(lane < LANES // 2, 1.0, 0.0).astype(BF16)
    high = jnp.where(lane < LANES // 2, 0.0, 1.0).astype(BF16)
    return lane < LANES // 2, low, high


def stacked(pair, low, high):
    return jnp.concatenate([pair * low, pair * high], axis=0)


def norm_rows(values, gain):
    return values * lax.rsqrt(jnp.mean(values * values, axis=-1, keepdims=True) + EPS) * gain


def norm_back(values, gain, grad):
    scale = lax.rsqrt(jnp.mean(values * values, axis=-1, keepdims=True) + EPS)
    scaled = grad * gain
    inner = jnp.mean(scaled * values, axis=-1, keepdims=True)
    back = scale * scaled - values * (scale * scale * scale * inner)
    gain_rows = grad * values * scale
    return back, jnp.sum(gain_rows.reshape(-1, 8, gain_rows.shape[-1]), axis=0)


def allowed_of(mask_row, length):
    row = lax.broadcasted_iota(jnp.int32, (length, length), 0)
    col = lax.broadcasted_iota(jnp.int32, (length, length), 1)
    return (col <= row) & (mask_row == 1)


class Loads:
    def __init__(self, sems):
        self.sems = sems
        self.count = 0
        self.open = {}

    def start(self, name, source, target):
        copy = pltpu.make_async_copy(source, target, self.sems.at[self.count])
        self.count += 1
        copy.start()
        self.open[name] = copy

    def wait(self, *names):
        for name in names:
            self.open.pop(name).wait()

    def drain(self):
        self.wait(*list(self.open))


class Ring:
    def __init__(self, send_sems, recv_sems):
        self.send_sems, self.recv_sems = send_sems, recv_sems
        self.count = 0
        dp, self.expert = lax.axis_index("dp"), lax.axis_index("expert")
        self.experts = lax.axis_size("expert")
        self.dp = dp
        self.spot = {"core": lax.rem(dp, 2), "x": lax.rem(lax.div(dp, 2), 2), "y": lax.div(dp, 4)}
        self.partner = {name: dp + step - 2 * step * self.spot[name] for name, step in (("core", 1), ("x", 2), ("y", 4))}

        low, high = lax.rem(self.expert, 2), lax.div(self.expert, 2)
        near, far = 1 - 2 * low, 2 - 4 * high
        self.peers = [self.expert, self.expert + near, self.expert + far, self.expert + near + far]

    def others(self):
        return self.peers[1:]

    def block(self, expert, capacity):
        return pl.ds(pl.multiple_of(expert * capacity, 16), capacity)

    def slot(self, k, capacity, sender=None):
        low = lax.rem(self.expert if sender is None else sender, 2)
        return pl.ds(pl.multiple_of((low + (2 if k >= 2 else 0)) * capacity, 16), capacity)

    def scatter(self, source, target):
        capacity = source.shape[0] // self.experts
        return [
            self.send(source.at[self.block(e, capacity), :], target.at[self.slot(k, capacity), :], self.dp, e)
            for k, e in enumerate(self.peers)
            if k
        ]

    def greet(self, names):
        barrier = pltpu.get_barrier_semaphore()
        targets = [(self.partner[name], self.expert) for name in names] + [(self.dp, e) for e in self.others()]
        for target in targets:
            pl.semaphore_signal(barrier, inc=1, device_id=target, device_id_type=pl.DeviceIdType.MESH)
        pl.semaphore_wait(barrier, len(targets))

    def send(self, source, target, dp, expert):
        copy = pltpu.make_async_remote_copy(
            src_ref=source, dst_ref=target, send_sem=self.send_sems.at[self.count], recv_sem=self.recv_sems.at[self.count],
            device_id=(dp, expert), device_id_type=pl.DeviceIdType.MESH,
        )
        self.count += 1
        copy.start()
        return copy

    def cross(self, name, source, target):
        return self.send(source, target, self.partner[name], self.expert)


def forward_kernel(
    targets, length, memory_length, heads, remote,
    table, tokens, memory, mask, buckets, gain_one, gain_two, gain_three, place, cotangent, wq, wk, wv, wo, cq, ck, cv, co,
    h1_out, q1_out, k1_out, v1_out, c1_out, h2_out, q2_out, c2_out, x1_out, x2_out, p1_out, p2_out, k2_out, v2_out, sent_out, grows_out,
    tokens_v, memory_v, weights_v, h1, q1, k1, v1, c1, h2, q2, c2, x1, x2, p1, p2, k2, v2, sent, gsent, bias, spread, scores, in_sems, out_sems,
    send_sems, recv_sems,
):
    rows, width = tokens_v.shape
    pairs = heads // 2
    loads, stores = Loads(in_sems), Loads(out_sems)
    loads.start("cot", cotangent, c2)
    loads.start("tokens", tokens, tokens_v)
    for index, (name, ref) in enumerate(zip(("wq", "wk", "wv"), (wq, wk, wv))):
        loads.start(name, ref, weights_v.at[index])
    loads.start("ck", ck, weights_v.at[5])
    loads.start("memory", memory, memory_v)
    loads.start("cv", cv, weights_v.at[6])
    loads.start("wo", wo, weights_v.at[3])
    loads.start("cq", cq, weights_v.at[4])
    loads.start("co", co, weights_v.at[7])
    gain = [g[...].astype(F32).reshape(1, -1) for g in (gain_one, gain_two, gain_three)]
    low_lane, low, high = half_masks()

    if remote:
        ring = Ring(send_sems, recv_sems)
        ring.greet(())
    loads.wait("cot")
    dispatch(place, c2, gsent)
    gsent_copies = []
    if remote:
        gsent_copies = ring.scatter(gsent, grows_out)
        block = ring.block(ring.expert, sent.shape[0] // ring.experts)
        stores.start("grows", gsent.at[block, :], grows_out.at[ring.slot(0, sent.shape[0] // ring.experts), :])
    else:
        stores.start("grows", gsent, grows_out)
    bucket_count = table.shape[1]
    by_head = table[...].astype(F32)
    for head in range(heads):
        row = jnp.broadcast_to(by_head[head : head + 1, :], (LANES, bucket_count))
        spread[head * bucket_count : (head + 1) * bucket_count, :] = row.T

    def bias_rows(r):
        here = buckets[r, :]
        hits = [here == b for b in range(bucket_count)]
        for head in range(heads):
            total = jnp.zeros(here.shape, F32)
            for b in range(bucket_count):
                at = head * bucket_count + b
                total = jnp.where(hits[b], spread[at : at + 1, :], total)
            start = (head % 2) * length
            bias[head // 2, pl.ds(pl.multiple_of(r.start + start, 8), r.size), :] = total

    row_loop(length, 16, bias_rows)

    loads.wait("tokens")

    def first_norm(r):
        h1[r, :] = norm_rows(tokens_v[r, :].astype(F32), gain[0]).astype(BF16)

    row_loop(rows, 32, first_norm)
    stores.start("h1", h1, h1_out)
    for index, (name, ref) in enumerate(zip(("wq", "wk", "wv"), (q1, k1, v1))):
        loads.wait(name)

        for cols in column_tiles(width):
            ref[:, cols] = dot(h1[...], weights_v[index, :, cols]).astype(BF16)
    stores.start("q1", q1, q1_out)
    stores.start("k1", k1, k1_out)
    stores.start("v1", v1, v1_out)

    def self_target(t, carry):
        r = pl.ds(pl.multiple_of(t * length, length), length)
        allowed = allowed_of(mask[pl.ds(t, 1), :], length)
        for pair in range(pairs):
            lanes = slice(pair * LANES, (pair + 1) * LANES)
            both = dot_nt(stacked(q1[r, lanes], low, high), k1[r, lanes])
            for half in range(2):
                part = slice(half * length, (half + 1) * length)
                score = jnp.where(allowed, both[part] + bias[pair, part, :], NEG)
                expo = jnp.exp(score - jnp.max(score, axis=-1, keepdims=True))
                total = jnp.sum(expo, axis=-1, keepdims=True)
                p1[t, pair, part, :] = (expo * (1.0 / total)).astype(BF16)
            context = dot(p1[t, pair], v1[r, lanes])
            c1[r, lanes] = jnp.where(low_lane, context[:length], context[length:]).astype(BF16)
        return carry

    lax.fori_loop(0, targets, self_target, 0)
    stores.start("p1", p1, p1_out)
    stores.start("c1", c1, c1_out)
    loads.wait("wo")

    for cols in column_tiles(width):
        x1[:, cols] = tokens_v[:, cols].astype(F32) + dot(c1[...], weights_v[3, :, cols])
    stores.start("x1", x1, x1_out)

    def second_norm(r):
        h2[r, :] = norm_rows(x1[r, :], gain[1]).astype(BF16)

    row_loop(rows, 32, second_norm)
    stores.start("h2", h2, h2_out)
    loads.wait("cq")

    for cols in column_tiles(width):
        q2[:, cols] = dot(h2[...], weights_v[4, :, cols]).astype(BF16)
    stores.start("q2", q2, q2_out)
    loads.wait("memory", "ck", "cv")

    def cross_keys(r):
        for cols in column_tiles(width):
            k2[r, cols] = dot(memory_v[r, :], weights_v[5, :, cols]).astype(BF16)
            v2[r, cols] = dot(memory_v[r, :], weights_v[6, :, cols]).astype(BF16)

    row_loop(targets * memory_length, memory_length, cross_keys)
    stores.start("k2", k2, k2_out)
    stores.start("v2", v2, v2_out)

    def cross_target(t, carry):
        r = pl.ds(pl.multiple_of(t * length, length), length)
        m = pl.ds(pl.multiple_of(t * memory_length, memory_length), memory_length)
        for pair in range(pairs):
            lanes = slice(pair * LANES, (pair + 1) * LANES)
            slot = pair % 2
            scores[slot] = dot_nt(stacked(q2[r, lanes], low, high), k2[m, lanes])
            for chunk in range(2 * length // 32):
                part = slice(chunk * 32, (chunk + 1) * 32)
                score = scores[slot, part, :]
                expo = jnp.exp(score - jnp.max(score, axis=-1, keepdims=True))
                total = jnp.sum(expo, axis=-1, keepdims=True)
                p2[t, pair, part, :] = (expo * (1.0 / total)).astype(BF16)
            context = dot(p2[t, pair], v2[m, lanes])
            c2[r, lanes] = jnp.where(low_lane, context[:length], context[length:]).astype(BF16)
        return carry

    lax.fori_loop(0, targets, cross_target, 0)
    stores.start("p2", p2, p2_out)
    stores.start("c2", c2, c2_out)
    loads.wait("co")

    for cols in column_tiles(width):
        x2[:, cols] = x1[:, cols] + dot(c2[...], weights_v[7, :, cols])
    stores.start("x2", x2, x2_out)

    def third_norm(r):
        tokens_v[r, :] = norm_rows(x2[r, :], gain[2]).astype(BF16)

    row_loop(rows, 32, third_norm)
    dispatch(place, tokens_v, sent)
    stores.start("sent", sent, sent_out)
    for copy in gsent_copies:
        copy.wait()
    stores.drain()


def dispatch(place, source, target):
    step = target.shape[0] // 2

    def one(r):
        spot = lax.broadcasted_iota(jnp.int32, (step, source.shape[0]), 0) + r.start
        hit = jnp.where(spot == place[...], 1.0, 0.0).astype(BF16)
        for cols in column_tiles(source.shape[1]):
            target[r, cols] = dot(hit, source[:, cols]).astype(target.dtype)

    row_loop(target.shape[0], step, one)


def collect(place_column, source, put):
    spot = lax.broadcasted_iota(jnp.int32, (place_column.shape[0], source.shape[0]), 1)
    hit = jnp.where(spot == place_column[...], 1.0, 0.0).astype(BF16)
    for cols in column_tiles(source.shape[1]):
        put(cols, dot(hit, source[:, cols]))


class ExpertSum:
    def __init__(self, ring, running, tiles, core_land, near_land, first, result, stores):
        self.ring, self.running, self.tiles, self.first = ring, running, tiles, first
        self.core_land, self.near_land = core_land, near_land
        self.result, self.stores = result, stores
        self.order = (0, 1, 2, 3) if first == "x" else (0, 2, 1, 3)
        self.ready, self.started = set(), False
        self.place = (lambda one, two: one + 2 * two) if first == "x" else (lambda one, two: 2 * one + two)

    def add(self, tile, other):
        core = self.ring.spot["core"]

        def rows(r):
            self.tiles[core, tile, r, :] += other[r, :]

        row_loop(self.tiles.shape[2], 64, rows)

    def start(self, tile):
        self.running.add(self.between_cores(tile))

    def between_cores(self, tile):
        core = self.ring.spot["core"]
        copy = self.ring.cross("core", self.tiles.at[1 - core, tile], self.core_land.at[tile])
        yield link_time("core", *self.tiles.shape[2:])
        copy.wait()
        self.add(tile, self.core_land.at[tile])
        self.ready.add(tile)
        if {self.place(0, 0), self.place(1, 0)} <= self.ready and not self.started:
            self.started = True
            self.running.add(self.near())
        if {self.place(0, 1), self.place(1, 1)} <= self.ready:
            spot = self.ring.spot[self.first]
            self.keep(1, self.place(spot, 1))
            self.keep(2, self.place(1 - spot, 1))

    def near(self):
        spot = self.ring.spot[self.first]
        source = self.tiles.at[self.ring.spot["core"], self.place(1 - spot, 0)]
        copy = self.ring.cross(self.first, source, self.near_land)
        yield link_time(self.first, *self.tiles.shape[2:])
        copy.wait()
        self.keep(0, self.place(spot, 0), self.near_land)

    def keep(self, index, tile, other=None):
        if other is not None:
            self.add(tile, other)
        source = self.tiles.at[self.ring.spot["core"], tile]
        self.stores.start(("sum", self.first, index), source, self.result.at[index])


def expert_kernel(
    experts, remote, inbound, grows, router_rows, first, second,
    ret_out, dh_out, grad_first, grad_second, grad_router,
    router, router_turned, router_sum, first_v, second_v, inbound_v, grows_v, inbound_t, dret, dret_t, probs, pre, dact, act, dpre, ret, dinb, ret_v, dh_v, sums, core_land, near_land,
    in_sems, out_sems, send_sems, recv_sems,
):
    rows, width = inbound_v.shape
    hidden = first.shape[1]
    step = width
    tiles = hidden // step
    loads, stores = Loads(in_sems), Loads(out_sems)
    capacity = rows // experts
    half_rows = rows // 2
    if remote:
        ring = Ring(send_sems, recv_sems)
        ring.greet(("core", "x", "y"))
        arriving = ring.scatter(inbound, inbound_v)
        loads.start("inbound", inbound.at[ring.block(ring.expert, capacity), :], inbound_v.at[ring.slot(0, capacity), :])
    else:
        loads.start("inbound", inbound, inbound_v)
        arriving = []
    loads.start("grows", grows, grows_v)
    for f in range(tiles):
        cols = slice(f * step, (f + 1) * step)
        loads.start(("first", f), first.at[:, cols], first_v.at[:, cols])
        loads.start(("second", f), second.at[cols, :], second_v.at[cols, :])
    me = lax.axis_index("expert")
    lane = lax.broadcasted_iota(jnp.int32, (1, LANES), 1)
    mine = lane == me
    root = (2.0 / jnp.pi) ** 0.5
    router_sum[...] = jnp.zeros_like(router_sum)
    router[...] = jnp.zeros_like(router)
    router[0:experts, :] = router_rows[...]
    for cols in column_tiles(width, LANES):
        router_turned[cols, :] = router[:, cols].T
    loads.wait("inbound", "grows")
    returning = []
    for side in range(2):
        start = side * half_rows
        here = slice(start, start + half_rows)
        for copy in (arriving[:1], arriving[1:])[side]:
            copy.wait_recv()

        def route(r, start=start):
            r = pl.ds(pl.multiple_of(start + r.start, 16), r.size)
            logits = jnp.where(lane < experts, dot(inbound_v[r, :], router_turned[...]), -1e30)
            expo = jnp.exp(logits - jnp.max(logits, axis=-1, keepdims=True))
            prob = expo / jnp.sum(expo, axis=-1, keepdims=True)
            probs[r, :] = prob
            gate = jnp.sum(jnp.where(mine, prob, 0.0), axis=-1, keepdims=True)
            dret[r, :] = (gate * grows_v[r, :].astype(F32)).astype(BF16)

        row_loop(half_rows, half_rows // 2, route)
        for f in range(tiles):
            cols = slice(f * step, (f + 1) * step)
            if side == 0:
                loads.wait(("first", f), ("second", f))
            for c in range(0, step, 256):
                tile = slice(f * step + c, f * step + c + 256)
                pre[:, c : c + 256] = dot(inbound_v[here, :], first_v[:, tile])
                dact[:, c : c + 256] = dot_nt(dret[here, :], second_v[tile, :])

            def middle(r, start=start, cols=cols):
                u = pre[r, :]
                square = u * u
                t = jnp.tanh(u * (root + (root * 0.044715) * square))
                half = 0.5 + 0.5 * t
                out = pl.ds(pl.multiple_of(start + r.start, 16), r.size)
                act[out, cols] = (u * half).astype(BF16)
                slope = half + (u * (0.5 * root + (1.5 * root * 0.044715) * square)) * (1.0 - t * t)
                dpre[out, cols] = (dact[r, :] * slope).astype(BF16)

            row_loop(half_rows, 16, middle)
            for c in range(0, width, 256):
                tile = slice(c, c + 256)
                one, two = dot(act[here, cols], second_v[cols, tile]), dot_nt(dpre[here, cols], first_v[tile, cols])
                if f:
                    one, two = one + ret[:, tile], two + dinb[:, tile]
                ret[:, tile] = one
                dinb[:, tile] = two

        def finish(r, start=start):
            out = pl.ds(pl.multiple_of(start + r.start, 16), r.size)
            result = ret[r, :].astype(BF16).astype(F32)
            prob = probs[out, :]
            gate = jnp.sum(jnp.where(mine, prob, 0.0), axis=-1, keepdims=True)
            dgate = jnp.sum(result * grows_v[out, :].astype(F32), axis=-1, keepdims=True)
            dlogits = (prob * (jnp.where(mine, 1.0, 0.0) - gate) * dgate).astype(BF16)
            ret_v[out, :] = (gate * result).astype(BF16)
            dh_v[out, :] = (dinb[r, :].astype(BF16).astype(F32) + dot(dlogits, router[...])).astype(BF16)
            router_sum[...] += dot_tn(dlogits, inbound_v[out, :])

        row_loop(half_rows, half_rows // 2, finish)
        if remote:
            target = dh_out.at[ring.block(ring.expert, capacity), :]
            for k in ((1,), (2, 3))[side]:
                source = dh_v.at[ring.slot(k, capacity, ring.peers[k]), :]
                returning.append(ring.send(source, target, ring.dp, ring.peers[k]))
            if side == 0:
                stores.start("dh", dh_v.at[ring.slot(0, capacity), :], target)
        elif side:
            stores.start("dh", dh_v, dh_out)
    stores.start("ret", ret_v, ret_out)
    grad_router[...] = router_sum[0:8, :]
    for copy in arriving:
        copy.wait_send()
    for c in range(width // LANES):
        cols = slice(c * LANES, (c + 1) * LANES)
        inbound_t[cols, :] = inbound_v[:, cols].T
        dret_t[cols, :] = dret[:, cols].T

    running = Running()
    if remote:
        expert_sums = [
            ExpertSum(ring, running, sums.at[j], core_land.at[j], near_land.at[j], axis, out, stores)
            for j, (axis, out) in enumerate((("x", grad_first), ("y", grad_second)))
        ]
    for i in range(tiles):
        for j, (left, right) in enumerate(((inbound_t, dpre), (dret_t, act))):
            f = expert_sums[j].order[i] if remote else i
            for cols in column_tiles(step):
                total = dot(left[...], right[:, f * step + cols.start : f * step + cols.stop]).astype(BF16)
                for c in range(cols.start, cols.stop, LANES):
                    b, at = divmod(c, step // 2)
                    sums[j, b, f, :, at : at + LANES] = total[:, c - cols.start : c - cols.start + LANES]
            if not remote:
                for b in range(2):
                    cols = slice(f * step + b * (step // 2), f * step + (b + 1) * (step // 2))
                    stores.start(("sum", j, b, f), sums.at[j, b, f], (grad_first, grad_second)[j].at[:, cols])
            running.tick(1.6)
            if remote:
                expert_sums[j].start(f)
    running.drain()
    for copy in returning:
        copy.wait()
    stores.drain()


def span(start, size):
    return pl.ds(pl.multiple_of(start, size), size)


def add_into(ref, rows, lanes, others, target=None):
    step = 48 if rows.size % 64 else 64
    for i in range(rows.size // step):
        here = pl.ds(pl.multiple_of(rows.start + i * step, 16), step)
        part = slice(i * step, (i + 1) * step)
        if len(others) == 1:
            total = ref[here, lanes] + others[0][part, :]
        else:
            total = ref[here, lanes].astype(F32) + sum(other[part, :].astype(F32) for other in others)
        if target is None:
            ref[here, lanes] = total.astype(BF16)
        else:
            target[here, :] = total.astype(BF16)


def reduce_matrix(ring, local, result, core_land, landing, axes, stores, ready):
    size = local.shape[0]
    half = size // 2
    core = ring.spot["core"]
    mine, other = span(core * half, half), span((1 - core) * half, half)
    copy = ring.cross("core", local.at[:, other], core_land)
    yield link_time("core", size, half)
    copy.wait()
    pl.semaphore_signal(ready, inc=1, device_id=(ring.partner["core"], ring.expert), device_id_type=pl.DeviceIdType.MESH)
    add_into(local, pl.ds(0, size), mine, [core_land])
    base, count, row, trail = 0, size, 0, []
    for axis in axes:
        parts = ring.experts if axis == "z" else 2
        part = count // parts
        lands = [landing.at[row + k * part : row + (k + 1) * part, :] for k in range(parts - 1)]
        if axis == "z":
            spot = ring.expert
            copies = [ring.send(local.at[span(base + e * part, part), mine], lands[k], ring.dp, e) for k, e in enumerate(ring.others())]
        else:
            spot = ring.spot[axis]
            copies = [ring.cross(axis, local.at[span(base + (1 - spot) * part, part), mine], lands[0])]
        yield link_time(axis, part, half)
        for copy in copies:
            copy.wait()
        base, count, row = base + spot * part, part, row + (parts - 1) * part
        here = span(base, count)
        add_into(local, here, mine, lands, core_land if axis == axes[-1] else None)
        trail.append((axis, here))
    for axis, here in reversed(trail):
        block = core_land.at[here, :]
        if axis == "z":
            copies = [ring.send(block, block, ring.dp, e) for e in ring.others()]
        else:
            copies = [ring.cross(axis, block, block)]
        yield link_time(axis, here.size, half)
        for copy in copies:
            copy.wait()
    pl.semaphore_wait(ready, 1)
    copy = ring.cross("core", core_land, local.at[:, mine])
    yield link_time("core", size, half)
    copy.wait()
    stores.start(("mine", stores.count), core_land, result.at[:, mine])
    stores.start(("other", stores.count), local.at[:, other], result.at[:, other])


def reduce_expert(ring, part, keep, extra, first, result, sems):
    size, block = part.shape[1], part.shape[2]
    second = "y" if first == "x" else "x"
    cols = [slice(i * block, (i + 1) * block) for i in range(2)]
    copies = [ring.cross(first, part.at[2], extra.at[:, cols[1]])]
    copies += [pltpu.make_async_copy(part.at[i], keep.at[:, cols[i]], sems.at[i]) for i in range(2)]
    for copy in copies[1:]:
        copy.start()
    yield link_time(first, size, block)
    for copy in copies:
        copy.wait()
    add_into(keep, pl.ds(0, size), cols[1], [extra.at[:, cols[1]]])
    spot = ring.spot[second]
    copy = ring.cross(second, keep.at[:, span((1 - spot) * block, block)], extra.at[:, cols[0]])
    yield link_time(second, size, block)
    copy.wait()
    stay = span(spot * block, block)
    add_into(keep, pl.ds(0, size), stay, [extra.at[:, cols[0]]])
    copy = pltpu.make_async_copy(keep.at[:, stay], result, sems.at[2])
    copy.start()
    copy.wait()


def reduce_small(ring, local, landing):
    for k, name in enumerate(("core", "x", "y")):
        copy = ring.cross(name, local, landing.at[k])
        yield link_time(name, *local.shape, 4)
        copy.wait()
        local[...] += landing[k]
    copies = [ring.send(local, landing.at[3 + ring.expert], ring.dp, e) for e in ring.others()]
    landing[3 + ring.expert] = local[...]
    yield link_time("z", *local.shape, 4)
    for copy in copies:
        copy.wait()
    total = landing[3]
    for e in range(1, ring.experts):
        total = total + landing[3 + e]
    local[...] = total


class Running:
    DELAY = 1.5

    def __init__(self):
        self.steps = []
        self.now = 0.0
        self.free = {}

    def land(self, entry, use):
        if use is None:
            self.steps = [e for e in self.steps if e is not entry]
            return
        link, time = use
        self.free[link] = max(self.now, self.free.get(link, 0.0)) + time
        entry[1] = self.free[link] + self.DELAY

    def add(self, steps, rank=0):
        entry = [steps, 0.0, rank]
        self.steps.append(entry)
        self.land(entry, next(steps))

    def advance(self, entry):
        self.now = max(self.now, entry[1]) + 0.5
        entry[2] += 1
        self.land(entry, next(entry[0], None))

    def tick(self, time):
        self.now += time
        while landed := [e for e in self.steps if e[1] <= self.now]:
            self.advance(min(landed, key=lambda e: (e[2], e[1])))

    def finish(self, steps):
        while any(e[0] is s for e in self.steps for s in steps):
            self.advance(min(self.steps, key=lambda e: e[1]))

    def drain(self):
        while self.steps:
            self.advance(min(self.steps, key=lambda e: e[1]))
            self.tick(0.0)


def link_time(name, rows, columns, itemsize=2):
    rate = {"core": 270e3, "x": 50e3, "y": 50e3, "z": 11.25e3}[name]
    return name, rows * columns * itemsize / rate


PLAN = (
    ("yxz", -2), ("xyz", -4), ("xyz", -1), ("yxz", -4), ("yxz", 2), ("xyz", -3), ("xyz", 2), ("yxz", -6),
)


def backward_kernel(
    targets, length, memory_length, heads, remote,
    dh_rows, ret_rows, place_column, mask, buckets, gain_one, gain_two, gain_three, grad_router, cotangent, tokens, h1, q1, k1, v1, c1, h2, q2, c2, x1, x2, p1, p2,
    k2, v2, memory, wq, wk, wv, wo, cq, ck, cv, co, part_first, part_second,
    *rest,
):
    grad_refs, rest = rest[:8], rest[8:]
    (
        output_out, grad_tokens_out, grad_memory_out, dv2_out, sum_first, sum_second, small,
        rows_v, ret_v, acts, x2_v, p1_v, weights_v, p2_v, kv_v, wide, grads, dscores, ds, dsum, gain_acc, table_v, core_land, landing, small_land, in_sems, out_sems, ring_sems, send_sems, recv_sems, expert_sems, ready,
    ) = rest
    rows, width = x2_v.shape
    pairs = heads // 2
    first_v, q2_v, dctx2, dq, dk, dv, q1_v, k1_v, v1_v, ctx_v, norm_v, do, dctx1, _ = [acts.at[i * rows : (i + 1) * rows, :] for i in range(14)]
    dv2, dk2 = acts.at[6 * rows : 10 * rows, :], acts.at[10 * rows : 14 * rows, :]
    x1_v, du, dx = wide.at[0:rows, :], wide.at[rows : 2 * rows, :], wide.at[2 * rows : 3 * rows, :]
    spare = (dctx2, q2_v)
    gv = wide.at[0:width, :]
    memory_slots, dv2_slots = (rows_v.at[0:memory_length, :], dk2.at[3 * rows : 4 * rows, :]), (do, dctx1)
    loads, stores, running = Loads(in_sems), Loads(out_sems), Running()
    loads.start("rows", dh_rows, rows_v)
    loads.start("cot", cotangent, first_v)
    loads.start("x2", x2, x2_v)
    loads.start("c2", c2, ctx_v)
    loads.start("co", co, weights_v.at[0])

    def fetch(t, sources, first=0):
        slot = t % 2
        m = pl.ds(t * memory_length, memory_length)
        for index, source in enumerate(sources, first):
            target = (p2_v.at[slot], kv_v.at[0, slot], kv_v.at[1, slot], memory_slots[slot])[index]
            copy = pltpu.make_async_copy(source.at[t] if index == 0 else source.at[m, :], target, ring_sems.at[index, slot])
            copy.start()
            yield copy

    fetched = list(fetch(0, (p2, k2, v2)))
    for name, source, target in (
        ("q2", q2, q2_v), ("cq", cq, weights_v.at[1]), ("h2", h2, norm_v), ("wo", wo, weights_v.at[2]),
        ("p1", p1, p1_v), ("q1", q1, q1_v), ("k1", k1, k1_v), ("v1", v1, v1_v), ("ck", ck, weights_v.at[3]),
        ("cv", cv, weights_v.at[4]),
    ):
        loads.start(name, source, target)
    if remote:
        ring = Ring(send_sems, recv_sems)
        ring.greet(("core", "x", "y"))
        capacity = rows_v.shape[0] // ring.experts
        mine = ring.block(ring.expert, capacity)
        ret_copies = [
            ring.send(ret_rows.at[ring.slot(k, capacity, e), :], ret_v.at[mine, :], ring.dp, e) for k, e in enumerate(ring.peers) if k
        ]
        loads.start("ret", ret_rows.at[ring.slot(0, capacity), :], ret_v.at[mine, :])
        expert_sums = [
            reduce_expert(ring, part_first, grads.at[0], grads.at[2], "x", sum_first, expert_sems.at[0]),
            reduce_expert(ring, part_second, grads.at[1], grads.at[5], "y", sum_second, expert_sems.at[1]),
        ]
        for steps in expert_sums:
            running.add(steps, -5)
        running.free["z"] = 20.0
    else:
        ret_copies, expert_sums = [], []
        loads.start("ret", ret_rows, ret_v)

    gain = [g[...].astype(F32).reshape(1, -1) for g in (gain_one, gain_two, gain_three)]
    low_lane, low, high = half_masks()
    gain_acc[...] = jnp.zeros_like(gain_acc)
    started = []

    def total_of(index):
        if remote:
            axes, rank = PLAN[len(started)]
            lands = core_land.at[index], landing.at[index]
            running.add(reduce_matrix(ring, grads.at[index], grad_refs[index], *lands, axes, stores, ready.at[index]), rank)
        else:
            stores.start(("grad", index), grads.at[index], grad_refs[index])
        started.append(index)

    def inner_grad(index, left, right):
        for c in range(width // 256):
            cols = slice(c * 256, (c + 1) * 256)
            grads[index, cols, :] = dot_tn(left[:, cols], right[...]).astype(BF16)
        total_of(index)

    def back_through(values, index, base, target):
        def one(r):
            back, gain_rows = norm_back(values[r, :].astype(F32), gain[index], du[r, :])
            total = base[r, :].astype(F32) + back
            target[r, :] = total
            if index:
                do[r, :] = total.astype(BF16)
            gain_acc[index] += gain_rows

        row_loop(rows, 32, one)

    loads.wait("rows", "cot", "x2")

    def gathered(cols, values):
        du[:, cols] = values

    collect(place_column, rows_v, gathered)
    fetched += list(fetch(0, (memory,), 3))
    back_through(x2_v, 2, first_v, dx)
    loads.start("tokens", tokens, first_v)
    loads.wait("c2", "co")
    inner_grad(7, ctx_v, do)
    loads.start("c1", c1, ctx_v)

    def out_back(slot, target):
        for cols in column_tiles(width):
            target[:, cols] = dot_nt(do[...], weights_v[slot, cols, :]).astype(BF16)

    out_back(0, dctx2)
    running.tick(4.9)
    loads.start("wq", wq, weights_v.at[0])
    loads.wait("q2")
    for t in range(targets):
        slot = t % 2
        ahead = list(fetch(t + 1, (p2, k2, v2, memory))) if t + 1 < targets else []
        if t >= 2:
            stores.wait(("dv2", t - 2))
        for copy in fetched:
            copy.wait()
        fetched = ahead
        r = slice(t * length, (t + 1) * length)
        for pair in range(pairs):
            lanes = slice(pair * LANES, (pair + 1) * LANES)
            side = pair % 2
            grad_rows = stacked(dctx2[r, lanes], low, high)
            dscores[side] = dot_nt(grad_rows, kv_v[1, slot, :, lanes])
            dv2_slots[slot][:, lanes] = dot_tn(p2_v[slot, pair], grad_rows).astype(BF16)
            for chunk in range(2 * length // 32):
                part = slice(chunk * 32, (chunk + 1) * 32)
                prob = p2_v[slot, pair, part, :].astype(F32)
                dprob = dscores[side, part, :]
                inner = jnp.sum(prob * dprob, axis=-1, keepdims=True)
                ds[t, pair, part, :] = (prob * (dprob - inner)).astype(BF16)
            back = dot(ds[t, pair], kv_v[0, slot, :, lanes])
            dq[r, lanes] = jnp.where(low_lane, back[:length], back[length:]).astype(BF16)
            if side:
                running.tick(1.26)
        stores.start(("dv2", t), dv2_slots[slot], dv2_out.at[pl.ds(t * memory_length, memory_length), :])
        for c in range(width // 256):
            cols = slice(c * 256, (c + 1) * 256)
            part = dot_tn(memory_slots[slot][:, cols], dv2_slots[slot][...])
            if t:
                part = part + gv[cols, :]
            if t + 1 < targets:
                gv[cols, :] = part
            else:
                grads[6, cols, :] = part.astype(BF16)
        running.tick(0.84)
    total_of(6)
    loads.start("x1", x1, x1_v)
    memory_copies = []
    for t in range(targets):
        source = memory.at[pl.ds(t * memory_length, memory_length), :]
        memory_copies.append(pltpu.make_async_copy(source, kv_v.at[t // 2, t % 2], ring_sems.at[1 + t // 2, t % 2]))
        memory_copies[-1].start()
    for t in range(max(0, targets - 2), targets):
        stores.wait(("dv2", t))
    loads.wait("h2", "cq", "x1")
    inner_grad(4, norm_v, dq)
    loads.start("h1", h1, norm_v)

    for cols in column_tiles(width):
        du[:, cols] = dot_nt(dq[...], weights_v[1, cols, :])
    loads.start("wk", wk, weights_v.at[1])
    running.tick(1.75)
    back_through(x1_v, 1, dx, dx)
    running.tick(1.05)
    loads.wait("c1", "wo")
    inner_grad(3, ctx_v, do)
    out_back(2, dctx1)
    loads.start("wv", wv, weights_v.at[2])
    running.tick(1.75)
    for copy in ret_copies:
        copy.wait()
    loads.wait("ret")

    def output_columns(cols, values):
        dk[:, cols] = (x2_v[:, cols] + values).astype(BF16)

    collect(place_column, ret_v, output_columns)
    stores.start("output", dk, output_out)
    running.tick(1.4)
    loads.wait("p1", "q1", "k1", "v1")
    stores.wait("output")
    for t in range(targets):
        r = slice(t * length, (t + 1) * length)
        allowed = allowed_of(mask[t : t + 1, :], length)
        for pair in range(pairs):
            lanes = slice(pair * LANES, (pair + 1) * LANES)
            side = pair % 2
            grad_rows = stacked(dctx1[r, lanes], low, high)
            both = dot_nt(grad_rows, v1_v[r, lanes])
            scratch = p2_v.at[1, side]
            for half in range(2):
                part = slice(half * length, (half + 1) * length)
                prob = p1_v[t, pair, part, :].astype(F32)
                dprob = both[part]
                inner = jnp.sum(prob * dprob, axis=-1, keepdims=True)
                score = jnp.where(allowed, prob * (dprob - inner), 0.0).astype(BF16)
                scratch[part, :length] = score
                wide_score = score.astype(F32)
                dsum[pair, part, :] = wide_score if t == 0 else dsum[pair, part, :] + wide_score
            dv[r, lanes] = dot_tn(p1_v[t, pair], grad_rows).astype(BF16)
            dk[r, lanes] = dot_tn(scratch[:, :length], stacked(q1_v[r, lanes], low, high)).astype(BF16)
            back = dot(scratch[:, :length], k1_v[r, lanes])
            dq[r, lanes] = jnp.where(low_lane, back[:length], back[length:]).astype(BF16)
        running.tick(1.75)
    loads.wait("h1", "wq", "wk", "wv", "tokens")
    running.finish(expert_sums)
    for index, right in enumerate((dq, dk, dv)):
        inner_grad(index, norm_v, right)
        running.tick(0.84)
    loads.start("dv2", dv2_out, dv2)

    for t in range(targets):
        r = slice(t * length, (t + 1) * length)
        m = slice(t * memory_length, (t + 1) * memory_length)
        for pair in range(pairs):
            lanes = slice(pair * LANES, (pair + 1) * LANES)
            dk2[m, lanes] = dot_tn(ds[t, pair], stacked(q2_v[r, lanes], low, high)).astype(BF16)
        running.tick(0.84)
    for copy in memory_copies:
        copy.wait()
    for c in range(width // 256):
        cols = slice(c * 256, (c + 1) * 256)
        total = 0.0
        for t in range(targets):
            m = slice(t * memory_length, (t + 1) * memory_length)
            total = total + dot_tn(kv_v[t // 2, t % 2, :, cols], dk2[m, :])
        grads[5, cols, :] = total.astype(BF16)
        running.tick(0.91)
    total_of(5)

    for cols in column_tiles(width):
        du[:, cols] = (
            dot_nt(dq[...], weights_v[0, cols, :]) + dot_nt(dk[...], weights_v[1, cols, :]) + dot_nt(dv[...], weights_v[2, cols, :])
        )
    running.tick(1.75)
    back_through(first_v, 0, dx, dx)
    stores.start("tokens", dx, grad_tokens_out)
    running.tick(1.05)
    small[...] = jnp.zeros_like(small)
    for i in range(3):
        small[i : i + 1, :] = jnp.sum(gain_acc[i], axis=0, keepdims=True)
    small[8:16, :] = grad_router[0:8, :]
    table_v[...] = jnp.zeros_like(table_v)

    def table_rows(b, carry):
        hit = buckets[...] == b
        for head in range(heads):
            start = (head % 2) * length
            part = jnp.where(hit, dsum[head // 2, start : start + length, :], 0.0)
            table_v[pl.ds(head, 1), :] = jnp.sum(part, axis=0, keepdims=True)
        sums = jnp.sum(table_v[0:16, :], axis=-1, keepdims=True)
        here = lax.broadcasted_iota(jnp.int32, (1, LANES), 1) == b
        table_v[16:32, :] += jnp.where(here, sums, 0.0)
        return carry

    for b in range(0, 32, 16):
        lax.fori_loop(b, b + 16, table_rows, 0)
        running.tick(1.4)
    small[16:24, 0:LANES] = table_v[16:24, :]
    small[16:24, LANES : 2 * LANES] = table_v[24:32, :]
    if remote:
        running.add(reduce_small(ring, small, small_land), 1)
    loads.wait("ck", "cv", "dv2")
    for t in range(targets):
        buffer = spare[t % 2]
        if t >= 2:
            stores.wait(("memory", t - 2))
        m = slice(t * memory_length, (t + 1) * memory_length)
        for cols in column_tiles(width):
            buffer[:, cols] = (dot_nt(dk2[m, :], weights_v[3, cols, :]) + dot_nt(dv2[m, :], weights_v[4, cols, :])).astype(BF16)
            running.tick(0.56)
        stores.start(("memory", t), buffer, grad_memory_out.at[pl.ds(t * memory_length, memory_length), :])
    running.drain()
    stores.drain()


def finish_kernel(*refs):
    sources, small, targets, table, routed, gain_refs = refs[:13], refs[13], refs[14:27], refs[27], refs[28], refs[29:32]
    narrow, wide, parts, first, second, *passed, in_sems, out_sems = refs[32:]
    loads, stores = Loads(in_sems), Loads(out_sems)
    landing = [narrow.at[i] for i in range(8)] + [parts.at[i] for i in range(2)] + passed
    order = [10, 11, 0, 1, 2, 12, 3, 4, 5, 6, 7, 8, 9]

    def ahead():
        if order:
            i = order.pop(0)
            loads.start(i, sources[i], landing[i])

    def arrive(*names):
        loads.wait(*names)
        for name in names:
            ahead()
            if name >= 10:
                stores.start(name, passed[name - 10], targets[name])

    for _ in range(4):
        ahead()
    for i in range(8):
        arrive(*{0: (10, 11, 0), 3: (12, 3)}.get(i, (i,)))

        def widen(r, i=i):
            wide[i, r, :] = narrow[i, r, :].astype(F32)

        row_loop(wide.shape[1], 64, widen)
        stores.start(i, wide.at[i], targets[i])
    arrive(8, 9)

    def widen_part(r):
        first[r, :] = parts[0, r, :].astype(F32)

    row_loop(first.shape[0], 64, widen_part)
    stores.start(8, first, targets[8])
    for c in range(0, first.shape[0], LANES):
        second[:, c : c + LANES] = parts[1, c : c + LANES, :].astype(F32).T
    stores.start(9, second, targets[9])
    heads, count = table.shape
    table[0:8, :] = small[16:24, 0:count]
    table[8:heads, :] = small[16 : 16 + heads - 8, LANES : LANES + count]
    routed[...] = small[8 : 8 + routed.shape[0], :]
    for i, ref in enumerate(gain_refs):
        ref[...] = small[i : i + 1, :].reshape(-1)
    stores.drain()


def params(**more):
    return pltpu.CompilerParams(vmem_limit_bytes=VMEM_LIMIT, **more)


def on_device(
    tokens, memory, target_mask, buckets, expert_ids, slots, gain_self, w_query, w_key, w_value, w_output, rel_table, gain_cross,
    c_query, c_key, c_value, c_output, gain_moe, router, expert_in, expert_out, cotangent,
):
    rows, width = tokens.shape
    targets, length = target_mask.shape
    bucket_count, heads = rel_table.shape
    memory_length = memory.shape[0] // targets
    pairs = heads // 2
    experts = lax.axis_size("expert")
    hidden = expert_in.shape[2]
    capacity = (5 * rows + 4 * experts - 1) // (4 * experts)
    slot_rows = experts * capacity
    place = jnp.where(slots < capacity, expert_ids * capacity + slots, -1)
    place_row, place_column = place.reshape(1, rows), place.reshape(rows, 1)
    gains = [gain_self, gain_cross, gain_moe]
    weights = (w_query, w_key, w_value, w_output, c_query, c_key, c_value, c_output)

    remote = lax.axis_size("dp") == 8 and experts == 4 and hidden == 4 * width

    def exchange(buffer):
        if remote:
            return buffer
        buffer = buffer.reshape(experts, capacity, width)
        return lax.all_to_all(buffer, "expert", split_axis=0, concat_axis=0, tiled=True).reshape(slot_rows, width)

    def remote_params(collective_id):
        return params(collective_id=collective_id, has_side_effects=True) if remote else params()

    row_shape = jax.ShapeDtypeStruct((slot_rows, width), BF16)
    act_shape = ((rows, width), BF16)
    wide_shape = ((rows, width), F32)
    key_shape = ((targets * memory_length, width), BF16)
    kept = (
        [act_shape] * 8
        + [wide_shape] * 2
        + [((targets, pairs, 2 * length, length), BF16), ((targets, pairs, 2 * length, memory_length), BF16), key_shape, key_shape]
        + [((slot_rows, width), BF16)] * 2
    )
    h1, q1, k1, v1, c1, h2, q2, c2, x1, x2, p1, p2, k2, v2, sent, grows = pl.pallas_call(
        functools.partial(forward_kernel, targets, length, memory_length, heads, remote),
        out_shape=[jax.ShapeDtypeStruct(*k) for k in kept],
        in_specs=[VMEM, ANY, ANY, VMEM, VMEM, VMEM, VMEM, VMEM, VMEM, ANY] + [ANY] * 8,
        out_specs=[ANY] * len(kept),
        scratch_shapes=[pltpu.VMEM((rows, width), BF16), pltpu.VMEM(*key_shape), pltpu.VMEM((8, width, width), BF16)]
        + [pltpu.VMEM(*k) for k in kept]
        + [
            pltpu.VMEM((pairs, 2 * length, length), F32),
            pltpu.VMEM((heads * bucket_count, length), F32),
            pltpu.VMEM((2, 2 * length, memory_length), F32),
            pltpu.SemaphoreType.DMA((11,)),
            pltpu.SemaphoreType.DMA((len(kept),)),
            pltpu.SemaphoreType.DMA((experts - 1,)),
            pltpu.SemaphoreType.DMA((experts - 1,)),
        ],
        compiler_params=remote_params(1),
        name="forward",
    )(rel_table.T, tokens, memory, target_mask, buckets, *gains, place_row, cotangent, *weights)

    sent, grows = exchange(sent), exchange(grows)
    tiles = hidden // width
    half = width // 2
    weight_grad = jax.ShapeDtypeStruct((3, width, half) if remote else (width, hidden), BF16)
    row_scratch, half_scratch = pltpu.VMEM((slot_rows, width), BF16), pltpu.VMEM((slot_rows // 2, width), F32)
    ret, dh, grad_first, grad_second, grad_router = pl.pallas_call(
        functools.partial(expert_kernel, experts, remote),
        out_shape=[row_shape, row_shape, weight_grad, weight_grad, jax.ShapeDtypeStruct((8, width), F32)],
        in_specs=[ANY, ANY, VMEM, ANY, ANY],
        out_specs=[ANY, ANY, ANY, ANY, VMEM],
        scratch_shapes=[
            pltpu.VMEM((LANES, width), BF16),
            pltpu.VMEM((width, LANES), BF16),
            pltpu.VMEM((LANES, width), F32),
            pltpu.VMEM((width, hidden), BF16),
            pltpu.VMEM((hidden, width), BF16),
            row_scratch,
            row_scratch,
            pltpu.VMEM((width, slot_rows), BF16),
            row_scratch,
            pltpu.VMEM((width, slot_rows), BF16),
            pltpu.VMEM((slot_rows, LANES), F32),
            half_scratch,
            half_scratch,
            pltpu.VMEM((slot_rows, hidden), BF16),
            pltpu.VMEM((slot_rows, hidden), BF16),
            half_scratch,
            half_scratch,
            row_scratch,
            row_scratch,
            pltpu.VMEM((2, 2, tiles, width, half), BF16),
            pltpu.VMEM((2, tiles, width, half), BF16),
            pltpu.VMEM((2, width, half), BF16),
            pltpu.SemaphoreType.DMA((2 * tiles + 2,)),
            pltpu.SemaphoreType.DMA((4 * tiles + 2,)),
            pltpu.SemaphoreType.DMA((2 * experts + 2 * tiles,)),
            pltpu.SemaphoreType.DMA((2 * experts + 2 * tiles,)),
        ],
        compiler_params=remote_params(2),
        name="experts",
    )(sent, grows, router.T, expert_in[0], expert_out[0])
    dh_rows, ret_rows = exchange(dh), exchange(ret)
    parts = (grad_first, grad_second)
    if not remote:
        parts = (ret, ret)

    square = (width, width)
    wide = pltpu.VMEM(*wide_shape)
    small_shape = (24, width)
    lands = 8 if remote else 1
    copies = 8 * (6 + 2 * (experts - 1)) + 2 * experts + 1 + 4
    block = jax.ShapeDtypeStruct((width, half), BF16)
    results = pl.pallas_call(
        functools.partial(backward_kernel, targets, length, memory_length, heads, remote),
        out_shape=[jax.ShapeDtypeStruct(square, BF16)] * 8
        + [
            jax.ShapeDtypeStruct((rows, width), BF16),
            jax.ShapeDtypeStruct((rows, width), F32),
            jax.ShapeDtypeStruct(memory.shape, BF16),
            jax.ShapeDtypeStruct(memory.shape, BF16),
            block,
            block,
            jax.ShapeDtypeStruct(small_shape, F32),
        ],
        in_specs=[ANY, ANY] + [VMEM] * 7 + [ANY] * 27,
        out_specs=[ANY] * 14 + [VMEM],
        scratch_shapes=[pltpu.VMEM((slot_rows, width), BF16)] * 2
        + [
            pltpu.VMEM((14 * rows, width), BF16),
            wide,
            pltpu.VMEM((targets, pairs, 2 * length, length), BF16),
            pltpu.VMEM((5,) + square, BF16),
            pltpu.VMEM((2, pairs, 2 * length, memory_length), BF16),
            pltpu.VMEM((2, 2, memory_length, width), BF16),
            pltpu.VMEM((3 * rows, width), F32),
            pltpu.VMEM((8,) + square, BF16),
            pltpu.VMEM((2, 2 * length, memory_length), F32),
            pltpu.VMEM((targets, pairs, 2 * length, memory_length), BF16),
            pltpu.VMEM((pairs, 2 * length, length), F32),
            pltpu.VMEM((3, 8, width), F32),
            pltpu.VMEM((32, LANES), F32),
            pltpu.VMEM((lands, width, half), BF16),
            pltpu.VMEM((lands, width - width // (4 * experts), half), BF16),
            pltpu.VMEM((experts + 3,) + small_shape, F32),
            pltpu.SemaphoreType.DMA((24,)),
            pltpu.SemaphoreType.DMA((28,)),
            pltpu.SemaphoreType.DMA((4, 2)),
            pltpu.SemaphoreType.DMA((copies,)),
            pltpu.SemaphoreType.DMA((copies,)),
            pltpu.SemaphoreType.DMA((2, 3)),
            pltpu.SemaphoreType.REGULAR((8,)),
        ],
        compiler_params=remote_params(0),
        name="backward",
    )(
        dh_rows, ret_rows, place_column, target_mask, buckets, *gains, grad_router, cotangent, tokens, h1, q1, k1, v1, c1, h2, q2, c2, x1, x2,
        p1, p2, k2, v2, memory, *weights, *parts,
    )
    summed, (output, grad_tokens, grad_memory, _, grad_first_sum, grad_second_sum), small = results[:8], results[8:14], results[-1]
    if not remote:
        summed, small = lax.psum((summed, small), ("dp", "expert"))
        grad_first_sum, grad_second_sum = (
            lax.psum_scatter(g, "dp", scatter_dimension=1, tiled=True) for g in (grad_first, grad_second)
        )
    wide_square = jax.ShapeDtypeStruct(square, F32)
    part_shape = grad_first_sum.shape
    finished = pl.pallas_call(
        finish_kernel,
        out_shape=[wide_square] * 8
        + [
            jax.ShapeDtypeStruct(part_shape, F32),
            jax.ShapeDtypeStruct(part_shape[::-1], F32),
            jax.ShapeDtypeStruct(output.shape, BF16),
            jax.ShapeDtypeStruct(grad_tokens.shape, F32),
            jax.ShapeDtypeStruct(grad_memory.shape, BF16),
            jax.ShapeDtypeStruct((heads, bucket_count), F32),
            jax.ShapeDtypeStruct((experts, width), F32),
        ]
        + [jax.ShapeDtypeStruct((width,), F32)] * 3,
        in_specs=[ANY] * 13 + [VMEM],
        out_specs=[ANY] * 8 + [ANY] * 5 + [VMEM] * 5,
        scratch_shapes=[
            pltpu.VMEM((8,) + square, BF16),
            pltpu.VMEM((8,) + square, F32),
            pltpu.VMEM((2,) + part_shape, BF16),
            pltpu.VMEM(part_shape, F32),
            pltpu.VMEM(part_shape[::-1], F32),
            pltpu.VMEM(output.shape, BF16),
            pltpu.VMEM(grad_tokens.shape, F32),
            pltpu.VMEM(grad_memory.shape, BF16),
            pltpu.SemaphoreType.DMA((13,)),
            pltpu.SemaphoreType.DMA((13,)),
        ],
        compiler_params=params(),
        name="finish",
    )(*summed, grad_first_sum, grad_second_sum, output, grad_tokens, grad_memory, small)
    wq_grad, wk_grad, wv_grad, wo_grad, cq_grad, ck_grad, cv_grad, co_grad, first, second, output, grad_tokens, grad_memory, table, routed, *gain_grads = finished
    return (
        output, grad_tokens, grad_memory, gain_grads[0], wq_grad, wk_grad, wv_grad, wo_grad, table.T, gain_grads[1], cq_grad, ck_grad, cv_grad,
        co_grad, gain_grads[2], routed.T, first[None], second[None],
    )


def solution(mesh):
    both, spread = P(("dp", "expert")), P(("dp", "expert"), None)
    placed = (
        (spread, spread, spread, P(), both, both) + (P(),) * 13 + (P("expert", None, None), P("expert", None, None), spread)
    )
    return jax.shard_map(
        on_device,
        mesh=mesh,
        in_specs=placed,
        out_specs=(spread, spread, spread) + (P(),) * 13 + (P("expert", None, "dp"), P("expert", "dp", None)),
        check_vma=False,
    )
```

```python
import functools

import jax
import jax.numpy as jnp
from jax import lax
from jax.experimental import pallas as pl
from jax.experimental.pallas import tpu as pltpu
from jax.sharding import PartitionSpec as P

EPS = 1e-06
NEG = -1000000000.0
F32 = jnp.float32
BF16 = jnp.bfloat16
LANES = 128
VMEM_LIMIT = 63_400_000
ANY = pl.BlockSpec(memory_space=pl.ANY)
VMEM = pl.BlockSpec(memory_space=pltpu.VMEM)
SMEM = pl.BlockSpec(memory_space=pltpu.SMEM)


def dot(left, right):
    return lax.dot_general(left, right, (((1,), (0,)), ((), ())), preferred_element_type=F32)


def dot_nt(left, right):
    return lax.dot_general(left, right, (((1,), (1,)), ((), ())), preferred_element_type=F32)


def dot_tn(left, right):
    return lax.dot_general(left, right, (((0,), (0,)), ((), ())), preferred_element_type=F32)


def column_tiles(width, step=256):
    return [slice(c, c + step) for c in range(0, width, step)]


def row_loop(count, step, body, times=1):
    def one(i, carry):
        for k in range(times):
            body(pl.ds(pl.multiple_of((i * times + k) * step, step), step))
        return carry

    lax.fori_loop(0, count // (step * times), one, 0)


def half_masks():
    lane = lax.broadcasted_iota(jnp.int32, (1, LANES), 1)
    low = jnp.where(lane < LANES // 2, 1.0, 0.0).astype(BF16)
    high = jnp.where(lane < LANES // 2, 0.0, 1.0).astype(BF16)
    return lane < LANES // 2, low, high


def stacked(pair, low, high):
    return jnp.concatenate([pair * low, pair * high], axis=0)


def norm_rows(values, gain):
    return values * lax.rsqrt(jnp.mean(values * values, axis=-1, keepdims=True) + EPS) * gain


def norm_back(values, gain, grad):
    scale = lax.rsqrt(jnp.mean(values * values, axis=-1, keepdims=True) + EPS)
    scaled = grad * gain
    inner = jnp.mean(scaled * values, axis=-1, keepdims=True)
    back = scale * scaled - values * (scale * scale * scale * inner)
    gain_rows = grad * values * scale
    return back, jnp.sum(gain_rows.reshape(-1, 8, gain_rows.shape[-1]), axis=0)


def allowed_of(mask_row, length):
    row = lax.broadcasted_iota(jnp.int32, (length, length), 0)
    col = lax.broadcasted_iota(jnp.int32, (length, length), 1)
    return (col <= row) & (mask_row == 1)


class Loads:
    def __init__(self, sems):
        self.sems = sems
        self.count = 0
        self.open = {}

    def start(self, name, source, target):
        copy = pltpu.make_async_copy(source, target, self.sems.at[self.count])
        self.count += 1
        copy.start()
        self.open[name] = copy

    def wait(self, *names):
        for name in names:
            self.open.pop(name).wait()

    def drain(self):
        self.wait(*list(self.open))


class Ring:
    def __init__(self, send_sems, recv_sems):
        self.send_sems, self.recv_sems = send_sems, recv_sems
        self.count = 0
        dp, self.expert = lax.axis_index("dp"), lax.axis_index("expert")
        self.experts = lax.axis_size("expert")
        self.dp = dp
        self.spot = {"core": lax.rem(dp, 2), "x": lax.rem(lax.div(dp, 2), 2), "y": lax.div(dp, 4)}
        self.partner = {name: dp + step - 2 * step * self.spot[name] for name, step in (("core", 1), ("x", 2), ("y", 4))}

        low, high = lax.rem(self.expert, 2), lax.div(self.expert, 2)
        near, far = 1 - 2 * low, 2 - 4 * high
        self.peers = [self.expert, self.expert + near, self.expert + far, self.expert + near + far]

    def others(self):
        return self.peers[1:]

    def block(self, expert, capacity):
        return pl.ds(pl.multiple_of(expert * capacity, 16), capacity)

    def slot(self, k, capacity, sender=None):
        low = lax.rem(self.expert if sender is None else sender, 2)
        return pl.ds(pl.multiple_of((low + (2 if k >= 2 else 0)) * capacity, 16), capacity)

    def scatter(self, source, target):
        capacity = source.shape[0] // self.experts
        return [
            self.send(source.at[self.block(e, capacity), :], target.at[self.slot(k, capacity), :], self.dp, e)
            for k, e in enumerate(self.peers)
            if k
        ]

    def greet(self, names):
        barrier = pltpu.get_barrier_semaphore()
        targets = [(self.partner[name], self.expert) for name in names] + [(self.dp, e) for e in self.others()]
        for target in targets:
            pl.semaphore_signal(barrier, inc=1, device_id=target, device_id_type=pl.DeviceIdType.MESH)
        pl.semaphore_wait(barrier, len(targets))

    def send(self, source, target, dp, expert):
        copy = pltpu.make_async_remote_copy(
            src_ref=source, dst_ref=target, send_sem=self.send_sems.at[self.count], recv_sem=self.recv_sems.at[self.count],
            device_id=(dp, expert), device_id_type=pl.DeviceIdType.MESH,
        )
        self.count += 1
        copy.start()
        return copy

    def cross(self, name, source, target):
        return self.send(source, target, self.partner[name], self.expert)


def forward_kernel(
    targets, length, memory_length, heads, remote,
    table, tokens, memory, mask, buckets, gain_one, gain_two, gain_three, place, cotangent, wq, wk, wv, wo, cq, ck, cv, co,
    h1_out, q1_out, k1_out, v1_out, c1_out, h2_out, q2_out, c2_out, x1_out, x2_out, p1_out, p2_out, k2_out, v2_out, sent_out, grows_out,
    tokens_v, memory_v, weights_v, h1, q1, k1, v1, c1, h2, q2, c2, x1, x2, p1, p2, k2, v2, sent, gsent, bias, spread, scores, in_sems, out_sems,
    send_sems, recv_sems,
):
    rows, width = tokens_v.shape
    pairs = heads // 2
    loads, stores = Loads(in_sems), Loads(out_sems)
    loads.start("cot", cotangent, c2)
    loads.start("tokens", tokens, tokens_v)
    for index, (name, ref) in enumerate(zip(("wq", "wk", "wv"), (wq, wk, wv))):
        loads.start(name, ref, weights_v.at[index])
    loads.start("ck", ck, weights_v.at[5])
    loads.start("memory", memory, memory_v)
    loads.start("cv", cv, weights_v.at[6])
    loads.start("wo", wo, weights_v.at[3])
    loads.start("cq", cq, weights_v.at[4])
    loads.start("co", co, weights_v.at[7])
    gain = [g[...].astype(F32).reshape(1, -1) for g in (gain_one, gain_two, gain_three)]
    low_lane, low, high = half_masks()

    if remote:
        ring = Ring(send_sems, recv_sems)
        ring.greet(())
    loads.wait("cot")
    dispatch(place, c2, gsent)
    gsent_copies = []
    if remote:
        gsent_copies = ring.scatter(gsent, grows_out)
        block = ring.block(ring.expert, sent.shape[0] // ring.experts)
        stores.start("grows", gsent.at[block, :], grows_out.at[ring.slot(0, sent.shape[0] // ring.experts), :])
    else:
        stores.start("grows", gsent, grows_out)
    bucket_count = table.shape[1]
    by_head = table[...].astype(F32)
    for head in range(heads):
        row = jnp.broadcast_to(by_head[head : head + 1, :], (LANES, bucket_count))
        spread[head * bucket_count : (head + 1) * bucket_count, :] = row.T

    def bias_rows(r):
        here = buckets[r, :]
        hits = [here == b for b in range(bucket_count)]
        for head in range(heads):
            total = jnp.zeros(here.shape, F32)
            for b in range(bucket_count):
                at = head * bucket_count + b
                total = jnp.where(hits[b], spread[at : at + 1, :], total)
            start = (head % 2) * length
            bias[head // 2, pl.ds(pl.multiple_of(r.start + start, 8), r.size), :] = total

    row_loop(length, 16, bias_rows)

    loads.wait("tokens")

    def first_norm(r):
        h1[r, :] = norm_rows(tokens_v[r, :].astype(F32), gain[0]).astype(BF16)

    row_loop(rows, 32, first_norm, 2)
    stores.start("h1", h1, h1_out)
    for index, (name, ref) in enumerate(zip(("wq", "wk", "wv"), (q1, k1, v1))):
        loads.wait(name)

        for cols in column_tiles(width):
            ref[:, cols] = dot(h1[...], weights_v[index, :, cols]).astype(BF16)
    stores.start("q1", q1, q1_out)
    stores.start("k1", k1, k1_out)
    stores.start("v1", v1, v1_out)

    def self_target(t, carry):
        r = pl.ds(pl.multiple_of(t * length, length), length)
        allowed = allowed_of(mask[pl.ds(t, 1), :], length)
        for pair in range(pairs):
            lanes = slice(pair * LANES, (pair + 1) * LANES)
            both = dot_nt(stacked(q1[r, lanes], low, high), k1[r, lanes])
            for half in range(2):
                part = slice(half * length, (half + 1) * length)
                score = jnp.where(allowed, both[part] + bias[pair, part, :], NEG)
                expo = jnp.exp(score - jnp.max(score, axis=-1, keepdims=True))
                total = jnp.sum(expo, axis=-1, keepdims=True)
                p1[t, pair, part, :] = (expo * (1.0 / total)).astype(BF16)
            context = dot(p1[t, pair], v1[r, lanes])
            c1[r, lanes] = jnp.where(low_lane, context[:length], context[length:]).astype(BF16)
        return carry

    lax.fori_loop(0, targets, self_target, 0)
    stores.start("p1", p1, p1_out)
    stores.start("c1", c1, c1_out)
    loads.wait("wo")

    for cols in column_tiles(width):
        x1[:, cols] = tokens_v[:, cols].astype(F32) + dot(c1[...], weights_v[3, :, cols])
    stores.start("x1", x1, x1_out)

    def second_norm(r):
        h2[r, :] = norm_rows(x1[r, :], gain[1]).astype(BF16)

    row_loop(rows, 32, second_norm, 2)
    stores.start("h2", h2, h2_out)
    loads.wait("cq")

    for cols in column_tiles(width):
        q2[:, cols] = dot(h2[...], weights_v[4, :, cols]).astype(BF16)
    stores.start("q2", q2, q2_out)
    loads.wait("memory", "ck", "cv")

    def cross_keys(r):
        for cols in column_tiles(width):
            k2[r, cols] = dot(memory_v[r, :], weights_v[5, :, cols]).astype(BF16)
            v2[r, cols] = dot(memory_v[r, :], weights_v[6, :, cols]).astype(BF16)

    row_loop(targets * memory_length, memory_length, cross_keys)
    stores.start("k2", k2, k2_out)
    stores.start("v2", v2, v2_out)

    def cross_target(t, carry):
        r = pl.ds(pl.multiple_of(t * length, length), length)
        m = pl.ds(pl.multiple_of(t * memory_length, memory_length), memory_length)
        for pair in range(pairs):
            lanes = slice(pair * LANES, (pair + 1) * LANES)
            slot = pair % 2
            scores[slot] = dot_nt(stacked(q2[r, lanes], low, high), k2[m, lanes])
            for chunk in range(2 * length // 32):
                part = slice(chunk * 32, (chunk + 1) * 32)
                score = scores[slot, part, :]
                expo = jnp.exp(score - jnp.max(score, axis=-1, keepdims=True))
                total = jnp.sum(expo, axis=-1, keepdims=True)
                p2[t, pair, part, :] = (expo * (1.0 / total)).astype(BF16)
            context = dot(p2[t, pair], v2[m, lanes])
            c2[r, lanes] = jnp.where(low_lane, context[:length], context[length:]).astype(BF16)
        return carry

    lax.fori_loop(0, targets, cross_target, 0)
    stores.start("p2", p2, p2_out)
    stores.start("c2", c2, c2_out)
    loads.wait("co")

    for cols in column_tiles(width):
        x2[:, cols] = x1[:, cols] + dot(c2[...], weights_v[7, :, cols])
    stores.start("x2", x2, x2_out)

    def third_norm(r):
        tokens_v[r, :] = norm_rows(x2[r, :], gain[2]).astype(BF16)

    row_loop(rows, 32, third_norm, 2)
    dispatch(place, tokens_v, sent)
    stores.start("sent", sent, sent_out)
    for copy in gsent_copies:
        copy.wait()
    stores.drain()


def dispatch(place, source, target):
    step = target.shape[0] // 2

    def one(r):
        spot = lax.broadcasted_iota(jnp.int32, (step, source.shape[0]), 0) + r.start
        hit = jnp.where(spot == place[...], 1.0, 0.0).astype(BF16)
        for cols in column_tiles(source.shape[1]):
            target[r, cols] = dot(hit, source[:, cols]).astype(target.dtype)

    row_loop(target.shape[0], step, one)


def collect(place_column, source, put):
    spot = lax.broadcasted_iota(jnp.int32, (place_column.shape[0], source.shape[0]), 1)
    hit = jnp.where(spot == place_column[...], 1.0, 0.0).astype(BF16)
    for cols in column_tiles(source.shape[1]):
        put(cols, dot(hit, source[:, cols]))


class ExpertSum:
    def __init__(self, ring, running, tiles, core_land, near_land, first, result, stores):
        self.ring, self.running, self.tiles, self.first = ring, running, tiles, first
        self.core_land, self.near_land = core_land, near_land
        self.result, self.stores = result, stores
        self.order = (0, 1, 2, 3) if first == "x" else (0, 2, 1, 3)
        self.ready, self.started = set(), False
        self.place = (lambda one, two: one + 2 * two) if first == "x" else (lambda one, two: 2 * one + two)

    def add(self, tile, other):
        core = self.ring.spot["core"]

        def rows(r):
            self.tiles[core, tile, r, :] += other[r, :]

        row_loop(self.tiles.shape[2], 64, rows)

    def start(self, tile):
        self.running.add(self.between_cores(tile))

    def between_cores(self, tile):
        core = self.ring.spot["core"]
        copy = self.ring.cross("core", self.tiles.at[1 - core, tile], self.core_land.at[tile])
        yield link_time("core", *self.tiles.shape[2:])
        copy.wait()
        self.add(tile, self.core_land.at[tile])
        self.ready.add(tile)
        if {self.place(0, 0), self.place(1, 0)} <= self.ready and not self.started:
            self.started = True
            self.running.add(self.near())
        if {self.place(0, 1), self.place(1, 1)} <= self.ready:
            spot = self.ring.spot[self.first]
            self.keep(1, self.place(spot, 1))
            self.keep(2, self.place(1 - spot, 1))

    def near(self):
        spot = self.ring.spot[self.first]
        source = self.tiles.at[self.ring.spot["core"], self.place(1 - spot, 0)]
        copy = self.ring.cross(self.first, source, self.near_land)
        yield link_time(self.first, *self.tiles.shape[2:])
        copy.wait()
        self.keep(0, self.place(spot, 0), self.near_land)

    def keep(self, index, tile, other=None):
        if other is not None:
            self.add(tile, other)
        source = self.tiles.at[self.ring.spot["core"], tile]
        self.stores.start(("sum", self.first, index), source, self.result.at[index])


def expert_kernel(
    experts, remote, inbound, grows, router_rows, first, second,
    ret_out, dh_out, grad_first, grad_second, grad_router,
    router, router_turned, router_sum, first_v, second_v, inbound_v, grows_v, inbound_t, dret, dret_t, probs, pre, dact, act, dpre, ret, dinb, ret_v, dh_v, sums, core_land, near_land,
    in_sems, out_sems, send_sems, recv_sems,
):
    rows, width = inbound_v.shape
    hidden = first.shape[1]
    step = width
    tiles = hidden // step
    loads, stores = Loads(in_sems), Loads(out_sems)
    capacity = rows // experts
    half_rows = rows // 2
    if remote:
        ring = Ring(send_sems, recv_sems)
        ring.greet(("core", "x", "y"))
        arriving = ring.scatter(inbound, inbound_v)
        loads.start("inbound", inbound.at[ring.block(ring.expert, capacity), :], inbound_v.at[ring.slot(0, capacity), :])
    else:
        loads.start("inbound", inbound, inbound_v)
        arriving = []
    loads.start("grows", grows, grows_v)
    for f in range(tiles):
        cols = slice(f * step, (f + 1) * step)
        loads.start(("first", f), first.at[:, cols], first_v.at[:, cols])
        loads.start(("second", f), second.at[cols, :], second_v.at[cols, :])
    me = lax.axis_index("expert")
    lane = lax.broadcasted_iota(jnp.int32, (1, LANES), 1)
    mine = lane == me
    root = (2.0 / jnp.pi) ** 0.5
    router_sum[...] = jnp.zeros_like(router_sum)
    router[...] = jnp.zeros_like(router)
    router[0:experts, :] = router_rows[...]
    for cols in column_tiles(width, LANES):
        router_turned[cols, :] = router[:, cols].T
    loads.wait("inbound", "grows")
    returning = []
    for side in range(2):
        start = side * half_rows
        here = slice(start, start + half_rows)
        for copy in (arriving[:1], arriving[1:])[side]:
            copy.wait_recv()

        def route(r, start=start):
            r = pl.ds(pl.multiple_of(start + r.start, 16), r.size)
            logits = jnp.where(lane < experts, dot(inbound_v[r, :], router_turned[...]), -1e30)
            expo = jnp.exp(logits - jnp.max(logits, axis=-1, keepdims=True))
            prob = expo / jnp.sum(expo, axis=-1, keepdims=True)
            probs[r, :] = prob
            gate = jnp.sum(jnp.where(mine, prob, 0.0), axis=-1, keepdims=True)
            dret[r, :] = (gate * grows_v[r, :].astype(F32)).astype(BF16)

        row_loop(half_rows, half_rows // 2, route)
        for f in range(tiles):
            cols = slice(f * step, (f + 1) * step)
            if side == 0:
                loads.wait(("first", f), ("second", f))
            for c in range(0, step, 256):
                tile = slice(f * step + c, f * step + c + 256)
                pre[:, c : c + 256] = dot(inbound_v[here, :], first_v[:, tile])
                dact[:, c : c + 256] = dot_nt(dret[here, :], second_v[tile, :])

            def middle(r, start=start, cols=cols):
                u = pre[r, :]
                square = u * u
                t = jnp.tanh(u * (root + (root * 0.044715) * square))
                half = 0.5 + 0.5 * t
                out = pl.ds(pl.multiple_of(start + r.start, 16), r.size)
                act[out, cols] = (u * half).astype(BF16)
                slope = half + (u * (0.5 * root + (1.5 * root * 0.044715) * square)) * (1.0 - t * t)
                dpre[out, cols] = (dact[r, :] * slope).astype(BF16)

            row_loop(half_rows, 16, middle, 2)
            for c in range(0, width, 256):
                tile = slice(c, c + 256)
                one, two = dot(act[here, cols], second_v[cols, tile]), dot_nt(dpre[here, cols], first_v[tile, cols])
                if f:
                    one, two = one + ret[:, tile], two + dinb[:, tile]
                ret[:, tile] = one
                dinb[:, tile] = two

        def finish(r, start=start):
            out = pl.ds(pl.multiple_of(start + r.start, 16), r.size)
            result = ret[r, :].astype(BF16).astype(F32)
            prob = probs[out, :]
            gate = jnp.sum(jnp.where(mine, prob, 0.0), axis=-1, keepdims=True)
            dgate = jnp.sum(result * grows_v[out, :].astype(F32), axis=-1, keepdims=True)
            dlogits = (prob * (jnp.where(mine, 1.0, 0.0) - gate) * dgate).astype(BF16)
            ret_v[out, :] = (gate * result).astype(BF16)
            dh_v[out, :] = (dinb[r, :].astype(BF16).astype(F32) + dot(dlogits, router[...])).astype(BF16)
            router_sum[...] += dot_tn(dlogits, inbound_v[out, :])

        row_loop(half_rows, half_rows // 2, finish)
        if remote:
            target = dh_out.at[ring.block(ring.expert, capacity), :]
            for k in ((1,), (2, 3))[side]:
                source = dh_v.at[ring.slot(k, capacity, ring.peers[k]), :]
                returning.append(ring.send(source, target, ring.dp, ring.peers[k]))
            if side == 0:
                stores.start("dh", dh_v.at[ring.slot(0, capacity), :], target)
        elif side:
            stores.start("dh", dh_v, dh_out)
    stores.start("ret", ret_v, ret_out)
    grad_router[...] = router_sum[0:8, :]
    for copy in arriving:
        copy.wait_send()
    for c in range(width // LANES):
        cols = slice(c * LANES, (c + 1) * LANES)
        inbound_t[cols, :] = inbound_v[:, cols].T
        dret_t[cols, :] = dret[:, cols].T

    running = Running()
    if remote:
        expert_sums = [
            ExpertSum(ring, running, sums.at[j], core_land.at[j], near_land.at[j], axis, out, stores)
            for j, (axis, out) in enumerate((("x", grad_first), ("y", grad_second)))
        ]
    for i in range(tiles):
        for j, (left, right) in enumerate(((inbound_t, dpre), (dret_t, act))):
            f = expert_sums[j].order[i] if remote else i
            for cols in column_tiles(step):
                total = dot(left[...], right[:, f * step + cols.start : f * step + cols.stop]).astype(BF16)
                for c in range(cols.start, cols.stop, LANES):
                    b, at = divmod(c, step // 2)
                    sums[j, b, f, :, at : at + LANES] = total[:, c - cols.start : c - cols.start + LANES]
            if not remote:
                for b in range(2):
                    cols = slice(f * step + b * (step // 2), f * step + (b + 1) * (step // 2))
                    stores.start(("sum", j, b, f), sums.at[j, b, f], (grad_first, grad_second)[j].at[:, cols])
            running.tick(1.6)
            if remote:
                expert_sums[j].start(f)
    running.drain()
    for copy in returning:
        copy.wait()
    stores.drain()


def span(start, size):
    return pl.ds(pl.multiple_of(start, size), size)


def add_into(ref, rows, lanes, others, target=None):
    step = 48 if rows.size % 64 else 64
    for i in range(rows.size // step):
        here = pl.ds(pl.multiple_of(rows.start + i * step, 16), step)
        part = slice(i * step, (i + 1) * step)
        if len(others) == 1:
            total = ref[here, lanes] + others[0][part, :]
        else:
            total = ref[here, lanes].astype(F32) + sum(other[part, :].astype(F32) for other in others)
        if target is None:
            ref[here, lanes] = total.astype(BF16)
        else:
            target[here, :] = total.astype(BF16)


def reduce_matrix(ring, local, result, core_land, landing, axes, stores, ready):
    size = local.shape[0]
    half = size // 2
    core = ring.spot["core"]
    mine, other = span(core * half, half), span((1 - core) * half, half)
    copy = ring.cross("core", local.at[:, other], core_land)
    yield link_time("core", size, half)
    copy.wait()
    pl.semaphore_signal(ready, inc=1, device_id=(ring.partner["core"], ring.expert), device_id_type=pl.DeviceIdType.MESH)
    add_into(local, pl.ds(0, size), mine, [core_land])
    base, count, row, trail = 0, size, 0, []
    for axis in axes:
        parts = ring.experts if axis == "z" else 2
        part = count // parts
        lands = [landing.at[row + k * part : row + (k + 1) * part, :] for k in range(parts - 1)]
        if axis == "z":
            spot = ring.expert
            copies = [ring.send(local.at[span(base + e * part, part), mine], lands[k], ring.dp, e) for k, e in enumerate(ring.others())]
        else:
            spot = ring.spot[axis]
            copies = [ring.cross(axis, local.at[span(base + (1 - spot) * part, part), mine], lands[0])]
        yield link_time(axis, part, half)
        for copy in copies:
            copy.wait()
        base, count, row = base + spot * part, part, row + (parts - 1) * part
        here = span(base, count)
        add_into(local, here, mine, lands, core_land if axis == axes[-1] else None)
        trail.append((axis, here))
    for axis, here in reversed(trail):
        block = core_land.at[here, :]
        if axis == "z":
            copies = [ring.send(block, block, ring.dp, e) for e in ring.others()]
        else:
            copies = [ring.cross(axis, block, block)]
        yield link_time(axis, here.size, half)
        for copy in copies:
            copy.wait()
    pl.semaphore_wait(ready, 1)
    copy = ring.cross("core", core_land, local.at[:, mine])
    yield link_time("core", size, half)
    copy.wait()
    stores.start(("mine", stores.count), core_land, result.at[:, mine])
    stores.start(("other", stores.count), local.at[:, other], result.at[:, other])


def reduce_expert(ring, part, keep, extra, first, result, sems):
    size, block = part.shape[1], part.shape[2]
    second = "y" if first == "x" else "x"
    cols = [slice(i * block, (i + 1) * block) for i in range(2)]
    copies = [ring.cross(first, part.at[2], extra.at[:, cols[1]])]
    copies += [pltpu.make_async_copy(part.at[i], keep.at[:, cols[i]], sems.at[i]) for i in range(2)]
    for copy in copies[1:]:
        copy.start()
    yield link_time(first, size, block)
    for copy in copies:
        copy.wait()
    add_into(keep, pl.ds(0, size), cols[1], [extra.at[:, cols[1]]])
    spot = ring.spot[second]
    copy = ring.cross(second, keep.at[:, span((1 - spot) * block, block)], extra.at[:, cols[0]])
    yield link_time(second, size, block)
    copy.wait()
    stay = span(spot * block, block)
    add_into(keep, pl.ds(0, size), stay, [extra.at[:, cols[0]]])
    copy = pltpu.make_async_copy(keep.at[:, stay], result, sems.at[2])
    copy.start()
    copy.wait()


def reduce_small(ring, local, landing):
    for k, name in enumerate(("core", "x", "y")):
        copy = ring.cross(name, local, landing.at[k])
        yield link_time(name, *local.shape, 4)
        copy.wait()
        local[...] += landing[k]
    copies = [ring.send(local, landing.at[3 + ring.expert], ring.dp, e) for e in ring.others()]
    landing[3 + ring.expert] = local[...]
    yield link_time("z", *local.shape, 4)
    for copy in copies:
        copy.wait()
    total = landing[3]
    for e in range(1, ring.experts):
        total = total + landing[3 + e]
    local[...] = total


class Running:
    DELAY = 1.5

    def __init__(self):
        self.steps = []
        self.now = 0.0
        self.free = {}

    def land(self, entry, use):
        if use is None:
            self.steps = [e for e in self.steps if e is not entry]
            return
        link, time = use
        self.free[link] = max(self.now, self.free.get(link, 0.0)) + time
        entry[1] = self.free[link] + self.DELAY

    def add(self, steps, rank=0):
        entry = [steps, 0.0, rank]
        self.steps.append(entry)
        self.land(entry, next(steps))

    def advance(self, entry):
        self.now = max(self.now, entry[1]) + 0.5
        entry[2] += 1
        self.land(entry, next(entry[0], None))

    def tick(self, time):
        self.now += time
        while landed := [e for e in self.steps if e[1] <= self.now]:
            self.advance(min(landed, key=lambda e: (e[2], e[1])))

    def finish(self, steps):
        while any(e[0] is s for e in self.steps for s in steps):
            self.advance(min(self.steps, key=lambda e: e[1]))

    def drain(self):
        while self.steps:
            self.advance(min(self.steps, key=lambda e: e[1]))
            self.tick(0.0)


def link_time(name, rows, columns, itemsize=2):
    rate = {"core": 270e3, "x": 50e3, "y": 50e3, "z": 11.25e3}[name]
    return name, rows * columns * itemsize / rate


PLAN = (
    ("yxz", 2), ("xyz", 2), ("yxz", 3), ("xyz", 4), ("xyz", -1), ("yxz", -1), ("yxz", 6), ("xyz", -2),
)


def backward_kernel(
    targets, length, memory_length, heads, remote,
    dh_rows, ret_rows, place_column, mask, buckets, gain_one, gain_two, gain_three, grad_router, cotangent, tokens, h1, q1, k1, v1, c1, h2, q2, c2, x1, x2, p1, p2,
    k2, v2, memory, wq, wk, wv, wo, cq, ck, cv, co, part_first, part_second,
    *rest,
):
    grad_refs, rest = rest[:8], rest[8:]
    (
        output_out, grad_tokens_out, grad_memory_out, dv2_out, sum_first, sum_second, small,
        rows_v, ret_v, acts, x2_v, p1_v, weights_v, p2_v, kv_v, wide, grads, dscores, ds, dsum, gain_acc, table_v, core_land, landing, small_land, in_sems, out_sems, ring_sems, send_sems, recv_sems, expert_sems, ready,
    ) = rest
    rows, width = x2_v.shape
    pairs = heads // 2
    first_v, q2_v, dctx2, dq, dk, dv, q1_v, k1_v, v1_v, ctx_v, norm_v, do, dctx1, _ = [acts.at[i * rows : (i + 1) * rows, :] for i in range(14)]
    dv2, dk2 = acts.at[6 * rows : 10 * rows, :], acts.at[10 * rows : 14 * rows, :]
    x1_v, du, dx = wide.at[0:rows, :], wide.at[rows : 2 * rows, :], wide.at[2 * rows : 3 * rows, :]
    spare = (dctx2, q2_v)
    gv = wide.at[0:width, :]
    memory_slots, dv2_slots = (rows_v.at[0:memory_length, :], dk2.at[3 * rows : 4 * rows, :]), (do, dctx1)
    loads, stores, running = Loads(in_sems), Loads(out_sems), Running()
    loads.start("rows", dh_rows, rows_v)
    loads.start("cot", cotangent, first_v)
    loads.start("x2", x2, x2_v)
    loads.start("c2", c2, ctx_v)
    loads.start("co", co, weights_v.at[0])

    def fetch(t, sources, first=0):
        slot = t % 2
        m = pl.ds(t * memory_length, memory_length)
        for index, source in enumerate(sources, first):
            target = (p2_v.at[slot], kv_v.at[0, slot], kv_v.at[1, slot], memory_slots[slot])[index]
            copy = pltpu.make_async_copy(source.at[t] if index == 0 else source.at[m, :], target, ring_sems.at[index, slot])
            copy.start()
            yield copy

    fetched = list(fetch(0, (p2, k2, v2)))
    for name, source, target in (
        ("q2", q2, q2_v), ("cq", cq, weights_v.at[1]), ("h2", h2, norm_v), ("wo", wo, weights_v.at[2]),
        ("p1", p1, p1_v), ("q1", q1, q1_v), ("k1", k1, k1_v), ("v1", v1, v1_v), ("ck", ck, weights_v.at[3]),
        ("cv", cv, weights_v.at[4]),
    ):
        loads.start(name, source, target)
    if remote:
        ring = Ring(send_sems, recv_sems)
        ring.greet(("core", "x", "y"))
        capacity = rows_v.shape[0] // ring.experts
        mine = ring.block(ring.expert, capacity)
        ret_copies = [
            ring.send(ret_rows.at[ring.slot(k, capacity, e), :], ret_v.at[mine, :], ring.dp, e) for k, e in enumerate(ring.peers) if k
        ]
        loads.start("ret", ret_rows.at[ring.slot(0, capacity), :], ret_v.at[mine, :])
        expert_sums = [
            reduce_expert(ring, part_first, grads.at[0], grads.at[2], "x", sum_first, expert_sems.at[0]),
            reduce_expert(ring, part_second, grads.at[1], grads.at[5], "y", sum_second, expert_sems.at[1]),
        ]
        for steps in expert_sums:
            running.add(steps, -5)
        running.free["z"] = 20.0
    else:
        ret_copies, expert_sums = [], []
        loads.start("ret", ret_rows, ret_v)

    gain = [g[...].astype(F32).reshape(1, -1) for g in (gain_one, gain_two, gain_three)]
    low_lane, low, high = half_masks()
    gain_acc[...] = jnp.zeros_like(gain_acc)
    started = []

    def total_of(index):
        if remote:
            axes, rank = PLAN[len(started)]
            lands = core_land.at[index], landing.at[index]
            running.add(reduce_matrix(ring, grads.at[index], grad_refs[index], *lands, axes, stores, ready.at[index]), rank)
        else:
            stores.start(("grad", index), grads.at[index], grad_refs[index])
        started.append(index)

    def inner_grad(index, left, right):
        for c in range(width // 256):
            cols = slice(c * 256, (c + 1) * 256)
            grads[index, cols, :] = dot_tn(left[:, cols], right[...]).astype(BF16)
        total_of(index)

    def back_through(values, index, base, target):
        def one(r):
            back, gain_rows = norm_back(values[r, :].astype(F32), gain[index], du[r, :])
            total = base[r, :].astype(F32) + back
            target[r, :] = total
            if index:
                do[r, :] = total.astype(BF16)
            gain_acc[index] += gain_rows

        row_loop(rows, 32, one, 2)

    loads.wait("rows", "cot", "x2")

    def gathered(cols, values):
        du[:, cols] = values

    collect(place_column, rows_v, gathered)
    fetched += list(fetch(0, (memory,), 3))
    back_through(x2_v, 2, first_v, dx)
    loads.start("tokens", tokens, first_v)
    loads.wait("c2", "co")
    inner_grad(7, ctx_v, do)
    loads.start("c1", c1, ctx_v)

    def out_back(slot, target):
        for cols in column_tiles(width):
            target[:, cols] = dot_nt(do[...], weights_v[slot, cols, :]).astype(BF16)

    out_back(0, dctx2)
    running.tick(4.9)
    loads.start("wq", wq, weights_v.at[0])
    loads.wait("q2")
    for t in range(targets):
        slot = t % 2
        ahead = list(fetch(t + 1, (p2, k2, v2, memory))) if t + 1 < targets else []
        if t >= 2:
            stores.wait(("dv2", t - 2))
        for copy in fetched:
            copy.wait()
        fetched = ahead
        r = slice(t * length, (t + 1) * length)
        for pair in range(pairs):
            lanes = slice(pair * LANES, (pair + 1) * LANES)
            side = pair % 2
            grad_rows = stacked(dctx2[r, lanes], low, high)
            dscores[side] = dot_nt(grad_rows, kv_v[1, slot, :, lanes])
            dv2_slots[slot][:, lanes] = dot_tn(p2_v[slot, pair], grad_rows).astype(BF16)
            for chunk in range(2 * length // 32):
                part = slice(chunk * 32, (chunk + 1) * 32)
                prob = p2_v[slot, pair, part, :].astype(F32)
                dprob = dscores[side, part, :]
                inner = jnp.sum(prob * dprob, axis=-1, keepdims=True)
                ds[t, pair, part, :] = (prob * (dprob - inner)).astype(BF16)
            back = dot(ds[t, pair], kv_v[0, slot, :, lanes])
            dq[r, lanes] = jnp.where(low_lane, back[:length], back[length:]).astype(BF16)
            if side:
                running.tick(1.26)
        stores.start(("dv2", t), dv2_slots[slot], dv2_out.at[pl.ds(t * memory_length, memory_length), :])
        for c in range(width // 256):
            cols = slice(c * 256, (c + 1) * 256)
            part = dot_tn(memory_slots[slot][:, cols], dv2_slots[slot][...])
            if t:
                part = part + gv[cols, :]
            if t + 1 < targets:
                gv[cols, :] = part
            else:
                grads[6, cols, :] = part.astype(BF16)
        running.tick(0.84)
    total_of(6)
    loads.start("x1", x1, x1_v)
    memory_copies = []
    for t in range(targets):
        source = memory.at[pl.ds(t * memory_length, memory_length), :]
        memory_copies.append(pltpu.make_async_copy(source, kv_v.at[t // 2, t % 2], ring_sems.at[1 + t // 2, t % 2]))
        memory_copies[-1].start()
    for t in range(max(0, targets - 2), targets):
        stores.wait(("dv2", t))
    loads.wait("h2", "cq", "x1")
    inner_grad(4, norm_v, dq)
    loads.start("h1", h1, norm_v)

    for cols in column_tiles(width):
        du[:, cols] = dot_nt(dq[...], weights_v[1, cols, :])
    loads.start("wk", wk, weights_v.at[1])
    running.tick(1.75)
    back_through(x1_v, 1, dx, dx)
    running.tick(1.05)
    loads.wait("c1", "wo")
    inner_grad(3, ctx_v, do)
    out_back(2, dctx1)
    loads.start("wv", wv, weights_v.at[2])
    running.tick(1.75)
    loads.wait("p1", "q1", "k1", "v1")
    for t in range(targets):
        r = slice(t * length, (t + 1) * length)
        allowed = allowed_of(mask[t : t + 1, :], length)
        for pair in range(pairs):
            lanes = slice(pair * LANES, (pair + 1) * LANES)
            side = pair % 2
            grad_rows = stacked(dctx1[r, lanes], low, high)
            both = dot_nt(grad_rows, v1_v[r, lanes])
            scratch = p2_v.at[1, side]
            for half in range(2):
                part = slice(half * length, (half + 1) * length)
                prob = p1_v[t, pair, part, :].astype(F32)
                dprob = both[part]
                inner = jnp.sum(prob * dprob, axis=-1, keepdims=True)
                score = jnp.where(allowed, prob * (dprob - inner), 0.0).astype(BF16)
                scratch[part, :length] = score
                wide_score = score.astype(F32)
                dsum[pair, part, :] = wide_score if t == 0 else dsum[pair, part, :] + wide_score
            dv[r, lanes] = dot_tn(p1_v[t, pair], grad_rows).astype(BF16)
            dk[r, lanes] = dot_tn(scratch[:, :length], stacked(q1_v[r, lanes], low, high)).astype(BF16)
            back = dot(scratch[:, :length], k1_v[r, lanes])
            dq[r, lanes] = jnp.where(low_lane, back[:length], back[length:]).astype(BF16)
        running.tick(1.75)
    loads.wait("h1", "wq", "wk", "wv", "tokens")
    running.finish(expert_sums)
    for index, right in enumerate((dq, dk, dv)):
        inner_grad(index, norm_v, right)
        running.tick(0.84)
    loads.start("dv2", dv2_out, dv2)

    for t in range(targets):
        r = slice(t * length, (t + 1) * length)
        m = slice(t * memory_length, (t + 1) * memory_length)
        for pair in range(pairs):
            lanes = slice(pair * LANES, (pair + 1) * LANES)
            dk2[m, lanes] = dot_tn(ds[t, pair], stacked(q2_v[r, lanes], low, high)).astype(BF16)
        running.tick(0.84)
    for copy in memory_copies:
        copy.wait()
    for c in range(width // 256):
        cols = slice(c * 256, (c + 1) * 256)
        total = 0.0
        for t in range(targets):
            m = slice(t * memory_length, (t + 1) * memory_length)
            total = total + dot_tn(kv_v[t // 2, t % 2, :, cols], dk2[m, :])
        grads[5, cols, :] = total.astype(BF16)
        running.tick(0.91)
    total_of(5)

    for cols in column_tiles(width):
        du[:, cols] = (
            dot_nt(dq[...], weights_v[0, cols, :]) + dot_nt(dk[...], weights_v[1, cols, :]) + dot_nt(dv[...], weights_v[2, cols, :])
        )
    for copy in ret_copies:
        copy.wait()
    loads.wait("ret")

    def output_columns(cols, values):
        dq[:, cols] = (x2_v[:, cols] + values).astype(BF16)

    collect(place_column, ret_v, output_columns)
    stores.start("output", dq, output_out)
    running.tick(1.4)
    running.tick(1.75)
    back_through(first_v, 0, dx, dx)
    stores.start("tokens", dx, grad_tokens_out)
    running.tick(1.05)
    small[...] = jnp.zeros_like(small)
    for i in range(3):
        small[i : i + 1, :] = jnp.sum(gain_acc[i], axis=0, keepdims=True)
    small[8:16, :] = grad_router[0:8, :]
    table_v[...] = jnp.zeros_like(table_v)

    def table_rows(b, carry):
        hit = buckets[...] == b
        for head in range(heads):
            start = (head % 2) * length
            part = jnp.where(hit, dsum[head // 2, start : start + length, :], 0.0)
            table_v[pl.ds(head, 1), :] = jnp.sum(part, axis=0, keepdims=True)
        sums = jnp.sum(table_v[0:16, :], axis=-1, keepdims=True)
        here = lax.broadcasted_iota(jnp.int32, (1, LANES), 1) == b
        table_v[16:32, :] += jnp.where(here, sums, 0.0)
        return carry

    for b in range(0, 32, 16):
        lax.fori_loop(b, b + 16, table_rows, 0)
        running.tick(1.4)
    small[16:24, 0:LANES] = table_v[16:24, :]
    small[16:24, LANES : 2 * LANES] = table_v[24:32, :]
    if remote:
        running.add(reduce_small(ring, small, small_land), 0)
    loads.wait("ck", "cv", "dv2")
    for t in range(targets):
        buffer = spare[t % 2]
        if t >= 2:
            stores.wait(("memory", t - 2))
        m = slice(t * memory_length, (t + 1) * memory_length)
        for cols in column_tiles(width):
            buffer[:, cols] = (dot_nt(dk2[m, :], weights_v[3, cols, :]) + dot_nt(dv2[m, :], weights_v[4, cols, :])).astype(BF16)
            running.tick(0.56)
        stores.start(("memory", t), buffer, grad_memory_out.at[pl.ds(t * memory_length, memory_length), :])
    running.drain()
    stores.drain()


def finish_kernel(*refs):
    sources, small, targets, table, routed, gain_refs = refs[:13], refs[13], refs[14:27], refs[27], refs[28], refs[29:32]
    narrow, wide, parts, first, second, *passed, in_sems, out_sems = refs[32:]
    loads, stores = Loads(in_sems), Loads(out_sems)
    landing = [narrow.at[i] for i in range(8)] + [parts.at[i] for i in range(2)] + passed
    order = [10, 11, 0, 1, 2, 12, 3, 4, 5, 6, 7, 8, 9]

    def ahead():
        if order:
            i = order.pop(0)
            loads.start(i, sources[i], landing[i])

    def arrive(*names):
        loads.wait(*names)
        for name in names:
            ahead()
            if name >= 10:
                stores.start(name, passed[name - 10], targets[name])

    for _ in range(4):
        ahead()
    for i in range(8):
        arrive(*{0: (10, 11, 0), 3: (12, 3)}.get(i, (i,)))

        def widen(r, i=i):
            wide[i, r, :] = narrow[i, r, :].astype(F32)

        row_loop(wide.shape[1], 64, widen)
        stores.start(i, wide.at[i], targets[i])
    arrive(8, 9)

    def widen_part(r):
        first[r, :] = parts[0, r, :].astype(F32)

    row_loop(first.shape[0], 64, widen_part)
    stores.start(8, first, targets[8])
    for c in range(0, first.shape[0], LANES):
        second[:, c : c + LANES] = parts[1, c : c + LANES, :].astype(F32).T
    stores.start(9, second, targets[9])
    heads, count = table.shape
    table[0:8, :] = small[16:24, 0:count]
    table[8:heads, :] = small[16 : 16 + heads - 8, LANES : LANES + count]
    routed[...] = small[8 : 8 + routed.shape[0], :]
    for i, ref in enumerate(gain_refs):
        ref[...] = small[i : i + 1, :].reshape(-1)
    stores.drain()


def params(**more):
    return pltpu.CompilerParams(vmem_limit_bytes=VMEM_LIMIT, **more)


def on_device(
    tokens, memory, target_mask, buckets, expert_ids, slots, gain_self, w_query, w_key, w_value, w_output, rel_table, gain_cross,
    c_query, c_key, c_value, c_output, gain_moe, router, expert_in, expert_out, cotangent,
):
    rows, width = tokens.shape
    targets, length = target_mask.shape
    bucket_count, heads = rel_table.shape
    memory_length = memory.shape[0] // targets
    pairs = heads // 2
    experts = lax.axis_size("expert")
    hidden = expert_in.shape[2]
    capacity = (5 * rows + 4 * experts - 1) // (4 * experts)
    slot_rows = experts * capacity
    place = jnp.where(slots < capacity, expert_ids * capacity + slots, -1)
    place_row, place_column = place.reshape(1, rows), place.reshape(rows, 1)
    gains = [gain_self, gain_cross, gain_moe]
    weights = (w_query, w_key, w_value, w_output, c_query, c_key, c_value, c_output)

    remote = lax.axis_size("dp") == 8 and experts == 4 and hidden == 4 * width

    def exchange(buffer):
        if remote:
            return buffer
        buffer = buffer.reshape(experts, capacity, width)
        return lax.all_to_all(buffer, "expert", split_axis=0, concat_axis=0, tiled=True).reshape(slot_rows, width)

    def remote_params(collective_id):
        return params(collective_id=collective_id, has_side_effects=True) if remote else params()

    row_shape = jax.ShapeDtypeStruct((slot_rows, width), BF16)
    act_shape = ((rows, width), BF16)
    wide_shape = ((rows, width), F32)
    key_shape = ((targets * memory_length, width), BF16)
    kept = (
        [act_shape] * 8
        + [wide_shape] * 2
        + [((targets, pairs, 2 * length, length), BF16), ((targets, pairs, 2 * length, memory_length), BF16), key_shape, key_shape]
        + [((slot_rows, width), BF16)] * 2
    )
    h1, q1, k1, v1, c1, h2, q2, c2, x1, x2, p1, p2, k2, v2, sent, grows = pl.pallas_call(
        functools.partial(forward_kernel, targets, length, memory_length, heads, remote),
        out_shape=[jax.ShapeDtypeStruct(*k) for k in kept],
        in_specs=[VMEM, ANY, ANY, VMEM, VMEM, VMEM, VMEM, VMEM, VMEM, ANY] + [ANY] * 8,
        out_specs=[ANY] * len(kept),
        scratch_shapes=[pltpu.VMEM((rows, width), BF16), pltpu.VMEM(*key_shape), pltpu.VMEM((8, width, width), BF16)]
        + [pltpu.VMEM(*k) for k in kept]
        + [
            pltpu.VMEM((pairs, 2 * length, length), F32),
            pltpu.VMEM((heads * bucket_count, length), F32),
            pltpu.VMEM((2, 2 * length, memory_length), F32),
            pltpu.SemaphoreType.DMA((11,)),
            pltpu.SemaphoreType.DMA((len(kept),)),
            pltpu.SemaphoreType.DMA((experts - 1,)),
            pltpu.SemaphoreType.DMA((experts - 1,)),
        ],
        compiler_params=remote_params(1),
        name="forward",
    )(rel_table.T, tokens, memory, target_mask, buckets, *gains, place_row, cotangent, *weights)

    sent, grows = exchange(sent), exchange(grows)
    tiles = hidden // width
    half = width // 2
    weight_grad = jax.ShapeDtypeStruct((3, width, half) if remote else (width, hidden), BF16)
    row_scratch, half_scratch = pltpu.VMEM((slot_rows, width), BF16), pltpu.VMEM((slot_rows // 2, width), F32)
    ret, dh, grad_first, grad_second, grad_router = pl.pallas_call(
        functools.partial(expert_kernel, experts, remote),
        out_shape=[row_shape, row_shape, weight_grad, weight_grad, jax.ShapeDtypeStruct((8, width), F32)],
        in_specs=[ANY, ANY, VMEM, ANY, ANY],
        out_specs=[ANY, ANY, ANY, ANY, VMEM],
        scratch_shapes=[
            pltpu.VMEM((LANES, width), BF16),
            pltpu.VMEM((width, LANES), BF16),
            pltpu.VMEM((LANES, width), F32),
            pltpu.VMEM((width, hidden), BF16),
            pltpu.VMEM((hidden, width), BF16),
            row_scratch,
            row_scratch,
            pltpu.VMEM((width, slot_rows), BF16),
            row_scratch,
            pltpu.VMEM((width, slot_rows), BF16),
            pltpu.VMEM((slot_rows, LANES), F32),
            half_scratch,
            half_scratch,
            pltpu.VMEM((slot_rows, hidden), BF16),
            pltpu.VMEM((slot_rows, hidden), BF16),
            half_scratch,
            half_scratch,
            row_scratch,
            row_scratch,
            pltpu.VMEM((2, 2, tiles, width, half), BF16),
            pltpu.VMEM((2, tiles, width, half), BF16),
            pltpu.VMEM((2, width, half), BF16),
            pltpu.SemaphoreType.DMA((2 * tiles + 2,)),
            pltpu.SemaphoreType.DMA((4 * tiles + 2,)),
            pltpu.SemaphoreType.DMA((2 * experts + 2 * tiles,)),
            pltpu.SemaphoreType.DMA((2 * experts + 2 * tiles,)),
        ],
        compiler_params=remote_params(2),
        name="experts",
    )(sent, grows, router.T, expert_in[0], expert_out[0])
    dh_rows, ret_rows = exchange(dh), exchange(ret)
    parts = (grad_first, grad_second)
    if not remote:
        parts = (ret, ret)

    square = (width, width)
    wide = pltpu.VMEM(*wide_shape)
    small_shape = (24, width)
    lands = 8 if remote else 1
    copies = 8 * (6 + 2 * (experts - 1)) + 2 * experts + 1 + 4
    block = jax.ShapeDtypeStruct((width, half), BF16)
    results = pl.pallas_call(
        functools.partial(backward_kernel, targets, length, memory_length, heads, remote),
        out_shape=[jax.ShapeDtypeStruct(square, BF16)] * 8
        + [
            jax.ShapeDtypeStruct((rows, width), BF16),
            jax.ShapeDtypeStruct((rows, width), F32),
            jax.ShapeDtypeStruct(memory.shape, BF16),
            jax.ShapeDtypeStruct(memory.shape, BF16),
            block,
            block,
            jax.ShapeDtypeStruct(small_shape, F32),
        ],
        in_specs=[ANY, ANY] + [VMEM] * 7 + [ANY] * 27,
        out_specs=[ANY] * 14 + [VMEM],
        scratch_shapes=[pltpu.VMEM((slot_rows, width), BF16)] * 2
        + [
            pltpu.VMEM((14 * rows, width), BF16),
            wide,
            pltpu.VMEM((targets, pairs, 2 * length, length), BF16),
            pltpu.VMEM((5,) + square, BF16),
            pltpu.VMEM((2, pairs, 2 * length, memory_length), BF16),
            pltpu.VMEM((2, 2, memory_length, width), BF16),
            pltpu.VMEM((3 * rows, width), F32),
            pltpu.VMEM((8,) + square, BF16),
            pltpu.VMEM((2, 2 * length, memory_length), F32),
            pltpu.VMEM((targets, pairs, 2 * length, memory_length), BF16),
            pltpu.VMEM((pairs, 2 * length, length), F32),
            pltpu.VMEM((3, 8, width), F32),
            pltpu.VMEM((32, LANES), F32),
            pltpu.VMEM((lands, width, half), BF16),
            pltpu.VMEM((lands, width - width // (4 * experts), half), BF16),
            pltpu.VMEM((experts + 3,) + small_shape, F32),
            pltpu.SemaphoreType.DMA((24,)),
            pltpu.SemaphoreType.DMA((28,)),
            pltpu.SemaphoreType.DMA((4, 2)),
            pltpu.SemaphoreType.DMA((copies,)),
            pltpu.SemaphoreType.DMA((copies,)),
            pltpu.SemaphoreType.DMA((2, 3)),
            pltpu.SemaphoreType.REGULAR((8,)),
        ],
        compiler_params=remote_params(0),
        name="backward",
    )(
        dh_rows, ret_rows, place_column, target_mask, buckets, *gains, grad_router, cotangent, tokens, h1, q1, k1, v1, c1, h2, q2, c2, x1, x2,
        p1, p2, k2, v2, memory, *weights, *parts,
    )
    summed, (output, grad_tokens, grad_memory, _, grad_first_sum, grad_second_sum), small = results[:8], results[8:14], results[-1]
    if not remote:
        summed, small = lax.psum((summed, small), ("dp", "expert"))
        grad_first_sum, grad_second_sum = (
            lax.psum_scatter(g, "dp", scatter_dimension=1, tiled=True) for g in (grad_first, grad_second)
        )
    wide_square = jax.ShapeDtypeStruct(square, F32)
    part_shape = grad_first_sum.shape
    finished = pl.pallas_call(
        finish_kernel,
        out_shape=[wide_square] * 8
        + [
            jax.ShapeDtypeStruct(part_shape, F32),
            jax.ShapeDtypeStruct(part_shape[::-1], F32),
            jax.ShapeDtypeStruct(output.shape, BF16),
            jax.ShapeDtypeStruct(grad_tokens.shape, F32),
            jax.ShapeDtypeStruct(grad_memory.shape, BF16),
            jax.ShapeDtypeStruct((heads, bucket_count), F32),
            jax.ShapeDtypeStruct((experts, width), F32),
        ]
        + [jax.ShapeDtypeStruct((width,), F32)] * 3,
        in_specs=[ANY] * 13 + [VMEM],
        out_specs=[ANY] * 8 + [ANY] * 5 + [VMEM] * 5,
        scratch_shapes=[
            pltpu.VMEM((8,) + square, BF16),
            pltpu.VMEM((8,) + square, F32),
            pltpu.VMEM((2,) + part_shape, BF16),
            pltpu.VMEM(part_shape, F32),
            pltpu.VMEM(part_shape[::-1], F32),
            pltpu.VMEM(output.shape, BF16),
            pltpu.VMEM(grad_tokens.shape, F32),
            pltpu.VMEM(grad_memory.shape, BF16),
            pltpu.SemaphoreType.DMA((13,)),
            pltpu.SemaphoreType.DMA((13,)),
        ],
        compiler_params=params(),
        name="finish",
    )(*summed, grad_first_sum, grad_second_sum, output, grad_tokens, grad_memory, small)
    wq_grad, wk_grad, wv_grad, wo_grad, cq_grad, ck_grad, cv_grad, co_grad, first, second, output, grad_tokens, grad_memory, table, routed, *gain_grads = finished
    return (
        output, grad_tokens, grad_memory, gain_grads[0], wq_grad, wk_grad, wv_grad, wo_grad, table.T, gain_grads[1], cq_grad, ck_grad, cv_grad,
        co_grad, gain_grads[2], routed.T, first[None], second[None],
    )


def solution(mesh):
    both, spread = P(("dp", "expert")), P(("dp", "expert"), None)
    placed = (
        (spread, spread, spread, P(), both, both) + (P(),) * 13 + (P("expert", None, None), P("expert", None, None), spread)
    )
    return jax.shard_map(
        on_device,
        mesh=mesh,
        in_specs=placed,
        out_specs=(spread, spread, spread) + (P(),) * 13 + (P("expert", None, "dp"), P("expert", "dp", None)),
        check_vma=False,
    )
```
